32 devices in a mesh: region: 4 (over z), tile: 8 (over y, x, core).
Axes of the slice: x: 2, y: 2, z: 4, core: 2. Of those that a mesh axis runs over, the one named last changes fastest.
Arguments:
- global_deriv: bfloat16 [6144, 32, 128], P(('region', 'tile')), may hold values from -0.15625 to 0.15625
- local_deriv: bfloat16 [6144, 5, 32], P(('region', 'tile')), may hold values from -4 to 4
- hit_weight: bfloat16 [6144, 32], P(('region', 'tile')), may hold values from 0.25 to 4
- hit_resid: bfloat16 [6144, 32], P(('region', 'tile')), may hold values from -6 to 6
- block_ids: int32 [6144, 32], P(('region', 'tile')), may hold values from 0 to 7
- hit_count: int32 [6144], P(('region', 'tile')), may hold values from 4 to 32
- track_region: int32 [6144, 1], P(('region', 'tile')), may hold values from 0 to 3; in each aligned block of 192 rows (0 to 191, 192 to 383, ...) at most 96 rows name the same one
- block_place: int32 [8], replicated, may hold values from 0 to 7, each once
Outputs:
- normal_matrix: float32 [4, 1024, 1024], P('region', 'tile')
- right_side: float32 [4, 1024], P('region', 'tile')
The draws below stay inside these ranges and needn't reach their ends.
Inputs may be any that keep to these rules, and one draw needn't show every extreme that they name: `track_region`: among the tracks of one device at most 96 share a region, and in every draw some device has exactly 96 tracks in some region. `block_place`: each position appears once.
All inputs are finite; a program needn't handle non-finite values.
Results may differ from the reference program's by a relative error of at most 0.0029.
Values may be sent and summed in bfloat16 or wider, within the bound.
No kernel may reach another device: no remote copies, remote signals or barrier semaphores. Data moves between devices by JAX's collectives and lax.ppermute only.
A program may use at most 128 MiB of HBM per device.

```python
import math
import jax
import jax.numpy as jnp
import numpy as np
from jax import lax

BS = 128
BR = 8
HITS = 32
TRK_DEV = 192
CAP = 96
TRACKS = 6144
N_REGION = 4
N_TILE = 8


def place_ends(array, rng, least, largest):
    spot = [jax.random.randint(jax.random.fold_in(rng, axis), (), 0, length) for axis, length in enumerate(array.shape)]
    longest = array.shape.index(max(array.shape))
    next_to = spot[:longest] + [(spot[longest] + 1) % array.shape[longest]] + spot[longest + 1:]
    return array.at[tuple(spot)].set(least).at[tuple(next_to)].set(largest)


def shard_levels(rng, shape, split, least, largest):
    factor_of = 1.0
    for position, shards_of in split:
        draws = jax.random.uniform(jax.random.fold_in(jax.random.fold_in(rng, 6), position), (shards_of,), jnp.float32, least / len(split), largest / len(split))
        factor_of = factor_of * jnp.repeat(jnp.exp(draws), shape[position] // shards_of).reshape((-1,) + (1,) * (len(shape) - 1 - position))
    return factor_of


def routed_block(stream_key, own, number, rows, count, top, reach, skew):
    order = jax.random.permutation(stream_key, count)
    heavy_load, common = portions_of(count, rows * top, reach, skew, True), portions_of(count, rows * top, reach, skew, False)
    places = jnp.arange(count)

    def named(lengths, offset_by):
        used = int((lengths > 0).sum())
        fixed = max(1, used // 4)
        passed = fixed + (places - fixed + offset_by * (used - fixed)) % max(1, count - fixed)
        return jnp.zeros((count,), jnp.int32).at[order[jnp.where(places < fixed, places, passed)]].set(jnp.asarray(lengths, jnp.int32))

    lengths = jnp.where(number % 4 == 0, named(heavy_load, number // 4), named(common, number - number // 4 - 1))
    mixed = jax.random.permutation(jax.random.fold_in(own, 3), count)
    giver, sink = mixed[0:count // 2 * 2:2], mixed[1:count // 2 * 2:2]
    slack = jnp.minimum(lengths[giver] - 1, reach - lengths[sink]) // 2
    slack = jnp.where((giver == order[0]) | (sink == order[0]) | (lengths[sink] == 0), 0, jnp.maximum(slack, 0))
    passed = jax.random.randint(jax.random.fold_in(own, 4), (count // 2,), 0, 1 << 20) % (slack + 1)
    lengths = lengths.at[giver].add(-passed).at[sink].add(passed)
    members = jnp.searchsorted(jnp.cumsum(lengths), jnp.arange(rows * top), side="right").astype(jnp.int32)
    listing = members.reshape(top, rows).T
    listing = listing[jax.random.permutation(jax.random.fold_in(own, 1), rows)]
    offset_by = jax.random.randint(jax.random.fold_in(own, 2), (rows, 1), 0, top)
    return jnp.take_along_axis(listing, (jnp.arange(top)[None, :] + offset_by) % top, axis=1)


def portions_of(amount, total, most, skew, full):
    weights = [(1 << 20) // math.isqrt(grade ** skew) + 1 for grade in range(1, amount + 1)]
    largest = most if full else min(most, max(-(-total // amount), total * weights[0] // sum(weights)))
    least = 1 if total - largest >= amount - 1 else 0
    holding, surplus = [largest] + [least] * (amount - 1), total - largest - least * (amount - 1)
    while surplus > 0:
        free = [i for i in range(1, amount) if holding[i] < largest] or [i for i in range(1, amount) if holding[i] < most]
        whole, budget = sum([weights[i] for i in free]), surplus
        for i in free:
            more = min(most - holding[i], max(1, budget * weights[i] // whole), surplus)
            holding[i] = holding[i] + more
            surplus = surplus - more
    return np.array(holding)


def noise(key, extent, deviation, most, split=(), kind=jnp.bfloat16):
    factor_of = shard_levels(key, extent, split, -0.22, 0.18) if split else 1.0
    array = jax.random.normal(key, extent, jnp.float32) * deviation * factor_of
    return jnp.minimum(jnp.maximum(array, -most), most).astype(kind)


def setup_inputs(seed: int = 0) -> dict:
    splits = jax.random.split(jax.random.key(seed), 9)
    global_deriv = noise(splits[0], (TRACKS, HITS, BS), (TRK_DEV * N_TILE) ** -0.5, 0.15625, ((0, 32),))
    local_deriv = noise(splits[1], (TRACKS, 5, HITS), 1.0, 4.0, ((0, 32),))
    hit_weight = jnp.clip(jnp.exp(math.log(4.0) - 2.7725887 * jax.random.uniform(splits[2], (TRACKS, HITS), jnp.float32) ** shard_levels(splits[2], (TRACKS, HITS), ((0, 32),), -0.2, 0.2)), 0.25, 4.0).astype(jnp.bfloat16)
    hit_resid = noise(splits[3], (TRACKS, HITS), 1.0, 6.0, ((0, 32),))
    block_ids = place_ends(jax.random.randint(splits[4], (TRACKS, HITS), 0, BR), jax.random.fold_in(splits[4], 1), 0, BR - 1).astype(jnp.int32)
    hit_count = place_ends(jax.random.randint(splits[5], (TRACKS,), 4, HITS + 1), jax.random.fold_in(splits[5], 1), 4, HITS).astype(jnp.int32)
    track_region_keys = jax.random.split(jax.random.fold_in(splits[6], 1), TRACKS // TRK_DEV)
    track_region_turns = jax.random.permutation(jax.random.fold_in(splits[6], 3), TRACKS // TRK_DEV)
    track_region = jax.vmap(lambda own, number: routed_block(jax.random.fold_in(splits[6], 2), own, number, TRK_DEV, N_REGION, 1, CAP, 2))(track_region_keys, track_region_turns).reshape((TRACKS, 1))
    block_place = jax.random.permutation(splits[7], BR).astype(jnp.int32)
    return dict(global_deriv=global_deriv, local_deriv=local_deriv, hit_weight=hit_weight, hit_resid=hit_resid, block_ids=block_ids, hit_count=hit_count, track_region=track_region, block_place=block_place)


def cholesky_fit(local_slopes, weight, misfit, live_hits):
    masked_w = live_hits * weight
    weighted_l = local_slopes * masked_w[:, None, :]
    gamma_mat = [[lax.optimization_barrier(jnp.sum(weighted_l[:, a, :] * local_slopes[:, b, :], axis=1)) + (1.0 if a == b else 0.0) for b in range(5)] for a in range(5)]
    beta_vec = [lax.optimization_barrier(jnp.sum(weighted_l[:, a, :] * misfit, axis=1)) for a in range(5)]
    factor = [[None for b in range(5)] for a in range(5)]
    for j in range(5):
        center = gamma_mat[j][j]
        for k in range(j):
            center = center - factor[j][k] * factor[j][k]
        factor[j][j] = jnp.sqrt(center)
        for i in range(j + 1, 5):
            offdiag = gamma_mat[i][j]
            for k in range(j):
                offdiag = offdiag - factor[i][k] * factor[j][k]
            factor[i][j] = offdiag / factor[j][j]
    solved = []
    solved_rhs = []
    for j in range(5):
        current = weighted_l[:, j, :]
        target = beta_vec[j]
        for k in range(j):
            current = current - factor[j][k][:, None] * solved[k]
            target = target - factor[j][k] * solved_rhs[k]
        solved.append(current / factor[j][j][:, None])
        solved_rhs.append(target / factor[j][j])
    scaled = jnp.stack(solved, axis=1)
    projection = solved[0] * solved_rhs[0][:, None]
    for k in range(1, 5):
        projection = projection + solved[k] * solved_rhs[k][:, None]
    hit_factor = masked_w * misfit - projection
    return (scaled, hit_factor, masked_w)

def fit_tracks(gderiv, packed, block_rows, counts, place):
    hit_slots = block_rows.shape[1]
    blocks = place.shape[0]
    live_hits = (jnp.arange(hit_slots)[None, :] < counts[:, None]).astype(jnp.float32)
    floats = packed.astype(jnp.float32)
    scaled, hit_factor, masked_w = cholesky_fit(floats[:, 0:5, :], floats[:, 5, :], floats[:, 6, :], live_hits)
    matches = (block_rows[:, :, None] == jnp.arange(blocks)[None, None, :]).astype(jnp.float32)
    placing = (place[:, None] == jnp.arange(blocks)[None, :]).astype(jnp.float32)
    onehot = jnp.einsum('nhb,bp->nhp', matches, placing, precision=lax.Precision.HIGHEST)
    gfloat = gderiv.astype(jnp.float32)
    expanded = scaled[:, :, :, None] * onehot[:, None, :, :]
    spread = jnp.einsum('nchp,nhi->ncpi', expanded, gfloat, precision=lax.Precision.HIGHEST).astype(jnp.bfloat16)
    weighted = (masked_w[:, :, None] * gfloat).astype(jnp.bfloat16)
    return (spread, weighted, hit_factor.astype(jnp.bfloat16), onehot)

def place_direct(weighted, gderiv, onehot):
    blocks = onehot.shape[2]
    block_size = gderiv.shape[2]
    flat_g = gderiv.reshape(-1, block_size)
    diagonal_part = jnp.zeros((blocks * block_size, blocks * block_size), jnp.float32)
    for column in range(blocks):
        picked = (weighted * onehot[:, :, column, None].astype(jnp.bfloat16)).reshape(-1, block_size)
        tile_sum = lax.dot_general(picked, flat_g, (((0,), (0,)), ((), ())), preferred_element_type=jnp.float32)
        diagonal_part = diagonal_part.at[column * block_size:(column + 1) * block_size, column * block_size:(column + 1) * block_size].set(tile_sum)
    return diagonal_part

def right_vector(hit_factor, gderiv, onehot):
    block_size = gderiv.shape[2]
    loads = (hit_factor[:, :, None] * onehot.astype(jnp.bfloat16)).reshape(-1, onehot.shape[2])
    summed = lax.dot_general(loads, gderiv.reshape(-1, block_size), (((0,), (0,)), ((), ())), preferred_element_type=jnp.float32)
    return summed.reshape(-1)

def reference(global_deriv, local_deriv, hit_weight, hit_resid, block_ids, hit_count, track_region, block_place):
    owning = track_region[:, 0]
    bound = N_REGION * N_TILE * CAP
    packed_all = jnp.concatenate([local_deriv, hit_weight[:, None, :], hit_resid[:, None, :]], axis=1)
    slab_width = BR * BS

    def region_term(index):
        inside = owning == index
        chosen = jnp.nonzero(inside, size=bound, fill_value=0)[0].astype(jnp.int32)
        total = jnp.sum(inside.astype(jnp.int32))
        filled = (jnp.arange(bound) < total).astype(jnp.int32)
        gderiv = jnp.take(global_deriv, chosen, axis=0)
        packed = jnp.take(packed_all, chosen, axis=0)
        block_rows = jnp.take(block_ids, chosen, axis=0)
        counts = jnp.take(hit_count, chosen, axis=0) * filled
        spread, weighted, hit_factor, onehot = fit_tracks(gderiv, packed, block_rows, counts, block_place)
        flat_spread = spread.reshape(-1, slab_width)
        schur = jnp.dot(flat_spread.T, flat_spread, preferred_element_type=jnp.float32)
        diagonal_part = place_direct(weighted, gderiv, onehot)
        return (diagonal_part - schur, right_vector(hit_factor, gderiv, onehot))
    normal_matrix, right_side = lax.map(region_term, jnp.arange(N_REGION).astype(jnp.int32))
    return (normal_matrix, right_side)
```

```python
import functools
import jax
import jax.numpy as jnp
from jax import lax
from jax.experimental import pallas as pl
from jax.experimental.pallas import tpu as pltpu
from jax.sharding import PartitionSpec as P

F32 = jnp.float32
BF16 = jnp.bfloat16
GROUP = 8
DEPTH = 256

NT = (((1,), (1,)), ((), ()))


def iota(shape, axis):
    return lax.broadcasted_iota(jnp.int32, shape, axis)


def fit(ld, weight, resid, counts):
    hits = weight.shape[0]
    live = iota(weight.shape, 0) < counts.astype(jnp.int32)
    masked_w = jnp.where(live, weight, 0.0)
    weighted_l = [v * masked_w for v in ld]
    gamma = [[None] * 5 for _ in range(5)]
    for a in range(5):
        for b in range(a + 1):
            gamma[a][b] = jnp.sum(weighted_l[a] * ld[b], axis=0, keepdims=True)
            if a == b:
                gamma[a][b] = gamma[a][b] + 1.0
    beta = [jnp.sum(weighted_l[a] * resid, axis=0, keepdims=True) for a in range(5)]
    factor = [[None] * 5 for _ in range(5)]
    inverse = [None] * 5
    for j in range(5):
        center = gamma[j][j]
        for k in range(j):
            center = center - factor[j][k] * factor[j][k]
        factor[j][j] = jnp.sqrt(center)
        inverse[j] = 1.0 / factor[j][j]
        for i in range(j + 1, 5):
            offdiag = gamma[i][j]
            for k in range(j):
                offdiag = offdiag - factor[i][k] * factor[j][k]
            factor[i][j] = offdiag * inverse[j]
    solved, rhs = [], []
    for j in range(5):
        current, target = weighted_l[j], beta[j]
        for k in range(j):
            current = current - factor[j][k] * solved[k]
            target = target - factor[j][k] * rhs[k]
        solved.append(current * inverse[j])
        rhs.append(target * inverse[j])
    projection = solved[0] * rhs[0]
    for k in range(1, 5):
        projection = projection + solved[k] * rhs[k]
    return solved, masked_w * resid - projection, masked_w


def prepare(place_ref, region_ref, packed_ref, scaled_s, lanes_s, table_v, table_s):
    tracks = packed_ref.shape[0]
    slots = scaled_s.shape[1]
    groups = slots // GROUP
    hits = DEPTH // GROUP
    blocks = place_ref.shape[0]
    rr = table_v.shape[0] - 8
    member = iota((rr, tracks), 0) == region_ref[...]
    member_f = member.astype(F32)
    before = (iota((tracks, tracks), 0) < iota((tracks, tracks), 1)).astype(F32).astype(BF16)
    rank = jnp.dot(member_f.astype(BF16), before, preferred_element_type=F32)
    count = jnp.sum(member_f, axis=1, keepdims=True)
    room = lax.shift_left(lax.shift_right_logical(count.astype(jnp.int32) + 7, 3), 3)
    room = jnp.broadcast_to(room.astype(F32), (rr, slots))
    lower = (iota((rr, rr), 1) < iota((rr, rr), 0)).astype(F32)
    start = jnp.zeros((rr, slots), F32)
    for g in range(rr):
        start = start + lower[:, g : g + 1] * room[g : g + 1, :]
    slot = jnp.sum(member_f * (rank + start[:, 0:1]), axis=0, keepdims=True)
    perm = (iota((slots, tracks), 0) == slot.astype(jnp.int32)).astype(F32).astype(BF16)
    numbers = iota((8, tracks), 1).astype(F32).astype(BF16)
    order = lax.dot_general(numbers, perm, NT, preferred_element_type=F32)
    table_v[0:8, :] = order.astype(jnp.int32)
    table_v[8:, :] = jnp.where(
        iota((rr, slots), 1) == 0, start.astype(jnp.int32), (start + room).astype(jnp.int32)
    )
    pltpu.sync_copy(table_v, table_s)
    rows = jnp.dot(perm, packed_ref[...], preferred_element_type=F32)
    flat = rows.T
    ld = [flat[c * hits : (c + 1) * hits] for c in range(5)]
    weight, resid, ids = (flat[c * hits : (c + 1) * hits] for c in range(5, 8))
    counts = flat[8 * hits : 8 * hits + 1]
    solved, hit_factor, masked_w = fit(ld, weight, resid, counts)
    position = jnp.zeros_like(ids)
    for b in range(blocks):
        position = jnp.where(ids == float(b), place_ref[b].astype(F32), position)
    own = (iota((DEPTH, slots), 0) // hits) == (iota((DEPTH, slots), 1) % GROUP)

    def spread_out(value):
        return jnp.where(own, jnp.concatenate([value] * GROUP, axis=0), 0.0)

    grouping = (iota((groups, slots), 1) // GROUP == iota((groups, slots), 0)).astype(F32)
    grouping = grouping.astype(BF16)
    for n, value in enumerate((masked_w, position, hit_factor)):
        lanes_s[n] = lax.dot_general(
            grouping, spread_out(value).astype(BF16), NT, preferred_element_type=F32
        )
    for c in range(5):
        scaled_s[c] = spread_out(solved[c]).T


def one_group(group, local, order_s, g_ref, scaled_s, lanes_s, g_s, direct_s, spread_s):
    hits, width = g_ref.shape[1:]
    blocks = spread_s.shape[0]
    for i in range(GROUP):
        g_s[i * hits : (i + 1) * hits, :] = g_ref[order_s[0, group * GROUP + i]]
    g = g_s[...]
    weight = lanes_s[0, pl.ds(group, 1), :]
    position = lanes_s[1, pl.ds(group, 1), :]
    hit_factor = lanes_s[2, pl.ds(group, 1), :]
    weighted = g.astype(F32).T * weight
    base = pl.multiple_of(group * GROUP, GROUP)
    scaled = jnp.concatenate([scaled_s[c, pl.ds(base, GROUP), :] for c in range(5)], axis=0)
    high = scaled.astype(BF16).astype(F32)
    low = scaled - high
    direct, highs, lows = [], [], []
    for p in range(blocks):
        here = position == float(p)
        direct.append(jnp.where(here, weighted, 0.0))
        highs.append(jnp.where(here, high, 0.0))
        lows.append(jnp.where(here, low, 0.0))
    sub = iota((16, DEPTH), 0).astype(F32)
    vector = jnp.where(sub == position, hit_factor, 0.0)
    total = jnp.dot(
        jnp.concatenate(direct + [vector], axis=0).astype(BF16), g, preferred_element_type=F32
    )
    direct_s[...] += total
    upper = jnp.dot(
        jnp.concatenate(highs, axis=0).astype(BF16), g, preferred_element_type=F32
    ) + jnp.dot(jnp.concatenate(lows, axis=0).astype(BF16), g, preferred_element_type=F32)
    step = 5 * GROUP
    at = pl.multiple_of(local * step, GROUP)
    for p in range(blocks):
        spread_s[p, pl.ds(at, step), :] = upper[p * step : (p + 1) * step]


def assemble_kernel(
    where_ref, place_ref, region_ref, packed_ref, g_ref,
    keep_a, send_a, keep_b, send_b,
    scaled_s, lanes_s, table_v, table_s, g_s, direct_s, spread_s, wide_s, turned_s, acc_s,
):
    k = pl.program_id(0)
    blocks, _, width = spread_s.shape

    @pl.when(k == 0)
    def _():
        prepare(place_ref, region_ref, packed_ref, scaled_s, lanes_s, table_v, table_s)

    region = where_ref[1] ^ k
    first = table_s[8 + region, 0] // GROUP
    groups = table_s[8 + region, 1] // GROUP - first
    direct_s[...] = jnp.zeros_like(direct_s)
    acc_s[...] = jnp.zeros_like(acc_s)

    def group_step(local, carry):
        one_group(
            first + local, local, table_s, g_ref, scaled_s, lanes_s, g_s, direct_s, spread_s
        )
        return carry

    lax.fori_loop(0, groups, group_step, 0)
    used = groups * 5
    depth_tiles = DEPTH // 8
    chunks = (used + depth_tiles - 1) // depth_tiles

    def clear(tile, carry):
        spread_s[:, pl.ds(pl.multiple_of(tile * 8, 8), 8), :] = jnp.zeros((blocks, 8, width), F32)
        return carry

    lax.fori_loop(used, chunks * depth_tiles, clear, 0)

    def chunk_step(chunk, carry):
        at = pl.multiple_of(chunk * DEPTH, DEPTH)
        for p in range(blocks):
            part = spread_s[p, pl.ds(at, DEPTH), :]
            narrow = part.astype(BF16)
            wide_s[:, p * width : (p + 1) * width] = narrow
            if p < blocks // 2:
                wide_s[:, (blocks + p) * width : (blocks + p + 1) * width] = narrow
            turned_s[p] = narrow.astype(F32).T.astype(BF16)
        for p in range(blocks):
            many = blocks // 2 + (1 if p < blocks // 2 else 0)
            acc_s[p, :, : many * width] += jnp.dot(
                turned_s[p],
                wide_s[:, p * width : (p + many) * width],
                preferred_element_type=F32,
            )
        return carry

    lax.fori_loop(0, chunks, chunk_step, 0)
    half = width // 2
    for j in range(blocks):
        p = where_ref[0] ^ j
        at = pl.multiple_of(p * width, width)
        d0 = direct_s[pl.ds(at, width), :] - acc_s[p, :, 0:width]
        d1, d2, d3 = (0.0 - acc_s[p, :, d * width : (d + 1) * width] for d in range(1, 4))
        upper = pl.multiple_of((p // (blocks // 2)) * half, half)
        ext = 0.0 - acc_s[p % (blocks // 2), pl.ds(upper, half), 4 * width : 5 * width]
        row = direct_s[pl.ds(blocks * width + p, 1), :]
        row_high = row.astype(BF16).astype(F32)
        sub = iota((16, width), 0)
        row_tile = jnp.where(sub == 0, row_high, jnp.where(sub == 1, row - row_high, 0.0))
        part_a = jnp.concatenate([d0, d1, ext[: half // 2], row_tile], axis=0).astype(BF16)
        part_b = jnp.concatenate([d2, d3, ext[half // 2 :]], axis=0).astype(BF16)
        (send_a if j & 1 else keep_a)[ORDER_A.index(j & 6), 0] = part_a
        (send_b if j & 1 else keep_b)[ORDER_B.index(j & 6), 0] = part_b


ORDER_A = (0, 4, 2, 6)
ORDER_B = (0, 2, 4, 6)


def assemble(where, place, region_row, packed, g, regions):
    tracks, hits, width = g.shape
    blocks = place.shape[0]
    rr = -(-regions // 8) * 8
    slots = -(-(tracks + regions * (GROUP - 1)) // 128) * 128
    rows_a, rows_b = width * 2 + width // 4 + 16, width * 2 + width // 4
    longest = -(-(-(-tracks // GROUP) * 5 * GROUP) // DEPTH) * DEPTH

    def out(rows):
        return jax.ShapeDtypeStruct((blocks // 2, regions, rows, width), BF16)

    def spec(rows):
        return pl.BlockSpec((blocks // 2, 1, rows, width), lambda k: (0, k, 0, 0))

    smem = pl.BlockSpec(memory_space=pltpu.SMEM)
    vmem = pl.BlockSpec(memory_space=pltpu.VMEM)
    return pl.pallas_call(
        assemble_kernel,
        grid=(regions,),
        in_specs=[smem, smem, vmem, vmem, vmem],
        out_specs=[spec(rows_a), spec(rows_a), spec(rows_b), spec(rows_b)],
        out_shape=[out(rows_a), out(rows_a), out(rows_b), out(rows_b)],
        scratch_shapes=[
            pltpu.VMEM((5, slots, DEPTH), F32),
            pltpu.VMEM((3, slots // GROUP, DEPTH), F32),
            pltpu.VMEM((8 + rr, slots), jnp.int32),
            pltpu.SMEM((8 + rr, slots), jnp.int32),
            pltpu.VMEM((DEPTH, width), BF16),
            pltpu.VMEM((blocks * width + 16, width), F32),
            pltpu.VMEM((blocks, longest, width), F32),
            pltpu.VMEM((DEPTH, (blocks + blocks // 2) * width), BF16),
            pltpu.VMEM((blocks, width, DEPTH), BF16),
            pltpu.VMEM((blocks, width, (blocks // 2 + 1) * width), F32),
        ],
        compiler_params=pltpu.CompilerParams(
            dimension_semantics=("arbitrary",), vmem_limit_bytes=48 * 1024 * 1024
        ),
        cost_estimate=pl.CostEstimate(
            flops=8 * 10**9, bytes_accessed=8 * 10**6, transcendentals=0
        ),
        name="assemble",
    )(where, place, region_row, packed, g)


def finish_kernel(where_ref, a_ref, b_ref, r1_ref, r2_ref, r3_ref, e_ref, out_ref, vec_ref):
    width = a_ref.shape[1]
    half = width // 2
    p = where_ref[0]
    blocks = out_ref.shape[1] // width

    def put(column, value):
        column = pl.multiple_of(((column + blocks) % blocks) * width, width)
        out_ref[:, pl.ds(column, width)] = value

    put(p, a_ref[0:width, :])
    put(p + 1, a_ref[width : 2 * width, :])
    put(p + 2, b_ref[0:width, :])
    put(p + 3, b_ref[width : 2 * width, :])
    for d, ref in ((1, r1_ref), (2, r2_ref), (3, r3_ref)):
        put(p - d, ref[...].astype(F32).T)
    mine = [a_ref[2 * width : 2 * width + half // 2, :], b_ref[2 * width :, :]]
    other = e_ref[...].astype(F32)

    @pl.when(p < blocks // 2)
    def _():
        put(p + blocks // 2, jnp.concatenate(mine + [other], axis=0))

    @pl.when(p >= blocks // 2)
    def _():
        put(p + blocks // 2, jnp.concatenate([other] + mine, axis=0).T)

    tail = 2 * width + half // 2
    vec_ref[...] = a_ref[tail : tail + 1, :] + a_ref[tail + 1 : tail + 2, :]


def finish(where, a, b, r1, r2, r3, ext, blocks):
    width = a.shape[1]
    smem = pl.BlockSpec(memory_space=pltpu.SMEM)
    vmem = pl.BlockSpec(memory_space=pltpu.VMEM)
    return pl.pallas_call(
        finish_kernel,
        in_specs=[smem] + [vmem] * 6,
        out_specs=[vmem, vmem],
        out_shape=[
            jax.ShapeDtypeStruct((width, blocks * width), F32),
            jax.ShapeDtypeStruct((1, width), F32),
        ],
        name="finish",
    )(where, a, b, r1, r2, r3, ext)


def local(
    tiles, global_deriv, local_deriv, hit_weight, hit_resid, block_ids, hit_count, track_region,
    block_place,
):
    regions = lax.axis_size("region")
    tracks, hits, width = global_deriv.shape
    blocks = block_place.shape[0]
    sub = tiles // blocks
    tile = lax.axis_index("tile")
    where = jnp.stack([tile // sub, lax.axis_index("region")]).astype(jnp.int32)
    packed = jnp.concatenate(
        [
            local_deriv.reshape(tracks, -1),
            hit_weight,
            hit_resid,
            block_ids.astype(BF16),
            jnp.broadcast_to(hit_count.astype(BF16)[:, None], (tracks, 32)),
        ],
        axis=1,
    )
    keep_a, send_a, keep_b, send_b = assemble(
        where, block_place, track_region.reshape(1, tracks), packed, global_deriv, regions
    )

    def swap(value, bit):
        return lax.ppermute(value, "tile", [(t, t ^ bit) for t in range(tiles)])

    def reduce_tile(keep, send, bits):
        bit = 1
        while bit < sub:
            keep, send = keep + swap(keep, bit), send + swap(send, bit)
            bit *= 2
        got = swap(send, sub * bits[0])
        total = keep.astype(F32) + got.astype(F32)
        got = swap(total[2:].astype(BF16), sub * bits[1])
        total = total[:2] + got.astype(F32)
        got = swap(total[1].astype(BF16), sub * bits[2])
        return total[0] + got.astype(F32)

    def reduce_region(total):
        narrow = total[1:].astype(BF16)
        result = total[0]
        for k in range(1, regions):
            result = result + lax.ppermute(
                narrow[k - 1], "region", [(r, r ^ k) for r in range(regions)]
            ).astype(F32)
        return result

    a = reduce_region(reduce_tile(keep_a, send_a, (1, 2, 4)))
    b = reduce_region(reduce_tile(keep_b, send_b, (1, 4, 2)))

    def onward(value, d):
        pairs = [
            (p * sub + s, ((p + d) % blocks) * sub + s) for p in range(blocks) for s in range(sub)
        ]
        return lax.ppermute(value.astype(BF16), "tile", pairs)

    ext = jnp.concatenate([a[2 * width : 2 * width + width // 4], b[2 * width :]], axis=0)
    matrix, vector = finish(
        where,
        a,
        b,
        onward(a[width : 2 * width], 1),
        onward(b[:width], 2),
        onward(b[width : 2 * width], 3),
        onward(ext, blocks // 2),
        blocks,
    )
    if sub > 1:
        part = tile % sub
        rows = width // sub
        matrix = lax.dynamic_slice(matrix, (part * rows, 0), (rows, blocks * width))
        vector = lax.dynamic_slice(vector, (0, part * rows), (1, rows))
    return matrix[None], vector


def solution(mesh):
    return jax.shard_map(
        functools.partial(local, mesh.shape["tile"]),
        mesh=mesh,
        in_specs=(
            P(("region", "tile"), None, None),
            P(("region", "tile"), None, None),
            P(("region", "tile"), None),
            P(("region", "tile"), None),
            P(("region", "tile"), None),
            P(("region", "tile")),
            P(("region", "tile"), None),
            P(),
        ),
        out_specs=(P("region", "tile", None), P("region", "tile")),
        check_vma=False,
    )
```

```python
import functools
import jax
import jax.numpy as jnp
from jax import lax
from jax.experimental import pallas as pl
from jax.experimental.pallas import tpu as pltpu
from jax.sharding import PartitionSpec as P

F32 = jnp.float32
BF16 = jnp.bfloat16
GROUP = 8
DEPTH = 256

NT = (((1,), (1,)), ((), ()))


def iota(shape, axis):
    return lax.broadcasted_iota(jnp.int32, shape, axis)


def fit(ld, weight, resid, counts):
    hits = weight.shape[0]
    live = iota(weight.shape, 0) < counts.astype(jnp.int32)
    masked_w = jnp.where(live, weight, 0.0)
    weighted_l = [v * masked_w for v in ld]
    gamma = [[None] * 5 for _ in range(5)]
    for a in range(5):
        for b in range(a + 1):
            gamma[a][b] = jnp.sum(weighted_l[a] * ld[b], axis=0, keepdims=True)
            if a == b:
                gamma[a][b] = gamma[a][b] + 1.0
    beta = [jnp.sum(weighted_l[a] * resid, axis=0, keepdims=True) for a in range(5)]
    factor = [[None] * 5 for _ in range(5)]
    inverse = [None] * 5
    for j in range(5):
        center = gamma[j][j]
        for k in range(j):
            center = center - factor[j][k] * factor[j][k]
        factor[j][j] = jnp.sqrt(center)
        inverse[j] = 1.0 / factor[j][j]
        for i in range(j + 1, 5):
            offdiag = gamma[i][j]
            for k in range(j):
                offdiag = offdiag - factor[i][k] * factor[j][k]
            factor[i][j] = offdiag * inverse[j]
    solved, rhs = [], []
    for j in range(5):
        current, target = weighted_l[j], beta[j]
        for k in range(j):
            current = current - factor[j][k] * solved[k]
            target = target - factor[j][k] * rhs[k]
        solved.append(current * inverse[j])
        rhs.append(target * inverse[j])
    projection = solved[0] * rhs[0]
    for k in range(1, 5):
        projection = projection + solved[k] * rhs[k]
    return solved, masked_w * resid - projection, masked_w


def prepare_kernel(
    place_ref, region_ref, count_ref, ld_ref, weight_ref, resid_ref, ids_ref,
    scaled_ref, lanes_ref, column_ref, table_ref,
):
    tracks = region_ref.shape[1]
    groups, _, depth = scaled_ref.shape
    slots = groups * GROUP
    hits = depth // GROUP
    blocks = place_ref.shape[0]
    rr = table_ref.shape[0] - 8
    member = (iota((rr, tracks), 0) == region_ref[...]).astype(F32)
    before = (iota((tracks, tracks), 0) < iota((tracks, tracks), 1)).astype(F32).astype(BF16)
    rank = jnp.dot(member.astype(BF16), before, preferred_element_type=F32)
    count = jnp.sum(member, axis=1, keepdims=True)
    room = lax.shift_left(lax.shift_right_logical(count.astype(jnp.int32) + 7, 3), 3)
    room = jnp.broadcast_to(room.astype(F32), (rr, slots))
    lower = (iota((rr, rr), 1) < iota((rr, rr), 0)).astype(F32)
    start = jnp.zeros((rr, slots), F32)
    for g in range(rr):
        start = start + lower[:, g : g + 1] * room[g : g + 1, :]
    slot = jnp.sum(member * (rank + start[:, 0:1]), axis=0, keepdims=True)
    perm = (iota((slots, tracks), 0) == slot.astype(jnp.int32)).astype(F32).astype(BF16)
    numbers = jnp.where(
        iota((8, tracks), 0) == 0, iota((8, tracks), 1), jnp.broadcast_to(count_ref[...], (8, tracks))
    )

    def sort(value):
        return lax.dot_general(value, perm, NT, preferred_element_type=F32)

    numbers = sort(numbers.astype(F32).astype(BF16))
    table_ref[0:8, :] = numbers.astype(jnp.int32)
    table_ref[8:, :] = jnp.where(
        iota((rr, slots), 1) == 0, start.astype(jnp.int32), (start + room).astype(jnp.int32)
    )
    flat = sort(ld_ref[...])
    ld = [flat[c * hits : (c + 1) * hits] for c in range(5)]
    solved, hit_factor, masked_w = fit(
        ld, sort(weight_ref[...]), sort(resid_ref[...]), numbers[1:2]
    )
    ids = sort(ids_ref[...].astype(F32).astype(BF16))
    position = jnp.zeros_like(ids)
    for b in range(blocks):
        position = jnp.where(ids == float(b), place_ref[b].astype(F32), position)
    own = (iota((depth, slots), 0) // hits) == (iota((depth, slots), 1) % GROUP)

    def spread_out(value):
        return jnp.where(own, jnp.concatenate([value] * GROUP, axis=0), 0.0)

    grouping = (iota((groups, slots), 1) // GROUP == iota((groups, slots), 0)).astype(F32)
    for n, value in enumerate((masked_w, hit_factor)):
        lanes_ref[n] = lax.dot_general(
            grouping.astype(BF16), spread_out(value).astype(BF16), NT, preferred_element_type=F32
        )
    columns = column_ref.shape[1]
    grouping = (iota((columns, slots), 1) // GROUP == iota((columns, slots), 0)).astype(F32)
    column_ref[...] = lax.dot_general(
        spread_out(position).astype(BF16), grouping.astype(BF16), NT, preferred_element_type=F32
    ).astype(BF16)
    for c in range(5):
        scaled_ref[:, c * GROUP : (c + 1) * GROUP, :] = spread_out(solved[c]).T.reshape(
            groups, GROUP, depth
        )


def prepare(place, region_row, count_row, ld, weight, resid, ids, regions):
    tracks = region_row.shape[1]
    hits = weight.shape[0]
    rr = -(-regions // 8) * 8
    slots = -(-(tracks + regions * (GROUP - 1)) // 128) * 128
    depth = GROUP * hits
    smem = pl.BlockSpec(memory_space=pltpu.SMEM)
    vmem = pl.BlockSpec(memory_space=pltpu.VMEM)
    return pl.pallas_call(
        prepare_kernel,
        in_specs=[smem] + [vmem] * 6,
        out_specs=[vmem] * 4,
        out_shape=[
            jax.ShapeDtypeStruct((slots // GROUP, 5 * GROUP, depth), F32),
            jax.ShapeDtypeStruct((2, slots // GROUP, depth), F32),
            jax.ShapeDtypeStruct((depth, 128), BF16),
            jax.ShapeDtypeStruct((8 + rr, slots), jnp.int32),
        ],
        compiler_params=pltpu.CompilerParams(vmem_limit_bytes=24 * 1024 * 1024),
        cost_estimate=pl.CostEstimate(flops=10**9, bytes_accessed=2 * 10**6, transcendentals=0),
        name="prepare",
    )(place, region_row, count_row, ld, weight, resid, ids)


def one_group(group, local, table_ref, g_ref, scaled_ref, lanes_ref, column_ref, g_s, direct_s, spread_s):
    hits, width = g_ref.shape[1:]
    depth = GROUP * hits
    blocks = spread_s.shape[1] // width
    for i in range(GROUP):
        g_s[i * hits : (i + 1) * hits, :] = g_ref[table_ref[0, group * GROUP + i]]
    g = g_s[...]
    chosen = (iota((128, width), 0) == group).astype(F32).astype(BF16)
    position = jnp.dot(column_ref[...], chosen, preferred_element_type=F32).astype(BF16)
    right = jnp.concatenate(
        [jnp.where(position == jnp.bfloat16(p), g, jnp.bfloat16(0)) for p in range(blocks)], axis=1
    )
    weighted = g.astype(F32).T * lanes_ref[0, pl.ds(group, 1), :]
    factor = jnp.where(iota((8, depth), 0) == 0, lanes_ref[1, pl.ds(group, 1), :], 0.0)
    scaled = scaled_ref[group]
    high = scaled.astype(BF16).astype(F32)
    left = jnp.concatenate(
        [weighted, factor, high, scaled - high, jnp.zeros((8, depth), F32)], axis=0
    )
    total = jnp.dot(left.astype(BF16), right, preferred_element_type=F32)
    head = width + 8
    step = 5 * GROUP
    direct_s[...] += total[:head]
    spread_s[pl.ds(pl.multiple_of(local * step, GROUP), step), :] = (
        total[head : head + step] + total[head + step : head + 2 * step]
    )


ODD = (0, 4, 2, 6)
EVEN = (0, 2, 4, 6)


def assemble_kernel(
    first_k, where_ref, table_ref, scaled_ref, lanes_ref, column_ref, g_ref,
    keep_ref, send_ref, g_s, direct_s, spread_s, wide_s, turned_s, acc_s,
):
    k = pl.program_id(0) + first_k
    width = g_ref.shape[2]
    blocks = spread_s.shape[1] // width
    many = blocks // 2
    region = where_ref[1] ^ k
    first = table_ref[8 + region, 0] // GROUP
    groups = table_ref[8 + region, 1] // GROUP - first
    direct_s[...] = jnp.zeros_like(direct_s)
    acc_s[...] = jnp.zeros_like(acc_s)

    def group_step(local, carry):
        one_group(
            first + local, local, table_ref, g_ref, scaled_ref, lanes_ref, column_ref,
            g_s, direct_s, spread_s,
        )
        return carry

    lax.fori_loop(0, groups, group_step, 0)
    used = groups * 5
    depth_tiles = DEPTH // 8
    chunks = (used + depth_tiles - 1) // depth_tiles

    def clear(tile, carry):
        spread_s[pl.ds(pl.multiple_of(tile * 8, 8), 8), :] = jnp.zeros((8, blocks * width), F32)
        return carry

    lax.fori_loop(used, chunks * depth_tiles, clear, 0)

    def chunk_step(chunk, carry):
        at = pl.multiple_of(chunk * DEPTH, DEPTH)
        narrow = spread_s[pl.ds(at, DEPTH), :].astype(BF16)
        wide_s[:, : blocks * width] = narrow
        wide_s[:, blocks * width :] = narrow[:, : many * width]
        turned_s[...] = narrow.astype(F32).T.astype(BF16)
        for p in range(blocks):
            columns = (many + (1 if p < many else 0)) * width
            acc_s[p, :, :columns] += jnp.dot(
                turned_s[p * width : (p + 1) * width],
                wide_s[:, p * width : p * width + columns],
                preferred_element_type=F32,
            )
        return carry

    lax.fori_loop(0, chunks, chunk_step, 0)
    half = width // 2
    for n in range(blocks // 2):
        for odd, out_ref in ((0, keep_ref), (1, send_ref)):
            p = where_ref[0] ^ (jnp.where(k % 2 == 1, ODD[n], EVEN[n]) + odd)
            columns = pl.ds(pl.multiple_of(p * width, width), width)
            parts = [direct_s[0:width, columns] - acc_s[p, :, 0:width]]
            parts += [0.0 - acc_s[p, :, d * width : (d + 1) * width] for d in range(1, many)]
            upper = pl.multiple_of((p // many) * half, half)
            parts.append(0.0 - acc_s[p % many, pl.ds(upper, half), many * width :])
            row = direct_s[width : width + 1, columns]
            high = row.astype(BF16).astype(F32)
            sub = iota((16, width), 0)
            parts.append(jnp.where(sub == 0, high, jnp.where(sub == 1, row - high, 0.0)))
            out_ref[n, 0] = jnp.concatenate(parts, axis=0).astype(BF16)


def assemble(first_k, number, where, table, scaled, lanes, column, g, blocks):
    tracks, hits, width = g.shape
    rows = width * (blocks // 2) + width // 2 + 16
    longest = -(-(-(-tracks // GROUP) * 5 * GROUP) // DEPTH) * DEPTH
    out = jax.ShapeDtypeStruct((blocks // 2, number, rows, width), BF16)
    spec = pl.BlockSpec((blocks // 2, 1, rows, width), lambda k: (0, k, 0, 0))
    smem = pl.BlockSpec(memory_space=pltpu.SMEM)
    vmem = pl.BlockSpec(memory_space=pltpu.VMEM)
    return pl.pallas_call(
        functools.partial(assemble_kernel, first_k),
        grid=(number,),
        in_specs=[smem, smem, vmem, vmem, vmem, vmem],
        out_specs=[spec, spec],
        out_shape=[out, out],
        scratch_shapes=[
            pltpu.VMEM((GROUP * hits, width), BF16),
            pltpu.VMEM((width + 8, blocks * width), F32),
            pltpu.VMEM((longest, blocks * width), F32),
            pltpu.VMEM((DEPTH, (blocks + blocks // 2) * width), BF16),
            pltpu.VMEM((blocks * width, DEPTH), BF16),
            pltpu.VMEM((blocks, width, (blocks // 2 + 1) * width), F32),
        ],
        compiler_params=pltpu.CompilerParams(
            dimension_semantics=("arbitrary",), vmem_limit_bytes=32 * 1024 * 1024
        ),
        cost_estimate=pl.CostEstimate(
            flops=3 * 10**9 * number // 2, bytes_accessed=4 * 10**6, transcendentals=0
        ),
        name="assemble",
    )(where, table, scaled, lanes, column, g)


def finish_kernel(where_ref, own_ref, r1_ref, r2_ref, r3_ref, e_ref, out_ref, vec_ref):
    width = own_ref.shape[1]
    p = where_ref[0]
    blocks = out_ref.shape[1] // width
    many = blocks // 2

    def put(column, value):
        column = pl.multiple_of(((column + blocks) % blocks) * width, width)
        out_ref[:, pl.ds(column, width)] = value

    for d in range(many):
        put(p + d, own_ref[d * width : (d + 1) * width, :])
    for d, ref in ((1, r1_ref), (2, r2_ref), (3, r3_ref)):
        put(p - d, ref[...].astype(F32).T)
    tail = many * width + width // 2
    mine = own_ref[many * width : tail, :]
    other = e_ref[...].astype(F32)

    @pl.when(p < many)
    def _():
        put(p + many, jnp.concatenate([mine, other], axis=0))

    @pl.when(p >= many)
    def _():
        put(p + many, jnp.concatenate([other, mine], axis=0).T)

    vec_ref[...] = own_ref[tail : tail + 1, :] + own_ref[tail + 1 : tail + 2, :]


def finish(where, own, r1, r2, r3, ext, blocks):
    width = own.shape[1]
    smem = pl.BlockSpec(memory_space=pltpu.SMEM)
    vmem = pl.BlockSpec(memory_space=pltpu.VMEM)
    return pl.pallas_call(
        finish_kernel,
        in_specs=[smem] + [vmem] * 5,
        out_specs=[vmem, vmem],
        out_shape=[
            jax.ShapeDtypeStruct((width, blocks * width), F32),
            jax.ShapeDtypeStruct((1, width), F32),
        ],
        name="finish",
    )(where, own, r1, r2, r3, ext)


def local(
    tiles, global_deriv, local_deriv, hit_weight, hit_resid, block_ids, hit_count, track_region,
    block_place,
):
    regions = lax.axis_size("region")
    tracks, hits, width = global_deriv.shape
    blocks = block_place.shape[0]
    sub = tiles // blocks
    tile = lax.axis_index("tile")
    where = jnp.stack([tile // sub, lax.axis_index("region")]).astype(jnp.int32)
    scaled, lanes, column, table = prepare(
        block_place,
        track_region.reshape(1, tracks),
        hit_count.reshape(1, tracks),
        local_deriv.transpose(1, 2, 0).reshape(-1, tracks),
        hit_weight.T,
        hit_resid.T,
        block_ids.T,
        regions,
    )

    def swap(value, bit):
        return lax.ppermute(value, "tile", [(t, t ^ bit) for t in range(tiles)])

    totals = [None] * regions
    for first in range(regions - 2, -1, -2):
        keep, send = assemble(first, 2, where, table, scaled, lanes, column, global_deriv, blocks)
        bit = 1
        while bit < sub:
            keep, send = keep + swap(keep, bit), send + swap(send, bit)
            bit *= 2
        got = swap(send, sub)
        for n in range(2):
            bits = ((4, 2), (2, 4))[n]
            total = keep[:, n].astype(F32) + got[:, n].astype(F32)
            more = swap(total[2:].astype(BF16), sub * bits[0])
            total = total[:2] + more.astype(F32)
            more = swap(total[1].astype(BF16), sub * bits[1])
            totals[first + n] = total[0] + more.astype(F32)
    own = totals[0]
    for k in range(regions - 1, 0, -1):
        pairs = [(r, r ^ k) for r in range(regions)]
        own = own + lax.ppermute(totals[k].astype(BF16), "region", pairs).astype(F32)

    def onward(value, d):
        pairs = [
            (p * sub + s, ((p + d) % blocks) * sub + s) for p in range(blocks) for s in range(sub)
        ]
        return lax.ppermute(value.astype(BF16), "tile", pairs)

    matrix, vector = finish(
        where,
        own,
        *(onward(own[d * width : (d + 1) * width], d) for d in range(1, blocks // 2)),
        onward(own[blocks // 2 * width : blocks // 2 * width + width // 2], blocks // 2),
        blocks,
    )
    if sub > 1:
        part = tile % sub
        rows = width // sub
        matrix = lax.dynamic_slice(matrix, (part * rows, 0), (rows, blocks * width))
        vector = lax.dynamic_slice(vector, (0, part * rows), (1, rows))
    return matrix[None], vector


def solution(mesh):
    return jax.shard_map(
        functools.partial(local, mesh.shape["tile"]),
        mesh=mesh,
        in_specs=(
            P(("region", "tile"), None, None),
            P(("region", "tile"), None, None),
            P(("region", "tile"), None),
            P(("region", "tile"), None),
            P(("region", "tile"), None),
            P(("region", "tile")),
            P(("region", "tile"), None),
            P(),
        ),
        out_specs=(P("region", "tile", None), P("region", "tile")),
        check_vma=False,
    )
```

```python
import functools
import jax
import jax.numpy as jnp
from jax import lax
from jax.experimental import pallas as pl
from jax.experimental.pallas import tpu as pltpu
from jax.sharding import PartitionSpec as P

F32 = jnp.float32
BF16 = jnp.bfloat16
GROUP = 8
PAIR = 2 * GROUP
DEPTH = 256

NT = (((1,), (1,)), ((), ()))


def iota(shape, axis):
    return lax.broadcasted_iota(jnp.int32, shape, axis)


def fit(ld, weight, resid, counts):
    hits = weight.shape[0]
    live = iota(weight.shape, 0) < counts.astype(jnp.int32)
    masked_w = jnp.where(live, weight, 0.0)
    weighted_l = [v * masked_w for v in ld]
    gamma = [[None] * 5 for _ in range(5)]
    for a in range(5):
        for b in range(a + 1):
            gamma[a][b] = jnp.sum(weighted_l[a] * ld[b], axis=0, keepdims=True)
            if a == b:
                gamma[a][b] = gamma[a][b] + 1.0
    beta = [jnp.sum(weighted_l[a] * resid, axis=0, keepdims=True) for a in range(5)]
    factor = [[None] * 5 for _ in range(5)]
    inverse = [None] * 5
    for j in range(5):
        center = gamma[j][j]
        for k in range(j):
            center = center - factor[j][k] * factor[j][k]
        factor[j][j] = jnp.sqrt(center)
        inverse[j] = 1.0 / factor[j][j]
        for i in range(j + 1, 5):
            offdiag = gamma[i][j]
            for k in range(j):
                offdiag = offdiag - factor[i][k] * factor[j][k]
            factor[i][j] = offdiag * inverse[j]
    solved, rhs = [], []
    for j in range(5):
        current, target = weighted_l[j], beta[j]
        for k in range(j):
            current = current - factor[j][k] * solved[k]
            target = target - factor[j][k] * rhs[k]
        solved.append(current * inverse[j])
        rhs.append(target * inverse[j])
    projection = solved[0] * rhs[0]
    for k in range(1, 5):
        projection = projection + solved[k] * rhs[k]
    return solved, masked_w * resid - projection, masked_w


def prepare_kernel(
    place_hbm, region_hbm, count_hbm, ld_hbm, weight_hbm, resid_hbm, ids_hbm,
    scaled_ref, lanes_ref, column_ref, table_ref,
    place_ref, region_ref, count_ref, ld_ref, weight_ref, resid_ref, ids_ref, sems,
):
    copies = [
        pltpu.make_async_copy(source, target, sems.at[n])
        for n, (source, target) in enumerate(
            (
                (region_hbm, region_ref), (count_hbm, count_ref), (place_hbm, place_ref),
                (ld_hbm, ld_ref), (weight_hbm, weight_ref), (resid_hbm, resid_ref),
                (ids_hbm, ids_ref),
            )
        )
    ]
    for copy in copies:
        copy.start()
    for copy in copies:
        copy.wait()
    tracks = region_ref.shape[1]
    groups, _, depth = scaled_ref.shape
    slots = groups * GROUP
    hits = depth // GROUP
    blocks = place_ref.shape[0]
    rr = table_ref.shape[0] - 8
    member = (iota((rr, tracks), 0) == region_ref[...]).astype(F32)
    before = (iota((tracks, tracks), 0) < iota((tracks, tracks), 1)).astype(F32).astype(BF16)
    rank = jnp.dot(member.astype(BF16), before, preferred_element_type=F32)
    count = jnp.sum(member, axis=1, keepdims=True)
    room = (count.astype(jnp.int32) + (PAIR - 1)) & -PAIR
    room = jnp.broadcast_to(room.astype(F32), (rr, slots))
    lower = (iota((rr, rr), 1) < iota((rr, rr), 0)).astype(F32)
    start = jnp.zeros((rr, slots), F32)
    for g in range(rr):
        start = start + lower[:, g : g + 1] * room[g : g + 1, :]
    slot = jnp.sum(member * (rank + start[:, 0:1]), axis=0, keepdims=True)
    perm = (iota((slots, tracks), 0) == slot.astype(jnp.int32)).astype(F32).astype(BF16)
    numbers = jnp.where(
        iota((8, tracks), 0) == 0, iota((8, tracks), 1), jnp.broadcast_to(count_ref[...], (8, tracks))
    )

    def sort(value):
        return lax.dot_general(value, perm, NT, preferred_element_type=F32)

    numbers = sort(numbers.astype(F32).astype(BF16))
    table_ref[0:8, :] = numbers.astype(jnp.int32)
    table_ref[8:, :] = jnp.where(
        iota((rr, slots), 1) == 0, start.astype(jnp.int32), (start + room).astype(jnp.int32)
    )
    flat = sort(ld_ref[...])
    ld = [flat[c * hits : (c + 1) * hits] for c in range(5)]
    solved, hit_factor, masked_w = fit(
        ld, sort(weight_ref[...]), sort(resid_ref[...]), numbers[1:2]
    )
    ids = sort(ids_ref[...].astype(F32).astype(BF16))
    position = jnp.zeros_like(ids)
    for b in range(blocks):
        position = jnp.where(ids == float(b), place_ref[b].astype(F32), position)
    own = (iota((depth, slots), 0) // hits) == (iota((depth, slots), 1) % GROUP)

    def spread_out(value):
        return jnp.where(own, jnp.concatenate([value] * GROUP, axis=0), 0.0)

    grouping = (iota((groups, slots), 1) // GROUP == iota((groups, slots), 0)).astype(F32)
    for n, value in enumerate((masked_w, hit_factor)):
        lanes_ref[n] = lax.dot_general(
            grouping.astype(BF16), spread_out(value).astype(BF16), NT, preferred_element_type=F32
        )
    columns = column_ref.shape[1]
    grouping = (iota((columns, slots), 1) // GROUP == iota((columns, slots), 0)).astype(F32)
    column_ref[...] = lax.dot_general(
        spread_out(position).astype(BF16), grouping.astype(BF16), NT, preferred_element_type=F32
    ).astype(BF16)
    for c in range(5):
        scaled_ref[:, c * GROUP : (c + 1) * GROUP, :] = spread_out(solved[c]).T.reshape(
            groups, GROUP, depth
        )


def prepare(place, region_row, count_row, ld, weight, resid, ids, regions):
    tracks = region_row.shape[1]
    hits = weight.shape[0]
    rr = -(-regions // 8) * 8
    slots = -(-(tracks + regions * (PAIR - 1)) // 128) * 128
    depth = GROUP * hits
    vmem = pl.BlockSpec(memory_space=pltpu.VMEM)
    values = (place, region_row, count_row, ld, weight, resid, ids)
    return pl.pallas_call(
        prepare_kernel,
        in_specs=[pl.BlockSpec(memory_space=pltpu.HBM)] * 7,
        out_specs=[vmem] * 4,
        out_shape=[
            jax.ShapeDtypeStruct((slots // GROUP, 5 * GROUP, depth), F32),
            jax.ShapeDtypeStruct((2, slots // GROUP, depth), F32),
            jax.ShapeDtypeStruct((depth, 128), BF16),
            jax.ShapeDtypeStruct((8 + rr, slots), jnp.int32),
        ],
        scratch_shapes=[pltpu.SMEM(place.shape, place.dtype)]
        + [pltpu.VMEM(value.shape, value.dtype) for value in values[1:]]
        + [pltpu.SemaphoreType.DMA((7,))],
        compiler_params=pltpu.CompilerParams(vmem_limit_bytes=24 * 1024 * 1024),
        cost_estimate=pl.CostEstimate(flops=10**9, bytes_accessed=2 * 10**6, transcendentals=0),
        name="prepare",
    )(*values)


def one_step(step, at, table_ref, g_ref, scaled_ref, lanes_ref, column_ref, g_s, direct_s, spread_s):
    hits, width = g_ref.shape[1:]
    depth = GROUP * hits
    blocks = spread_s.shape[1] // width
    rows = 5 * GROUP
    head = width + 8
    direct = []
    for u in range(2):
        group = step * 2 + u
        for i in range(GROUP):
            g_s[u, i * hits : (i + 1) * hits, :] = g_ref[table_ref[0, group * GROUP + i]]
        g = g_s[u]
        chosen = (iota((128, width), 0) == group).astype(F32).astype(BF16)
        position = jnp.dot(column_ref[...], chosen, preferred_element_type=F32).astype(BF16)
        right = jnp.concatenate(
            [jnp.where(position == jnp.bfloat16(p), g, jnp.bfloat16(0)) for p in range(blocks)],
            axis=1,
        )
        weighted = g.astype(F32).T * lanes_ref[0, pl.ds(group, 1), :]
        factor = jnp.where(iota((8, depth), 0) == 0, lanes_ref[1, pl.ds(group, 1), :], 0.0)
        scaled = scaled_ref[group]
        high = scaled.astype(BF16).astype(F32)
        left = jnp.concatenate(
            [weighted, factor, high, scaled - high, jnp.zeros((8, depth), F32)], axis=0
        )
        total = jnp.dot(left.astype(BF16), right, preferred_element_type=F32)
        direct.append(total[:head])
        spread_s[pl.ds(pl.multiple_of(at + u * rows, GROUP), rows), :] = (
            total[head : head + rows] + total[head + rows : head + 2 * rows]
        )
    direct_s[...] += direct[0] + direct[1]


EVEN = (0, 4, 2, 6)
ODD = (0, 2, 4, 6)


def assemble_kernel(
    first_k, sub, table_ref, scaled_ref, lanes_ref, column_ref, g_ref,
    keep_ref, send_ref, g_s, direct_s, spread_s, wide_s, turned_s, acc_s,
):
    k = pl.program_id(0) + first_k
    width = g_ref.shape[2]
    blocks = spread_s.shape[1] // width
    many = blocks // 2
    region = lax.axis_index("region") ^ k
    block = lax.axis_index("tile") // sub
    first = table_ref[8 + region, 0] // PAIR
    steps = table_ref[8 + region, 1] // PAIR - first
    direct_s[...] = jnp.zeros_like(direct_s)

    def group_step(n, carry):
        one_step(
            first + n, n * (10 * GROUP), table_ref, g_ref, scaled_ref, lanes_ref, column_ref,
            g_s, direct_s, spread_s,
        )
        return carry

    lax.fori_loop(0, steps, group_step, 0)
    used = steps * 10
    depth_tiles = DEPTH // 8
    chunks = jnp.maximum((used + depth_tiles - 1) // depth_tiles, 1)

    def clear(tile, carry):
        spread_s[pl.ds(pl.multiple_of(tile * 8, 8), 8), :] = jnp.zeros((8, blocks * width), F32)
        return carry

    lax.fori_loop(used, chunks * depth_tiles, clear, 0)

    def chunk_step(chunk, carry):
        at = pl.multiple_of(chunk * DEPTH, DEPTH)
        narrow = spread_s[pl.ds(at, DEPTH), :].astype(BF16)
        wide_s[:, : blocks * width] = narrow
        wide_s[:, blocks * width :] = narrow[:, : many * width]
        turned_s[...] = -narrow.T

        def product(p):
            columns = (many + (1 if p < many else 0)) * width
            return columns, jnp.dot(
                turned_s[p * width : (p + 1) * width],
                wide_s[:, p * width : p * width + columns],
                preferred_element_type=F32,
            )

        @pl.when(chunk == 0)
        def _():
            for p in range(blocks):
                columns, value = product(p)
                acc_s[p, :, :columns] = value

        @pl.when(chunk > 0)
        def _():
            for p in range(blocks):
                columns, value = product(p)
                acc_s[p, :, :columns] += value

        return carry

    lax.fori_loop(0, chunks, chunk_step, 0)
    half = width // 2
    for n in range(blocks // 2):
        for odd, out_ref in ((0, keep_ref), (1, send_ref)):
            p = block ^ (jnp.where(block % 2 == 1 - odd, ODD[n], EVEN[n]) + odd)
            columns = pl.ds(pl.multiple_of(p * width, width), width)
            parts = [direct_s[0:width, columns] + acc_s[p, :, 0:width]]
            parts += [acc_s[p, :, d * width : (d + 1) * width] for d in range(1, many)]
            upper = pl.multiple_of((p // many) * half, half)
            parts.append(acc_s[p % many, pl.ds(upper, half), many * width :])
            row = direct_s[width : width + 1, columns]
            high = row.astype(BF16).astype(F32)
            sub = iota((16, width), 0)
            parts.append(jnp.where(sub == 0, high, jnp.where(sub == 1, row - high, 0.0)))
            out_ref[n, 0] = jnp.concatenate(parts, axis=0).astype(BF16)


def assemble(first_k, number, sub, table, scaled, lanes, column, g, blocks):
    tracks, hits, width = g.shape
    rows = width * (blocks // 2) + width // 2 + 16
    longest = -(-(-(-tracks // PAIR) * 5 * PAIR) // DEPTH) * DEPTH
    out = jax.ShapeDtypeStruct((blocks // 2, number, rows, width), BF16)
    spec = pl.BlockSpec((blocks // 2, 1, rows, width), lambda k: (0, k, 0, 0))
    smem = pl.BlockSpec(memory_space=pltpu.SMEM)
    vmem = pl.BlockSpec(memory_space=pltpu.VMEM)
    return pl.pallas_call(
        functools.partial(assemble_kernel, first_k, sub),
        grid=(number,),
        in_specs=[smem, vmem, vmem, vmem, vmem],
        out_specs=[spec, spec],
        out_shape=[out, out],
        scratch_shapes=[
            pltpu.VMEM((2, GROUP * hits, width), BF16),
            pltpu.VMEM((width + 8, blocks * width), F32),
            pltpu.VMEM((longest, blocks * width), F32),
            pltpu.VMEM((DEPTH, (blocks + blocks // 2) * width), BF16),
            pltpu.VMEM((blocks * width, DEPTH), BF16),
            pltpu.VMEM((blocks, width, (blocks // 2 + 1) * width), F32),
        ],
        compiler_params=pltpu.CompilerParams(
            dimension_semantics=("arbitrary",), vmem_limit_bytes=32 * 1024 * 1024
        ),
        cost_estimate=pl.CostEstimate(
            flops=3 * 10**9 * number // 2, bytes_accessed=4 * 10**6, transcendentals=0
        ),
        name="assemble",
    )(table, scaled, lanes, column, g)


def finish_kernel(sub, own_ref, r1_ref, r2_ref, r3_ref, e_ref, out_ref, vec_ref):
    width = own_ref.shape[1]
    p = lax.axis_index("tile") // sub
    blocks = out_ref.shape[1] // width
    many = blocks // 2

    def put(column, value):
        column = pl.multiple_of(((column + blocks) % blocks) * width, width)
        out_ref[:, pl.ds(column, width)] = value

    for d in range(many):
        put(p + d, own_ref[d * width : (d + 1) * width, :])
    for d, ref in ((1, r1_ref), (2, r2_ref), (3, r3_ref)):
        put(p - d, ref[...].astype(F32).T)
    tail = many * width + width // 2
    mine = own_ref[many * width : tail, :]
    other = e_ref[...].astype(F32)

    @pl.when(p < many)
    def _():
        put(p + many, jnp.concatenate([mine, other], axis=0))

    @pl.when(p >= many)
    def _():
        put(p + many, jnp.concatenate([other, mine], axis=0).T)

    vec_ref[...] = own_ref[tail : tail + 1, :] + own_ref[tail + 1 : tail + 2, :]


def finish(sub, own, r1, r2, r3, ext, blocks):
    width = own.shape[1]
    vmem = pl.BlockSpec(memory_space=pltpu.VMEM)
    return pl.pallas_call(
        functools.partial(finish_kernel, sub),
        in_specs=[vmem] * 5,
        out_specs=[vmem, vmem],
        out_shape=[
            jax.ShapeDtypeStruct((width, blocks * width), F32),
            jax.ShapeDtypeStruct((1, width), F32),
        ],
        name="finish",
    )(own, r1, r2, r3, ext)


def local(
    tiles, global_deriv, local_deriv, hit_weight, hit_resid, block_ids, hit_count, track_region,
    block_place,
):
    regions = lax.axis_size("region")
    tracks, hits, width = global_deriv.shape
    blocks = block_place.shape[0]
    sub = tiles // blocks
    tile = lax.axis_index("tile")
    scaled, lanes, column, table = prepare(
        block_place,
        track_region.reshape(1, tracks),
        hit_count.reshape(1, tracks),
        local_deriv.transpose(1, 2, 0).reshape(-1, tracks),
        hit_weight.T,
        hit_resid.T,
        block_ids.T,
        regions,
    )

    def swap(value, even, odd):
        pairs = [(t, t ^ (sub * (odd if t // sub % 2 else even))) for t in range(tiles)]
        return lax.ppermute(value, "tile", pairs)

    def across(value, k):
        return lax.ppermute(value.astype(BF16), "region", [(r, r ^ k) for r in range(regions)])

    totals = [None] * regions
    for first in range(regions - 2, -1, -2):
        keep, send = assemble(first, 2, sub, table, scaled, lanes, column, global_deriv, blocks)
        bit = 1
        while bit < sub:
            near = [(t, t ^ bit) for t in range(tiles)]
            keep, send = (v + lax.ppermute(v, "tile", near) for v in (keep, send))
            bit *= 2
        total = keep.astype(F32) + swap(send, 1, 1).astype(F32)
        third = total[2:].astype(BF16)
        if first:
            third, table = lax.optimization_barrier((third, table))
        total = total[:2] + swap(third, 2, 4).astype(F32)
        total = total[0] + swap(total[1].astype(BF16), 4, 2).astype(F32)
        totals[first], totals[first + 1] = total[0], total[1]
    bit = 1
    for k in range(regions - 1, 0, -1):
        step = k & -k
        totals[k - step] = totals[k - step] + across(totals[k], step).astype(F32)
    own = totals[0]

    def onward(value, d):
        pairs = [
            (p * sub + s, ((p + d) % blocks) * sub + s) for p in range(blocks) for s in range(sub)
        ]
        return lax.ppermute(value.astype(BF16), "tile", pairs)

    matrix, vector = finish(
        sub,
        own,
        *(onward(own[d * width : (d + 1) * width], d) for d in range(1, blocks // 2)),
        onward(own[blocks // 2 * width : blocks // 2 * width + width // 2], blocks // 2),
        blocks,
    )
    if sub > 1:
        part = tile % sub
        rows = width // sub
        matrix = lax.dynamic_slice(matrix, (part * rows, 0), (rows, blocks * width))
        vector = lax.dynamic_slice(vector, (0, part * rows), (1, rows))
    return matrix[None], vector


def solution(mesh):
    return jax.shard_map(
        functools.partial(local, mesh.shape["tile"]),
        mesh=mesh,
        in_specs=(
            P(("region", "tile"), None, None),
            P(("region", "tile"), None, None),
            P(("region", "tile"), None),
            P(("region", "tile"), None),
            P(("region", "tile"), None),
            P(("region", "tile")),
            P(("region", "tile"), None),
            P(),
        ),
        out_specs=(P("region", "tile", None), P("region", "tile")),
        check_vma=False,
    )
```

```python
import functools
import jax
import jax.numpy as jnp
from jax import lax
from jax.experimental import pallas as pl
from jax.experimental.pallas import tpu as pltpu
from jax.sharding import PartitionSpec as P

F32 = jnp.float32
BF16 = jnp.bfloat16
GROUP = 8
PAIR = 2 * GROUP
DEPTH = 256

NT = (((1,), (1,)), ((), ()))


def iota(shape, axis):
    return lax.broadcasted_iota(jnp.int32, shape, axis)


def fit(ld, weight, resid, counts):
    hits = weight.shape[0]
    live = iota(weight.shape, 0) < counts.astype(jnp.int32)
    masked_w = jnp.where(live, weight, 0.0)
    weighted_l = [v * masked_w for v in ld]
    gamma = [[None] * 5 for _ in range(5)]
    for a in range(5):
        for b in range(a + 1):
            gamma[a][b] = jnp.sum(weighted_l[a] * ld[b], axis=0, keepdims=True)
            if a == b:
                gamma[a][b] = gamma[a][b] + 1.0
    beta = [jnp.sum(weighted_l[a] * resid, axis=0, keepdims=True) for a in range(5)]
    factor = [[None] * 5 for _ in range(5)]
    inverse = [None] * 5
    for j in range(5):
        center = gamma[j][j]
        for k in range(j):
            center = center - factor[j][k] * factor[j][k]
        factor[j][j] = jnp.sqrt(center)
        inverse[j] = 1.0 / factor[j][j]
        for i in range(j + 1, 5):
            offdiag = gamma[i][j]
            for k in range(j):
                offdiag = offdiag - factor[i][k] * factor[j][k]
            factor[i][j] = offdiag * inverse[j]
    solved, rhs = [], []
    for j in range(5):
        current, target = weighted_l[j], beta[j]
        for k in range(j):
            current = current - factor[j][k] * solved[k]
            target = target - factor[j][k] * rhs[k]
        solved.append(current * inverse[j])
        rhs.append(target * inverse[j])
    projection = solved[0] * rhs[0]
    for k in range(1, 5):
        projection = projection + solved[k] * rhs[k]
    return solved, masked_w * resid - projection, masked_w


def prepare(
    place_ref, region_ref, count_ref, ld_ref, weight_ref, resid_ref, ids_ref,
    scaled_ref, lanes_ref, column_ref, table_ref,
):
    tracks = region_ref.shape[1]
    groups, _, depth = scaled_ref.shape
    slots = groups * GROUP
    hits = depth // GROUP
    blocks = place_ref.shape[0]
    rr = table_ref.shape[0] - 8
    member = (iota((rr, tracks), 0) == region_ref[...]).astype(F32)
    before = (iota((tracks, tracks), 0) < iota((tracks, tracks), 1)).astype(F32).astype(BF16)
    rank = jnp.dot(member.astype(BF16), before, preferred_element_type=F32)
    count = jnp.sum(member, axis=1, keepdims=True)
    room = (count.astype(jnp.int32) + (PAIR - 1)) & -PAIR
    room = jnp.broadcast_to(room.astype(F32), (rr, slots))
    lower = (iota((rr, rr), 1) < iota((rr, rr), 0)).astype(F32)
    start = jnp.zeros((rr, slots), F32)
    for g in range(rr):
        start = start + lower[:, g : g + 1] * room[g : g + 1, :]
    slot = jnp.sum(member * (rank + start[:, 0:1]), axis=0, keepdims=True)
    perm = (iota((slots, tracks), 0) == slot.astype(jnp.int32)).astype(F32).astype(BF16)
    numbers = jnp.where(
        iota((8, tracks), 0) == 0, iota((8, tracks), 1), jnp.broadcast_to(count_ref[...], (8, tracks))
    )

    def sort(value):
        return lax.dot_general(value, perm, NT, preferred_element_type=F32)

    numbers = sort(numbers.astype(F32).astype(BF16))
    table_ref[0:8, :] = numbers.astype(jnp.int32)
    table_ref[8:, :] = jnp.where(
        iota((rr, slots), 1) == 0, start.astype(jnp.int32), (start + room).astype(jnp.int32)
    )
    flat = sort(ld_ref[...])
    ld = [flat[c * hits : (c + 1) * hits] for c in range(5)]
    solved, hit_factor, masked_w = fit(
        ld, sort(weight_ref[...]), sort(resid_ref[...]), numbers[1:2]
    )
    ids = sort(ids_ref[...].astype(F32).astype(BF16))
    position = jnp.zeros_like(ids)
    for b in range(blocks):
        position = jnp.where(ids == float(b), place_ref[b].astype(F32), position)
    own = (iota((depth, slots), 0) // hits) == (iota((depth, slots), 1) % GROUP)

    def spread_out(value):
        return jnp.where(own, jnp.concatenate([value] * GROUP, axis=0), 0.0)

    grouping = (iota((groups, slots), 1) // GROUP == iota((groups, slots), 0)).astype(F32)
    for n, value in enumerate((masked_w, hit_factor)):
        lanes_ref[n] = lax.dot_general(
            grouping.astype(BF16), spread_out(value).astype(BF16), NT, preferred_element_type=F32
        )
    columns = column_ref.shape[1]
    grouping = (iota((columns, slots), 1) // GROUP == iota((columns, slots), 0)).astype(F32)
    column_ref[...] = lax.dot_general(
        spread_out(position).astype(BF16), grouping.astype(BF16), NT, preferred_element_type=F32
    ).astype(BF16)
    for c in range(5):
        scaled_ref[:, c * GROUP : (c + 1) * GROUP, :] = spread_out(solved[c]).T.reshape(
            groups, GROUP, depth
        )


def one_step(step, at, table_ref, g_ref, scaled_ref, lanes_ref, column_ref, g_s, direct_s, spread_s):
    hits, width = g_ref.shape[1:]
    depth = GROUP * hits
    blocks = spread_s.shape[1] // width
    rows = 5 * GROUP
    head = width + 8
    direct = []
    for u in range(2):
        group = step * 2 + u
        for i in range(GROUP):
            g_s[u, i * hits : (i + 1) * hits, :] = g_ref[table_ref[0, group * GROUP + i]]
        g = g_s[u]
        chosen = (iota((128, width), 0) == group).astype(F32).astype(BF16)
        position = jnp.dot(column_ref[...], chosen, preferred_element_type=F32).astype(BF16)
        right = jnp.concatenate(
            [jnp.where(position == jnp.bfloat16(p), g, jnp.bfloat16(0)) for p in range(blocks)],
            axis=1,
        )
        weighted = g.astype(F32).T * lanes_ref[0, pl.ds(group, 1), :]
        factor = jnp.where(iota((8, depth), 0) == 0, lanes_ref[1, pl.ds(group, 1), :], 0.0)
        scaled = scaled_ref[group]
        high = scaled.astype(BF16).astype(F32)
        left = jnp.concatenate(
            [weighted, factor, high, scaled - high, jnp.zeros((8, depth), F32)], axis=0
        )
        total = jnp.dot(left.astype(BF16), right, preferred_element_type=F32)
        direct.append(total[:head])
        spread_s[pl.ds(pl.multiple_of(at + u * rows, GROUP), rows), :] = (
            total[head : head + rows] + total[head + rows : head + 2 * rows]
        )
    direct_s[...] += direct[0] + direct[1]


EVEN = (0, 4, 2, 6)
ODD = (0, 2, 4, 6)


def fetch(pairs, sems):
    copies = [
        pltpu.make_async_copy(source, target, sems.at[n])
        for n, (source, target) in enumerate(pairs)
    ]
    for copy in copies:
        copy.start()
    return copies


def lead_kernel(ks, sub, *refs):
    small, g_hbm, (keep_ref, send_ref), shared = refs[:7], refs[7], refs[8:10], refs[10:14]
    local_small, g_ref, table_s, sems, scratch = refs[14:21], refs[21], refs[22], refs[23], refs[24:]

    @pl.when(pl.program_id(0) == 0)
    def _():
        copies = fetch([*zip(small, local_small), (g_hbm, g_ref)], sems)
        for copy in copies[:-1]:
            copy.wait()
        prepare(*local_small, *shared)
        copy = pltpu.make_async_copy(shared[3], table_s, sems.at[0])
        copy.start()
        copy.wait()
        copies[-1].wait()

    assemble_region(ks, sub, table_s, *shared[:3], g_ref, keep_ref, send_ref, *scratch)


def follow_kernel(ks, sub, *refs):
    shared, (keep_ref, send_ref), mine, sems, scratch = (
        refs[:5], refs[5:7], refs[7:12], refs[12], refs[13:]
    )

    @pl.when(pl.program_id(0) == 0)
    def _():
        for copy in fetch(list(zip(shared, mine)), sems):
            copy.wait()

    assemble_region(ks, sub, mine[3], *mine[:3], mine[4], keep_ref, send_ref, *scratch)


def assemble_region(
    ks, sub, table_ref, scaled_ref, lanes_ref, column_ref, g_ref,
    keep_ref, send_ref, g_s, direct_s, spread_s, wide_s, turned_s, acc_s,
):
    k = jnp.where(pl.program_id(0) == 0, ks[0], ks[1])
    width = g_ref.shape[2]
    blocks = spread_s.shape[1] // width
    many = blocks // 2
    region = lax.axis_index("region") ^ k
    block = lax.axis_index("tile") // sub
    first = table_ref[8 + region, 0] // PAIR
    steps = table_ref[8 + region, 1] // PAIR - first
    direct_s[...] = jnp.zeros_like(direct_s)

    def group_step(n, carry):
        one_step(
            first + n, n * (10 * GROUP), table_ref, g_ref, scaled_ref, lanes_ref, column_ref,
            g_s, direct_s, spread_s,
        )
        return carry

    lax.fori_loop(0, steps, group_step, 0)
    used = steps * 10
    depth_tiles = DEPTH // 8
    chunks = jnp.maximum((used + depth_tiles - 1) // depth_tiles, 1)

    def clear(tile, carry):
        spread_s[pl.ds(pl.multiple_of(tile * 8, 8), 8), :] = jnp.zeros((8, blocks * width), F32)
        return carry

    lax.fori_loop(used, chunks * depth_tiles, clear, 0)

    def chunk_step(chunk, carry):
        at = pl.multiple_of(chunk * DEPTH, DEPTH)
        narrow = spread_s[pl.ds(at, DEPTH), :].astype(BF16)
        wide_s[:, : blocks * width] = narrow
        wide_s[:, blocks * width :] = narrow[:, : many * width]
        turned_s[...] = -narrow.T

        def product(p):
            columns = (many + (1 if p < many else 0)) * width
            return columns, jnp.dot(
                turned_s[p * width : (p + 1) * width],
                wide_s[:, p * width : p * width + columns],
                preferred_element_type=F32,
            )

        @pl.when(chunk == 0)
        def _():
            for p in range(blocks):
                columns, value = product(p)
                acc_s[p, :, :columns] = value

        @pl.when(chunk > 0)
        def _():
            for p in range(blocks):
                columns, value = product(p)
                acc_s[p, :, :columns] += value

        return carry

    lax.fori_loop(0, chunks, chunk_step, 0)
    half = width // 2
    for n in range(blocks // 2):
        for odd, out_ref in ((0, keep_ref), (1, send_ref)):
            p = block ^ (jnp.where(block % 2 == 1 - odd, ODD[n], EVEN[n]) + odd)
            columns = pl.ds(pl.multiple_of(p * width, width), width)
            parts = [direct_s[0:width, columns] + acc_s[p, :, 0:width]]
            parts += [acc_s[p, :, d * width : (d + 1) * width] for d in range(1, many)]
            upper = pl.multiple_of((p // many) * half, half)
            parts.append(acc_s[p % many, pl.ds(upper, half), many * width :])
            row = direct_s[width : width + 1, columns]
            high = row.astype(BF16).astype(F32)
            sub = iota((16, width), 0)
            parts.append(jnp.where(sub == 0, high, jnp.where(sub == 1, row - high, 0.0)))
            out_ref[0, n] = jnp.concatenate(parts, axis=0).astype(BF16)


def assemble(ks, sub, inputs, g, blocks, regions):
    tracks, hits, width = g.shape
    lead = len(inputs) == 7
    rows = width * (blocks // 2) + width // 2 + 16
    longest = -(-(-(-tracks // PAIR) * 5 * PAIR) // DEPTH) * DEPTH
    rr = -(-regions // 8) * 8
    slots = -(-(tracks + regions * (PAIR - 1)) // 128) * 128
    shared = [
        jax.ShapeDtypeStruct((slots // GROUP, 5 * GROUP, GROUP * hits), F32),
        jax.ShapeDtypeStruct((2, slots // GROUP, GROUP * hits), F32),
        jax.ShapeDtypeStruct((GROUP * hits, 128), BF16),
        jax.ShapeDtypeStruct((8 + rr, slots), jnp.int32),
    ]
    out = jax.ShapeDtypeStruct((2, blocks // 2, rows, width), BF16)
    spec = pl.BlockSpec((1, blocks // 2, rows, width), lambda k: (k, 0, 0, 0))
    vmem = pl.BlockSpec(memory_space=pltpu.VMEM)
    table = pltpu.SMEM(shared[3].shape, jnp.int32)
    arrived = pltpu.VMEM(g.shape, g.dtype)
    if lead:
        copies = [pltpu.SMEM(inputs[0].shape, jnp.int32)]
        copies += [pltpu.VMEM(value.shape, value.dtype) for value in inputs[1:]]
        copies += [arrived, table]
    else:
        copies = [pltpu.VMEM(value.shape, value.dtype) for value in inputs[:3]]
        copies += [table, arrived]
    return pl.pallas_call(
        functools.partial(lead_kernel if lead else follow_kernel, ks, sub),
        grid=(2,),
        in_specs=[pl.BlockSpec(memory_space=pltpu.HBM)] * (len(inputs) + 1),
        out_specs=[spec, spec] + [vmem] * (4 * lead),
        out_shape=[out, out] + shared * lead,
        scratch_shapes=copies
        + [
            pltpu.SemaphoreType.DMA((8,)),
            pltpu.VMEM((2, GROUP * hits, width), BF16),
            pltpu.VMEM((width + 8, blocks * width), F32),
            pltpu.VMEM((longest, blocks * width), F32),
            pltpu.VMEM((DEPTH, (blocks + blocks // 2) * width), BF16),
            pltpu.VMEM((blocks * width, DEPTH), BF16),
            pltpu.VMEM((blocks, width, (blocks // 2 + 1) * width), F32),
        ],
        compiler_params=pltpu.CompilerParams(
            dimension_semantics=("arbitrary",), vmem_limit_bytes=60 * 1024 * 1024
        ),
        cost_estimate=pl.CostEstimate(
            flops=8 * 10**9, bytes_accessed=4 * 10**6, transcendentals=0
        ),
        name="assemble",
    )(*inputs, g)


def finish_kernel(sub, own_ref, r1_ref, r2_ref, r3_ref, e_ref, out_ref, vec_ref):
    width = own_ref.shape[1]
    p = lax.axis_index("tile") // sub
    blocks = out_ref.shape[1] // width
    many = blocks // 2

    def put(column, value):
        column = pl.multiple_of(((column + blocks) % blocks) * width, width)
        out_ref[:, pl.ds(column, width)] = value

    for d in range(many):
        put(p + d, own_ref[d * width : (d + 1) * width, :])
    for d, ref in ((1, r1_ref), (2, r2_ref), (3, r3_ref)):
        put(p - d, ref[...].astype(F32).T)
    tail = many * width + width // 2
    mine = own_ref[many * width : tail, :]
    other = e_ref[...].astype(F32)

    @pl.when(p < many)
    def _():
        put(p + many, jnp.concatenate([mine, other], axis=0))

    @pl.when(p >= many)
    def _():
        put(p + many, jnp.concatenate([other, mine], axis=0).T)

    vec_ref[...] = own_ref[tail : tail + 1, :] + own_ref[tail + 1 : tail + 2, :]


def finish(sub, own, r1, r2, r3, ext, blocks):
    width = own.shape[1]
    vmem = pl.BlockSpec(memory_space=pltpu.VMEM)
    return pl.pallas_call(
        functools.partial(finish_kernel, sub),
        in_specs=[vmem] * 5,
        out_specs=[vmem, vmem],
        out_shape=[
            jax.ShapeDtypeStruct((width, blocks * width), F32),
            jax.ShapeDtypeStruct((1, width), F32),
        ],
        name="finish",
    )(own, r1, r2, r3, ext)


def local(
    tiles, global_deriv, local_deriv, hit_weight, hit_resid, block_ids, hit_count, track_region,
    block_place,
):
    regions = lax.axis_size("region")
    tracks, hits, width = global_deriv.shape
    blocks = block_place.shape[0]
    sub = tiles // blocks
    tile = lax.axis_index("tile")
    inputs = (
        block_place,
        track_region.reshape(1, tracks),
        hit_count.reshape(1, tracks),
        local_deriv.transpose(1, 2, 0).reshape(-1, tracks),
        hit_weight.T,
        hit_resid.T,
        block_ids.T,
    )

    def swap(value, even, odd):
        pairs = [(t, t ^ (sub * (odd if t // sub % 2 else even))) for t in range(tiles)]
        return lax.ppermute(value, "tile", pairs)

    def across(value, k):
        return lax.ppermute(value.astype(BF16), "region", [(r, r ^ k) for r in range(regions)])

    def near(keep, send):
        bit = 1
        while bit < sub:
            pairs = [(t, t ^ bit) for t in range(tiles)]
            keep, send = (v + lax.ppermute(v, "tile", pairs) for v in (keep, send))
            bit *= 2
        return keep.astype(F32) + swap(send, 1, 1).astype(F32)

    def halve(total, even, odd):
        half = total.shape[0] // 2
        return total[:half], swap(total[half:].astype(BF16), even, odd).astype(F32)

    def plane(total):
        total = sum(halve(total, 2, 4))
        total = sum(halve(total, 4, 2))
        return total[0]

    arrived = []
    for n in range(0, regions, 2):
        ks = (n + 1, (n + 2) % regions)
        keep, send, *made = assemble(ks, sub, inputs, global_deriv, blocks, regions)
        if n == 0:
            inputs = tuple(made)
        else:
            send, *waited = lax.optimization_barrier((send, *waited))
            if n == 2:
                early = waited[1]
            total = kept + waited[0].astype(F32)
            total = sum(halve(total, 4, 2))[0]
            arrived.append(across(total, ks[0] - 1))
        pair = near(keep, send)
        if n == 0:
            early, late = across(pair[0, 2:], 1), across(pair[0, :2], 1)
        else:
            arrived.append(across(plane(pair[0]), ks[0]))
        if n + 2 < regions:
            kept, third = pair[1, :2], pair[1, 2:].astype(BF16)
            third, rest = lax.optimization_barrier((third, inputs[3]))
            inputs = inputs[:3] + (rest,)
            waited = [swap(third, 2, 4)] + [early] * (n == 0)
    last = pair[1]
    upper = swap((last[2:] + early.astype(F32)).astype(BF16), 2, 4)
    last = last[:2] + late.astype(F32) + upper.astype(F32)
    own = sum(halve(last, 4, 2))[0]
    for value in arrived:
        own = own + value.astype(F32)

    def onward(value, d):
        pairs = [
            (p * sub + s, ((p + d) % blocks) * sub + s) for p in range(blocks) for s in range(sub)
        ]
        return lax.ppermute(value.astype(BF16), "tile", pairs)

    matrix, vector = finish(
        sub,
        own,
        *(onward(own[d * width : (d + 1) * width], d) for d in range(1, blocks // 2)),
        onward(own[blocks // 2 * width : blocks // 2 * width + width // 2], blocks // 2),
        blocks,
    )
    if sub > 1:
        part = tile % sub
        rows = width // sub
        matrix = lax.dynamic_slice(matrix, (part * rows, 0), (rows, blocks * width))
        vector = lax.dynamic_slice(vector, (0, part * rows), (1, rows))
    return matrix[None], vector


def solution(mesh):
    return jax.shard_map(
        functools.partial(local, mesh.shape["tile"]),
        mesh=mesh,
        in_specs=(
            P(("region", "tile"), None, None),
            P(("region", "tile"), None, None),
            P(("region", "tile"), None),
            P(("region", "tile"), None),
            P(("region", "tile"), None),
            P(("region", "tile")),
            P(("region", "tile"), None),
            P(),
        ),
        out_specs=(P("region", "tile", None), P("region", "tile")),
        check_vma=False,
    )
```

```python
import functools
import jax
import jax.numpy as jnp
from jax import lax
from jax.experimental import pallas as pl
from jax.experimental.pallas import tpu as pltpu
from jax.sharding import PartitionSpec as P

F32 = jnp.float32
BF16 = jnp.bfloat16
GROUP = 8
PAIR = 2 * GROUP
DEPTH = 256

NT = (((1,), (1,)), ((), ()))


def iota(shape, axis):
    return lax.broadcasted_iota(jnp.int32, shape, axis)


def fit(ld, weight, resid, counts):
    hits = weight.shape[0]
    live = iota(weight.shape, 0) < counts.astype(jnp.int32)
    masked_w = jnp.where(live, weight, 0.0)
    weighted_l = [v * masked_w for v in ld]
    gamma = [[None] * 5 for _ in range(5)]
    for a in range(5):
        for b in range(a + 1):
            gamma[a][b] = jnp.sum(weighted_l[a] * ld[b], axis=0, keepdims=True)
            if a == b:
                gamma[a][b] = gamma[a][b] + 1.0
    beta = [jnp.sum(weighted_l[a] * resid, axis=0, keepdims=True) for a in range(5)]
    factor = [[None] * 5 for _ in range(5)]
    inverse = [None] * 5
    for j in range(5):
        center = gamma[j][j]
        for k in range(j):
            center = center - factor[j][k] * factor[j][k]
        factor[j][j] = jnp.sqrt(center)
        inverse[j] = 1.0 / factor[j][j]
        for i in range(j + 1, 5):
            offdiag = gamma[i][j]
            for k in range(j):
                offdiag = offdiag - factor[i][k] * factor[j][k]
            factor[i][j] = offdiag * inverse[j]
    solved, rhs = [], []
    for j in range(5):
        current, target = weighted_l[j], beta[j]
        for k in range(j):
            current = current - factor[j][k] * solved[k]
            target = target - factor[j][k] * rhs[k]
        solved.append(current * inverse[j])
        rhs.append(target * inverse[j])
    projection = solved[0] * rhs[0]
    for k in range(1, 5):
        projection = projection + solved[k] * rhs[k]
    return solved, masked_w * resid - projection, masked_w


def prepare(
    place_ref, region_ref, count_ref, ld_ref, weight_ref, resid_ref, ids_ref,
    scaled_ref, lanes_ref, column_ref, table_ref,
):
    tracks = region_ref.shape[1]
    groups, _, depth = scaled_ref.shape
    slots = groups * GROUP
    hits = depth // GROUP
    blocks = place_ref.shape[0]
    rr = table_ref.shape[0] - 8
    member = (iota((rr, tracks), 0) == region_ref[...]).astype(F32)
    before = (iota((tracks, tracks), 0) < iota((tracks, tracks), 1)).astype(F32).astype(BF16)
    rank = jnp.dot(member.astype(BF16), before, preferred_element_type=F32)
    count = jnp.sum(member, axis=1, keepdims=True)
    room = (count.astype(jnp.int32) + (PAIR - 1)) & -PAIR
    room = jnp.broadcast_to(room.astype(F32), (rr, slots))
    lower = (iota((rr, rr), 1) < iota((rr, rr), 0)).astype(F32)
    start = jnp.zeros((rr, slots), F32)
    for g in range(rr):
        start = start + lower[:, g : g + 1] * room[g : g + 1, :]
    slot = jnp.sum(member * (rank + start[:, 0:1]), axis=0, keepdims=True)
    perm = (iota((slots, tracks), 0) == slot.astype(jnp.int32)).astype(F32).astype(BF16)
    numbers = jnp.where(
        iota((8, tracks), 0) == 0, iota((8, tracks), 1), jnp.broadcast_to(count_ref[...], (8, tracks))
    )

    def sort(value):
        return lax.dot_general(value, perm, NT, preferred_element_type=F32)

    numbers = sort(numbers.astype(F32).astype(BF16))
    table_ref[0:8, :] = numbers.astype(jnp.int32)
    table_ref[8:, :] = jnp.where(
        iota((rr, slots), 1) == 0, start.astype(jnp.int32), (start + room).astype(jnp.int32)
    )
    flat = sort(ld_ref[...])
    ld = [flat[c * hits : (c + 1) * hits] for c in range(5)]
    solved, hit_factor, masked_w = fit(
        ld, sort(weight_ref[...]), sort(resid_ref[...]), numbers[1:2]
    )
    ids = sort(ids_ref[...].astype(F32).astype(BF16))
    position = jnp.zeros_like(ids)
    for b in range(blocks):
        position = jnp.where(ids == float(b), place_ref[b].astype(F32), position)
    own = (iota((depth, slots), 0) // hits) == (iota((depth, slots), 1) % GROUP)

    def spread_out(value):
        return jnp.where(own, jnp.concatenate([value] * GROUP, axis=0), 0.0)

    grouping = (iota((groups, slots), 1) // GROUP == iota((groups, slots), 0)).astype(F32)
    for n, value in enumerate((masked_w, hit_factor)):
        lanes_ref[n] = lax.dot_general(
            grouping.astype(BF16), spread_out(value).astype(BF16), NT, preferred_element_type=F32
        )
    columns = column_ref.shape[1]
    grouping = (iota((columns, slots), 1) // GROUP == iota((columns, slots), 0)).astype(F32)
    column_ref[...] = lax.dot_general(
        spread_out(position).astype(BF16), grouping.astype(BF16), NT, preferred_element_type=F32
    ).astype(BF16)
    for c in range(5):
        scaled_ref[:, c * GROUP : (c + 1) * GROUP, :] = spread_out(solved[c]).T.reshape(
            groups, GROUP, depth
        )


def one_step(step, at, table_ref, g_ref, scaled_ref, lanes_ref, column_ref, g_s, direct_s, spread_s):
    hits, width = g_ref.shape[1:]
    depth = GROUP * hits
    blocks = spread_s.shape[1] // width
    rows = 5 * GROUP
    head = width + 8
    unit = (iota((width, width), 0) == iota((width, width), 1)).astype(F32).astype(BF16)
    lefts, values, positions = [], [], []
    for u in range(2):
        group = step * 2 + u
        for i in range(GROUP):
            g_s[u, i * hits : (i + 1) * hits, :] = g_ref[table_ref[0, group * GROUP + i]]
        g = g_s[u]
        chosen = (iota((128, width), 0) == group).astype(F32).astype(BF16)
        position = jnp.dot(column_ref[...], chosen, preferred_element_type=F32)
        turned = lax.dot_general(unit, g, NT, preferred_element_type=F32)
        weighted = turned * lanes_ref[0, pl.ds(group, 1), :]
        factor = jnp.where(iota((8, depth), 0) == 0, lanes_ref[1, pl.ds(group, 1), :], 0.0)
        scaled = scaled_ref[group]
        high = scaled.astype(BF16).astype(F32)
        left = jnp.concatenate(
            [weighted, factor, high, scaled - high, jnp.zeros((8, depth), F32)], axis=0
        )
        lefts.append(left.astype(BF16))
        values.append(g)
        positions.append(position.astype(BF16))
    for p in range(0, blocks, 2):
        columns = slice(p * width, (p + 2) * width)
        direct = direct_s[:, columns]
        for u in range(2):
            right = jnp.concatenate(
                [
                    jnp.where(positions[u] == jnp.bfloat16(q), values[u], jnp.bfloat16(0))
                    for q in (p, p + 1)
                ],
                axis=1,
            )
            total = jnp.dot(lefts[u], right, preferred_element_type=F32)
            direct = direct + total[:head]
            spread_s[pl.ds(pl.multiple_of(at + u * rows, GROUP), rows), columns] = (
                total[head : head + rows] + total[head + rows : head + 2 * rows]
            )
        direct_s[:, columns] = direct


EVEN = (0, 4, 2, 6)
ODD = (0, 2, 4, 6)


def fetch(pairs, sems):
    copies = [
        pltpu.make_async_copy(source, target, sems.at[n])
        for n, (source, target) in enumerate(pairs)
    ]
    for copy in copies:
        copy.start()
    return copies


def lead_kernel(ks, sub, *refs):
    small, g_hbm, (keep_ref, send_ref), shared = refs[:7], refs[7], refs[8:10], refs[10:14]
    local_small, g_ref, table_s, sems, scratch = refs[14:21], refs[21], refs[22], refs[23], refs[24:]

    @pl.when(pl.program_id(0) == 0)
    def _():
        copies = fetch([*zip(small, local_small), (g_hbm, g_ref)], sems)
        for copy in copies[:-1]:
            copy.wait()
        prepare(*local_small, *shared)
        copy = pltpu.make_async_copy(shared[3], table_s, sems.at[0])
        copy.start()
        copy.wait()
        copies[-1].wait()

    assemble_region(ks, sub, table_s, *shared[:3], g_ref, keep_ref, send_ref, *scratch)


def follow_kernel(ks, sub, *refs):
    shared, (keep_ref, send_ref), mine, sems, scratch = (
        refs[:5], refs[5:7], refs[7:12], refs[12], refs[13:]
    )

    @pl.when(pl.program_id(0) == 0)
    def _():
        for copy in fetch(list(zip(shared, mine)), sems):
            copy.wait()

    assemble_region(ks, sub, mine[3], *mine[:3], mine[4], keep_ref, send_ref, *scratch)


def assemble_region(
    ks, sub, table_ref, scaled_ref, lanes_ref, column_ref, g_ref,
    keep_ref, send_ref, g_s, direct_s, spread_s, wide_s, turned_s, acc_s,
):
    k = jnp.where(pl.program_id(0) == 0, ks[0], ks[1])
    width = g_ref.shape[2]
    blocks = spread_s.shape[1] // width
    many = blocks // 2
    region = lax.axis_index("region") ^ k
    block = lax.axis_index("tile") // sub
    first = table_ref[8 + region, 0] // PAIR
    steps = table_ref[8 + region, 1] // PAIR - first
    direct_s[...] = jnp.zeros_like(direct_s)

    def group_step(n, carry):
        one_step(
            first + n, n * (10 * GROUP), table_ref, g_ref, scaled_ref, lanes_ref, column_ref,
            g_s, direct_s, spread_s,
        )
        return carry

    lax.fori_loop(0, steps, group_step, 0)
    used = steps * 10
    depth_tiles = DEPTH // 8
    chunks = jnp.maximum((used + depth_tiles - 1) // depth_tiles, 1)

    def clear(tile, carry):
        spread_s[pl.ds(pl.multiple_of(tile * 8, 8), 8), :] = jnp.zeros((8, blocks * width), F32)
        return carry

    lax.fori_loop(used, chunks * depth_tiles, clear, 0)

    def chunk_step(chunk, carry):
        at = pl.multiple_of(chunk * DEPTH, DEPTH)
        narrow = spread_s[pl.ds(at, DEPTH), :].astype(BF16)
        wide_s[:, : blocks * width] = narrow
        wide_s[:, blocks * width :] = narrow[:, : many * width]
        turned_s[...] = -narrow.T

        def product(p):
            columns = (many + (1 if p < many else 0)) * width
            return columns, jnp.dot(
                turned_s[p * width : (p + 1) * width],
                wide_s[:, p * width : p * width + columns],
                preferred_element_type=F32,
            )

        @pl.when(chunk == 0)
        def _():
            for p in range(blocks):
                columns, value = product(p)
                acc_s[p, :, :columns] = value

        @pl.when(chunk > 0)
        def _():
            for p in range(blocks):
                columns, value = product(p)
                acc_s[p, :, :columns] += value

        return carry

    lax.fori_loop(0, chunks, chunk_step, 0)
    half = width // 2
    for n in range(blocks // 2):
        for odd, out_ref in ((0, keep_ref), (1, send_ref)):
            p = block ^ (jnp.where(block % 2 == 1 - odd, ODD[n], EVEN[n]) + odd)
            columns = pl.ds(pl.multiple_of(p * width, width), width)
            parts = [direct_s[0:width, columns] + acc_s[p, :, 0:width]]
            parts += [acc_s[p, :, d * width : (d + 1) * width] for d in range(1, many)]
            upper = pl.multiple_of((p // many) * half, half)
            parts.append(acc_s[p % many, pl.ds(upper, half), many * width :])
            row = direct_s[width : width + 1, columns]
            high = row.astype(BF16).astype(F32)
            sub = iota((16, width), 0)
            parts.append(jnp.where(sub == 0, high, jnp.where(sub == 1, row - high, 0.0)))
            out_ref[0, n] = jnp.concatenate(parts, axis=0).astype(BF16)


def assemble(ks, sub, inputs, g, blocks, regions):
    tracks, hits, width = g.shape
    lead = len(inputs) == 7
    rows = width * (blocks // 2) + width // 2 + 16
    longest = -(-(-(-tracks // PAIR) * 5 * PAIR) // DEPTH) * DEPTH
    rr = -(-regions // 8) * 8
    slots = -(-(tracks + regions * (PAIR - 1)) // 128) * 128
    shared = [
        jax.ShapeDtypeStruct((slots // GROUP, 5 * GROUP, GROUP * hits), F32),
        jax.ShapeDtypeStruct((2, slots // GROUP, GROUP * hits), F32),
        jax.ShapeDtypeStruct((GROUP * hits, 128), BF16),
        jax.ShapeDtypeStruct((8 + rr, slots), jnp.int32),
    ]
    out = jax.ShapeDtypeStruct((2, blocks // 2, rows, width), BF16)
    spec = pl.BlockSpec((1, blocks // 2, rows, width), lambda k: (k, 0, 0, 0))
    vmem = pl.BlockSpec(memory_space=pltpu.VMEM)
    table = pltpu.SMEM(shared[3].shape, jnp.int32)
    arrived = pltpu.VMEM(g.shape, g.dtype)
    if lead:
        copies = [pltpu.SMEM(inputs[0].shape, jnp.int32)]
        copies += [pltpu.VMEM(value.shape, value.dtype) for value in inputs[1:]]
        copies += [arrived, table]
    else:
        copies = [pltpu.VMEM(value.shape, value.dtype) for value in inputs[:3]]
        copies += [table, arrived]
    return pl.pallas_call(
        functools.partial(lead_kernel if lead else follow_kernel, ks, sub),
        grid=(2,),
        in_specs=[pl.BlockSpec(memory_space=pltpu.HBM)] * (len(inputs) + 1),
        out_specs=[spec, spec] + [vmem] * (4 * lead),
        out_shape=[out, out] + shared * lead,
        scratch_shapes=copies
        + [
            pltpu.SemaphoreType.DMA((8,)),
            pltpu.VMEM((2, GROUP * hits, width), BF16),
            pltpu.VMEM((width + 8, blocks * width), F32),
            pltpu.VMEM((longest, blocks * width), F32),
            pltpu.VMEM((DEPTH, (blocks + blocks // 2) * width), BF16),
            pltpu.VMEM((blocks * width, DEPTH), BF16),
            pltpu.VMEM((blocks, width, (blocks // 2 + 1) * width), F32),
        ],
        compiler_params=pltpu.CompilerParams(
            dimension_semantics=("arbitrary",), vmem_limit_bytes=60 * 1024 * 1024
        ),
        cost_estimate=pl.CostEstimate(
            flops=8 * 10**9, bytes_accessed=4 * 10**6, transcendentals=0
        ),
        name="assemble",
    )(*inputs, g)


def finish_kernel(sub, own_ref, r1_ref, r2_ref, r3_ref, e_ref, out_ref, vec_ref):
    width = own_ref.shape[1]
    p = lax.axis_index("tile") // sub
    blocks = out_ref.shape[1] // width
    many = blocks // 2

    def put(column, value):
        column = pl.multiple_of(((column + blocks) % blocks) * width, width)
        out_ref[:, pl.ds(column, width)] = value

    for d in range(many):
        put(p + d, own_ref[d * width : (d + 1) * width, :])
    for d, ref in ((1, r1_ref), (2, r2_ref), (3, r3_ref)):
        put(p - d, ref[...].astype(F32).T)
    tail = many * width + width // 2
    mine = own_ref[many * width : tail, :]
    other = e_ref[...].astype(F32)

    @pl.when(p < many)
    def _():
        put(p + many, jnp.concatenate([mine, other], axis=0))

    @pl.when(p >= many)
    def _():
        put(p + many, jnp.concatenate([other, mine], axis=0).T)

    vec_ref[...] = own_ref[tail : tail + 1, :] + own_ref[tail + 1 : tail + 2, :]


def finish(sub, own, r1, r2, r3, ext, blocks):
    width = own.shape[1]
    vmem = pl.BlockSpec(memory_space=pltpu.VMEM)
    return pl.pallas_call(
        functools.partial(finish_kernel, sub),
        in_specs=[vmem] * 5,
        out_specs=[vmem, vmem],
        out_shape=[
            jax.ShapeDtypeStruct((width, blocks * width), F32),
            jax.ShapeDtypeStruct((1, width), F32),
        ],
        name="finish",
    )(own, r1, r2, r3, ext)


def local(
    tiles, global_deriv, local_deriv, hit_weight, hit_resid, block_ids, hit_count, track_region,
    block_place,
):
    regions = lax.axis_size("region")
    tracks, hits, width = global_deriv.shape
    blocks = block_place.shape[0]
    sub = tiles // blocks
    tile = lax.axis_index("tile")
    inputs = (
        block_place,
        track_region.reshape(1, tracks),
        hit_count.reshape(1, tracks),
        local_deriv.transpose(1, 2, 0).reshape(-1, tracks),
        hit_weight.T,
        hit_resid.T,
        block_ids.T,
    )

    def swap(value, even, odd):
        pairs = [(t, t ^ (sub * (odd if t // sub % 2 else even))) for t in range(tiles)]
        return lax.ppermute(value, "tile", pairs)

    def across(value, k):
        return lax.ppermute(value.astype(BF16), "region", [(r, r ^ k) for r in range(regions)])

    def near(keep, send):
        bit = 1
        while bit < sub:
            pairs = [(t, t ^ bit) for t in range(tiles)]
            keep, send = (v + lax.ppermute(v, "tile", pairs) for v in (keep, send))
            bit *= 2
        return keep, swap(send, 1, 1)

    def both(pair, n, part):
        return pair[0][n, part].astype(F32) + pair[1][n, part].astype(F32)

    def halve(total, even, odd):
        half = total.shape[0] // 2
        return total[:half], swap(total[half:].astype(BF16), even, odd).astype(F32)

    low, top = slice(0, blocks // 4), slice(blocks // 4, blocks // 2)
    arrived = []
    for n in range(0, regions, 2):
        ks = (n + 1, (n + 2) % regions)
        keep, send, *made = assemble(ks, sub, inputs, global_deriv, blocks, regions)
        if n == 0:
            inputs = tuple(made)
            pair = near(keep, send)
            early, late = across(both(pair, 0, top), 1), across(both(pair, 0, low), 1)
        else:
            send, pair, waited = lax.optimization_barrier((send, pair, waited))
            if n == 2:
                early = waited[1]
            half, more = halve(both(pair, 1, low) + waited[0].astype(F32), 4, 2)
            pair, more = lax.optimization_barrier((near(keep, send), more))
            value = across((half + more)[0], ks[0] - 1)
            more = swap(both(pair, 0, top).astype(BF16), 2, 4)
            if not ks[1]:
                upper = swap((both(pair, 1, top) + early.astype(F32)).astype(BF16), 2, 4)
                more, late, value = lax.optimization_barrier((more, late, value))
            half, more = halve(both(pair, 0, low) + more.astype(F32), 4, 2)
            if not ks[1]:
                more, upper, pair = lax.optimization_barrier((more, upper, pair))
            arrived += [value, across((half + more)[0], ks[0])]
        if ks[1]:
            third = both(pair, 1, top).astype(BF16)
            third, rest = lax.optimization_barrier((third, inputs[3]))
            inputs = inputs[:3] + (rest,)
            waited = [swap(third, 2, 4)] + [early] * (n == 0)
    last = both(pair, 1, low) + late.astype(F32) + upper.astype(F32)
    own = sum(halve(last, 4, 2))[0]
    for value in arrived:
        own = own + value.astype(F32)

    def onward(value, d):
        pairs = [
            (p * sub + s, ((p + d) % blocks) * sub + s) for p in range(blocks) for s in range(sub)
        ]
        return lax.ppermute(value.astype(BF16), "tile", pairs)

    matrix, vector = finish(
        sub,
        own,
        *(onward(own[d * width : (d + 1) * width], d) for d in range(1, blocks // 2)),
        onward(own[blocks // 2 * width : blocks // 2 * width + width // 2], blocks // 2),
        blocks,
    )
    if sub > 1:
        part = tile % sub
        rows = width // sub
        matrix = lax.dynamic_slice(matrix, (part * rows, 0), (rows, blocks * width))
        vector = lax.dynamic_slice(vector, (0, part * rows), (1, rows))
    return matrix[None], vector


def solution(mesh):
    return jax.shard_map(
        functools.partial(local, mesh.shape["tile"]),
        mesh=mesh,
        in_specs=(
            P(("region", "tile"), None, None),
            P(("region", "tile"), None, None),
            P(("region", "tile"), None),
            P(("region", "tile"), None),
            P(("region", "tile"), None),
            P(("region", "tile")),
            P(("region", "tile"), None),
            P(),
        ),
        out_specs=(P("region", "tile", None), P("region", "tile")),
        check_vma=False,
    )
```

```python
import functools
import jax
import jax.numpy as jnp
from jax import lax
from jax.experimental import pallas as pl
from jax.experimental.pallas import tpu as pltpu
from jax.sharding import PartitionSpec as P

F32 = jnp.float32
BF16 = jnp.bfloat16
GROUP = 8
PAIR = 2 * GROUP
DEPTH = 256

NT = (((1,), (1,)), ((), ()))


def iota(shape, axis):
    return lax.broadcasted_iota(jnp.int32, shape, axis)


def fit(ld, weight, resid, counts):
    hits = weight.shape[0]
    live = iota(weight.shape, 0) < counts.astype(jnp.int32)
    masked_w = jnp.where(live, weight, 0.0)
    weighted_l = [v * masked_w for v in ld]
    gamma = [[None] * 5 for _ in range(5)]
    for a in range(5):
        for b in range(a + 1):
            gamma[a][b] = jnp.sum(weighted_l[a] * ld[b], axis=0, keepdims=True)
            if a == b:
                gamma[a][b] = gamma[a][b] + 1.0
    beta = [jnp.sum(weighted_l[a] * resid, axis=0, keepdims=True) for a in range(5)]
    factor = [[None] * 5 for _ in range(5)]
    inverse = [None] * 5
    for j in range(5):
        center = gamma[j][j]
        for k in range(j):
            center = center - factor[j][k] * factor[j][k]
        factor[j][j] = jnp.sqrt(center)
        inverse[j] = 1.0 / factor[j][j]
        for i in range(j + 1, 5):
            offdiag = gamma[i][j]
            for k in range(j):
                offdiag = offdiag - factor[i][k] * factor[j][k]
            factor[i][j] = offdiag * inverse[j]
    solved, rhs = [], []
    for j in range(5):
        current, target = weighted_l[j], beta[j]
        for k in range(j):
            current = current - factor[j][k] * solved[k]
            target = target - factor[j][k] * rhs[k]
        solved.append(current * inverse[j])
        rhs.append(target * inverse[j])
    projection = solved[0] * rhs[0]
    for k in range(1, 5):
        projection = projection + solved[k] * rhs[k]
    return solved, masked_w * resid - projection, masked_w


def prepare(
    place_ref, region_ref, count_ref, ld_ref, weight_ref, resid_ref, ids_ref,
    scaled_ref, lanes_ref, column_ref, table_ref,
):
    tracks = region_ref.shape[1]
    groups, _, depth = scaled_ref.shape
    slots = groups * GROUP
    hits = depth // GROUP
    blocks = place_ref.shape[0]
    rr = table_ref.shape[0] - 8
    member = (iota((rr, tracks), 0) == region_ref[...]).astype(F32)
    before = (iota((tracks, tracks), 0) < iota((tracks, tracks), 1)).astype(F32).astype(BF16)
    rank = jnp.dot(member.astype(BF16), before, preferred_element_type=F32)
    count = jnp.sum(member, axis=1, keepdims=True)
    room = (count.astype(jnp.int32) + (PAIR - 1)) & -PAIR
    room = jnp.broadcast_to(room.astype(F32), (rr, slots))
    lower = (iota((rr, rr), 1) < iota((rr, rr), 0)).astype(F32)
    start = jnp.zeros((rr, slots), F32)
    for g in range(rr):
        start = start + lower[:, g : g + 1] * room[g : g + 1, :]
    slot = jnp.sum(member * (rank + start[:, 0:1]), axis=0, keepdims=True)
    perm = (iota((slots, tracks), 0) == slot.astype(jnp.int32)).astype(F32).astype(BF16)
    numbers = jnp.where(
        iota((8, tracks), 0) == 0, iota((8, tracks), 1), jnp.broadcast_to(count_ref[...], (8, tracks))
    )

    def sort(value):
        return lax.dot_general(value, perm, NT, preferred_element_type=F32)

    numbers = sort(numbers.astype(F32).astype(BF16))
    table_ref[0:8, :] = numbers.astype(jnp.int32)
    table_ref[8:, :] = jnp.where(
        iota((rr, slots), 1) == 0, start.astype(jnp.int32), (start + room).astype(jnp.int32)
    )
    flat = sort(ld_ref[...])
    ld = [flat[c * hits : (c + 1) * hits] for c in range(5)]
    solved, hit_factor, masked_w = fit(
        ld, sort(weight_ref[...]), sort(resid_ref[...]), numbers[1:2]
    )
    ids = sort(ids_ref[...].astype(F32).astype(BF16))
    position = jnp.zeros_like(ids)
    for b in range(blocks):
        position = jnp.where(ids == float(b), place_ref[b].astype(F32), position)
    own = (iota((depth, slots), 0) // hits) == (iota((depth, slots), 1) % GROUP)

    def spread_out(value):
        return jnp.where(own, jnp.concatenate([value] * GROUP, axis=0), 0.0)

    grouping = (iota((groups, slots), 1) // GROUP == iota((groups, slots), 0)).astype(F32)
    for n, value in enumerate((masked_w, hit_factor)):
        lanes_ref[n] = lax.dot_general(
            grouping.astype(BF16), spread_out(value).astype(BF16), NT, preferred_element_type=F32
        )
    columns = column_ref.shape[1]
    grouping = (iota((columns, slots), 1) // GROUP == iota((columns, slots), 0)).astype(F32)
    column_ref[...] = lax.dot_general(
        spread_out(position).astype(BF16), grouping.astype(BF16), NT, preferred_element_type=F32
    ).astype(BF16)
    for c in range(5):
        scaled_ref[:, c * GROUP : (c + 1) * GROUP, :] = spread_out(solved[c]).T.reshape(
            groups, GROUP, depth
        )


def one_step(step, at, table_ref, g_ref, scaled_ref, lanes_ref, column_ref, g_s, direct_s, spread_s):
    hits, width = g_ref.shape[1:]
    depth = GROUP * hits
    blocks = spread_s.shape[1] // width
    rows = 5 * GROUP
    head = width + 8
    unit = (iota((width, width), 0) == iota((width, width), 1)).astype(F32).astype(BF16)
    lefts, values, positions = [], [], []
    for u in range(2):
        group = step * 2 + u
        for i in range(GROUP):
            g_s[u, i * hits : (i + 1) * hits, :] = g_ref[table_ref[0, group * GROUP + i]]
        g = g_s[u]
        chosen = (iota((128, width), 0) == group).astype(F32).astype(BF16)
        position = jnp.dot(column_ref[...], chosen, preferred_element_type=F32)
        turned = lax.dot_general(unit, g, NT, preferred_element_type=F32)
        weighted = turned * lanes_ref[0, pl.ds(group, 1), :]
        factor = jnp.where(iota((8, depth), 0) == 0, lanes_ref[1, pl.ds(group, 1), :], 0.0)
        scaled = scaled_ref[group]
        high = scaled.astype(BF16).astype(F32)
        left = jnp.concatenate(
            [weighted, factor, high, scaled - high, jnp.zeros((8, depth), F32)], axis=0
        )
        lefts.append(left.astype(BF16))
        values.append(g)
        positions.append(position.astype(BF16))
    for p in range(0, blocks, 2):
        columns = slice(p * width, (p + 2) * width)
        direct = direct_s[:, columns]
        for u in range(2):
            right = jnp.concatenate(
                [
                    jnp.where(positions[u] == jnp.bfloat16(q), values[u], jnp.bfloat16(0))
                    for q in (p, p + 1)
                ],
                axis=1,
            )
            total = jnp.dot(lefts[u], right, preferred_element_type=F32)
            direct = direct + total[:head]
            spread_s[pl.ds(pl.multiple_of(at + u * rows, GROUP), rows), columns] = (
                total[head : head + rows] + total[head + rows : head + 2 * rows]
            )
        direct_s[:, columns] = direct


EVEN = (0, 4, 2, 6)
ODD = (0, 2, 4, 6)


def fetch(pairs, sems):
    copies = [
        pltpu.make_async_copy(source, target, sems.at[n])
        for n, (source, target) in enumerate(pairs)
    ]
    for copy in copies:
        copy.start()
    return copies


def lead_kernel(ks, sub, *refs):
    small, g_hbm, (keep_ref, send_ref), shared = refs[:7], refs[7], refs[8:10], refs[10:14]
    local_small, g_ref, table_s, sems, scratch = refs[14:21], refs[21], refs[22], refs[23], refs[24:]

    @pl.when(pl.program_id(0) == 0)
    def _():
        copies = fetch([*zip(small, local_small), (g_hbm, g_ref)], sems)
        for copy in copies[:-1]:
            copy.wait()
        prepare(*local_small, *shared)
        copy = pltpu.make_async_copy(shared[3], table_s, sems.at[0])
        copy.start()
        copy.wait()
        copies[-1].wait()

    assemble_region(ks, sub, table_s, *shared[:3], g_ref, keep_ref, send_ref, *scratch)


def follow_kernel(ks, sub, *refs):
    shared, (keep_ref, send_ref), mine, sems, scratch = (
        refs[:5], refs[5:7], refs[7:12], refs[12], refs[13:]
    )

    @pl.when(pl.program_id(0) == 0)
    def _():
        for copy in fetch(list(zip(shared, mine)), sems):
            copy.wait()

    assemble_region(ks, sub, mine[3], *mine[:3], mine[4], keep_ref, send_ref, *scratch)


def assemble_region(
    ks, sub, table_ref, scaled_ref, lanes_ref, column_ref, g_ref,
    keep_ref, send_ref, g_s, direct_s, spread_s, wide_s, turned_s, acc_s,
):
    k = jnp.where(pl.program_id(0) == 0, ks[0], ks[1])
    width = g_ref.shape[2]
    blocks = spread_s.shape[1] // width
    many = blocks // 2
    region = lax.axis_index("region") ^ k
    block = lax.axis_index("tile") // sub
    first = table_ref[8 + region, 0] // PAIR
    steps = table_ref[8 + region, 1] // PAIR - first
    direct_s[...] = jnp.zeros_like(direct_s)

    def group_step(n, carry):
        one_step(
            first + n, n * (10 * GROUP), table_ref, g_ref, scaled_ref, lanes_ref, column_ref,
            g_s, direct_s, spread_s,
        )
        return carry

    lax.fori_loop(0, steps, group_step, 0)
    used = steps * 10
    depth_tiles = DEPTH // 8
    chunks = jnp.maximum((used + depth_tiles - 1) // depth_tiles, 1)

    def clear(tile, carry):
        spread_s[pl.ds(pl.multiple_of(tile * 8, 8), 8), :] = jnp.zeros((8, blocks * width), F32)
        return carry

    lax.fori_loop(used, chunks * depth_tiles, clear, 0)

    unit = (iota((width, width), 0) == iota((width, width), 1)).astype(F32).astype(BF16)

    def chunk_step(chunk, carry):
        at = pl.multiple_of(chunk * DEPTH, DEPTH)
        wide_s[...] = spread_s[pl.ds(at, DEPTH), :].astype(BF16)
        for p in range(blocks):
            turned = lax.dot_general(
                unit, wide_s[:, p * width : (p + 1) * width], NT, preferred_element_type=F32
            )
            turned = (0.0 - turned).astype(BF16)
            turned_s[p * width : (p + 1) * width] = turned
            if p < many:
                turned_s[(blocks + p) * width : (blocks + p + 1) * width] = turned

        def products(add):
            for q in range(0, blocks, 2):
                upper = (q + blocks - many) % blocks
                value = jnp.dot(
                    turned_s[upper * width : (upper + many + 2) * width],
                    wide_s[:, q * width : (q + 2) * width],
                    preferred_element_type=F32,
                )
                for r in range(many + 2):
                    p = (upper + r) % blocks
                    for c in range(2):
                        d = many - r + c
                        if 0 <= d <= many and (d < many or p < many):
                            part = value[r * width : (r + 1) * width, c * width : (c + 1) * width]
                            columns = slice(d * width, (d + 1) * width)
                            acc_s[p, :, columns] = acc_s[p, :, columns] + part if add else part

        @pl.when(chunk == 0)
        def _():
            products(False)

        @pl.when(chunk > 0)
        def _():
            products(True)

        return carry

    lax.fori_loop(0, chunks, chunk_step, 0)
    half = width // 2
    for n in range(blocks // 2):
        for odd, out_ref in ((0, keep_ref), (1, send_ref)):
            p = block ^ (jnp.where(block % 2 == 1 - odd, ODD[n], EVEN[n]) + odd)
            columns = pl.ds(pl.multiple_of(p * width, width), width)
            parts = [direct_s[0:width, columns] + acc_s[p, :, 0:width]]
            parts += [acc_s[p, :, d * width : (d + 1) * width] for d in range(1, many)]
            upper = pl.multiple_of((p // many) * half, half)
            parts.append(acc_s[p % many, pl.ds(upper, half), many * width :])
            row = direct_s[width : width + 1, columns]
            high = row.astype(BF16).astype(F32)
            sub = iota((16, width), 0)
            parts.append(jnp.where(sub == 0, high, jnp.where(sub == 1, row - high, 0.0)))
            out_ref[n, 0] = jnp.concatenate(parts, axis=0).astype(BF16)


def assemble(ks, sub, inputs, g, blocks, regions):
    tracks, hits, width = g.shape
    lead = len(inputs) == 7
    rows = width * (blocks // 2) + width // 2 + 16
    longest = -(-(-(-tracks // PAIR) * 5 * PAIR) // DEPTH) * DEPTH
    rr = -(-regions // 8) * 8
    slots = -(-(tracks + regions * (PAIR - 1)) // 128) * 128
    shared = [
        jax.ShapeDtypeStruct((slots // GROUP, 5 * GROUP, GROUP * hits), F32),
        jax.ShapeDtypeStruct((2, slots // GROUP, GROUP * hits), F32),
        jax.ShapeDtypeStruct((GROUP * hits, 128), BF16),
        jax.ShapeDtypeStruct((8 + rr, slots), jnp.int32),
    ]
    out = jax.ShapeDtypeStruct((blocks // 2, 2, rows, width), BF16)
    spec = pl.BlockSpec((blocks // 2, 1, rows, width), lambda k: (0, k, 0, 0))
    vmem = pl.BlockSpec(memory_space=pltpu.VMEM)
    table = pltpu.SMEM(shared[3].shape, jnp.int32)
    arrived = pltpu.VMEM(g.shape, g.dtype)
    if lead:
        copies = [pltpu.SMEM(inputs[0].shape, jnp.int32)]
        copies += [pltpu.VMEM(value.shape, value.dtype) for value in inputs[1:]]
        copies += [arrived, table]
    else:
        copies = [pltpu.VMEM(value.shape, value.dtype) for value in inputs[:3]]
        copies += [table, arrived]
    return pl.pallas_call(
        functools.partial(lead_kernel if lead else follow_kernel, ks, sub),
        grid=(2,),
        in_specs=[pl.BlockSpec(memory_space=pltpu.HBM)] * (len(inputs) + 1),
        out_specs=[spec, spec] + [vmem] * (4 * lead),
        out_shape=[out, out] + shared * lead,
        scratch_shapes=copies
        + [
            pltpu.SemaphoreType.DMA((8,)),
            pltpu.VMEM((2, GROUP * hits, width), BF16),
            pltpu.VMEM((width + 8, blocks * width), F32),
            pltpu.VMEM((longest, blocks * width), F32),
            pltpu.VMEM((DEPTH, blocks * width), BF16),
            pltpu.VMEM(((blocks + blocks // 2) * width, DEPTH), BF16),
            pltpu.VMEM((blocks, width, (blocks // 2 + 1) * width), F32),
        ],
        compiler_params=pltpu.CompilerParams(
            dimension_semantics=("arbitrary",), vmem_limit_bytes=(60 if lead else 32) * 1024 * 1024
        ),
        cost_estimate=pl.CostEstimate(
            flops=8 * 10**9, bytes_accessed=4 * 10**6, transcendentals=0
        ),
        name="assemble",
    )(*inputs, g)


def finish_kernel(sub, own_ref, r1_ref, r2_ref, r3_ref, e_ref, out_ref, vec_ref):
    width = own_ref.shape[1]
    p = lax.axis_index("tile") // sub
    blocks = out_ref.shape[1] // width
    many = blocks // 2

    def put(column, value):
        column = pl.multiple_of(((column + blocks) % blocks) * width, width)
        out_ref[:, pl.ds(column, width)] = value

    for d in range(many):
        put(p + d, own_ref[d * width : (d + 1) * width, :])
    for d, ref in ((1, r1_ref), (2, r2_ref), (3, r3_ref)):
        put(p - d, ref[...].astype(F32).T)
    tail = many * width + width // 2
    mine = own_ref[many * width : tail, :]
    other = e_ref[...].astype(F32)

    @pl.when(p < many)
    def _():
        put(p + many, jnp.concatenate([mine, other], axis=0))

    @pl.when(p >= many)
    def _():
        put(p + many, jnp.concatenate([other, mine], axis=0).T)

    vec_ref[...] = own_ref[tail : tail + 1, :] + own_ref[tail + 1 : tail + 2, :]


def finish(sub, own, r1, r2, r3, ext, blocks):
    width = own.shape[1]
    vmem = pl.BlockSpec(memory_space=pltpu.VMEM)
    return pl.pallas_call(
        functools.partial(finish_kernel, sub),
        in_specs=[vmem] * 5,
        out_specs=[vmem, vmem],
        out_shape=[
            jax.ShapeDtypeStruct((width, blocks * width), F32),
            jax.ShapeDtypeStruct((1, width), F32),
        ],
        name="finish",
    )(own, r1, r2, r3, ext)


def local(
    tiles, global_deriv, local_deriv, hit_weight, hit_resid, block_ids, hit_count, track_region,
    block_place,
):
    regions = lax.axis_size("region")
    tracks, hits, width = global_deriv.shape
    blocks = block_place.shape[0]
    sub = tiles // blocks
    tile = lax.axis_index("tile")
    inputs = (
        block_place,
        track_region.reshape(1, tracks),
        hit_count.reshape(1, tracks),
        local_deriv.transpose(1, 2, 0).reshape(-1, tracks),
        hit_weight.T,
        hit_resid.T,
        block_ids.T,
    )

    def swap(value, even, odd):
        pairs = [(t, t ^ (sub * (odd if t // sub % 2 else even))) for t in range(tiles)]
        return lax.ppermute(value, "tile", pairs)

    def across(value, k):
        return lax.ppermute(value.astype(BF16), "region", [(r, r ^ k) for r in range(regions)])

    def near(keep, send):
        bit = 1
        while bit < sub:
            pairs = [(t, t ^ bit) for t in range(tiles)]
            keep, send = (v + lax.ppermute(v, "tile", pairs) for v in (keep, send))
            bit *= 2
        return keep, swap(send, 1, 1)

    def both(pair, part):
        return pair[0][part].astype(F32) + pair[1][part].astype(F32)

    low, top = slice(0, blocks // 4), slice(blocks // 4, blocks // 2)
    totals, more, second = [None] * regions, None, None
    for first in range(regions - 2, -1, -2):
        ks = (first, first + 1)
        keep, send, *made = assemble(ks, sub, inputs, global_deriv, blocks, regions)
        if made:
            inputs = tuple(made)
        else:
            send, pair, more = lax.optimization_barrier((send, pair, more))
            value = both(pair, low) + more.astype(F32)
            second = value[0], swap(value[1].astype(BF16), 4, 2)
        pair = near(keep, send)
        if second is not None:
            pair, arrived = lax.optimization_barrier((pair, second[1]))
            value = second[0] + arrived.astype(F32)
            totals[first + 2], totals[first + 3] = value[0], value[1]
        more = both(pair, top).astype(BF16)
        if first:
            more, rest = lax.optimization_barrier((more, inputs[3]))
            inputs = inputs[:3] + (rest,)
        more = swap(more, 2, 4)
    value = both(pair, low) + more.astype(F32)
    value = value[0] + swap(value[1].astype(BF16), 4, 2).astype(F32)
    totals[0], totals[1] = value[0], value[1]
    for k in range(regions - 1, 0, -1):
        step = k & -k
        totals[k - step] = totals[k - step] + across(totals[k], step).astype(F32)
    own = totals[0]

    def onward(value, d):
        pairs = [
            (p * sub + s, ((p + d) % blocks) * sub + s) for p in range(blocks) for s in range(sub)
        ]
        return lax.ppermute(value.astype(BF16), "tile", pairs)

    matrix, vector = finish(
        sub,
        own,
        *(onward(own[d * width : (d + 1) * width], d) for d in range(1, blocks // 2)),
        onward(own[blocks // 2 * width : blocks // 2 * width + width // 2], blocks // 2),
        blocks,
    )
    if sub > 1:
        part = tile % sub
        rows = width // sub
        matrix = lax.dynamic_slice(matrix, (part * rows, 0), (rows, blocks * width))
        vector = lax.dynamic_slice(vector, (0, part * rows), (1, rows))
    return matrix[None], vector


def solution(mesh):
    return jax.shard_map(
        functools.partial(local, mesh.shape["tile"]),
        mesh=mesh,
        in_specs=(
            P(("region", "tile"), None, None),
            P(("region", "tile"), None, None),
            P(("region", "tile"), None),
            P(("region", "tile"), None),
            P(("region", "tile"), None),
            P(("region", "tile")),
            P(("region", "tile"), None),
            P(),
        ),
        out_specs=(P("region", "tile", None), P("region", "tile")),
        check_vma=False,
    )
```

```python
import functools
import jax
import jax.numpy as jnp
from jax import lax
from jax.experimental import pallas as pl
from jax.experimental.pallas import tpu as pltpu
from jax.sharding import PartitionSpec as P

F32 = jnp.float32
BF16 = jnp.bfloat16
GROUP = 8
PAIR = 2 * GROUP

NT = (((1,), (1,)), ((), ()))


def iota(shape, axis):
    return lax.broadcasted_iota(jnp.int32, shape, axis)


def fit(ld, weight, resid, counts):
    hits = weight.shape[0]
    live = iota(weight.shape, 0) < counts.astype(jnp.int32)
    masked_w = jnp.where(live, weight, 0.0)
    weighted_l = [v * masked_w for v in ld]
    gamma = [[None] * 5 for _ in range(5)]
    for a in range(5):
        for b in range(a + 1):
            gamma[a][b] = jnp.sum(weighted_l[a] * ld[b], axis=0, keepdims=True)
            if a == b:
                gamma[a][b] = gamma[a][b] + 1.0
    beta = [jnp.sum(weighted_l[a] * resid, axis=0, keepdims=True) for a in range(5)]
    factor = [[None] * 5 for _ in range(5)]
    inverse = [None] * 5
    for j in range(5):
        center = gamma[j][j]
        for k in range(j):
            center = center - factor[j][k] * factor[j][k]
        factor[j][j] = jnp.sqrt(center)
        inverse[j] = 1.0 / factor[j][j]
        for i in range(j + 1, 5):
            offdiag = gamma[i][j]
            for k in range(j):
                offdiag = offdiag - factor[i][k] * factor[j][k]
            factor[i][j] = offdiag * inverse[j]
    solved, rhs = [], []
    for j in range(5):
        current, target = weighted_l[j], beta[j]
        for k in range(j):
            current = current - factor[j][k] * solved[k]
            target = target - factor[j][k] * rhs[k]
        solved.append(current * inverse[j])
        rhs.append(target * inverse[j])
    projection = solved[0] * rhs[0]
    for k in range(1, 5):
        projection = projection + solved[k] * rhs[k]
    return solved, masked_w * resid - projection, masked_w


def prepare(
    place_ref, region_ref, count_ref, ld_ref, weight_ref, resid_ref, ids_ref,
    scaled_ref, lanes_ref, table_ref,
):
    tracks = region_ref.shape[1]
    groups, _, depth = scaled_ref.shape
    slots = groups * GROUP
    hits = depth // GROUP
    blocks = place_ref.shape[0]
    rr = table_ref.shape[0] - 8
    member = (iota((rr, tracks), 0) == region_ref[...]).astype(F32)
    before = (iota((tracks, tracks), 0) < iota((tracks, tracks), 1)).astype(F32).astype(BF16)
    rank = jnp.dot(member.astype(BF16), before, preferred_element_type=F32)
    count = jnp.sum(member, axis=1, keepdims=True)
    room = (count.astype(jnp.int32) + (PAIR - 1)) & -PAIR
    room = jnp.broadcast_to(room.astype(F32), (rr, slots))
    lower = (iota((rr, rr), 1) < iota((rr, rr), 0)).astype(F32)
    start = jnp.zeros((rr, slots), F32)
    for g in range(rr):
        start = start + lower[:, g : g + 1] * room[g : g + 1, :]
    slot = jnp.sum(member * (rank + start[:, 0:1]), axis=0, keepdims=True)
    perm = (iota((slots, tracks), 0) == slot.astype(jnp.int32)).astype(F32).astype(BF16)
    numbers = jnp.where(
        iota((8, tracks), 0) == 0, iota((8, tracks), 1), jnp.broadcast_to(count_ref[...], (8, tracks))
    )

    def sort(value):
        return lax.dot_general(value, perm, NT, preferred_element_type=F32)

    numbers = sort(numbers.astype(F32).astype(BF16))
    table_ref[0:8, :] = numbers.astype(jnp.int32)
    table_ref[8:, :] = jnp.where(
        iota((rr, slots), 1) == 0, start.astype(jnp.int32), (start + room).astype(jnp.int32)
    )
    flat = sort(ld_ref[...])
    ld = [flat[c * hits : (c + 1) * hits] for c in range(5)]
    solved, hit_factor, masked_w = fit(
        ld, sort(weight_ref[...]), sort(resid_ref[...]), numbers[1:2]
    )
    ids = sort(ids_ref[...].astype(F32).astype(BF16))
    position = jnp.zeros_like(ids)
    for b in range(blocks):
        position = jnp.where(ids == float(b), place_ref[b].astype(F32), position)
    own = (iota((depth, slots), 0) // hits) == (iota((depth, slots), 1) % GROUP)

    def spread_out(value):
        return jnp.where(own, jnp.concatenate([value] * GROUP, axis=0), 0.0)

    grouping = (iota((groups, slots), 1) // GROUP == iota((groups, slots), 0)).astype(F32)
    for n, value in enumerate((masked_w, hit_factor, position)):
        lanes_ref[n] = lax.dot_general(
            grouping.astype(BF16), spread_out(value).astype(BF16), NT, preferred_element_type=F32
        )
    for c in range(5):
        scaled_ref[:, c * GROUP : (c + 1) * GROUP, :] = spread_out(solved[c]).T.reshape(
            groups, GROUP, depth
        )


def one_step(step, n, table_ref, g_ref, scaled_ref, lanes_ref, g_s, direct_s, vector_s, spread_s):
    hits, width = g_ref.shape[1:]
    depth = GROUP * hits
    blocks = direct_s.shape[0] // width
    rows = 5 * GROUP
    sub = iota((16, depth), 0).astype(F32)
    totals, vector = [], vector_s[...]
    for u in range(2):
        group = step * 2 + u
        for i in range(GROUP):
            g_s[u, i * hits : (i + 1) * hits, :] = g_ref[table_ref[0, group * GROUP + i]]
        g = g_s[u]
        turned = g.T
        position = jnp.broadcast_to(lanes_ref[2, pl.ds(group, 1), :], (16, depth))
        masks = [jnp.where(position == float(p), 1.0, 0.0).astype(BF16) for p in range(blocks)]
        streamed = jnp.concatenate(
            [turned * jnp.concatenate([mask] * (width // 16), axis=0) for mask in masks], axis=0
        )
        weighted = turned.astype(F32) * lanes_ref[0, pl.ds(group, 1), :]
        scaled = scaled_ref[group]
        high = scaled.astype(BF16).astype(F32)
        low = scaled - high
        if u == 0:
            parts = [high, jnp.zeros((rows, depth), F32), low, jnp.zeros((8, depth), F32)]
        else:
            parts = [low[8:], jnp.zeros((8, depth), F32), high, jnp.zeros((rows, depth), F32), low[:8]]
        held = jnp.concatenate([weighted] + parts, axis=0).astype(BF16)
        totals.append(lax.dot_general(streamed, held, NT, preferred_element_type=F32))
        factor = jnp.where(sub == position, lanes_ref[1, pl.ds(group, 1), :], 0.0).astype(BF16)
        vector = vector + jnp.dot(factor, g, preferred_element_type=F32)
    vector_s[...] = vector
    lane = iota((width, width), 1)
    at = pl.ds(pl.multiple_of((n % 2) * width, width), width)
    many = blocks // 2
    for p in range(blocks):
        part = slice(p * width, (p + 1) * width)
        direct_s[part] = direct_s[part] + (totals[0][part, :width] + totals[1][part, :width])
        first, second = totals[0][part, width:], totals[1][part, width:]
        near = jnp.where(lane < rows, first, second)
        far = jnp.where((lane >= 2 * rows) & (lane < 3 * rows), first, second)
        far = pltpu.roll(far, width - 2 * rows, 1)
        value = jnp.where(lane < 2 * rows, near + far, 0.0).astype(BF16)
        spread_s[n // 2, part, at] = value
        if p < many:
            spread_s[n // 2, (blocks + p) * width : (blocks + p + 1) * width, at] = value


EVEN = (0, 4, 2, 6)
ODD = (0, 2, 4, 6)


def fetch(pairs, sems):
    copies = [
        pltpu.make_async_copy(source, target, sems.at[n])
        for n, (source, target) in enumerate(pairs)
    ]
    for copy in copies:
        copy.start()
    return copies


def lead_kernel(ks, sub, *refs):
    small, g_hbm, (keep_ref, send_ref), shared = refs[:7], refs[7], refs[8:10], refs[10:13]
    local_small, g_ref, table_s, sems, scratch = refs[13:20], refs[20], refs[21], refs[22], refs[23:]

    @pl.when(pl.program_id(0) == 0)
    def _():
        copies = fetch([*zip(small, local_small), (g_hbm, g_ref)], sems)
        for copy in copies[:-1]:
            copy.wait()
        prepare(*local_small, *shared)
        copy = pltpu.make_async_copy(shared[2], table_s, sems.at[0])
        copy.start()
        copy.wait()
        copies[-1].wait()

    assemble_region(ks, sub, table_s, *shared[:2], g_ref, keep_ref, send_ref, *scratch)


def follow_kernel(ks, sub, *refs):
    shared, (keep_ref, send_ref), mine, sems, scratch = (
        refs[:4], refs[4:6], refs[6:10], refs[10], refs[11:]
    )

    @pl.when(pl.program_id(0) == 0)
    def _():
        for copy in fetch(list(zip(shared, mine)), sems):
            copy.wait()

    assemble_region(ks, sub, mine[2], *mine[:2], mine[3], keep_ref, send_ref, *scratch)


def assemble_region(
    ks, sub, table_ref, scaled_ref, lanes_ref, g_ref,
    keep_ref, send_ref, g_s, direct_s, vector_s, spread_s, acc_s,
):
    k = jnp.where(pl.program_id(0) == 0, ks[0], ks[1])
    width = g_ref.shape[2]
    blocks = direct_s.shape[0] // width
    many = blocks // 2
    region = lax.axis_index("region") ^ k
    block = lax.axis_index("tile") // sub
    first = table_ref[8 + region, 0] // PAIR
    steps = table_ref[8 + region, 1] // PAIR - first
    chunks = jnp.maximum((steps + 1) // 2, 1)
    direct_s[...] = jnp.zeros_like(direct_s)
    vector_s[...] = jnp.zeros_like(vector_s)

    @pl.when(steps % 2 == 1)
    def _():
        spread_s[chunks - 1, :, width:] = jnp.zeros((spread_s.shape[1], width), BF16)

    @pl.when(steps == 0)
    def _():
        spread_s[0] = jnp.zeros(spread_s.shape[1:], BF16)

    def group_step(n, carry):
        one_step(
            first + n, n, table_ref, g_ref, scaled_ref, lanes_ref, g_s, direct_s, vector_s, spread_s
        )
        return carry

    lax.fori_loop(0, steps, group_step, 0)

    def chunk_step(chunk, carry):
        def products(add):
            for q in range(0, blocks, 2):
                upper = (q + blocks - many) % blocks
                value = lax.dot_general(
                    spread_s[chunk, upper * width : (upper + many + 2) * width, :],
                    spread_s[chunk, q * width : (q + 2) * width, :],
                    NT,
                    preferred_element_type=F32,
                )
                for r in range(many + 2):
                    p = (upper + r) % blocks
                    for c in range(2):
                        d = many - r + c
                        if 0 <= d <= many and (d < many or p < many):
                            part = value[r * width : (r + 1) * width, c * width : (c + 1) * width]
                            columns = slice(d * width, (d + 1) * width)
                            acc_s[p, :, columns] = acc_s[p, :, columns] - part if add else 0.0 - part

        @pl.when(chunk == 0)
        def _():
            products(False)

        @pl.when(chunk > 0)
        def _():
            products(True)

        return carry

    lax.fori_loop(0, chunks, chunk_step, 0)
    half = width // 2
    for n in range(blocks // 2):
        for odd, out_ref in ((0, keep_ref), (1, send_ref)):
            p = block ^ (jnp.where(block % 2 == 1 - odd, ODD[n], EVEN[n]) + odd)
            at = pl.ds(pl.multiple_of(p * width, width), width)
            parts = [direct_s[at, :] + acc_s[p, :, 0:width]]
            parts += [acc_s[p, :, d * width : (d + 1) * width] for d in range(1, many)]
            upper = pl.multiple_of((p // many) * half, half)
            parts.append(acc_s[p % many, pl.ds(upper, half), many * width :])
            row = vector_s[pl.ds(p, 1), :]
            high = row.astype(BF16).astype(F32)
            sub = iota((16, width), 0)
            parts.append(jnp.where(sub == 0, high, jnp.where(sub == 1, row - high, 0.0)))
            out_ref[n, 0] = jnp.concatenate(parts, axis=0).astype(BF16)


def assemble(ks, sub, inputs, g, blocks, regions):
    tracks, hits, width = g.shape
    lead = len(inputs) == 7
    rows = width * (blocks // 2) + width // 2 + 16
    longest = -(-tracks // (2 * PAIR))
    rr = -(-regions // 8) * 8
    slots = -(-(tracks + regions * (PAIR - 1)) // 128) * 128
    shared = [
        jax.ShapeDtypeStruct((slots // GROUP, 5 * GROUP, GROUP * hits), F32),
        jax.ShapeDtypeStruct((3, slots // GROUP, GROUP * hits), F32),
        jax.ShapeDtypeStruct((8 + rr, slots), jnp.int32),
    ]
    out = jax.ShapeDtypeStruct((blocks // 2, 2, rows, width), BF16)
    spec = pl.BlockSpec((blocks // 2, 1, rows, width), lambda k: (0, k, 0, 0))
    vmem = pl.BlockSpec(memory_space=pltpu.VMEM)
    table = pltpu.SMEM(shared[2].shape, jnp.int32)
    arrived = pltpu.VMEM(g.shape, g.dtype)
    if lead:
        copies = [pltpu.SMEM(inputs[0].shape, jnp.int32)]
        copies += [pltpu.VMEM(value.shape, value.dtype) for value in inputs[1:]]
        copies += [arrived, table]
    else:
        copies = [pltpu.VMEM(value.shape, value.dtype) for value in inputs[:2]]
        copies += [table, arrived]
    return pl.pallas_call(
        functools.partial(lead_kernel if lead else follow_kernel, ks, sub),
        grid=(2,),
        in_specs=[pl.BlockSpec(memory_space=pltpu.HBM)] * (len(inputs) + 1),
        out_specs=[spec, spec] + [vmem] * (3 * lead),
        out_shape=[out, out] + shared * lead,
        scratch_shapes=copies
        + [
            pltpu.SemaphoreType.DMA((8,)),
            pltpu.VMEM((2, GROUP * hits, width), BF16),
            pltpu.VMEM((blocks * width, width), F32),
            pltpu.VMEM((16, width), F32),
            pltpu.VMEM((longest, (blocks + blocks // 2) * width, 2 * width), BF16),
            pltpu.VMEM((blocks, width, (blocks // 2 + 1) * width), F32),
        ],
        compiler_params=pltpu.CompilerParams(
            dimension_semantics=("arbitrary",), vmem_limit_bytes=(60 if lead else 32) * 1024 * 1024
        ),
        cost_estimate=pl.CostEstimate(
            flops=8 * 10**9, bytes_accessed=4 * 10**6, transcendentals=0
        ),
        name="assemble",
    )(*inputs, g)


def finish_kernel(sub, own_ref, r1_ref, r2_ref, r3_ref, e_ref, out_ref, vec_ref):
    width = own_ref.shape[1]
    p = lax.axis_index("tile") // sub
    blocks = out_ref.shape[1] // width
    many = blocks // 2

    def put(column, value):
        column = pl.multiple_of(((column + blocks) % blocks) * width, width)
        out_ref[:, pl.ds(column, width)] = value

    put(p, own_ref[0:width, :].T)
    for d in range(1, many):
        put(p + d, own_ref[d * width : (d + 1) * width, :])
    for d, ref in ((1, r1_ref), (2, r2_ref), (3, r3_ref)):
        put(p - d, ref[...].astype(F32).T)
    tail = many * width + width // 2
    mine = own_ref[many * width : tail, :]
    other = e_ref[...].astype(F32)

    @pl.when(p < many)
    def _():
        put(p + many, jnp.concatenate([mine, other], axis=0))

    @pl.when(p >= many)
    def _():
        put(p + many, jnp.concatenate([other, mine], axis=0).T)

    vec_ref[...] = own_ref[tail : tail + 1, :] + own_ref[tail + 1 : tail + 2, :]


def finish(sub, own, r1, r2, r3, ext, blocks):
    width = own.shape[1]
    vmem = pl.BlockSpec(memory_space=pltpu.VMEM)
    return pl.pallas_call(
        functools.partial(finish_kernel, sub),
        in_specs=[vmem] * 5,
        out_specs=[vmem, vmem],
        out_shape=[
            jax.ShapeDtypeStruct((width, blocks * width), F32),
            jax.ShapeDtypeStruct((1, width), F32),
        ],
        name="finish",
    )(own, r1, r2, r3, ext)


def local(
    tiles, global_deriv, local_deriv, hit_weight, hit_resid, block_ids, hit_count, track_region,
    block_place,
):
    regions = lax.axis_size("region")
    tracks, hits, width = global_deriv.shape
    blocks = block_place.shape[0]
    sub = tiles // blocks
    tile = lax.axis_index("tile")
    inputs = (
        block_place,
        track_region.reshape(1, tracks),
        hit_count.reshape(1, tracks),
        local_deriv.transpose(1, 2, 0).reshape(-1, tracks),
        hit_weight.T,
        hit_resid.T,
        block_ids.T,
    )

    def swap(value, even, odd):
        pairs = [(t, t ^ (sub * (odd if t // sub % 2 else even))) for t in range(tiles)]
        return lax.ppermute(value, "tile", pairs)

    def across(value, k):
        return lax.ppermute(value.astype(BF16), "region", [(r, r ^ k) for r in range(regions)])

    def near(keep, send):
        bit = 1
        while bit < sub:
            pairs = [(t, t ^ bit) for t in range(tiles)]
            keep, send = (v + lax.ppermute(v, "tile", pairs) for v in (keep, send))
            bit *= 2
        return keep, swap(send, 1, 1)

    def both(pair, part):
        return pair[0][part].astype(F32) + pair[1][part].astype(F32)

    low, top = slice(0, blocks // 4), slice(blocks // 4, blocks // 2)
    totals, more, second = [None] * regions, None, None
    for first in range(regions - 2, -1, -2):
        ks = (first, first + 1)
        keep, send, *made = assemble(ks, sub, inputs, global_deriv, blocks, regions)
        if made:
            inputs = tuple(made)
        else:
            send, pair, more = lax.optimization_barrier((send, pair, more))
            value = both(pair, low) + more.astype(F32)
            second = value[0], swap(value[1].astype(BF16), 4, 2)
        pair = near(keep, send)
        if second is not None:
            pair, arrived = lax.optimization_barrier((pair, second[1]))
            value = second[0] + arrived.astype(F32)
            totals[first + 2], totals[first + 3] = value[0], value[1]
        more = both(pair, top).astype(BF16)
        if first:
            more, rest = lax.optimization_barrier((more, inputs[2]))
            inputs = inputs[:2] + (rest,)
        more = swap(more, 2, 4)
    value = both(pair, low) + more.astype(F32)
    value = value[0] + swap(value[1].astype(BF16), 4, 2).astype(F32)
    totals[0], totals[1] = value[0], value[1]
    for k in range(regions - 1, 0, -1):
        step = k & -k
        totals[k - step] = totals[k - step] + across(totals[k], step).astype(F32)
    own = totals[0]

    def onward(value, d):
        pairs = [
            (p * sub + s, ((p + d) % blocks) * sub + s) for p in range(blocks) for s in range(sub)
        ]
        return lax.ppermute(value.astype(BF16), "tile", pairs)

    matrix, vector = finish(
        sub,
        own,
        *(onward(own[d * width : (d + 1) * width], d) for d in range(1, blocks // 2)),
        onward(own[blocks // 2 * width : blocks // 2 * width + width // 2], blocks // 2),
        blocks,
    )
    if sub > 1:
        part = tile % sub
        rows = width // sub
        matrix = lax.dynamic_slice(matrix, (part * rows, 0), (rows, blocks * width))
        vector = lax.dynamic_slice(vector, (0, part * rows), (1, rows))
    return matrix[None], vector


def solution(mesh):
    return jax.shard_map(
        functools.partial(local, mesh.shape["tile"]),
        mesh=mesh,
        in_specs=(
            P(("region", "tile"), None, None),
            P(("region", "tile"), None, None),
            P(("region", "tile"), None),
            P(("region", "tile"), None),
            P(("region", "tile"), None),
            P(("region", "tile")),
            P(("region", "tile"), None),
            P(),
        ),
        out_specs=(P("region", "tile", None), P("region", "tile")),
        check_vma=False,
    )
```

```python
import functools
import jax
import jax.numpy as jnp
from jax import lax
from jax.experimental import pallas as pl
from jax.experimental.pallas import tpu as pltpu
from jax.sharding import PartitionSpec as P

F32 = jnp.float32
BF16 = jnp.bfloat16
GROUP = 8
PAIR = 2 * GROUP

NT = (((1,), (1,)), ((), ()))


def iota(shape, axis):
    return lax.broadcasted_iota(jnp.int32, shape, axis)


def fit(ld, weight, resid, counts):
    hits = weight.shape[0]
    live = iota(weight.shape, 0) < counts.astype(jnp.int32)
    masked_w = jnp.where(live, weight, 0.0)
    weighted_l = [v * masked_w for v in ld]
    gamma = [[None] * 5 for _ in range(5)]
    for a in range(5):
        for b in range(a + 1):
            gamma[a][b] = jnp.sum(weighted_l[a] * ld[b], axis=0, keepdims=True)
            if a == b:
                gamma[a][b] = gamma[a][b] + 1.0
    beta = [jnp.sum(weighted_l[a] * resid, axis=0, keepdims=True) for a in range(5)]
    factor = [[None] * 5 for _ in range(5)]
    inverse = [None] * 5
    for j in range(5):
        center = gamma[j][j]
        for k in range(j):
            center = center - factor[j][k] * factor[j][k]
        factor[j][j] = jnp.sqrt(center)
        inverse[j] = 1.0 / factor[j][j]
        for i in range(j + 1, 5):
            offdiag = gamma[i][j]
            for k in range(j):
                offdiag = offdiag - factor[i][k] * factor[j][k]
            factor[i][j] = offdiag * inverse[j]
    solved, rhs = [], []
    for j in range(5):
        current, target = weighted_l[j], beta[j]
        for k in range(j):
            current = current - factor[j][k] * solved[k]
            target = target - factor[j][k] * rhs[k]
        solved.append(current * inverse[j])
        rhs.append(target * inverse[j])
    projection = solved[0] * rhs[0]
    for k in range(1, 5):
        projection = projection + solved[k] * rhs[k]
    return solved, masked_w * resid - projection, masked_w


def prepare(
    place_ref, region_ref, count_ref, ld_ref, weight_ref, resid_ref, ids_ref,
    scaled_ref, lanes_ref, table_ref,
):
    tracks = region_ref.shape[1]
    groups, _, depth = scaled_ref.shape
    slots = groups * GROUP
    hits = depth // GROUP
    blocks = place_ref.shape[0]
    rr = table_ref.shape[0] - 8
    member = (iota((rr, tracks), 0) == region_ref[...]).astype(F32)
    before = (iota((tracks, tracks), 0) < iota((tracks, tracks), 1)).astype(F32).astype(BF16)
    rank = jnp.dot(member.astype(BF16), before, preferred_element_type=F32)
    count = jnp.sum(member, axis=1, keepdims=True)
    room = (count.astype(jnp.int32) + (PAIR - 1)) & -PAIR
    room = jnp.broadcast_to(room.astype(F32), (rr, slots))
    lower = (iota((rr, rr), 1) < iota((rr, rr), 0)).astype(F32)
    start = jnp.zeros((rr, slots), F32)
    for g in range(rr):
        start = start + lower[:, g : g + 1] * room[g : g + 1, :]
    slot = jnp.sum(member * (rank + start[:, 0:1]), axis=0, keepdims=True)
    perm = (iota((slots, tracks), 0) == slot.astype(jnp.int32)).astype(F32).astype(BF16)
    numbers = jnp.where(
        iota((8, tracks), 0) == 0, iota((8, tracks), 1), jnp.broadcast_to(count_ref[...], (8, tracks))
    )

    def sort(value):
        return lax.dot_general(value, perm, NT, preferred_element_type=F32)

    numbers = sort(numbers.astype(F32).astype(BF16))
    table_ref[0:8, :] = numbers.astype(jnp.int32)
    table_ref[8:, :] = jnp.where(
        iota((rr, slots), 1) == 0, start.astype(jnp.int32), (start + room).astype(jnp.int32)
    )
    flat = sort(ld_ref[...])
    ld = [flat[c * hits : (c + 1) * hits] for c in range(5)]
    solved, hit_factor, masked_w = fit(
        ld, sort(weight_ref[...]), sort(resid_ref[...]), numbers[1:2]
    )
    ids = sort(ids_ref[...].astype(F32).astype(BF16))
    position = jnp.zeros_like(ids)
    for b in range(blocks):
        position = jnp.where(ids == float(b), place_ref[b].astype(F32), position)
    own = (iota((depth, slots), 0) // hits) == (iota((depth, slots), 1) % GROUP)

    def spread_out(value):
        return jnp.where(own, jnp.concatenate([value] * GROUP, axis=0), 0.0)

    grouping = (iota((groups, slots), 1) // GROUP == iota((groups, slots), 0)).astype(F32)
    for n, value in enumerate((masked_w, hit_factor, position)):
        lanes_ref[n] = lax.dot_general(
            grouping.astype(BF16), spread_out(value).astype(BF16), NT, preferred_element_type=F32
        )
    for c in range(5):
        scaled_ref[:, c * GROUP : (c + 1) * GROUP, :] = spread_out(solved[c]).T.reshape(
            groups, GROUP, depth
        )


def one_step(step, n, table_ref, g_ref, scaled_ref, lanes_ref, g_s, direct_s, vector_s, spread_s):
    hits, width = g_ref.shape[1:]
    depth = PAIR * hits
    blocks = direct_s.shape[0] // width
    many = blocks // 2
    rows = 5 * GROUP

    def lanes(which):
        return jnp.concatenate(
            [lanes_ref[which, pl.ds(step * 2 + u, 1), :] for u in range(2)], axis=1
        )

    for i in range(PAIR):
        g_s[i * hits : (i + 1) * hits, :] = g_ref[table_ref[0, step * PAIR + i]]
    g = g_s[...]
    turned = g.T
    position = jnp.broadcast_to(lanes(2), (16, depth))
    masks = [jnp.where(position == float(p), 1.0, 0.0).astype(BF16) for p in range(blocks)]
    streamed = jnp.concatenate(
        [turned * jnp.concatenate([mask] * (width // 16), axis=0) for mask in masks], axis=0
    )
    weighted = turned.astype(F32) * lanes(0)
    none = jnp.zeros((rows, depth // 2), F32)
    rest = jnp.zeros((width - 2 * rows, depth), F32)
    scaled = [scaled_ref[step * 2 + u] for u in range(2)]
    high = [value.astype(BF16).astype(F32) for value in scaled]
    low = [value - part for value, part in zip(scaled, high)]
    held = [weighted]
    for part in (high, low):
        held += [
            jnp.concatenate([part[0], none], axis=1),
            jnp.concatenate([none, part[1]], axis=1),
            rest,
        ]
    held = jnp.concatenate(held, axis=0).astype(BF16)
    total = lax.dot_general(streamed, held, NT, preferred_element_type=F32)
    factor = jnp.where(iota((16, depth), 0).astype(F32) == position, lanes(1), 0.0).astype(BF16)
    vector_s[...] += jnp.dot(factor, g, preferred_element_type=F32)
    at = pl.ds(pl.multiple_of((n % 2) * width, width), width)
    for p in range(blocks):
        part = slice(p * width, (p + 1) * width)
        direct_s[part] += total[part, :width]
        value = (total[part, width : 2 * width] + total[part, 2 * width :]).astype(BF16)
        spread_s[n // 2, part, at] = value
        if p < many:
            spread_s[n // 2, (blocks + p) * width : (blocks + p + 1) * width, at] = value


EVEN = (0, 4, 2, 6)
ODD = (0, 2, 4, 6)


def fetch(pairs, sems):
    copies = [
        pltpu.make_async_copy(source, target, sems.at[n])
        for n, (source, target) in enumerate(pairs)
    ]
    for copy in copies:
        copy.start()
    return copies


def lead_kernel(ks, sub, apart, *refs):
    small, g_hbm, (keep_ref, send_ref), shared = refs[:7], refs[7], refs[8:10], refs[10:13]
    local_small, g_ref, table_s, sems, scratch = refs[13:20], refs[20], refs[21], refs[22], refs[23:]

    @pl.when(pl.program_id(0) == 0)
    def _():
        copies = fetch([*zip(small, local_small), (g_hbm, g_ref)], sems)
        for copy in copies[:-1]:
            copy.wait()
        prepare(*local_small, *shared)
        copy = pltpu.make_async_copy(shared[2], table_s, sems.at[0])
        copy.start()
        copy.wait()
        copies[-1].wait()

    assemble_region(ks, sub, False, table_s, *shared[:2], g_ref, keep_ref, send_ref, *scratch)


def follow_kernel(ks, sub, apart, *refs):
    shared, (keep_ref, send_ref), mine, sems, scratch = (
        refs[:4], refs[4:6], refs[6:10], refs[10], refs[11:]
    )

    @pl.when(pl.program_id(0) == 0)
    def _():
        for copy in fetch(list(zip(shared, mine)), sems):
            copy.wait()

    assemble_region(ks, sub, apart, mine[2], *mine[:2], mine[3], keep_ref, send_ref, *scratch)


def assemble_region(
    ks, sub, apart, table_ref, scaled_ref, lanes_ref, g_ref,
    keep_ref, send_ref, g_s, direct_s, vector_s, spread_s, acc_s,
):
    k = jnp.where(pl.program_id(0) == 0, ks[0], ks[1])
    width = g_ref.shape[2]
    blocks = direct_s.shape[0] // width
    many = blocks // 2
    region = lax.axis_index("region") ^ k
    block = lax.axis_index("tile") // sub
    first = table_ref[8 + region, 0] // PAIR
    steps = table_ref[8 + region, 1] // PAIR - first
    chunks = jnp.maximum((steps + 1) // 2, 1)
    direct_s[...] = jnp.zeros_like(direct_s)
    vector_s[...] = jnp.zeros_like(vector_s)

    @pl.when(steps % 2 == 1)
    def _():
        spread_s[chunks - 1, :, width:] = jnp.zeros((spread_s.shape[1], width), BF16)

    @pl.when(steps == 0)
    def _():
        spread_s[0] = jnp.zeros(spread_s.shape[1:], BF16)

    def group_step(n, carry):
        one_step(
            first + n, n, table_ref, g_ref, scaled_ref, lanes_ref, g_s, direct_s, vector_s, spread_s
        )
        return carry

    lax.fori_loop(0, steps, group_step, 0)

    def chunk_step(chunk, carry):
        def products(add):
            for q in range(0, blocks, 2):
                upper = (q + blocks - many) % blocks
                value = lax.dot_general(
                    spread_s[chunk, upper * width : (upper + many + 2) * width, :],
                    spread_s[chunk, q * width : (q + 2) * width, :],
                    NT,
                    preferred_element_type=F32,
                )
                for r in range(many + 2):
                    p = (upper + r) % blocks
                    for c in range(2):
                        d = many - r + c
                        if 0 <= d <= many and (d < many or p < many):
                            part = value[r * width : (r + 1) * width, c * width : (c + 1) * width]
                            columns = slice(d * width, (d + 1) * width)
                            acc_s[p, :, columns] = acc_s[p, :, columns] - part if add else 0.0 - part

        @pl.when(chunk == 0)
        def _():
            products(False)

        @pl.when(chunk > 0)
        def _():
            products(True)

        return carry

    lax.fori_loop(0, chunks, chunk_step, 0)
    half = width // 2
    for n in range(blocks // 2):
        for odd, out_ref in ((0, keep_ref), (1, send_ref)):
            p = block ^ (jnp.where(block % 2 == 1 - odd, ODD[n], EVEN[n]) + odd)
            at = pl.ds(pl.multiple_of(p * width, width), width)
            parts = [direct_s[at, :] + acc_s[p, :, 0:width]]
            parts += [acc_s[p, :, d * width : (d + 1) * width] for d in range(1, many)]
            upper = pl.multiple_of((p // many) * half, half)
            parts.append(acc_s[p % many, pl.ds(upper, half), many * width :])
            row = vector_s[pl.ds(p, 1), :]
            high = row.astype(BF16).astype(F32)
            sub = iota((16, width), 0)
            parts.append(jnp.where(sub == 0, high, jnp.where(sub == 1, row - high, 0.0)))
            place = (0, n) if apart else (n, 0)
            out_ref[place] = jnp.concatenate(parts, axis=0).astype(BF16)


def assemble(ks, sub, apart, inputs, g, blocks, regions):
    tracks, hits, width = g.shape
    lead = len(inputs) == 7
    rows = width * (blocks // 2) + width // 2 + 16
    longest = -(-tracks // (2 * PAIR))
    rr = -(-regions // 8) * 8
    slots = -(-(tracks + regions * (PAIR - 1)) // 128) * 128
    shared = [
        jax.ShapeDtypeStruct((slots // GROUP, 5 * GROUP, GROUP * hits), F32),
        jax.ShapeDtypeStruct((3, slots // GROUP, GROUP * hits), F32),
        jax.ShapeDtypeStruct((8 + rr, slots), jnp.int32),
    ]
    if apart:
        out = jax.ShapeDtypeStruct((2, blocks // 2, rows, width), BF16)
        spec = pl.BlockSpec((1, blocks // 2, rows, width), lambda k: (k, 0, 0, 0))
    else:
        out = jax.ShapeDtypeStruct((blocks // 2, 2, rows, width), BF16)
        spec = pl.BlockSpec((blocks // 2, 1, rows, width), lambda k: (0, k, 0, 0))
    vmem = pl.BlockSpec(memory_space=pltpu.VMEM)
    table = pltpu.SMEM(shared[2].shape, jnp.int32)
    arrived = pltpu.VMEM(g.shape, g.dtype)
    if lead:
        copies = [pltpu.SMEM(inputs[0].shape, jnp.int32)]
        copies += [pltpu.VMEM(value.shape, value.dtype) for value in inputs[1:]]
        copies += [arrived, table]
    else:
        copies = [pltpu.VMEM(value.shape, value.dtype) for value in inputs[:2]]
        copies += [table, arrived]
    return pl.pallas_call(
        functools.partial(lead_kernel if lead else follow_kernel, ks, sub, apart),
        grid=(2,),
        in_specs=[pl.BlockSpec(memory_space=pltpu.HBM)] * (len(inputs) + 1),
        out_specs=[spec, spec] + [vmem] * (3 * lead),
        out_shape=[out, out] + shared * lead,
        scratch_shapes=copies
        + [
            pltpu.SemaphoreType.DMA((8,)),
            pltpu.VMEM((PAIR * hits, width), BF16),
            pltpu.VMEM((blocks * width, width), F32),
            pltpu.VMEM((16, width), F32),
            pltpu.VMEM((longest, (blocks + blocks // 2) * width, 2 * width), BF16),
            pltpu.VMEM((blocks, width, (blocks // 2 + 1) * width), F32),
        ],
        compiler_params=pltpu.CompilerParams(
            dimension_semantics=("arbitrary",), vmem_limit_bytes=(60 if lead else 32) * 1024 * 1024
        ),
        cost_estimate=pl.CostEstimate(
            flops=8 * 10**9, bytes_accessed=4 * 10**6, transcendentals=0
        ),
        name="assemble",
    )(*inputs, g)


def finish_kernel(sub, own_ref, r1_ref, r2_ref, r3_ref, e_ref, out_ref, vec_ref):
    width = own_ref.shape[1]
    p = lax.axis_index("tile") // sub
    blocks = out_ref.shape[1] // width
    many = blocks // 2

    def put(column, value):
        column = pl.multiple_of(((column + blocks) % blocks) * width, width)
        out_ref[:, pl.ds(column, width)] = value

    put(p, own_ref[0:width, :].T)
    for d in range(1, many):
        put(p + d, own_ref[d * width : (d + 1) * width, :])
    for d, ref in ((1, r1_ref), (2, r2_ref), (3, r3_ref)):
        put(p - d, ref[...].astype(F32).T)
    tail = many * width + width // 2
    mine = own_ref[many * width : tail, :]
    other = e_ref[...].astype(F32)

    @pl.when(p < many)
    def _():
        put(p + many, jnp.concatenate([mine, other], axis=0))

    @pl.when(p >= many)
    def _():
        put(p + many, jnp.concatenate([other, mine], axis=0).T)

    vec_ref[...] = own_ref[tail : tail + 1, :] + own_ref[tail + 1 : tail + 2, :]


def finish(sub, own, r1, r2, r3, ext, blocks):
    width = own.shape[1]
    vmem = pl.BlockSpec(memory_space=pltpu.VMEM)
    return pl.pallas_call(
        functools.partial(finish_kernel, sub),
        in_specs=[vmem] * 5,
        out_specs=[vmem, vmem],
        out_shape=[
            jax.ShapeDtypeStruct((width, blocks * width), F32),
            jax.ShapeDtypeStruct((1, width), F32),
        ],
        name="finish",
    )(own, r1, r2, r3, ext)


def local(
    tiles, global_deriv, local_deriv, hit_weight, hit_resid, block_ids, hit_count, track_region,
    block_place,
):
    regions = lax.axis_size("region")
    tracks, hits, width = global_deriv.shape
    blocks = block_place.shape[0]
    sub = tiles // blocks
    tile = lax.axis_index("tile")
    inputs = (
        block_place,
        track_region.reshape(1, tracks),
        hit_count.reshape(1, tracks),
        local_deriv.transpose(1, 2, 0).reshape(-1, tracks),
        hit_weight.T,
        hit_resid.T,
        block_ids.T,
    )

    def swap(value, even, odd):
        pairs = [(t, t ^ (sub * (odd if t // sub % 2 else even))) for t in range(tiles)]
        return lax.ppermute(value, "tile", pairs)

    def across(value, k):
        return lax.ppermute(value.astype(BF16), "region", [(r, r ^ k) for r in range(regions)])

    def near(keep, send):
        bit = 1
        while bit < sub:
            pairs = [(t, t ^ bit) for t in range(tiles)]
            keep, send = (v + lax.ppermute(v, "tile", pairs) for v in (keep, send))
            bit *= 2
        return keep, swap(send, 1, 1)

    def both(pair, part):
        return pair[0][part].astype(F32) + pair[1][part].astype(F32)

    low, top = slice(0, blocks // 4), slice(blocks // 4, blocks // 2)
    totals, more, second = [None] * regions, None, None
    for first in range(regions - 2, -1, -2):
        ks = (first, first + 1)
        keep, send, *made = assemble(ks, sub, not first, inputs, global_deriv, blocks, regions)
        if made:
            inputs = tuple(made)
        else:
            send, pair, more = lax.optimization_barrier((send, pair, more))
            value = both(pair, low) + more.astype(F32)
            second = value[0], swap(value[1].astype(BF16), 4, 2)
        pair = near(keep, send)
        if second is not None:
            pair, arrived = lax.optimization_barrier((pair, second[1]))
            value = second[0] + arrived.astype(F32)
            totals[first + 2], totals[first + 3] = value[0], value[1]
        if first:
            more = both(pair, top).astype(BF16)
            more, rest = lax.optimization_barrier((more, inputs[2]))
            inputs = inputs[:2] + (rest,)
            more = swap(more, 2, 4)
    uppers = [swap(both(pair, (n, top)).astype(BF16), 2, 4) for n in (1, 0)]
    for n in (1, 0):
        value = both(pair, (n, low)) + uppers[1 - n].astype(F32)
        value = value[0], swap(value[1].astype(BF16), 4, 2)
        if n:
            pair, uppers[1], more = lax.optimization_barrier((pair, uppers[1], value[1]))
            value = value[0], more
        totals[n] = value[0] + value[1].astype(F32)
    for k in range(regions - 1, 0, -1):
        step = k & -k
        totals[k - step] = totals[k - step] + across(totals[k], step).astype(F32)
    own = totals[0]

    def onward(value, d):
        pairs = [
            (p * sub + s, ((p + d) % blocks) * sub + s) for p in range(blocks) for s in range(sub)
        ]
        return lax.ppermute(value.astype(BF16), "tile", pairs)

    matrix, vector = finish(
        sub,
        own,
        *(onward(own[d * width : (d + 1) * width], d) for d in range(1, blocks // 2)),
        onward(own[blocks // 2 * width : blocks // 2 * width + width // 2], blocks // 2),
        blocks,
    )
    if sub > 1:
        part = tile % sub
        rows = width // sub
        matrix = lax.dynamic_slice(matrix, (part * rows, 0), (rows, blocks * width))
        vector = lax.dynamic_slice(vector, (0, part * rows), (1, rows))
    return matrix[None], vector


def solution(mesh):
    return jax.shard_map(
        functools.partial(local, mesh.shape["tile"]),
        mesh=mesh,
        in_specs=(
            P(("region", "tile"), None, None),
            P(("region", "tile"), None, None),
            P(("region", "tile"), None),
            P(("region", "tile"), None),
            P(("region", "tile"), None),
            P(("region", "tile")),
            P(("region", "tile"), None),
            P(),
        ),
        out_specs=(P("region", "tile", None), P("region", "tile")),
        check_vma=False,
    )
```

```python
import functools
import jax
import jax.numpy as jnp
from jax import lax
from jax.experimental import pallas as pl
from jax.experimental.pallas import tpu as pltpu
from jax.sharding import PartitionSpec as P

F32 = jnp.float32
BF16 = jnp.bfloat16
GROUP = 8
PAIR = 2 * GROUP
DEPTH = 256

NT = (((1,), (1,)), ((), ()))


def iota(shape, axis):
    return lax.broadcasted_iota(jnp.int32, shape, axis)


def fit(ld, weight, resid, counts):
    hits = weight.shape[0]
    live = iota(weight.shape, 0) < counts.astype(jnp.int32)
    masked_w = jnp.where(live, weight, 0.0)
    weighted_l = [v * masked_w for v in ld]
    gamma = [[None] * 5 for _ in range(5)]
    for a in range(5):
        for b in range(a + 1):
            gamma[a][b] = jnp.sum(weighted_l[a] * ld[b], axis=0, keepdims=True)
            if a == b:
                gamma[a][b] = gamma[a][b] + 1.0
    beta = [jnp.sum(weighted_l[a] * resid, axis=0, keepdims=True) for a in range(5)]
    factor = [[None] * 5 for _ in range(5)]
    inverse = [None] * 5
    for j in range(5):
        center = gamma[j][j]
        for k in range(j):
            center = center - factor[j][k] * factor[j][k]
        factor[j][j] = jnp.sqrt(center)
        inverse[j] = 1.0 / factor[j][j]
        for i in range(j + 1, 5):
            offdiag = gamma[i][j]
            for k in range(j):
                offdiag = offdiag - factor[i][k] * factor[j][k]
            factor[i][j] = offdiag * inverse[j]
    solved, rhs = [], []
    for j in range(5):
        current, target = weighted_l[j], beta[j]
        for k in range(j):
            current = current - factor[j][k] * solved[k]
            target = target - factor[j][k] * rhs[k]
        solved.append(current * inverse[j])
        rhs.append(target * inverse[j])
    projection = solved[0] * rhs[0]
    for k in range(1, 5):
        projection = projection + solved[k] * rhs[k]
    return solved, masked_w * resid - projection, masked_w


def prepare(
    place_ref, region_ref, count_ref, ld_ref, weight_ref, resid_ref, ids_ref,
    scaled_ref, lanes_ref, column_ref, table_ref,
):
    tracks = region_ref.shape[1]
    groups, _, depth = scaled_ref.shape
    slots = groups * GROUP
    hits = depth // GROUP
    blocks = place_ref.shape[0]
    rr = table_ref.shape[0] - 8
    member = (iota((rr, tracks), 0) == region_ref[...]).astype(F32)
    before = (iota((tracks, tracks), 0) < iota((tracks, tracks), 1)).astype(F32).astype(BF16)
    rank = jnp.dot(member.astype(BF16), before, preferred_element_type=F32)
    count = jnp.sum(member, axis=1, keepdims=True)
    room = (count.astype(jnp.int32) + (PAIR - 1)) & -PAIR
    room = jnp.broadcast_to(room.astype(F32), (rr, slots))
    lower = (iota((rr, rr), 1) < iota((rr, rr), 0)).astype(F32)
    start = jnp.zeros((rr, slots), F32)
    for g in range(rr):
        start = start + lower[:, g : g + 1] * room[g : g + 1, :]
    slot = jnp.sum(member * (rank + start[:, 0:1]), axis=0, keepdims=True)
    perm = (iota((slots, tracks), 0) == slot.astype(jnp.int32)).astype(F32).astype(BF16)
    numbers = jnp.where(
        iota((8, tracks), 0) == 0, iota((8, tracks), 1), jnp.broadcast_to(count_ref[...], (8, tracks))
    )

    def sort(value):
        return lax.dot_general(value, perm, NT, preferred_element_type=F32)

    numbers = sort(numbers.astype(F32).astype(BF16))
    table_ref[0:8, :] = numbers.astype(jnp.int32)
    table_ref[8:, :] = jnp.where(
        iota((rr, slots), 1) == 0, start.astype(jnp.int32), (start + room).astype(jnp.int32)
    )
    flat = sort(ld_ref[...])
    ld = [flat[c * hits : (c + 1) * hits] for c in range(5)]
    solved, hit_factor, masked_w = fit(
        ld, sort(weight_ref[...]), sort(resid_ref[...]), numbers[1:2]
    )
    ids = sort(ids_ref[...].astype(F32).astype(BF16))
    position = jnp.zeros_like(ids)
    for b in range(blocks):
        position = jnp.where(ids == float(b), place_ref[b].astype(F32), position)
    own = (iota((depth, slots), 0) // hits) == (iota((depth, slots), 1) % GROUP)

    def spread_out(value):
        return jnp.where(own, jnp.concatenate([value] * GROUP, axis=0), 0.0)

    grouping = (iota((groups, slots), 1) // GROUP == iota((groups, slots), 0)).astype(F32)
    for n, value in enumerate((masked_w, hit_factor)):
        lanes_ref[n] = lax.dot_general(
            grouping.astype(BF16), spread_out(value).astype(BF16), NT, preferred_element_type=F32
        )
    columns = column_ref.shape[1]
    grouping = (iota((columns, slots), 1) // GROUP == iota((columns, slots), 0)).astype(F32)
    column_ref[...] = lax.dot_general(
        spread_out(position).astype(BF16), grouping.astype(BF16), NT, preferred_element_type=F32
    )
    for c in range(5):
        scaled_ref[:, c * GROUP : (c + 1) * GROUP, :] = spread_out(solved[c]).T.reshape(
            groups, GROUP, depth
        )


def one_step(step, at, table_ref, g_ref, scaled_ref, lanes_ref, column_ref, g_s, direct_s, spread_s):
    hits, width = g_ref.shape[1:]
    depth = GROUP * hits
    blocks = spread_s.shape[1] // width
    rows = 5 * GROUP
    head = width + 8
    unit = (iota((width, width), 0) == iota((width, width), 1)).astype(F32).astype(BF16)
    lefts, values, positions = [], [], []
    for u in range(2):
        group = step * 2 + u
        for i in range(GROUP):
            g_s[u, i * hits : (i + 1) * hits, :] = g_ref[table_ref[0, group * GROUP + i]]
        g = g_s[u]
        chosen = jnp.full(column_ref.shape, group, jnp.int32)
        position = jnp.take_along_axis(column_ref[...], chosen, axis=1, mode="promise_in_bounds")
        turned = lax.dot_general(unit, g, NT, preferred_element_type=F32)
        weighted = turned * lanes_ref[0, pl.ds(group, 1), :]
        factor = jnp.where(iota((8, depth), 0) == 0, lanes_ref[1, pl.ds(group, 1), :], 0.0)
        scaled = scaled_ref[group]
        high = scaled.astype(BF16).astype(F32)
        left = jnp.concatenate(
            [weighted, factor, high, scaled - high, jnp.zeros((8, depth), F32)], axis=0
        )
        lefts.append(left.astype(BF16))
        values.append(g)
        positions.append(position.astype(BF16))
    for p in range(0, blocks, 2):
        columns = slice(p * width, (p + 2) * width)
        direct = direct_s[:, columns]
        for u in range(2):
            right = jnp.concatenate(
                [
                    jnp.where(positions[u] == jnp.bfloat16(q), values[u], jnp.bfloat16(0))
                    for q in (p, p + 1)
                ],
                axis=1,
            )
            total = jnp.dot(lefts[u], right, preferred_element_type=F32)
            direct = direct + total[:head]
            spread_s[pl.ds(pl.multiple_of(at + u * rows, GROUP), rows), columns] = (
                total[head : head + rows] + total[head + rows : head + 2 * rows]
            )
        direct_s[:, columns] = direct


EVEN = (0, 4, 2, 6)
ODD = (0, 2, 4, 6)


def fetch(pairs, sems):
    copies = [
        pltpu.make_async_copy(source, target, sems.at[n])
        for n, (source, target) in enumerate(pairs)
    ]
    for copy in copies:
        copy.start()
    return copies


def lead_kernel(ks, sub, *refs):
    small, g_hbm, (keep_ref, send_ref), shared = refs[:7], refs[7], refs[8:10], refs[10:14]
    local_small, g_ref, table_s, sems, scratch = refs[14:21], refs[21], refs[22], refs[23], refs[24:]

    @pl.when(pl.program_id(0) == 0)
    def _():
        copies = fetch([*zip(small, local_small), (g_hbm, g_ref)], sems)
        for copy in copies[:-1]:
            copy.wait()
        prepare(*local_small, *shared)
        copy = pltpu.make_async_copy(shared[3], table_s, sems.at[0])
        copy.start()
        copy.wait()
        copies[-1].wait()

    assemble_region(ks, sub, table_s, *shared[:3], g_ref, keep_ref, send_ref, *scratch)


def follow_kernel(ks, sub, scaled_ref, lanes_ref, column_ref, table_ref, g_ref, *refs):
    assemble_region(ks, sub, table_ref, scaled_ref, lanes_ref, column_ref, g_ref, *refs)


def assemble_region(
    ks, sub, table_ref, scaled_ref, lanes_ref, column_ref, g_ref,
    keep_ref, send_ref, g_s, direct_s, spread_s, wide_s, turned_s, acc_s,
):
    k = jnp.where(pl.program_id(0) == 0, ks[0], ks[-1])
    width = g_ref.shape[2]
    blocks = spread_s.shape[1] // width
    many = blocks // 2
    region = lax.axis_index("region") ^ k
    block = lax.axis_index("tile") // sub
    first = table_ref[8 + region, 0] // PAIR
    steps = table_ref[8 + region, 1] // PAIR - first
    direct_s[...] = jnp.zeros_like(direct_s)

    def group_step(n, carry):
        one_step(
            first + n, n * (10 * GROUP), table_ref, g_ref, scaled_ref, lanes_ref, column_ref,
            g_s, direct_s, spread_s,
        )
        return carry

    lax.fori_loop(0, steps, group_step, 0)
    used = steps * 10
    depth_tiles = DEPTH // 8
    chunks = jnp.maximum((used + depth_tiles - 1) // depth_tiles, 1)

    def clear(tile, carry):
        spread_s[pl.ds(pl.multiple_of(tile * 8, 8), 8), :] = jnp.zeros((8, blocks * width), F32)
        return carry

    lax.fori_loop(used, chunks * depth_tiles, clear, 0)

    unit = (iota((width, width), 0) == iota((width, width), 1)).astype(F32).astype(BF16)

    def chunk_step(chunk, carry):
        at = pl.multiple_of(chunk * DEPTH, DEPTH)
        wide_s[...] = spread_s[pl.ds(at, DEPTH), :].astype(BF16)
        for p in range(blocks):
            turned = lax.dot_general(
                unit, wide_s[:, p * width : (p + 1) * width], NT, preferred_element_type=F32
            )
            turned = (0.0 - turned).astype(BF16)
            turned_s[p * width : (p + 1) * width] = turned
            if p < many:
                turned_s[(blocks + p) * width : (blocks + p + 1) * width] = turned

        def products(add):
            for q in range(0, blocks, 2):
                upper = (q + blocks - many) % blocks
                value = jnp.dot(
                    turned_s[upper * width : (upper + many + 2) * width],
                    wide_s[:, q * width : (q + 2) * width],
                    preferred_element_type=F32,
                )
                for r in range(many + 2):
                    p = (upper + r) % blocks
                    for c in range(2):
                        d = many - r + c
                        if 0 <= d <= many and (d < many or p < many):
                            part = value[r * width : (r + 1) * width, c * width : (c + 1) * width]
                            columns = slice(d * width, (d + 1) * width)
                            acc_s[p, :, columns] = acc_s[p, :, columns] + part if add else part

        @pl.when(chunk == 0)
        def _():
            products(False)

        @pl.when(chunk > 0)
        def _():
            products(True)

        return carry

    lax.fori_loop(0, chunks, chunk_step, 0)
    half = width // 2
    for n in range(blocks // 2):
        for odd, out_ref in ((0, keep_ref), (1, send_ref)):
            p = block ^ (jnp.where(block % 2 == 1 - odd, ODD[n], EVEN[n]) + odd)
            columns = pl.ds(pl.multiple_of(p * width, width), width)
            parts = [direct_s[0:width, columns] + acc_s[p, :, 0:width]]
            parts += [acc_s[p, :, d * width : (d + 1) * width] for d in range(1, many)]
            upper = pl.multiple_of((p // many) * half, half)
            parts.append(acc_s[p % many, pl.ds(upper, half), many * width :])
            row = direct_s[width : width + 1, columns]
            high = row.astype(BF16).astype(F32)
            sub = iota((16, width), 0)
            parts.append(jnp.where(sub == 0, high, jnp.where(sub == 1, row - high, 0.0)))
            out_ref[n, 0] = jnp.concatenate(parts, axis=0).astype(BF16)


def assemble(ks, sub, inputs, g, blocks, regions):
    tracks, hits, width = g.shape
    lead = len(inputs) == 7
    rows = width * (blocks // 2) + width // 2 + 16
    longest = -(-(-(-tracks // PAIR) * 5 * PAIR) // DEPTH) * DEPTH
    rr = -(-regions // 8) * 8
    slots = -(-(tracks + regions * (PAIR - 1)) // 128) * 128
    shared = [
        jax.ShapeDtypeStruct((slots // GROUP, 5 * GROUP, GROUP * hits), F32),
        jax.ShapeDtypeStruct((2, slots // GROUP, GROUP * hits), F32),
        jax.ShapeDtypeStruct((GROUP * hits, 128), F32),
        jax.ShapeDtypeStruct((8 + rr, slots), jnp.int32),
    ]
    out = jax.ShapeDtypeStruct((blocks // 2, len(ks), rows, width), BF16)
    spec = pl.BlockSpec((blocks // 2, 1, rows, width), lambda k: (0, k, 0, 0))
    vmem = pl.BlockSpec(memory_space=pltpu.VMEM)
    table = pltpu.SMEM(shared[3].shape, jnp.int32)
    arrived = pltpu.VMEM(g.shape, g.dtype)
    if lead:
        copies = [pltpu.SMEM(inputs[0].shape, jnp.int32)]
        copies += [pltpu.VMEM(value.shape, value.dtype) for value in inputs[1:]]
        copies += [arrived, table, pltpu.SemaphoreType.DMA((8,))]
        in_specs = [pl.BlockSpec(memory_space=pltpu.HBM)] * 8
    else:
        copies = []
        in_specs = [vmem, vmem, vmem, pl.BlockSpec(memory_space=pltpu.SMEM), vmem]
    return pl.pallas_call(
        functools.partial(lead_kernel if lead else follow_kernel, ks, sub),
        grid=(len(ks),),
        in_specs=in_specs,
        out_specs=[spec, spec] + [vmem] * (4 * lead),
        out_shape=[out, out] + shared * lead,
        scratch_shapes=copies
        + [
            pltpu.VMEM((2, GROUP * hits, width), BF16),
            pltpu.VMEM((width + 8, blocks * width), F32),
            pltpu.VMEM((longest, blocks * width), F32),
            pltpu.VMEM((DEPTH, blocks * width), BF16),
            pltpu.VMEM(((blocks + blocks // 2) * width, DEPTH), BF16),
            pltpu.VMEM((blocks, width, (blocks // 2 + 1) * width), F32),
        ],
        compiler_params=pltpu.CompilerParams(
            dimension_semantics=("arbitrary",), vmem_limit_bytes=(60 if lead else 32) * 1024 * 1024
        ),
        cost_estimate=pl.CostEstimate(
            flops=4 * 10**9 * len(ks), bytes_accessed=4 * 10**6, transcendentals=0
        ),
        name="assemble",
    )(*inputs, g)


def finish_kernel(sub, own_ref, r1_ref, r2_ref, r3_ref, e_ref, out_ref, vec_ref):
    width = own_ref.shape[1]
    p = lax.axis_index("tile") // sub
    blocks = out_ref.shape[1] // width
    many = blocks // 2

    def put(column, value):
        column = pl.multiple_of(((column + blocks) % blocks) * width, width)
        out_ref[:, pl.ds(column, width)] = value

    for d in range(many):
        put(p + d, own_ref[d * width : (d + 1) * width, :])
    for d, ref in ((1, r1_ref), (2, r2_ref), (3, r3_ref)):
        put(p - d, ref[...].astype(F32).T)
    tail = many * width + width // 2
    mine = own_ref[many * width : tail, :]
    other = e_ref[...].astype(F32)

    @pl.when(p < many)
    def _():
        put(p + many, jnp.concatenate([mine, other], axis=0))

    @pl.when(p >= many)
    def _():
        put(p + many, jnp.concatenate([other, mine], axis=0).T)

    vec_ref[...] = own_ref[tail : tail + 1, :] + own_ref[tail + 1 : tail + 2, :]


def finish(sub, own, r1, r2, r3, ext, blocks):
    width = own.shape[1]
    vmem = pl.BlockSpec(memory_space=pltpu.VMEM)
    return pl.pallas_call(
        functools.partial(finish_kernel, sub),
        in_specs=[vmem] * 5,
        out_specs=[vmem, vmem],
        out_shape=[
            jax.ShapeDtypeStruct((width, blocks * width), F32),
            jax.ShapeDtypeStruct((1, width), F32),
        ],
        name="finish",
    )(own, r1, r2, r3, ext)


def local(
    tiles, global_deriv, local_deriv, hit_weight, hit_resid, block_ids, hit_count, track_region,
    block_place,
):
    regions = lax.axis_size("region")
    tracks, hits, width = global_deriv.shape
    blocks = block_place.shape[0]
    sub = tiles // blocks
    tile = lax.axis_index("tile")
    inputs = (
        block_place,
        track_region.reshape(1, tracks),
        hit_count.reshape(1, tracks),
        local_deriv.transpose(1, 2, 0).reshape(-1, tracks),
        hit_weight.T,
        hit_resid.T,
        block_ids.T,
    )

    def swap(value, even, odd):
        pairs = [(t, t ^ (sub * (odd if t // sub % 2 else even))) for t in range(tiles)]
        return lax.ppermute(value, "tile", pairs)

    def across(value, k):
        return lax.ppermute(value.astype(BF16), "region", [(r, r ^ k) for r in range(regions)])

    def near(keep, send):
        bit = 1
        while bit < sub:
            pairs = [(t, t ^ bit) for t in range(tiles)]
            keep, send = (v + lax.ppermute(v, "tile", pairs) for v in (keep, send))
            bit *= 2
        return keep, swap(send, 1, 1)

    def both(pair, part):
        return pair[0][part].astype(F32) + pair[1][part].astype(F32)

    low, top = slice(0, blocks // 4), slice(blocks // 4, blocks // 2)
    def upper(pair):
        return swap(both(pair, top).astype(BF16), 2, 4)

    def lower(pair, more):
        value = both(pair, low) + more.astype(F32)
        return value[0], swap(value[1].astype(BF16), 4, 2)

    groups = [(k + 1, k) for k in range(regions - 2, 0, -2)] + [(1,), (0,)]
    cores, firsts, seconds = [], [], []
    for n, ks in enumerate(groups):
        keep, send, *made = assemble(ks, sub, inputs, global_deriv, blocks, regions)
        if n == 0:
            cores.append(near(keep, send))
            made[3], more = lax.optimization_barrier((made[3], both(cores[0], top).astype(BF16)))
            inputs = tuple(made)
            firsts.append(swap(more, 2, 4))
            continue
        if n > 1:
            send, cores[-1], firsts[-1] = lax.optimization_barrier((send, cores[-1], firsts[-1]))
            seconds.append(lower(cores[-2], firsts[-1]))
            firsts.append(upper(cores[-1]))
        else:
            rest, send = lax.optimization_barrier((inputs[3], send))
            inputs = inputs[:3] + (rest,)
        core = near(keep, send)
        if n > 1:
            core, firsts[-1], value = lax.optimization_barrier((core, firsts[-1], seconds[-1][1]))
            seconds[-1] = seconds[-1][0], value
        cores.append(core)
    seconds.append(lower(cores[-2], firsts[-1]))
    firsts.append(upper(cores[-1]))
    firsts[-1], value = lax.optimization_barrier((firsts[-1], seconds[-1][1]))
    seconds[-1] = seconds[-1][0], value
    seconds.append(lower(cores[-1], firsts[-1]))
    totals = [None] * regions
    for ks, (own, value) in zip(groups, seconds):
        value = own + value.astype(F32)
        for n, k in enumerate(ks):
            totals[k] = value[n]
    for k in range(regions - 1, 0, -1):
        step = k & -k
        totals[k - step] = totals[k - step] + across(totals[k], step).astype(F32)
    own = totals[0]

    def onward(value, d):
        pairs = [
            (p * sub + s, ((p + d) % blocks) * sub + s) for p in range(blocks) for s in range(sub)
        ]
        return lax.ppermute(value.astype(BF16), "tile", pairs)

    matrix, vector = finish(
        sub,
        own,
        *(onward(own[d * width : (d + 1) * width], d) for d in range(1, blocks // 2)),
        onward(own[blocks // 2 * width : blocks // 2 * width + width // 2], blocks // 2),
        blocks,
    )
    if sub > 1:
        part = tile % sub
        rows = width // sub
        matrix = lax.dynamic_slice(matrix, (part * rows, 0), (rows, blocks * width))
        vector = lax.dynamic_slice(vector, (0, part * rows), (1, rows))
    return matrix[None], vector


def solution(mesh):
    return jax.shard_map(
        functools.partial(local, mesh.shape["tile"]),
        mesh=mesh,
        in_specs=(
            P(("region", "tile"), None, None),
            P(("region", "tile"), None, None),
            P(("region", "tile"), None),
            P(("region", "tile"), None),
            P(("region", "tile"), None),
            P(("region", "tile")),
            P(("region", "tile"), None),
            P(),
        ),
        out_specs=(P("region", "tile", None), P("region", "tile")),
        check_vma=False,
    )
```

```python
import functools
import jax
import jax.numpy as jnp
from jax import lax
from jax.experimental import pallas as pl
from jax.experimental.pallas import tpu as pltpu
from jax.sharding import PartitionSpec as P

F32 = jnp.float32
BF16 = jnp.bfloat16
GROUP = 8
PAIR = 2 * GROUP
DEPTH = 256

NT = (((1,), (1,)), ((), ()))


def iota(shape, axis):
    return lax.broadcasted_iota(jnp.int32, shape, axis)


def fit(ld, weight, resid, counts):
    hits = weight.shape[0]
    live = iota(weight.shape, 0) < counts.astype(jnp.int32)
    masked_w = jnp.where(live, weight, 0.0)
    weighted_l = [v * masked_w for v in ld]
    gamma = [[None] * 5 for _ in range(5)]
    for a in range(5):
        for b in range(a + 1):
            gamma[a][b] = jnp.sum(weighted_l[a] * ld[b], axis=0, keepdims=True)
            if a == b:
                gamma[a][b] = gamma[a][b] + 1.0
    beta = [jnp.sum(weighted_l[a] * resid, axis=0, keepdims=True) for a in range(5)]
    factor = [[None] * 5 for _ in range(5)]
    inverse = [None] * 5
    for j in range(5):
        center = gamma[j][j]
        for k in range(j):
            center = center - factor[j][k] * factor[j][k]
        factor[j][j] = jnp.sqrt(center)
        inverse[j] = 1.0 / factor[j][j]
        for i in range(j + 1, 5):
            offdiag = gamma[i][j]
            for k in range(j):
                offdiag = offdiag - factor[i][k] * factor[j][k]
            factor[i][j] = offdiag * inverse[j]
    solved, rhs = [], []
    for j in range(5):
        current, target = weighted_l[j], beta[j]
        for k in range(j):
            current = current - factor[j][k] * solved[k]
            target = target - factor[j][k] * rhs[k]
        solved.append(current * inverse[j])
        rhs.append(target * inverse[j])
    projection = solved[0] * rhs[0]
    for k in range(1, 5):
        projection = projection + solved[k] * rhs[k]
    return solved, masked_w * resid - projection, masked_w


def prepare(blocks, floats_ref, numbers_ref, scaled_ref, lanes_ref, column_ref, table_ref):
    tracks = floats_ref.shape[1]
    groups, _, depth = scaled_ref.shape
    slots = groups * GROUP
    hits = depth // GROUP
    count_row, region_row, place_row = (
        numbers_ref[hits + n : hits + n + 1, :] for n in range(3)
    )
    rr = table_ref.shape[0] - 8
    member = (iota((rr, tracks), 0) == region_row).astype(F32)
    before = (iota((tracks, tracks), 0) < iota((tracks, tracks), 1)).astype(F32).astype(BF16)
    rank = jnp.dot(member.astype(BF16), before, preferred_element_type=F32)
    count = jnp.sum(member, axis=1, keepdims=True)
    room = (count.astype(jnp.int32) + (PAIR - 1)) & -PAIR
    room = jnp.broadcast_to(room.astype(F32), (rr, slots))
    lower = (iota((rr, rr), 1) < iota((rr, rr), 0)).astype(F32)
    start = jnp.zeros((rr, slots), F32)
    for g in range(rr):
        start = start + lower[:, g : g + 1] * room[g : g + 1, :]
    slot = jnp.sum(member * (rank + start[:, 0:1]), axis=0, keepdims=True)
    perm = (iota((slots, tracks), 0) == slot.astype(jnp.int32)).astype(F32).astype(BF16)
    numbers = jnp.where(
        iota((8, tracks), 0) == 0, iota((8, tracks), 1), jnp.broadcast_to(count_row, (8, tracks))
    )

    def sort(value):
        return lax.dot_general(value, perm, NT, preferred_element_type=F32)

    numbers = sort(numbers.astype(F32).astype(BF16))
    table_ref[0:8, :] = numbers.astype(jnp.int32)
    table_ref[8:, :] = jnp.where(
        iota((rr, slots), 1) == 0, start.astype(jnp.int32), (start + room).astype(jnp.int32)
    )
    flat = sort(floats_ref[...])
    flat = [flat[c * hits : (c + 1) * hits] for c in range(7)]
    solved, hit_factor, masked_w = fit(flat[:5], flat[5], flat[6], numbers[1:2])
    ids = sort(numbers_ref[:hits, :].astype(F32).astype(BF16))
    position = jnp.zeros_like(ids)
    for b in range(blocks):
        position = jnp.where(ids == float(b), place_row[:, b : b + 1].astype(F32), position)
    own = (iota((depth, slots), 0) // hits) == (iota((depth, slots), 1) % GROUP)

    def spread_out(value):
        return jnp.where(own, jnp.concatenate([value] * GROUP, axis=0), 0.0)

    grouping = (iota((groups, slots), 1) // GROUP == iota((groups, slots), 0)).astype(F32)
    for n, value in enumerate((masked_w, hit_factor)):
        lanes_ref[n] = lax.dot_general(
            grouping.astype(BF16), spread_out(value).astype(BF16), NT, preferred_element_type=F32
        )
    columns = column_ref.shape[1]
    grouping = (iota((columns, slots), 1) // GROUP == iota((columns, slots), 0)).astype(F32)
    column_ref[...] = lax.dot_general(
        spread_out(position).astype(BF16), grouping.astype(BF16), NT, preferred_element_type=F32
    )
    for c in range(5):
        scaled_ref[:, c * GROUP : (c + 1) * GROUP, :] = spread_out(solved[c]).T.reshape(
            groups, GROUP, depth
        )


def one_step(step, at, table_ref, g_ref, scaled_ref, lanes_ref, column_ref, g_s, direct_s, spread_s):
    hits, width = g_ref.shape[1:]
    depth = GROUP * hits
    blocks = spread_s.shape[1] // width
    rows = 5 * GROUP
    head = width + 8
    unit = (iota((width, width), 0) == iota((width, width), 1)).astype(F32).astype(BF16)
    lefts, values, positions = [], [], []
    for u in range(2):
        group = step * 2 + u
        for i in range(GROUP):
            g_s[u, i * hits : (i + 1) * hits, :] = g_ref[table_ref[0, group * GROUP + i]]
        g = g_s[u]
        chosen = jnp.full(column_ref.shape, group, jnp.int32)
        position = jnp.take_along_axis(column_ref[...], chosen, axis=1, mode="promise_in_bounds")
        turned = lax.dot_general(unit, g, NT, preferred_element_type=F32)
        weighted = turned * lanes_ref[0, pl.ds(group, 1), :]
        factor = jnp.where(iota((8, depth), 0) == 0, lanes_ref[1, pl.ds(group, 1), :], 0.0)
        scaled = scaled_ref[group]
        high = scaled.astype(BF16).astype(F32)
        left = jnp.concatenate(
            [weighted, factor, high, scaled - high, jnp.zeros((8, depth), F32)], axis=0
        )
        lefts.append(left.astype(BF16))
        values.append(g)
        positions.append(position.astype(BF16))
    for p in range(0, blocks, 2):
        columns = slice(p * width, (p + 2) * width)
        direct = direct_s[:, columns]
        for u in range(2):
            right = jnp.concatenate(
                [
                    jnp.where(positions[u] == jnp.bfloat16(q), values[u], jnp.bfloat16(0))
                    for q in (p, p + 1)
                ],
                axis=1,
            )
            total = jnp.dot(lefts[u], right, preferred_element_type=F32)
            direct = direct + total[:head]
            spread_s[pl.ds(pl.multiple_of(at + u * rows, GROUP), rows), columns] = (
                total[head : head + rows] + total[head + rows : head + 2 * rows]
            )
        direct_s[:, columns] = direct


EVEN = (0, 4, 2, 6)
ODD = (0, 2, 4, 6)


def lead_kernel(
    ks, sub, blocks, floats_ref, numbers_ref, g_ref,
    keep_ref, send_ref, scaled_ref, lanes_ref, column_ref, table_ref, table_s, sem, *scratch,
):
    prepare(blocks, floats_ref, numbers_ref, scaled_ref, lanes_ref, column_ref, table_ref)
    copy = pltpu.make_async_copy(table_ref, table_s, sem)
    copy.start()
    copy.wait()

    def region(n, carry):
        assemble_region(
            n, ks, sub, table_s, scaled_ref, lanes_ref, column_ref, g_ref, keep_ref, send_ref,
            *scratch,
        )
        return carry

    lax.fori_loop(0, len(ks), region, 0)


def follow_kernel(ks, sub, blocks, scaled_ref, lanes_ref, column_ref, table_ref, g_ref, *refs):
    def region(n, carry):
        assemble_region(n, ks, sub, table_ref, scaled_ref, lanes_ref, column_ref, g_ref, *refs)
        return carry

    if len(ks) == 1:
        region(0, 0)
    else:
        lax.fori_loop(0, len(ks), region, 0)


def assemble_region(
    number, ks, sub, table_ref, scaled_ref, lanes_ref, column_ref, g_ref,
    keep_ref, send_ref, g_s, direct_s, spread_s, wide_s, turned_s, acc_s,
):
    k = jnp.where(number == 0, ks[0], ks[-1])
    width = g_ref.shape[2]
    blocks = spread_s.shape[1] // width
    many = blocks // 2
    region = lax.axis_index("region") ^ k
    block = lax.axis_index("tile") // sub
    first = table_ref[8 + region, 0] // PAIR
    steps = table_ref[8 + region, 1] // PAIR - first
    direct_s[...] = jnp.zeros_like(direct_s)

    def group_step(n, carry):
        one_step(
            first + n, n * (10 * GROUP), table_ref, g_ref, scaled_ref, lanes_ref, column_ref,
            g_s, direct_s, spread_s,
        )
        return carry

    lax.fori_loop(0, steps, group_step, 0)
    used = steps * 10
    depth_tiles = DEPTH // 8
    chunks = jnp.maximum((used + depth_tiles - 1) // depth_tiles, 1)

    def clear(tile, carry):
        spread_s[pl.ds(pl.multiple_of(tile * 8, 8), 8), :] = jnp.zeros((8, blocks * width), F32)
        return carry

    lax.fori_loop(used, chunks * depth_tiles, clear, 0)

    unit = (iota((width, width), 0) == iota((width, width), 1)).astype(F32).astype(BF16)

    def chunk_step(chunk, carry):
        at = pl.multiple_of(chunk * DEPTH, DEPTH)
        wide_s[...] = spread_s[pl.ds(at, DEPTH), :].astype(BF16)
        for p in range(blocks):
            turned = lax.dot_general(
                unit, wide_s[:, p * width : (p + 1) * width], NT, preferred_element_type=F32
            )
            turned = (0.0 - turned).astype(BF16)
            turned_s[p * width : (p + 1) * width] = turned
            if p < many:
                turned_s[(blocks + p) * width : (blocks + p + 1) * width] = turned

        def products(add):
            for q in range(0, blocks, 2):
                upper = (q + blocks - many) % blocks
                value = jnp.dot(
                    turned_s[upper * width : (upper + many + 2) * width],
                    wide_s[:, q * width : (q + 2) * width],
                    preferred_element_type=F32,
                )
                for r in range(many + 2):
                    p = (upper + r) % blocks
                    for c in range(2):
                        d = many - r + c
                        if 0 <= d <= many and (d < many or p < many):
                            part = value[r * width : (r + 1) * width, c * width : (c + 1) * width]
                            columns = slice(d * width, (d + 1) * width)
                            acc_s[p, :, columns] = acc_s[p, :, columns] + part if add else part

        @pl.when(chunk == 0)
        def _():
            products(False)

        @pl.when(chunk > 0)
        def _():
            products(True)

        return carry

    lax.fori_loop(0, chunks, chunk_step, 0)
    half = width // 2
    for n in range(blocks // 2):
        for odd, out_ref in ((0, keep_ref), (1, send_ref)):
            p = block ^ (jnp.where(block % 2 == 1 - odd, ODD[n], EVEN[n]) + odd)
            columns = pl.ds(pl.multiple_of(p * width, width), width)
            parts = [direct_s[0:width, columns] + acc_s[p, :, 0:width]]
            parts += [acc_s[p, :, d * width : (d + 1) * width] for d in range(1, many)]
            upper = pl.multiple_of((p // many) * half, half)
            parts.append(acc_s[p % many, pl.ds(upper, half), many * width :])
            row = direct_s[width : width + 1, columns]
            high = row.astype(BF16).astype(F32)
            sub = iota((16, width), 0)
            parts.append(jnp.where(sub == 0, high, jnp.where(sub == 1, row - high, 0.0)))
            out_ref[n, number] = jnp.concatenate(parts, axis=0).astype(BF16)


def assemble(ks, sub, inputs, g, blocks, regions):
    tracks, hits, width = g.shape
    lead = len(inputs) == 2
    rows = width * (blocks // 2) + width // 2 + 16
    longest = -(-(-(-tracks // PAIR) * 5 * PAIR) // DEPTH) * DEPTH
    rr = -(-regions // 8) * 8
    slots = -(-(tracks + regions * (PAIR - 1)) // 128) * 128
    shared = [
        jax.ShapeDtypeStruct((slots // GROUP, 5 * GROUP, GROUP * hits), F32),
        jax.ShapeDtypeStruct((2, slots // GROUP, GROUP * hits), F32),
        jax.ShapeDtypeStruct((GROUP * hits, 128), F32),
        jax.ShapeDtypeStruct((8 + rr, slots), jnp.int32),
    ]
    out = jax.ShapeDtypeStruct((blocks // 2, len(ks), rows, width), BF16)
    vmem = pl.BlockSpec(memory_space=pltpu.VMEM)
    smem = pl.BlockSpec(memory_space=pltpu.SMEM)
    local_table = [pltpu.SMEM(shared[3].shape, jnp.int32), pltpu.SemaphoreType.DMA]
    return pl.pallas_call(
        functools.partial(lead_kernel if lead else follow_kernel, ks, sub, blocks),
        in_specs=[vmem] * 3 if lead else [vmem, vmem, vmem, smem, vmem],
        out_specs=[vmem] * (6 if lead else 2),
        out_shape=[out, out] + shared * lead,
        scratch_shapes=local_table * lead
        + [
            pltpu.VMEM((2, GROUP * hits, width), BF16),
            pltpu.VMEM((width + 8, blocks * width), F32),
            pltpu.VMEM((longest, blocks * width), F32),
            pltpu.VMEM((DEPTH, blocks * width), BF16),
            pltpu.VMEM(((blocks + blocks // 2) * width, DEPTH), BF16),
            pltpu.VMEM((blocks, width, (blocks // 2 + 1) * width), F32),
        ],
        compiler_params=pltpu.CompilerParams(vmem_limit_bytes=28 * 1024 * 1024),
        cost_estimate=pl.CostEstimate(
            flops=4 * 10**9 * len(ks), bytes_accessed=4 * 10**6, transcendentals=0
        ),
        name="assemble",
    )(*inputs, g)


def finish_kernel(sub, own_ref, r1_ref, r2_ref, r3_ref, e_ref, out_ref, vec_ref):
    width = own_ref.shape[1]
    p = lax.axis_index("tile") // sub
    blocks = out_ref.shape[1] // width
    many = blocks // 2

    def put(column, value):
        column = pl.multiple_of(((column + blocks) % blocks) * width, width)
        out_ref[:, pl.ds(column, width)] = value

    for d in range(many):
        put(p + d, own_ref[d * width : (d + 1) * width, :])
    for d, ref in ((1, r1_ref), (2, r2_ref), (3, r3_ref)):
        put(p - d, ref[...].astype(F32).T)
    tail = many * width + width // 2
    mine = own_ref[many * width : tail, :]
    other = e_ref[...].astype(F32)

    @pl.when(p < many)
    def _():
        put(p + many, jnp.concatenate([mine, other], axis=0))

    @pl.when(p >= many)
    def _():
        put(p + many, jnp.concatenate([other, mine], axis=0).T)

    vec_ref[...] = own_ref[tail : tail + 1, :] + own_ref[tail + 1 : tail + 2, :]


def finish(sub, own, r1, r2, r3, ext, blocks):
    width = own.shape[1]
    vmem = pl.BlockSpec(memory_space=pltpu.VMEM)
    return pl.pallas_call(
        functools.partial(finish_kernel, sub),
        in_specs=[vmem] * 5,
        out_specs=[vmem, vmem],
        out_shape=[
            jax.ShapeDtypeStruct((width, blocks * width), F32),
            jax.ShapeDtypeStruct((1, width), F32),
        ],
        name="finish",
    )(own, r1, r2, r3, ext)


def local(
    tiles, global_deriv, local_deriv, hit_weight, hit_resid, block_ids, hit_count, track_region,
    block_place,
):
    regions = lax.axis_size("region")
    tracks, hits, width = global_deriv.shape
    blocks = block_place.shape[0]
    sub = tiles // blocks
    tile = lax.axis_index("tile")
    floats = [local_deriv.transpose(1, 2, 0).reshape(-1, tracks), hit_weight.T, hit_resid.T]
    numbers = [
        block_ids.T,
        hit_count.reshape(1, tracks),
        track_region.reshape(1, tracks),
        jnp.pad(block_place, (0, tracks - blocks)).reshape(1, tracks),
    ]
    inputs = (jnp.concatenate(floats, axis=0), jnp.concatenate(numbers, axis=0))

    def swap(value, even, odd):
        pairs = [(t, t ^ (sub * (odd if t // sub % 2 else even))) for t in range(tiles)]
        return lax.ppermute(value, "tile", pairs)

    def across(value, k):
        return lax.ppermute(value.astype(BF16), "region", [(r, r ^ k) for r in range(regions)])

    def near(keep, send):
        bit = 1
        while bit < sub:
            pairs = [(t, t ^ bit) for t in range(tiles)]
            keep, send = (v + lax.ppermute(v, "tile", pairs) for v in (keep, send))
            bit *= 2
        return keep, swap(send, 1, 1)

    def both(pair, part):
        return pair[0][part].astype(F32) + pair[1][part].astype(F32)

    low, top = slice(0, blocks // 4), slice(blocks // 4, blocks // 2)
    def upper(pair):
        return swap(both(pair, top).astype(BF16), 2, 4)

    def lower(pair, more):
        value = both(pair, low) + more.astype(F32)
        return value[0], swap(value[1].astype(BF16), 4, 2)

    groups = [(k + 1, k) for k in range(regions - 2, 0, -2)] + [(1,), (0,)]
    totals, cores, firsts, seconds = [None] * regions, [], [], []

    def after(value, other):
        return lax.optimization_barrier((value, other))[0]

    def settle(n):
        value = seconds[n][0] + seconds[n][1].astype(F32)
        for place, k in enumerate(groups[n]):
            totals[k] = value[place]

    for n, ks in enumerate(groups):
        keep, send, *made = assemble(ks, sub, inputs, global_deriv, blocks, regions)
        if n == 0:
            cores.append(near(keep, send))
            made[3], more = lax.optimization_barrier((made[3], both(cores[0], top).astype(BF16)))
            inputs = tuple(made)
            firsts.append(swap(more, 2, 4))
            continue
        if n > 1:
            send = after(send, firsts[n - 2])
        rest, send = lax.optimization_barrier((inputs[3], send))
        inputs = inputs[:3] + (rest,)
        cores.append(near(keep, send))
        if n > 1:
            seconds.append(lower(cores[n - 2], firsts[n - 2]))
            firsts.append(upper(cores[n - 1]))
            settle(n - 2)
    last = len(groups) - 1
    firsts[last - 1] = after(firsts[last - 1], cores[last])
    half, more = lower(cores[last - 1], firsts[last - 1])
    firsts.append(upper(cores[last]))
    seconds.append((half, after(more, firsts[last])))
    settle(last - 1)
    crossed = []
    for k in range(regions - 1, 1, -1):
        step = k & -k
        value = across(totals[k], step)
        if k == 3:
            value = after(value, cores[last])
            firsts[last] = after(firsts[last], value)
        if k == step:
            crossed.append(value)
        else:
            totals[k - step] = totals[k - step] + value.astype(F32)
    seconds.append(lower(cores[last], firsts[last]))
    settle(last)
    own = totals[0]
    for value in crossed + [across(totals[1], 1)]:
        own = own + value.astype(F32)

    def onward(value, d):
        pairs = [
            (p * sub + s, ((p + d) % blocks) * sub + s) for p in range(blocks) for s in range(sub)
        ]
        return lax.ppermute(value.astype(BF16), "tile", pairs)

    matrix, vector = finish(
        sub,
        own,
        *(onward(own[d * width : (d + 1) * width], d) for d in range(1, blocks // 2)),
        onward(own[blocks // 2 * width : blocks // 2 * width + width // 2], blocks // 2),
        blocks,
    )
    if sub > 1:
        part = tile % sub
        rows = width // sub
        matrix = lax.dynamic_slice(matrix, (part * rows, 0), (rows, blocks * width))
        vector = lax.dynamic_slice(vector, (0, part * rows), (1, rows))
    return matrix[None], vector


def solution(mesh):
    return jax.shard_map(
        functools.partial(local, mesh.shape["tile"]),
        mesh=mesh,
        in_specs=(
            P(("region", "tile"), None, None),
            P(("region", "tile"), None, None),
            P(("region", "tile"), None),
            P(("region", "tile"), None),
            P(("region", "tile"), None),
            P(("region", "tile")),
            P(("region", "tile"), None),
            P(),
        ),
        out_specs=(P("region", "tile", None), P("region", "tile")),
        check_vma=False,
    )
```

```python
import functools
import jax
import jax.numpy as jnp
from jax import lax
from jax.experimental import pallas as pl
from jax.experimental.pallas import tpu as pltpu
from jax.sharding import PartitionSpec as P

F32 = jnp.float32
BF16 = jnp.bfloat16
GROUP = 8
PAIR = 2 * GROUP
DEPTH = 256

NT = (((1,), (1,)), ((), ()))


def iota(shape, axis):
    return lax.broadcasted_iota(jnp.int32, shape, axis)


def fit(ld, weight, resid, counts):
    hits = weight.shape[0]
    live = iota(weight.shape, 0) < counts.astype(jnp.int32)
    masked_w = jnp.where(live, weight, 0.0)
    weighted_l = [v * masked_w for v in ld]
    gamma = [[None] * 5 for _ in range(5)]
    for a in range(5):
        for b in range(a + 1):
            gamma[a][b] = jnp.sum(weighted_l[a] * ld[b], axis=0, keepdims=True)
            if a == b:
                gamma[a][b] = gamma[a][b] + 1.0
    beta = [jnp.sum(weighted_l[a] * resid, axis=0, keepdims=True) for a in range(5)]
    factor = [[None] * 5 for _ in range(5)]
    inverse = [None] * 5
    for j in range(5):
        center = gamma[j][j]
        for k in range(j):
            center = center - factor[j][k] * factor[j][k]
        factor[j][j] = jnp.sqrt(center)
        inverse[j] = 1.0 / factor[j][j]
        for i in range(j + 1, 5):
            offdiag = gamma[i][j]
            for k in range(j):
                offdiag = offdiag - factor[i][k] * factor[j][k]
            factor[i][j] = offdiag * inverse[j]
    solved, rhs = [], []
    for j in range(5):
        current, target = weighted_l[j], beta[j]
        for k in range(j):
            current = current - factor[j][k] * solved[k]
            target = target - factor[j][k] * rhs[k]
        solved.append(current * inverse[j])
        rhs.append(target * inverse[j])
    projection = solved[0] * rhs[0]
    for k in range(1, 5):
        projection = projection + solved[k] * rhs[k]
    return solved, masked_w * resid - projection, masked_w


def prepare(blocks, floats_ref, numbers_ref, scaled_ref, lanes_ref, column_ref, table_ref):
    tracks = floats_ref.shape[1]
    groups, _, depth = scaled_ref.shape
    slots = groups * GROUP
    hits = depth // GROUP
    count_row, region_row = (numbers_ref[hits + n : hits + n + 1, :] for n in range(2))
    rr = table_ref.shape[0] - 8
    member = (iota((rr, tracks), 0) == region_row).astype(F32)
    before = (iota((tracks, tracks), 0) < iota((tracks, tracks), 1)).astype(F32).astype(BF16)
    rank = jnp.dot(member.astype(BF16), before, preferred_element_type=F32)
    count = jnp.sum(member, axis=1, keepdims=True)
    room = (count.astype(jnp.int32) + (PAIR - 1)) & -PAIR
    room = jnp.broadcast_to(room.astype(F32), (rr, slots))
    lower = (iota((rr, rr), 1) < iota((rr, rr), 0)).astype(F32)
    start = jnp.zeros((rr, slots), F32)
    for g in range(rr):
        start = start + lower[:, g : g + 1] * room[g : g + 1, :]
    slot = jnp.sum(member * (rank + start[:, 0:1]), axis=0, keepdims=True)
    perm = (iota((slots, tracks), 0) == slot.astype(jnp.int32)).astype(F32).astype(BF16)
    numbers = jnp.where(
        iota((8, tracks), 0) == 0, iota((8, tracks), 1), jnp.broadcast_to(count_row, (8, tracks))
    )

    def sort(value):
        return lax.dot_general(value, perm, NT, preferred_element_type=F32)

    numbers = sort(numbers.astype(F32).astype(BF16))
    table_ref[0:8, :] = numbers.astype(jnp.int32)
    table_ref[8:, :] = jnp.where(
        iota((rr, slots), 1) == 0, start.astype(jnp.int32), (start + room).astype(jnp.int32)
    )
    flat = sort(floats_ref[...])
    flat = [flat[c * hits : (c + 1) * hits] for c in range(7)]
    solved, hit_factor, masked_w = fit(flat[:5], flat[5], flat[6], numbers[1:2])
    ids = sort(numbers_ref[:hits, :].astype(F32).astype(BF16))
    places = [numbers_ref[hits + 2 + b : hits + 3 + b, 0:1].astype(F32) for b in range(blocks)]
    position = jnp.zeros_like(ids)
    for b in range(blocks):
        position = jnp.where(ids == float(b), places[b], position)
    own = (iota((depth, slots), 0) // hits) == (iota((depth, slots), 1) % GROUP)

    def spread_out(value):
        return jnp.where(own, jnp.concatenate([value] * GROUP, axis=0), 0.0)

    grouping = (iota((groups, slots), 1) // GROUP == iota((groups, slots), 0)).astype(F32)
    for n, value in enumerate((masked_w, hit_factor)):
        lanes_ref[n] = lax.dot_general(
            grouping.astype(BF16), spread_out(value).astype(BF16), NT, preferred_element_type=F32
        )
    columns = column_ref.shape[1]
    grouping = (iota((columns, slots), 1) // GROUP == iota((columns, slots), 0)).astype(F32)
    column_ref[...] = lax.dot_general(
        spread_out(position).astype(BF16), grouping.astype(BF16), NT, preferred_element_type=F32
    )
    for c in range(5):
        scaled_ref[:, c * GROUP : (c + 1) * GROUP, :] = spread_out(solved[c]).T.reshape(
            groups, GROUP, depth
        )


def one_step(step, at, table_ref, g_ref, scaled_ref, lanes_ref, column_ref, g_s, direct_s, spread_s):
    hits, width = g_ref.shape[1:]
    depth = GROUP * hits
    blocks = spread_s.shape[1] // width
    rows = 5 * GROUP
    head = width + 8
    unit = (iota((width, width), 0) == iota((width, width), 1)).astype(F32).astype(BF16)
    lefts, values, positions = [], [], []
    for u in range(2):
        group = step * 2 + u
        for i in range(GROUP):
            g_s[u, i * hits : (i + 1) * hits, :] = g_ref[table_ref[0, group * GROUP + i]]
        g = g_s[u]
        chosen = jnp.full(column_ref.shape, group, jnp.int32)
        position = jnp.take_along_axis(column_ref[...], chosen, axis=1, mode="promise_in_bounds")
        turned = lax.dot_general(unit, g, NT, preferred_element_type=F32)
        weighted = turned * lanes_ref[0, pl.ds(group, 1), :]
        factor = jnp.where(iota((8, depth), 0) == 0, lanes_ref[1, pl.ds(group, 1), :], 0.0)
        scaled = scaled_ref[group]
        high = scaled.astype(BF16).astype(F32)
        left = jnp.concatenate(
            [weighted, factor, high, scaled - high, jnp.zeros((8, depth), F32)], axis=0
        )
        lefts.append(left.astype(BF16))
        values.append(g)
        positions.append(position.astype(BF16))
    for p in range(0, blocks, 2):
        columns = slice(p * width, (p + 2) * width)
        direct = direct_s[:, columns]
        for u in range(2):
            right = jnp.concatenate(
                [
                    jnp.where(positions[u] == jnp.bfloat16(q), values[u], jnp.bfloat16(0))
                    for q in (p, p + 1)
                ],
                axis=1,
            )
            total = jnp.dot(lefts[u], right, preferred_element_type=F32)
            direct = direct + total[:head]
            spread_s[pl.ds(pl.multiple_of(at + u * rows, GROUP), rows), columns] = (
                total[head : head + rows] + total[head + rows : head + 2 * rows]
            )
        direct_s[:, columns] = direct


EVEN = (0, 4, 2, 6)
ODD = (0, 2, 4, 6)


def lead_kernel(
    ks, sub, blocks, floats_ref, numbers_ref, g_ref,
    keep_ref, send_ref, scaled_ref, lanes_ref, column_ref, table_ref, table_s, sem, *scratch,
):
    prepare(blocks, floats_ref, numbers_ref, scaled_ref, lanes_ref, column_ref, table_ref)
    copy = pltpu.make_async_copy(table_ref, table_s, sem)
    copy.start()
    copy.wait()

    def region(n, carry):
        assemble_region(
            n, ks, sub, table_s, scaled_ref, lanes_ref, column_ref, g_ref, keep_ref, send_ref,
            *scratch,
        )
        return carry

    lax.fori_loop(0, len(ks), region, 0)


def follow_kernel(ks, sub, blocks, scaled_ref, lanes_ref, column_ref, table_ref, g_ref, *refs):
    def region(n, carry):
        assemble_region(n, ks, sub, table_ref, scaled_ref, lanes_ref, column_ref, g_ref, *refs)
        return carry

    if len(ks) == 1:
        region(0, 0)
    else:
        lax.fori_loop(0, len(ks), region, 0)


def assemble_region(
    number, ks, sub, table_ref, scaled_ref, lanes_ref, column_ref, g_ref,
    keep_ref, send_ref, g_s, direct_s, spread_s, wide_s, turned_s, acc_s,
):
    k = jnp.where(number == 0, ks[0], ks[-1])
    width = g_ref.shape[2]
    blocks = spread_s.shape[1] // width
    many = blocks // 2
    region = lax.axis_index("region") ^ k
    block = lax.axis_index("tile") // sub
    first = table_ref[8 + region, 0] // PAIR
    steps = table_ref[8 + region, 1] // PAIR - first
    direct_s[...] = jnp.zeros_like(direct_s)

    def group_step(n, carry):
        one_step(
            first + n, n * (10 * GROUP), table_ref, g_ref, scaled_ref, lanes_ref, column_ref,
            g_s, direct_s, spread_s,
        )
        return carry

    lax.fori_loop(0, steps, group_step, 0)
    used = steps * 10
    depth_tiles = DEPTH // 8
    chunks = jnp.maximum((used + depth_tiles - 1) // depth_tiles, 1)

    def clear(tile, carry):
        spread_s[pl.ds(pl.multiple_of(tile * 8, 8), 8), :] = jnp.zeros((8, blocks * width), F32)
        return carry

    lax.fori_loop(used, chunks * depth_tiles, clear, 0)

    unit = (iota((width, width), 0) == iota((width, width), 1)).astype(F32).astype(BF16)

    def chunk_step(chunk, carry):
        at = pl.multiple_of(chunk * DEPTH, DEPTH)
        wide_s[...] = spread_s[pl.ds(at, DEPTH), :].astype(BF16)
        for p in range(blocks):
            turned = lax.dot_general(
                unit, wide_s[:, p * width : (p + 1) * width], NT, preferred_element_type=F32
            )
            turned = (0.0 - turned).astype(BF16)
            turned_s[p * width : (p + 1) * width] = turned
            if p < many:
                turned_s[(blocks + p) * width : (blocks + p + 1) * width] = turned

        def products(add):
            for q in range(0, blocks, 2):
                upper = (q + blocks - many) % blocks
                value = jnp.dot(
                    turned_s[upper * width : (upper + many + 2) * width],
                    wide_s[:, q * width : (q + 2) * width],
                    preferred_element_type=F32,
                )
                for r in range(many + 2):
                    p = (upper + r) % blocks
                    for c in range(2):
                        d = many - r + c
                        if 0 <= d <= many and (d < many or p < many):
                            part = value[r * width : (r + 1) * width, c * width : (c + 1) * width]
                            columns = slice(d * width, (d + 1) * width)
                            acc_s[p, :, columns] = acc_s[p, :, columns] + part if add else part

        @pl.when(chunk == 0)
        def _():
            products(False)

        @pl.when(chunk > 0)
        def _():
            products(True)

        return carry

    lax.fori_loop(0, chunks, chunk_step, 0)
    half = width // 2
    for n in range(blocks // 2):
        for odd, out_ref in ((0, keep_ref), (1, send_ref)):
            p = block ^ (jnp.where(block % 2 == 1 - odd, ODD[n], EVEN[n]) + odd)
            columns = pl.ds(pl.multiple_of(p * width, width), width)
            parts = [direct_s[0:width, columns] + acc_s[p, :, 0:width]]
            parts += [acc_s[p, :, d * width : (d + 1) * width] for d in range(1, many)]
            upper = pl.multiple_of((p // many) * half, half)
            parts.append(acc_s[p % many, pl.ds(upper, half), many * width :])
            row = direct_s[width : width + 1, columns]
            high = row.astype(BF16).astype(F32)
            sub = iota((16, width), 0)
            parts.append(jnp.where(sub == 0, high, jnp.where(sub == 1, row - high, 0.0)))
            out_ref[n, number] = jnp.concatenate(parts, axis=0).astype(BF16)


def assemble(ks, sub, inputs, g, blocks, regions):
    tracks, hits, width = g.shape
    lead = len(inputs) == 2
    rows = width * (blocks // 2) + width // 2 + 16
    longest = -(-(-(-tracks // PAIR) * 5 * PAIR) // DEPTH) * DEPTH
    rr = -(-regions // 8) * 8
    slots = -(-(tracks + regions * (PAIR - 1)) // 128) * 128
    shared = [
        jax.ShapeDtypeStruct((slots // GROUP, 5 * GROUP, GROUP * hits), F32),
        jax.ShapeDtypeStruct((2, slots // GROUP, GROUP * hits), F32),
        jax.ShapeDtypeStruct((GROUP * hits, 128), F32),
        jax.ShapeDtypeStruct((8 + rr, slots), jnp.int32),
    ]
    out = jax.ShapeDtypeStruct((blocks // 2, len(ks), rows, width), BF16)
    vmem = pl.BlockSpec(memory_space=pltpu.VMEM)
    smem = pl.BlockSpec(memory_space=pltpu.SMEM)
    local_table = [pltpu.SMEM(shared[3].shape, jnp.int32), pltpu.SemaphoreType.DMA]
    return pl.pallas_call(
        functools.partial(lead_kernel if lead else follow_kernel, ks, sub, blocks),
        in_specs=[vmem] * 3 if lead else [vmem, vmem, vmem, smem, vmem],
        out_specs=[vmem] * (6 if lead else 2),
        out_shape=[out, out] + shared * lead,
        scratch_shapes=local_table * lead
        + [
            pltpu.VMEM((2, GROUP * hits, width), BF16),
            pltpu.VMEM((width + 8, blocks * width), F32),
            pltpu.VMEM((longest, blocks * width), F32),
            pltpu.VMEM((DEPTH, blocks * width), BF16),
            pltpu.VMEM(((blocks + blocks // 2) * width, DEPTH), BF16),
            pltpu.VMEM((blocks, width, (blocks // 2 + 1) * width), F32),
        ],
        compiler_params=pltpu.CompilerParams(vmem_limit_bytes=28 * 1024 * 1024),
        cost_estimate=pl.CostEstimate(
            flops=10**9 * len(ks), bytes_accessed=4 * 10**6, transcendentals=0
        ),
        name="assemble",
    )(*inputs, g)


def finish_kernel(sub, own_ref, r1_ref, r2_ref, r3_ref, e_ref, out_ref, vec_ref):
    width = own_ref.shape[1]
    p = lax.axis_index("tile") // sub
    blocks = out_ref.shape[1] // width
    many = blocks // 2

    def put(column, value):
        column = pl.multiple_of(((column + blocks) % blocks) * width, width)
        out_ref[:, pl.ds(column, width)] = value

    for d in range(many):
        put(p + d, own_ref[d * width : (d + 1) * width, :])
    for d, ref in ((1, r1_ref), (2, r2_ref), (3, r3_ref)):
        put(p - d, ref[...].astype(F32).T)
    tail = many * width + width // 2
    mine = own_ref[many * width : tail, :]
    other = e_ref[...].astype(F32)

    @pl.when(p < many)
    def _():
        put(p + many, jnp.concatenate([mine, other], axis=0))

    @pl.when(p >= many)
    def _():
        put(p + many, jnp.concatenate([other, mine], axis=0).T)

    vec_ref[...] = own_ref[tail : tail + 1, :] + own_ref[tail + 1 : tail + 2, :]


def finish(sub, own, r1, r2, r3, ext, blocks):
    width = own.shape[1]
    vmem = pl.BlockSpec(memory_space=pltpu.VMEM)
    return pl.pallas_call(
        functools.partial(finish_kernel, sub),
        in_specs=[vmem] * 5,
        out_specs=[vmem, vmem],
        out_shape=[
            jax.ShapeDtypeStruct((width, blocks * width), F32),
            jax.ShapeDtypeStruct((1, width), F32),
        ],
        compiler_params=pltpu.CompilerParams(vmem_limit_bytes=8 * 1024 * 1024),
        name="finish",
    )(own, r1, r2, r3, ext)


def local(
    tiles, global_deriv, local_deriv, hit_weight, hit_resid, block_ids, hit_count, track_region,
    block_place,
):
    regions = lax.axis_size("region")
    tracks, hits, width = global_deriv.shape
    blocks = block_place.shape[0]
    sub = tiles // blocks
    tile = lax.axis_index("tile")
    floats = [local_deriv.transpose(1, 2, 0).reshape(-1, tracks), hit_weight.T, hit_resid.T]
    numbers = [
        block_ids.T,
        hit_count.reshape(1, tracks),
        track_region.reshape(1, tracks),
        jnp.broadcast_to(block_place[:, None], (blocks, tracks)),
    ]
    inputs = (jnp.concatenate(floats, axis=0), jnp.concatenate(numbers, axis=0))

    def swap(value, even, odd):
        pairs = [(t, t ^ (sub * (odd if t // sub % 2 else even))) for t in range(tiles)]
        return lax.ppermute(value, "tile", pairs)

    def across(value, k):
        return lax.ppermute(value.astype(BF16), "region", [(r, r ^ k) for r in range(regions)])

    def near(keep, send):
        bit = 1
        while bit < sub:
            pairs = [(t, t ^ bit) for t in range(tiles)]
            keep, send = (v + lax.ppermute(v, "tile", pairs) for v in (keep, send))
            bit *= 2
        return keep, swap(send, 1, 1)

    def both(pair, part):
        return pair[0][part].astype(F32) + pair[1][part].astype(F32)

    low, top = slice(0, blocks // 4), slice(blocks // 4, blocks // 2)
    def upper(pair):
        return swap(both(pair, top).astype(BF16), 2, 4)

    def lower(pair, more):
        value = both(pair, low) + more.astype(F32)
        return value[0], swap(value[1].astype(BF16), 4, 2)

    groups = [(k + 1, k) for k in range(regions - 2, 0, -2)] + [(1,), (0,)]
    totals, cores, firsts, seconds = [None] * regions, [], [], []

    def after(value, other):
        return lax.optimization_barrier((value, other))[0]

    def settle(n):
        value = seconds[n][0] + seconds[n][1].astype(F32)
        for place, k in enumerate(groups[n]):
            totals[k] = value[place]

    for n, ks in enumerate(groups):
        keep, send, *made = assemble(ks, sub, inputs, global_deriv, blocks, regions)
        if n == 0:
            cores.append(near(keep, send))
            made[3], more = lax.optimization_barrier((made[3], both(cores[0], top).astype(BF16)))
            inputs = tuple(made)
            firsts.append(swap(more, 2, 4))
            continue
        if n > 1:
            firsts[n - 2] = after(firsts[n - 2], send)
            send = after(send, cores[n - 1][1])
        rest, send = lax.optimization_barrier((inputs[3], send))
        inputs = inputs[:3] + (rest,)
        cores.append(near(keep, send))
        if n > 1:
            seconds.append(lower(cores[n - 2], firsts[n - 2]))
            firsts.append(upper(cores[n - 1]))
            settle(n - 2)
    last = len(groups) - 1
    operand = both(cores[last], top).astype(BF16)
    firsts[last - 1] = after(firsts[last - 1], operand)
    value = both(cores[last - 1], low) + firsts[last - 1].astype(F32)
    half, more = value[0], value[1].astype(BF16)
    firsts.append(swap(operand, 2, 4))
    seconds.append((half, after(swap(more, 4, 2), firsts[last])))
    settle(last - 1)
    crossed = []
    for k in range(regions - 1, 1, -1):
        step = k & -k
        value = across(totals[k], step)
        if k == 3:
            value = after(value, more)
            firsts[last] = after(firsts[last], value)
        if k == step:
            crossed.append(value)
        else:
            totals[k - step] = totals[k - step] + value.astype(F32)
    seconds.append(lower(cores[last], firsts[last]))
    settle(last)
    own = totals[0]
    for value in crossed + [across(totals[1], 1)]:
        own = own + value.astype(F32)

    def onward(value, d):
        pairs = [
            (p * sub + s, ((p + d) % blocks) * sub + s) for p in range(blocks) for s in range(sub)
        ]
        return lax.ppermute(value.astype(BF16), "tile", pairs)

    matrix, vector = finish(
        sub,
        own,
        *(onward(own[d * width : (d + 1) * width], d) for d in range(1, blocks // 2)),
        onward(own[blocks // 2 * width : blocks // 2 * width + width // 2], blocks // 2),
        blocks,
    )
    if sub > 1:
        part = tile % sub
        rows = width // sub
        matrix = lax.dynamic_slice(matrix, (part * rows, 0), (rows, blocks * width))
        vector = lax.dynamic_slice(vector, (0, part * rows), (1, rows))
    return matrix[None], vector


def solution(mesh):
    return jax.shard_map(
        functools.partial(local, mesh.shape["tile"]),
        mesh=mesh,
        in_specs=(
            P(("region", "tile"), None, None),
            P(("region", "tile"), None, None),
            P(("region", "tile"), None),
            P(("region", "tile"), None),
            P(("region", "tile"), None),
            P(("region", "tile")),
            P(("region", "tile"), None),
            P(),
        ),
        out_specs=(P("region", "tile", None), P("region", "tile")),
        check_vma=False,
    )
```

```python
import functools
import jax
import jax.numpy as jnp
from jax import lax
from jax.experimental import pallas as pl
from jax.experimental.pallas import tpu as pltpu
from jax.sharding import PartitionSpec as P

F32 = jnp.float32
BF16 = jnp.bfloat16
GROUP = 8
PAIR = 2 * GROUP
DEPTH = 256

NT = (((1,), (1,)), ((), ()))


def iota(shape, axis):
    return lax.broadcasted_iota(jnp.int32, shape, axis)


def fit(ld, weight, resid, counts):
    hits = weight.shape[0]
    live = iota(weight.shape, 0) < counts.astype(jnp.int32)
    masked_w = jnp.where(live, weight, 0.0)
    weighted_l = [v * masked_w for v in ld]
    gamma = [[None] * 5 for _ in range(5)]
    for a in range(5):
        for b in range(a + 1):
            gamma[a][b] = jnp.sum(weighted_l[a] * ld[b], axis=0, keepdims=True)
            if a == b:
                gamma[a][b] = gamma[a][b] + 1.0
    beta = [jnp.sum(weighted_l[a] * resid, axis=0, keepdims=True) for a in range(5)]
    factor = [[None] * 5 for _ in range(5)]
    inverse = [None] * 5
    for j in range(5):
        center = gamma[j][j]
        for k in range(j):
            center = center - factor[j][k] * factor[j][k]
        factor[j][j] = jnp.sqrt(center)
        inverse[j] = 1.0 / factor[j][j]
        for i in range(j + 1, 5):
            offdiag = gamma[i][j]
            for k in range(j):
                offdiag = offdiag - factor[i][k] * factor[j][k]
            factor[i][j] = offdiag * inverse[j]
    solved, rhs = [], []
    for j in range(5):
        current, target = weighted_l[j], beta[j]
        for k in range(j):
            current = current - factor[j][k] * solved[k]
            target = target - factor[j][k] * rhs[k]
        solved.append(current * inverse[j])
        rhs.append(target * inverse[j])
    projection = solved[0] * rhs[0]
    for k in range(1, 5):
        projection = projection + solved[k] * rhs[k]
    return solved, masked_w * resid - projection, masked_w


def prepare(blocks, floats_ref, numbers_ref, scaled_ref, lanes_ref, column_ref, table_ref):
    tracks = floats_ref.shape[1]
    groups, _, depth = scaled_ref.shape
    slots = groups * GROUP
    hits = depth // GROUP
    count_row, region_row = (numbers_ref[hits + n : hits + n + 1, :] for n in range(2))
    rr = table_ref.shape[0] - 8
    member = (iota((rr, tracks), 0) == region_row).astype(F32)
    before = (iota((tracks, tracks), 0) < iota((tracks, tracks), 1)).astype(F32).astype(BF16)
    rank = jnp.dot(member.astype(BF16), before, preferred_element_type=F32)
    count = jnp.sum(member, axis=1, keepdims=True)
    room = (count.astype(jnp.int32) + (PAIR - 1)) & -PAIR
    room = jnp.broadcast_to(room.astype(F32), (rr, slots))
    lower = (iota((rr, rr), 1) < iota((rr, rr), 0)).astype(F32)
    start = jnp.zeros((rr, slots), F32)
    for g in range(rr):
        start = start + lower[:, g : g + 1] * room[g : g + 1, :]
    slot = jnp.sum(member * (rank + start[:, 0:1]), axis=0, keepdims=True)
    perm = (iota((slots, tracks), 0) == slot.astype(jnp.int32)).astype(F32).astype(BF16)
    numbers = jnp.where(
        iota((8, tracks), 0) == 0, iota((8, tracks), 1), jnp.broadcast_to(count_row, (8, tracks))
    )

    def sort(value):
        return lax.dot_general(value, perm, NT, preferred_element_type=F32)

    numbers = sort(numbers.astype(F32).astype(BF16))
    table_ref[0:8, :] = numbers.astype(jnp.int32)
    table_ref[8:, :] = jnp.where(
        iota((rr, slots), 1) == 0, start.astype(jnp.int32), (start + room).astype(jnp.int32)
    )
    flat = sort(floats_ref[...])
    flat = [flat[c * hits : (c + 1) * hits] for c in range(7)]
    solved, hit_factor, masked_w = fit(flat[:5], flat[5], flat[6], numbers[1:2])
    ids = sort(numbers_ref[:hits, :].astype(F32).astype(BF16))
    places = [numbers_ref[hits + 2 + b : hits + 3 + b, 0:1].astype(F32) for b in range(blocks)]
    position = jnp.zeros_like(ids)
    for b in range(blocks):
        position = jnp.where(ids == float(b), places[b], position)
    own = (iota((depth, slots), 0) // hits) == (iota((depth, slots), 1) % GROUP)

    def spread_out(value):
        return jnp.where(own, jnp.concatenate([value] * GROUP, axis=0), 0.0)

    grouping = (iota((groups, slots), 1) // GROUP == iota((groups, slots), 0)).astype(F32)
    for n, value in enumerate((masked_w, hit_factor)):
        lanes_ref[n] = lax.dot_general(
            grouping.astype(BF16), spread_out(value).astype(BF16), NT, preferred_element_type=F32
        )
    columns = column_ref.shape[1]
    grouping = (iota((columns, slots), 1) // GROUP == iota((columns, slots), 0)).astype(F32)
    column_ref[...] = lax.dot_general(
        spread_out(position).astype(BF16), grouping.astype(BF16), NT, preferred_element_type=F32
    )
    for c in range(5):
        scaled_ref[:, c * GROUP : (c + 1) * GROUP, :] = spread_out(solved[c]).T.reshape(
            groups, GROUP, depth
        )


def one_step(step, at, table_ref, g_ref, scaled_ref, lanes_ref, column_ref, g_s, direct_s, spread_s):
    hits, width = g_ref.shape[1:]
    depth = GROUP * hits
    blocks = spread_s.shape[1] // width
    rows = 5 * GROUP
    head = width + 8
    unit = (iota((width, width), 0) == iota((width, width), 1)).astype(F32).astype(BF16)
    lefts, values, positions = [], [], []
    for u in range(2):
        group = step * 2 + u
        for i in range(GROUP):
            g_s[u, i * hits : (i + 1) * hits, :] = g_ref[table_ref[0, group * GROUP + i]]
        g = g_s[u]
        chosen = jnp.full(column_ref.shape, group, jnp.int32)
        position = jnp.take_along_axis(column_ref[...], chosen, axis=1, mode="promise_in_bounds")
        turned = lax.dot_general(unit, g, NT, preferred_element_type=F32)
        weighted = turned * lanes_ref[0, pl.ds(group, 1), :]
        factor = jnp.where(iota((8, depth), 0) == 0, lanes_ref[1, pl.ds(group, 1), :], 0.0)
        scaled = scaled_ref[group]
        high = scaled.astype(BF16).astype(F32)
        left = jnp.concatenate(
            [weighted, factor, high, scaled - high, jnp.zeros((8, depth), F32)], axis=0
        )
        lefts.append(left.astype(BF16))
        values.append(g)
        positions.append(position.astype(BF16))
    for p in range(0, blocks, 2):
        columns = slice(p * width, (p + 2) * width)
        direct = direct_s[:, columns]
        for u in range(2):
            right = jnp.concatenate(
                [
                    jnp.where(positions[u] == jnp.bfloat16(q), values[u], jnp.bfloat16(0))
                    for q in (p, p + 1)
                ],
                axis=1,
            )
            total = jnp.dot(lefts[u], right, preferred_element_type=F32)
            direct = direct + total[:head]
            spread_s[pl.ds(pl.multiple_of(at + u * rows, GROUP), rows), columns] = (
                total[head : head + rows] + total[head + rows : head + 2 * rows]
            )
        direct_s[:, columns] = direct


EVEN = (0, 4, 2, 6)
ODD = (0, 2, 4, 6)


def lead_kernel(
    ks, sub, blocks, floats_ref, numbers_ref, g_ref,
    keep_ref, send_ref, scaled_ref, lanes_ref, column_ref, table_ref, table_s, sem, *scratch,
):
    prepare(blocks, floats_ref, numbers_ref, scaled_ref, lanes_ref, column_ref, table_ref)
    copy = pltpu.make_async_copy(table_ref, table_s, sem)
    copy.start()
    copy.wait()

    def region(n, carry):
        assemble_region(
            n, ks, sub, table_s, scaled_ref, lanes_ref, column_ref, g_ref, keep_ref, send_ref,
            *scratch,
        )
        return carry

    lax.fori_loop(0, len(ks), region, 0)


def follow_kernel(ks, sub, blocks, scaled_ref, lanes_ref, column_ref, table_ref, g_ref, *refs):
    def region(n, carry):
        assemble_region(n, ks, sub, table_ref, scaled_ref, lanes_ref, column_ref, g_ref, *refs)
        return carry

    if len(ks) == 1:
        region(0, 0)
    else:
        lax.fori_loop(0, len(ks), region, 0)


def assemble_region(
    number, ks, sub, table_ref, scaled_ref, lanes_ref, column_ref, g_ref,
    keep_ref, send_ref, g_s, direct_s, spread_s, wide_s, turned_s, acc_s,
):
    k = jnp.where(number == 0, ks[0], ks[-1])
    width = g_ref.shape[2]
    blocks = spread_s.shape[1] // width
    many = blocks // 2
    region = lax.axis_index("region") ^ k
    block = lax.axis_index("tile") // sub
    first = table_ref[8 + region, 0] // PAIR
    steps = table_ref[8 + region, 1] // PAIR - first
    direct_s[...] = jnp.zeros_like(direct_s)

    def group_step(n, carry):
        one_step(
            first + n, n * (10 * GROUP), table_ref, g_ref, scaled_ref, lanes_ref, column_ref,
            g_s, direct_s, spread_s,
        )
        return carry

    lax.fori_loop(0, steps, group_step, 0)
    used = steps * 10
    depth_tiles = DEPTH // 8
    chunks = jnp.maximum((used + depth_tiles - 1) // depth_tiles, 1)

    def clear(tile, carry):
        spread_s[pl.ds(pl.multiple_of(tile * 8, 8), 8), :] = jnp.zeros((8, blocks * width), F32)
        return carry

    lax.fori_loop(used, chunks * depth_tiles, clear, 0)

    unit = (iota((width, width), 0) == iota((width, width), 1)).astype(F32).astype(BF16)

    def chunk_step(chunk, carry):
        at = pl.multiple_of(chunk * DEPTH, DEPTH)
        wide_s[...] = spread_s[pl.ds(at, DEPTH), :].astype(BF16)
        for p in range(blocks):
            turned = lax.dot_general(
                unit, wide_s[:, p * width : (p + 1) * width], NT, preferred_element_type=F32
            )
            turned = (0.0 - turned).astype(BF16)
            turned_s[p * width : (p + 1) * width] = turned
            if p < many:
                turned_s[(blocks + p) * width : (blocks + p + 1) * width] = turned

        def products(add):
            for q in range(0, blocks, 2):
                upper = (q + blocks - many) % blocks
                value = jnp.dot(
                    turned_s[upper * width : (upper + many + 2) * width],
                    wide_s[:, q * width : (q + 2) * width],
                    preferred_element_type=F32,
                )
                for r in range(many + 2):
                    p = (upper + r) % blocks
                    for c in range(2):
                        d = many - r + c
                        if 0 <= d <= many and (d < many or p < many):
                            part = value[r * width : (r + 1) * width, c * width : (c + 1) * width]
                            columns = slice(d * width, (d + 1) * width)
                            acc_s[p, :, columns] = acc_s[p, :, columns] + part if add else part

        @pl.when(chunk == 0)
        def _():
            products(False)

        @pl.when(chunk > 0)
        def _():
            products(True)

        return carry

    lax.fori_loop(0, chunks, chunk_step, 0)
    half = width // 2
    for n in range(blocks // 2):
        for odd, out_ref in ((0, keep_ref), (1, send_ref)):
            p = block ^ (jnp.where(block % 2 == 1 - odd, ODD[n], EVEN[n]) + odd)
            columns = pl.ds(pl.multiple_of(p * width, width), width)
            parts = [direct_s[0:width, columns] + acc_s[p, :, 0:width]]
            parts += [acc_s[p, :, d * width : (d + 1) * width] for d in range(1, many)]
            upper = pl.multiple_of((p // many) * half, half)
            parts.append(acc_s[p % many, pl.ds(upper, half), many * width :])
            row = direct_s[width : width + 1, columns]
            high = row.astype(BF16).astype(F32)
            sub = iota((16, width), 0)
            parts.append(jnp.where(sub == 0, high, jnp.where(sub == 1, row - high, 0.0)))
            out_ref[n, number] = jnp.concatenate(parts, axis=0).astype(BF16)


def assemble(ks, sub, inputs, g, blocks, regions):
    tracks, hits, width = g.shape
    lead = len(inputs) == 2
    rows = width * (blocks // 2) + width // 2 + 16
    longest = -(-(-(-tracks // PAIR) * 5 * PAIR) // DEPTH) * DEPTH
    rr = -(-regions // 8) * 8
    slots = -(-(tracks + regions * (PAIR - 1)) // 128) * 128
    shared = [
        jax.ShapeDtypeStruct((slots // GROUP, 5 * GROUP, GROUP * hits), F32),
        jax.ShapeDtypeStruct((2, slots // GROUP, GROUP * hits), F32),
        jax.ShapeDtypeStruct((GROUP * hits, 128), F32),
        jax.ShapeDtypeStruct((8 + rr, slots), jnp.int32),
    ]
    out = jax.ShapeDtypeStruct((blocks // 2, len(ks), rows, width), BF16)
    vmem = pl.BlockSpec(memory_space=pltpu.VMEM)
    smem = pl.BlockSpec(memory_space=pltpu.SMEM)
    local_table = [pltpu.SMEM(shared[3].shape, jnp.int32), pltpu.SemaphoreType.DMA]
    return pl.pallas_call(
        functools.partial(lead_kernel if lead else follow_kernel, ks, sub, blocks),
        in_specs=[vmem] * 3 if lead else [vmem, vmem, vmem, smem, vmem],
        out_specs=[vmem] * (6 if lead else 2),
        out_shape=[out, out] + shared * lead,
        scratch_shapes=local_table * lead
        + [
            pltpu.VMEM((2, GROUP * hits, width), BF16),
            pltpu.VMEM((width + 8, blocks * width), F32),
            pltpu.VMEM((longest, blocks * width), F32),
            pltpu.VMEM((DEPTH, blocks * width), BF16),
            pltpu.VMEM(((blocks + blocks // 2) * width, DEPTH), BF16),
            pltpu.VMEM((blocks, width, (blocks // 2 + 1) * width), F32),
        ],
        compiler_params=pltpu.CompilerParams(vmem_limit_bytes=28 * 1024 * 1024),
        cost_estimate=pl.CostEstimate(
            flops=10**9 * len(ks), bytes_accessed=4 * 10**6, transcendentals=0
        ),
        name="assemble",
    )(*inputs, g)


def finish_kernel(sub, own_ref, r1_ref, r2_ref, r3_ref, e_ref, out_ref, vec_ref):
    width = own_ref.shape[1]
    p = lax.axis_index("tile") // sub
    blocks = out_ref.shape[1] // width
    many = blocks // 2

    def put(column, value):
        column = pl.multiple_of(((column + blocks) % blocks) * width, width)
        out_ref[:, pl.ds(column, width)] = value

    for d in range(many):
        put(p + d, own_ref[d * width : (d + 1) * width, :])
    for d, ref in ((1, r1_ref), (2, r2_ref), (3, r3_ref)):
        put(p - d, ref[...].astype(F32).T)
    tail = many * width + width // 2
    mine = own_ref[many * width : tail, :]
    other = e_ref[...].astype(F32)

    @pl.when(p < many)
    def _():
        put(p + many, jnp.concatenate([mine, other], axis=0))

    @pl.when(p >= many)
    def _():
        put(p + many, jnp.concatenate([other, mine], axis=0).T)

    vec_ref[...] = own_ref[tail : tail + 1, :] + own_ref[tail + 1 : tail + 2, :]


def finish(sub, own, r1, r2, r3, ext, blocks):
    width = own.shape[1]
    vmem = pl.BlockSpec(memory_space=pltpu.VMEM)
    return pl.pallas_call(
        functools.partial(finish_kernel, sub),
        in_specs=[vmem] * 5,
        out_specs=[vmem, vmem],
        out_shape=[
            jax.ShapeDtypeStruct((width, blocks * width), F32),
            jax.ShapeDtypeStruct((1, width), F32),
        ],
        compiler_params=pltpu.CompilerParams(vmem_limit_bytes=8 * 1024 * 1024),
        name="finish",
    )(own, r1, r2, r3, ext)


def local(
    tiles, global_deriv, local_deriv, hit_weight, hit_resid, block_ids, hit_count, track_region,
    block_place,
):
    regions = lax.axis_size("region")
    tracks, hits, width = global_deriv.shape
    blocks = block_place.shape[0]
    sub = tiles // blocks
    tile = lax.axis_index("tile")
    floats = [local_deriv.transpose(1, 2, 0).reshape(-1, tracks), hit_weight.T, hit_resid.T]
    numbers = [
        block_ids.T,
        hit_count.reshape(1, tracks),
        track_region.reshape(1, tracks),
        jnp.broadcast_to(block_place[:, None], (blocks, tracks)),
    ]
    inputs = (jnp.concatenate(floats, axis=0), jnp.concatenate(numbers, axis=0))

    def swap(value, even, odd):
        pairs = [(t, t ^ (sub * (odd if t // sub % 2 else even))) for t in range(tiles)]
        return lax.ppermute(value, "tile", pairs)

    def across(value, k):
        return lax.ppermute(value.astype(BF16), "region", [(r, r ^ k) for r in range(regions)])

    def near(keep, send):
        bit = 1
        while bit < sub:
            pairs = [(t, t ^ bit) for t in range(tiles)]
            keep, send = (v + lax.ppermute(v, "tile", pairs) for v in (keep, send))
            bit *= 2
        return keep, swap(send, 1, 1)

    def both(pair, part):
        return pair[0][part].astype(F32) + pair[1][part].astype(F32)

    low, top = slice(0, blocks // 4), slice(blocks // 4, blocks // 2)
    def upper(pair):
        return swap(both(pair, top).astype(BF16), 2, 4)

    def lower(pair, more):
        value = both(pair, low) + more.astype(F32)
        return value[0], swap(value[1].astype(BF16), 4, 2)

    groups = [(k + 1, k) for k in range(regions - 2, 0, -2)] + [(1,), (0,)]
    totals, cores, firsts, seconds = [None] * regions, [], [], []

    def after(value, other):
        return lax.optimization_barrier((value, other))[0]

    def settle(n):
        value = seconds[n][0] + seconds[n][1].astype(F32)
        for place, k in enumerate(groups[n]):
            totals[k] = value[place]

    last = len(groups) - 1
    for n, ks in enumerate(groups):
        keep, send, *made = assemble(ks, sub, inputs, global_deriv, blocks, regions)
        if n == 0:
            inputs = tuple(made)
            cores.append(near(keep, send))
            continue
        table = after(inputs[3], send)
        cores[n - 1] = after(cores[n - 1], send)
        if n > 1:
            firsts[n - 2] = after(firsts[n - 2], send)
            send = after(send, cores[n - 1][1])
            seconds.append(lower(cores[n - 2], firsts[n - 2]))
            settle(n - 2)
        if n < last:
            operand = both(cores[n - 1], top).astype(BF16)
            table = after(table, operand)
            firsts.append(swap(operand, 2, 4))
        inputs = inputs[:3] + (table,)
        cores.append(near(keep, send))
    operand = after(both(cores[last - 1], top).astype(BF16), cores[last][1])
    firsts.append(swap(operand, 2, 4))
    operand = both(cores[last], top).astype(BF16)
    firsts[last - 1] = after(firsts[last - 1], operand)
    value = both(cores[last - 1], low) + firsts[last - 1].astype(F32)
    half, more = value[0], value[1].astype(BF16)
    firsts.append(swap(operand, 2, 4))
    seconds.append((half, after(swap(more, 4, 2), firsts[last])))
    settle(last - 1)
    crossed = []
    for k in range(regions - 1, 1, -1):
        step = k & -k
        operand = totals[k].astype(BF16)
        if k == 2:
            firsts[last] = after(firsts[last], operand)
        value = across(operand, step)
        if k == 3:
            value = after(value, more)
        if k == step:
            crossed.append(value)
        else:
            totals[k - step] = totals[k - step] + value.astype(F32)
    seconds.append(lower(cores[last], firsts[last]))
    settle(last)
    own = totals[0]
    for value in crossed + [across(totals[1], 1)]:
        own = own + value.astype(F32)

    def onward(value, d):
        pairs = [
            (p * sub + s, ((p + d) % blocks) * sub + s) for p in range(blocks) for s in range(sub)
        ]
        return lax.ppermute(value.astype(BF16), "tile", pairs)

    matrix, vector = finish(
        sub,
        own,
        *(onward(own[d * width : (d + 1) * width], d) for d in range(1, blocks // 2)),
        onward(own[blocks // 2 * width : blocks // 2 * width + width // 2], blocks // 2),
        blocks,
    )
    if sub > 1:
        part = tile % sub
        rows = width // sub
        matrix = lax.dynamic_slice(matrix, (part * rows, 0), (rows, blocks * width))
        vector = lax.dynamic_slice(vector, (0, part * rows), (1, rows))
    return matrix[None], vector


def solution(mesh):
    return jax.shard_map(
        functools.partial(local, mesh.shape["tile"]),
        mesh=mesh,
        in_specs=(
            P(("region", "tile"), None, None),
            P(("region", "tile"), None, None),
            P(("region", "tile"), None),
            P(("region", "tile"), None),
            P(("region", "tile"), None),
            P(("region", "tile")),
            P(("region", "tile"), None),
            P(),
        ),
        out_specs=(P("region", "tile", None), P("region", "tile")),
        check_vma=False,
    )
```

```python
import functools
import jax
import jax.numpy as jnp
from jax import lax
from jax.experimental import pallas as pl
from jax.experimental.pallas import tpu as pltpu
from jax.sharding import PartitionSpec as P

F32 = jnp.float32
BF16 = jnp.bfloat16
GROUP = 8
PAIR = 2 * GROUP
DEPTH = 256

NT = (((1,), (1,)), ((), ()))


def iota(shape, axis):
    return lax.broadcasted_iota(jnp.int32, shape, axis)


def fit(ld, weight, resid, counts):
    hits = weight.shape[0]
    live = iota(weight.shape, 0) < counts.astype(jnp.int32)
    masked_w = jnp.where(live, weight, 0.0)
    weighted_l = [v * masked_w for v in ld]
    gamma = [[None] * 5 for _ in range(5)]
    for a in range(5):
        for b in range(a + 1):
            gamma[a][b] = jnp.sum(weighted_l[a] * ld[b], axis=0, keepdims=True)
            if a == b:
                gamma[a][b] = gamma[a][b] + 1.0
    beta = [jnp.sum(weighted_l[a] * resid, axis=0, keepdims=True) for a in range(5)]
    factor = [[None] * 5 for _ in range(5)]
    inverse = [None] * 5
    for j in range(5):
        center = gamma[j][j]
        for k in range(j):
            center = center - factor[j][k] * factor[j][k]
        factor[j][j] = jnp.sqrt(center)
        inverse[j] = 1.0 / factor[j][j]
        for i in range(j + 1, 5):
            offdiag = gamma[i][j]
            for k in range(j):
                offdiag = offdiag - factor[i][k] * factor[j][k]
            factor[i][j] = offdiag * inverse[j]
    solved, rhs = [], []
    for j in range(5):
        current, target = weighted_l[j], beta[j]
        for k in range(j):
            current = current - factor[j][k] * solved[k]
            target = target - factor[j][k] * rhs[k]
        solved.append(current * inverse[j])
        rhs.append(target * inverse[j])
    projection = solved[0] * rhs[0]
    for k in range(1, 5):
        projection = projection + solved[k] * rhs[k]
    return solved, masked_w * resid - projection, masked_w


def prepare(
    place_ref, region_ref, count_ref, ld_ref, weight_ref, resid_ref, ids_ref, shared_ref, table_ref
):
    tracks = region_ref.shape[1]
    slots = table_ref.shape[1]
    groups = slots // GROUP
    depth = shared_ref.shape[1]
    hits = depth // GROUP
    lanes_at, column_at = groups * 5 * GROUP, groups * (5 * GROUP + 2)
    blocks = place_ref.shape[0]
    rr = table_ref.shape[0] - 8
    member = (iota((rr, tracks), 0) == region_ref[...]).astype(F32)
    before = (iota((tracks, tracks), 0) < iota((tracks, tracks), 1)).astype(F32).astype(BF16)
    rank = jnp.dot(member.astype(BF16), before, preferred_element_type=F32)
    count = jnp.sum(member, axis=1, keepdims=True)
    room = (count.astype(jnp.int32) + (PAIR - 1)) & -PAIR
    room = jnp.broadcast_to(room.astype(F32), (rr, slots))
    lower = (iota((rr, rr), 1) < iota((rr, rr), 0)).astype(F32)
    start = jnp.zeros((rr, slots), F32)
    for g in range(rr):
        start = start + lower[:, g : g + 1] * room[g : g + 1, :]
    slot = jnp.sum(member * (rank + start[:, 0:1]), axis=0, keepdims=True)
    perm = (iota((slots, tracks), 0) == slot.astype(jnp.int32)).astype(F32).astype(BF16)
    numbers = jnp.where(
        iota((8, tracks), 0) == 0, iota((8, tracks), 1), jnp.broadcast_to(count_ref[...], (8, tracks))
    )

    def sort(value):
        return lax.dot_general(value, perm, NT, preferred_element_type=F32)

    numbers = sort(numbers.astype(F32).astype(BF16))
    table_ref[0:8, :] = numbers.astype(jnp.int32)
    table_ref[8:, :] = jnp.where(
        iota((rr, slots), 1) == 0, start.astype(jnp.int32), (start + room).astype(jnp.int32)
    )
    flat = sort(ld_ref[...])
    ld = [flat[c * hits : (c + 1) * hits] for c in range(5)]
    solved, hit_factor, masked_w = fit(
        ld, sort(weight_ref[...]), sort(resid_ref[...]), numbers[1:2]
    )
    ids = sort(ids_ref[...].astype(F32).astype(BF16))
    position = jnp.zeros_like(ids)
    for b in range(blocks):
        position = jnp.where(ids == float(b), place_ref[b].astype(F32), position)
    own = (iota((depth, slots), 0) // hits) == (iota((depth, slots), 1) % GROUP)

    def spread_out(value):
        return jnp.where(own, jnp.concatenate([value] * GROUP, axis=0), 0.0)

    grouping = (iota((groups, slots), 1) // GROUP == iota((groups, slots), 0)).astype(F32)
    for n, value in enumerate((masked_w, hit_factor)):
        shared_ref[lanes_at + n * groups : lanes_at + (n + 1) * groups, :] = lax.dot_general(
            grouping.astype(BF16), spread_out(value).astype(BF16), NT, preferred_element_type=F32
        )
    columns = 128
    grouping = (iota((columns, slots), 1) // GROUP == iota((columns, slots), 0)).astype(F32)
    shared_ref[column_at : column_at + depth, :columns] = lax.dot_general(
        spread_out(position).astype(BF16), grouping.astype(BF16), NT, preferred_element_type=F32
    )
    for c in range(5):
        value = spread_out(solved[c]).T
        for g in range(groups):
            at = (g * 5 + c) * GROUP
            shared_ref[at : at + GROUP, :] = value[g * GROUP : (g + 1) * GROUP, :]


def one_step(step, at, table_ref, shared_ref, g_ref, g_s, direct_s, spread_s):
    hits, width = g_ref.shape[1:]
    depth = GROUP * hits
    blocks = spread_s.shape[1] // width
    rows = 5 * GROUP
    head = width + 8
    groups = table_ref.shape[1] // GROUP
    lanes_at, column_at = groups * rows, groups * (rows + 2)
    column = shared_ref[column_at : column_at + depth, :128]
    unit = (iota((width, width), 0) == iota((width, width), 1)).astype(F32).astype(BF16)
    lefts, values, positions = [], [], []
    for u in range(2):
        group = step * 2 + u
        for i in range(GROUP):
            g_s[u, i * hits : (i + 1) * hits, :] = g_ref[table_ref[0, group * GROUP + i]]
        g = g_s[u]
        chosen = jnp.full(column.shape, group, jnp.int32)
        position = jnp.take_along_axis(column, chosen, axis=1, mode="promise_in_bounds")
        turned = lax.dot_general(unit, g, NT, preferred_element_type=F32)
        weighted = turned * shared_ref[pl.ds(lanes_at + group, 1), :]
        factor = jnp.where(iota((8, depth), 0) == 0, shared_ref[pl.ds(lanes_at + groups + group, 1), :], 0.0)
        scaled = shared_ref[pl.ds(pl.multiple_of(group * rows, GROUP), rows), :]
        high = scaled.astype(BF16).astype(F32)
        left = jnp.concatenate(
            [weighted, factor, high, scaled - high, jnp.zeros((8, depth), F32)], axis=0
        )
        lefts.append(left.astype(BF16))
        values.append(g)
        positions.append(position.astype(BF16))
    for p in range(0, blocks, 2):
        columns = slice(p * width, (p + 2) * width)
        direct = direct_s[:, columns]
        for u in range(2):
            right = jnp.concatenate(
                [
                    jnp.where(positions[u] == jnp.bfloat16(q), values[u], jnp.bfloat16(0))
                    for q in (p, p + 1)
                ],
                axis=1,
            )
            total = jnp.dot(lefts[u], right, preferred_element_type=F32)
            direct = direct + total[:head]
            spread_s[pl.ds(pl.multiple_of(at + u * rows, GROUP), rows), columns] = (
                total[head : head + rows] + total[head + rows : head + 2 * rows]
            )
        direct_s[:, columns] = direct


EVEN = (0, 4, 2, 6)
ODD = (0, 2, 4, 6)


def lead_kernel(ks, sub, *refs):
    small, g_hbm, (keep_ref, send_ref, shared_ref, table_ref) = refs[:7], refs[7], refs[8:12]
    local_small, g_ref, table_s, sems, scratch = refs[12:19], refs[19], refs[20], refs[21], refs[22:]
    copies = [
        pltpu.make_async_copy(source, target, sems.at[n])
        for n, (source, target) in enumerate([*zip(small, local_small), (g_hbm, g_ref)])
    ]
    for copy in copies:
        copy.start()
    for copy in copies[:-1]:
        copy.wait()
    prepare(*local_small, shared_ref, table_ref)
    copy = pltpu.make_async_copy(table_ref, table_s, sems.at[0])
    copy.start()
    copy.wait()
    copies[-1].wait()

    def region(n, carry):
        assemble_region(
            n, ks, sub, table_s, shared_ref, g_ref, keep_ref, send_ref, *scratch
        )
        return carry

    lax.fori_loop(0, len(ks), region, 0)


def follow_kernel(ks, sub, shared_ref, table_ref, g_ref, *refs):
    def region(n, carry):
        assemble_region(n, ks, sub, table_ref, shared_ref, g_ref, *refs)
        return carry

    if len(ks) == 1:
        region(0, 0)
    else:
        lax.fori_loop(0, len(ks), region, 0)


def assemble_region(
    number, ks, sub, table_ref, shared_ref, g_ref,
    keep_ref, send_ref, g_s, direct_s, spread_s, wide_s, turned_s, acc_s,
):
    k = jnp.where(number == 0, ks[0], ks[-1])
    width = g_ref.shape[2]
    blocks = spread_s.shape[1] // width
    many = blocks // 2
    region = lax.axis_index("region") ^ k
    block = lax.axis_index("tile") // sub
    first = table_ref[8 + region, 0] // PAIR
    steps = table_ref[8 + region, 1] // PAIR - first
    direct_s[...] = jnp.zeros_like(direct_s)

    def group_step(n, carry):
        one_step(
            first + n, n * (10 * GROUP), table_ref, shared_ref, g_ref, g_s, direct_s, spread_s
        )
        return carry

    lax.fori_loop(0, steps, group_step, 0)
    used = steps * 10
    depth_tiles = DEPTH // 8
    chunks = jnp.maximum((used + depth_tiles - 1) // depth_tiles, 1)

    def clear(tile, carry):
        spread_s[pl.ds(pl.multiple_of(tile * 8, 8), 8), :] = jnp.zeros((8, blocks * width), F32)
        return carry

    lax.fori_loop(used, chunks * depth_tiles, clear, 0)

    unit = (iota((width, width), 0) == iota((width, width), 1)).astype(F32).astype(BF16)

    def chunk_step(chunk, carry):
        at = pl.multiple_of(chunk * DEPTH, DEPTH)
        wide_s[...] = spread_s[pl.ds(at, DEPTH), :].astype(BF16)
        for p in range(blocks):
            turned = lax.dot_general(
                unit, wide_s[:, p * width : (p + 1) * width], NT, preferred_element_type=F32
            )
            turned = (0.0 - turned).astype(BF16)
            turned_s[p * width : (p + 1) * width] = turned
            if p < many:
                turned_s[(blocks + p) * width : (blocks + p + 1) * width] = turned

        def products(add):
            for q in range(0, blocks, 2):
                reach = many if q >= many else many - 1
                upper = (q + blocks - reach) % blocks
                value = jnp.dot(
                    turned_s[upper * width : (upper + reach + 2) * width],
                    wide_s[:, q * width : (q + 2) * width],
                    preferred_element_type=F32,
                )
                for r in range(reach + 2):
                    p = (upper + r) % blocks
                    for c in range(2):
                        d = reach - r + c
                        if 0 <= d <= many and (d < many or p < many):
                            part = value[r * width : (r + 1) * width, c * width : (c + 1) * width]
                            columns = slice(d * width, (d + 1) * width)
                            acc_s[p, :, columns] = acc_s[p, :, columns] + part if add else part

        @pl.when(chunk == 0)
        def _():
            products(False)

        @pl.when(chunk > 0)
        def _():
            products(True)

        return carry

    lax.fori_loop(0, chunks, chunk_step, 0)
    half = width // 2
    for n in range(blocks // 2):
        for odd, out_ref in ((0, keep_ref), (1, send_ref)):
            p = block ^ (jnp.where(block % 2 == 1 - odd, ODD[n], EVEN[n]) + odd)
            columns = pl.ds(pl.multiple_of(p * width, width), width)
            parts = [direct_s[0:width, columns] + acc_s[p, :, 0:width]]
            parts += [acc_s[p, :, d * width : (d + 1) * width] for d in range(1, many)]
            upper = pl.multiple_of((p // many) * half, half)
            parts.append(acc_s[p % many, pl.ds(upper, half), many * width :])
            row = direct_s[width : width + 1, columns]
            high = row.astype(BF16).astype(F32)
            sub = iota((16, width), 0)
            parts.append(jnp.where(sub == 0, high, jnp.where(sub == 1, row - high, 0.0)))
            out_ref[n, number] = jnp.concatenate(parts, axis=0).astype(BF16)


def assemble(ks, sub, inputs, g, blocks, regions):
    tracks, hits, width = g.shape
    lead = len(inputs) == 7
    rows = width * (blocks // 2) + width // 2 + 16
    longest = -(-(-(-tracks // PAIR) * 5 * PAIR) // DEPTH) * DEPTH
    rr = -(-regions // 8) * 8
    slots = -(-(tracks + regions * (PAIR - 1)) // 128) * 128
    shared = [
        jax.ShapeDtypeStruct((slots // GROUP * (5 * GROUP + 2) + GROUP * hits, GROUP * hits), F32),
        jax.ShapeDtypeStruct((8 + rr, slots), jnp.int32),
    ]
    out = jax.ShapeDtypeStruct((blocks // 2, len(ks), rows, width), BF16)
    vmem = pl.BlockSpec(memory_space=pltpu.VMEM)
    smem = pl.BlockSpec(memory_space=pltpu.SMEM)
    copies = [pltpu.SMEM(inputs[0].shape, jnp.int32)]
    copies += [pltpu.VMEM(value.shape, value.dtype) for value in inputs[1:]]
    copies += [
        pltpu.VMEM(g.shape, g.dtype),
        pltpu.SMEM(shared[1].shape, jnp.int32),
        pltpu.SemaphoreType.DMA((8,)),
    ]
    return pl.pallas_call(
        functools.partial(lead_kernel if lead else follow_kernel, ks, sub),
        in_specs=[pl.BlockSpec(memory_space=pltpu.HBM)] * 8 if lead else [vmem, smem, vmem],
        out_specs=[vmem] * (4 if lead else 2),
        out_shape=[out, out] + shared * lead,
        scratch_shapes=copies * lead
        + [
            pltpu.VMEM((2, GROUP * hits, width), BF16),
            pltpu.VMEM((width + 8, blocks * width), F32),
            pltpu.VMEM((longest, blocks * width), F32),
            pltpu.VMEM((DEPTH, blocks * width), BF16),
            pltpu.VMEM(((blocks + blocks // 2) * width, DEPTH), BF16),
            pltpu.VMEM((blocks, width, (blocks // 2 + 1) * width), F32),
        ],
        compiler_params=pltpu.CompilerParams(vmem_limit_bytes=(60 if lead else 28) * 1024 * 1024),
        cost_estimate=pl.CostEstimate(
            flops=10**9 * len(ks), bytes_accessed=4 * 10**6, transcendentals=0
        ),
        name="assemble",
    )(*inputs, g)


def finish_kernel(sub, own_ref, r1_ref, r2_ref, r3_ref, e_ref, out_ref, vec_ref):
    width = own_ref.shape[1]
    p = lax.axis_index("tile") // sub
    blocks = out_ref.shape[1] // width
    many = blocks // 2

    def put(column, value):
        column = pl.multiple_of(((column + blocks) % blocks) * width, width)
        out_ref[:, pl.ds(column, width)] = value

    for d in range(many):
        put(p + d, own_ref[d * width : (d + 1) * width, :])
    for d, ref in ((1, r1_ref), (2, r2_ref), (3, r3_ref)):
        put(p - d, ref[...].astype(F32).T)
    tail = many * width + width // 2
    mine = own_ref[many * width : tail, :]
    other = e_ref[...].astype(F32)

    @pl.when(p < many)
    def _():
        put(p + many, jnp.concatenate([mine, other], axis=0))

    @pl.when(p >= many)
    def _():
        put(p + many, jnp.concatenate([other, mine], axis=0).T)

    vec_ref[...] = own_ref[tail : tail + 1, :] + own_ref[tail + 1 : tail + 2, :]


def finish(sub, own, r1, r2, r3, ext, blocks):
    width = own.shape[1]
    vmem = pl.BlockSpec(memory_space=pltpu.VMEM)
    return pl.pallas_call(
        functools.partial(finish_kernel, sub),
        in_specs=[vmem] * 5,
        out_specs=[vmem, vmem],
        out_shape=[
            jax.ShapeDtypeStruct((width, blocks * width), F32),
            jax.ShapeDtypeStruct((1, width), F32),
        ],
        compiler_params=pltpu.CompilerParams(vmem_limit_bytes=8 * 1024 * 1024),
        name="finish",
    )(own, r1, r2, r3, ext)


def local(
    tiles, global_deriv, local_deriv, hit_weight, hit_resid, block_ids, hit_count, track_region,
    block_place,
):
    regions = lax.axis_size("region")
    tracks, hits, width = global_deriv.shape
    blocks = block_place.shape[0]
    sub = tiles // blocks
    tile = lax.axis_index("tile")
    inputs = (
        block_place,
        track_region.reshape(1, tracks),
        hit_count.reshape(1, tracks),
        local_deriv.transpose(1, 2, 0).reshape(-1, tracks),
        hit_weight.T,
        hit_resid.T,
        block_ids.T,
    )

    def swap(value, even, odd):
        pairs = [(t, t ^ (sub * (odd if t // sub % 2 else even))) for t in range(tiles)]
        return lax.ppermute(value, "tile", pairs)

    def across(value, k):
        return lax.ppermute(value.astype(BF16), "region", [(r, r ^ k) for r in range(regions)])

    def near(keep, send):
        bit = 1
        while bit < sub:
            pairs = [(t, t ^ bit) for t in range(tiles)]
            keep, send = (v + lax.ppermute(v, "tile", pairs) for v in (keep, send))
            bit *= 2
        return keep, swap(send, 1, 1)

    def both(pair, part):
        return pair[0][part].astype(F32) + pair[1][part].astype(F32)

    low, top = slice(0, blocks // 4), slice(blocks // 4, blocks // 2)
    def upper(pair):
        return swap(both(pair, top).astype(BF16), 2, 4)

    def lower(pair, more):
        value = both(pair, low) + more.astype(F32)
        return value[0], swap(value[1].astype(BF16), 4, 2)

    groups = [(k + 1, k) for k in range(regions - 2, 0, -2)] + [(1,), (0,)]
    totals, cores, firsts, seconds = [None] * regions, [], [], []

    def after(value, other):
        return lax.optimization_barrier((value, other))[0]

    def settle(n):
        value = seconds[n][0] + seconds[n][1].astype(F32)
        for place, k in enumerate(groups[n]):
            totals[k] = value[place]

    last = len(groups) - 1
    for n, ks in enumerate(groups):
        keep, send, *made = assemble(ks, sub, inputs, global_deriv, blocks, regions)
        if n == 0:
            cores.append(near(keep, send))
            operand = both(cores[0], top).astype(BF16)
            inputs = made[0], after(made[1], operand)
            firsts.append(swap(operand, 2, 4))
            continue
        if n > 1:
            cores[n - 1] = after(cores[n - 1], send)
            firsts[n - 2] = after(firsts[n - 2], send)
            send = after(send, cores[n - 1][1])
            seconds.append(lower(cores[n - 2], firsts[n - 2]))
            settle(n - 2)
        if 1 < n < last:
            firsts.append(swap(both(cores[n - 1], top).astype(BF16), 2, 4))
        inputs = inputs[0], after(inputs[1], send)
        cores.append(near(keep, send))
    cores[last] = after(cores[last], seconds[-1][1])
    operand = after(both(cores[last - 1], top).astype(BF16), cores[last][1])
    firsts.append(swap(operand, 2, 4))
    operand = both(cores[last], top).astype(BF16)
    firsts[last - 1] = after(firsts[last - 1], operand)
    value = both(cores[last - 1], low) + firsts[last - 1].astype(F32)
    half, more = value[0], value[1].astype(BF16)
    firsts.append(swap(operand, 2, 4))
    seconds.append((half, after(swap(more, 4, 2), firsts[last])))
    settle(last - 1)
    crossed = []
    for k in range(regions - 1, 1, -1):
        step = k & -k
        operand = totals[k].astype(BF16)
        if k == 2:
            firsts[last] = after(firsts[last], operand)
        value = across(operand, step)
        if k == 3:
            value = after(value, more)
        if k == step:
            crossed.append(value)
        else:
            totals[k - step] = totals[k - step] + value.astype(F32)
    seconds.append(lower(cores[last], firsts[last]))
    settle(last)
    own = totals[0]
    for value in crossed + [across(totals[1], 1)]:
        own = own + value.astype(F32)

    def onward(value, d):
        pairs = [
            (p * sub + s, ((p + d) % blocks) * sub + s) for p in range(blocks) for s in range(sub)
        ]
        return lax.ppermute(value.astype(BF16), "tile", pairs)

    matrix, vector = finish(
        sub,
        own,
        *(onward(own[d * width : (d + 1) * width], d) for d in range(1, blocks // 2)),
        onward(own[blocks // 2 * width : blocks // 2 * width + width // 2], blocks // 2),
        blocks,
    )
    if sub > 1:
        part = tile % sub
        rows = width // sub
        matrix = lax.dynamic_slice(matrix, (part * rows, 0), (rows, blocks * width))
        vector = lax.dynamic_slice(vector, (0, part * rows), (1, rows))
    return matrix[None], vector


def solution(mesh):
    return jax.shard_map(
        functools.partial(local, mesh.shape["tile"]),
        mesh=mesh,
        in_specs=(
            P(("region", "tile"), None, None),
            P(("region", "tile"), None, None),
            P(("region", "tile"), None),
            P(("region", "tile"), None),
            P(("region", "tile"), None),
            P(("region", "tile")),
            P(("region", "tile"), None),
            P(),
        ),
        out_specs=(P("region", "tile", None), P("region", "tile")),
        check_vma=False,
    )
```

```python
import functools
import jax
import jax.numpy as jnp
from jax import lax
from jax.experimental import pallas as pl
from jax.experimental.pallas import tpu as pltpu
from jax.sharding import PartitionSpec as P

F32 = jnp.float32
BF16 = jnp.bfloat16
GROUP = 8
PAIR = 2 * GROUP
DEPTH = 256

NT = (((1,), (1,)), ((), ()))


def iota(shape, axis):
    return lax.broadcasted_iota(jnp.int32, shape, axis)


def fit(ld, weight, resid, counts):
    hits = weight.shape[0]
    live = iota(weight.shape, 0) < counts.astype(jnp.int32)
    masked_w = jnp.where(live, weight, 0.0)
    weighted_l = [v * masked_w for v in ld]
    gamma = [[None] * 5 for _ in range(5)]
    for a in range(5):
        for b in range(a + 1):
            gamma[a][b] = jnp.sum(weighted_l[a] * ld[b], axis=0, keepdims=True)
            if a == b:
                gamma[a][b] = gamma[a][b] + 1.0
    beta = [jnp.sum(weighted_l[a] * resid, axis=0, keepdims=True) for a in range(5)]
    factor = [[None] * 5 for _ in range(5)]
    inverse = [None] * 5
    for j in range(5):
        center = gamma[j][j]
        for k in range(j):
            center = center - factor[j][k] * factor[j][k]
        factor[j][j] = jnp.sqrt(center)
        inverse[j] = 1.0 / factor[j][j]
        for i in range(j + 1, 5):
            offdiag = gamma[i][j]
            for k in range(j):
                offdiag = offdiag - factor[i][k] * factor[j][k]
            factor[i][j] = offdiag * inverse[j]
    solved, rhs = [], []
    for j in range(5):
        current, target = weighted_l[j], beta[j]
        for k in range(j):
            current = current - factor[j][k] * solved[k]
            target = target - factor[j][k] * rhs[k]
        solved.append(current * inverse[j])
        rhs.append(target * inverse[j])
    projection = solved[0] * rhs[0]
    for k in range(1, 5):
        projection = projection + solved[k] * rhs[k]
    return solved, masked_w * resid - projection, masked_w


def prepare(
    place_ref, region_ref, count_ref, ld_ref, weight_ref, resid_ref, ids_ref, shared_ref, table_ref
):
    tracks = region_ref.shape[1]
    slots = table_ref.shape[1]
    groups = slots // GROUP
    depth = shared_ref.shape[1]
    hits = depth // GROUP
    lanes_at, column_at = groups * 5 * GROUP, groups * (5 * GROUP + 2)
    blocks = place_ref.shape[0]
    rr = table_ref.shape[0] - 8
    member = (iota((rr, tracks), 0) == region_ref[...]).astype(F32)
    before = (iota((tracks, tracks), 0) < iota((tracks, tracks), 1)).astype(F32).astype(BF16)
    rank = jnp.dot(member.astype(BF16), before, preferred_element_type=F32)
    count = jnp.sum(member, axis=1, keepdims=True)
    room = (count.astype(jnp.int32) + (PAIR - 1)) & -PAIR
    room = jnp.broadcast_to(room.astype(F32), (rr, slots))
    lower = (iota((rr, rr), 1) < iota((rr, rr), 0)).astype(F32)
    start = jnp.zeros((rr, slots), F32)
    for g in range(rr):
        start = start + lower[:, g : g + 1] * room[g : g + 1, :]
    slot = jnp.sum(member * (rank + start[:, 0:1]), axis=0, keepdims=True)
    perm = (iota((slots, tracks), 0) == slot.astype(jnp.int32)).astype(F32).astype(BF16)
    numbers = jnp.where(
        iota((8, tracks), 0) == 0, iota((8, tracks), 1), jnp.broadcast_to(count_ref[...], (8, tracks))
    )

    def sort(value):
        return lax.dot_general(value, perm, NT, preferred_element_type=F32)

    numbers = sort(numbers.astype(F32).astype(BF16))
    table_ref[0:8, :] = numbers.astype(jnp.int32)
    table_ref[8:, :] = jnp.where(
        iota((rr, slots), 1) == 0, start.astype(jnp.int32), (start + room).astype(jnp.int32)
    )
    flat = sort(ld_ref[...])
    ld = [flat[c * hits : (c + 1) * hits] for c in range(5)]
    solved, hit_factor, masked_w = fit(
        ld, sort(weight_ref[...]), sort(resid_ref[...]), numbers[1:2]
    )
    ids = sort(ids_ref[...].astype(F32).astype(BF16))
    position = jnp.zeros_like(ids)
    for b in range(blocks):
        position = jnp.where(ids == float(b), place_ref[b].astype(F32), position)
    own = (iota((depth, slots), 0) // hits) == (iota((depth, slots), 1) % GROUP)

    def spread_out(value):
        return jnp.where(own, jnp.concatenate([value] * GROUP, axis=0), 0.0)

    grouping = (iota((groups, slots), 1) // GROUP == iota((groups, slots), 0)).astype(F32)
    for n, value in enumerate((masked_w, hit_factor)):
        shared_ref[lanes_at + n * groups : lanes_at + (n + 1) * groups, :] = lax.dot_general(
            grouping.astype(BF16), spread_out(value).astype(BF16), NT, preferred_element_type=F32
        )
    columns = 128
    grouping = (iota((columns, slots), 1) // GROUP == iota((columns, slots), 0)).astype(F32)
    shared_ref[column_at : column_at + depth, :columns] = lax.dot_general(
        spread_out(position).astype(BF16), grouping.astype(BF16), NT, preferred_element_type=F32
    )
    for c in range(5):
        value = spread_out(solved[c]).T
        for g in range(groups):
            at = (g * 5 + c) * GROUP
            shared_ref[at : at + GROUP, :] = value[g * GROUP : (g + 1) * GROUP, :]


def one_step(step, at, table_ref, shared_ref, g_ref, g_s, direct_s, spread_s):
    hits, width = g_ref.shape[1:]
    depth = GROUP * hits
    blocks = spread_s.shape[1] // width
    rows = 5 * GROUP
    head = width + 8
    groups = table_ref.shape[1] // GROUP
    lanes_at, column_at = groups * rows, groups * (rows + 2)
    column = shared_ref[column_at : column_at + depth, :128]
    lefts, values, positions = [], [], []
    for u in range(2):
        group = step * 2 + u
        for i in range(GROUP):
            g_s[u, i * hits : (i + 1) * hits, :] = g_ref[table_ref[0, group * GROUP + i]]
        g = g_s[u]
        chosen = jnp.full(column.shape, group, jnp.int32)
        position = jnp.take_along_axis(column, chosen, axis=1, mode="promise_in_bounds")
        turned = g.T.astype(F32)
        weighted = turned * shared_ref[pl.ds(lanes_at + group, 1), :]
        factor = jnp.where(iota((8, depth), 0) == 0, shared_ref[pl.ds(lanes_at + groups + group, 1), :], 0.0)
        scaled = shared_ref[pl.ds(pl.multiple_of(group * rows, GROUP), rows), :]
        high = scaled.astype(BF16).astype(F32)
        left = jnp.concatenate(
            [weighted, factor, high, scaled - high, jnp.zeros((8, depth), F32)], axis=0
        )
        lefts.append(left.astype(BF16))
        values.append(g)
        positions.append(position.astype(BF16))
    for p in range(0, blocks, 2):
        columns = slice(p * width, (p + 2) * width)
        direct = direct_s[:, columns]
        for u in range(2):
            right = jnp.concatenate(
                [
                    jnp.where(positions[u] == jnp.bfloat16(q), values[u], jnp.bfloat16(0))
                    for q in (p, p + 1)
                ],
                axis=1,
            )
            total = jnp.dot(lefts[u], right, preferred_element_type=F32)
            direct = direct + total[:head]
            spread_s[pl.ds(pl.multiple_of(at + u * rows, GROUP), rows), columns] = (
                total[head : head + rows] + total[head + rows : head + 2 * rows]
            )
        direct_s[:, columns] = direct


EVEN = (0, 4, 2, 6)
ODD = (0, 2, 4, 6)


def lead_kernel(ks, sub, *refs):
    small, g_hbm, (keep_ref, send_ref, shared_ref, table_ref) = refs[:7], refs[7], refs[8:12]
    local_small, g_ref, table_s, sems, scratch = refs[12:19], refs[19], refs[20], refs[21], refs[22:]
    copies = [
        pltpu.make_async_copy(source, target, sems.at[n])
        for n, (source, target) in enumerate([*zip(small, local_small), (g_hbm, g_ref)])
    ]
    for copy in copies:
        copy.start()
    for copy in copies[:-1]:
        copy.wait()
    prepare(*local_small, shared_ref, table_ref)
    copy = pltpu.make_async_copy(table_ref, table_s, sems.at[0])
    copy.start()
    copy.wait()
    copies[-1].wait()

    def region(n, carry):
        assemble_region(
            n, ks, sub, table_s, shared_ref, g_ref, keep_ref, send_ref, *scratch
        )
        return carry

    lax.fori_loop(0, len(ks), region, 0)


def follow_kernel(ks, sub, shared_ref, table_ref, g_ref, *refs):
    def region(n, carry):
        assemble_region(n, ks, sub, table_ref, shared_ref, g_ref, *refs)
        return carry

    if len(ks) == 1:
        region(0, 0)
    else:
        lax.fori_loop(0, len(ks), region, 0)


def assemble_region(
    number, ks, sub, table_ref, shared_ref, g_ref,
    keep_ref, send_ref, g_s, direct_s, spread_s, wide_s, turned_s, acc_s,
):
    k = jnp.where(number == 0, ks[0], ks[-1])
    width = g_ref.shape[2]
    blocks = spread_s.shape[1] // width
    many = blocks // 2
    region = lax.axis_index("region") ^ k
    block = lax.axis_index("tile") // sub
    first = table_ref[8 + region, 0] // PAIR
    steps = table_ref[8 + region, 1] // PAIR - first
    direct_s[...] = jnp.zeros_like(direct_s)

    def group_step(n, carry):
        one_step(
            first + n, n * (10 * GROUP), table_ref, shared_ref, g_ref, g_s, direct_s, spread_s
        )
        return carry

    lax.fori_loop(0, steps, group_step, 0)
    used = steps * 10
    depth_tiles = DEPTH // 8
    chunks = jnp.maximum((used + depth_tiles - 1) // depth_tiles, 1)

    def clear(tile, carry):
        spread_s[pl.ds(pl.multiple_of(tile * 8, 8), 8), :] = jnp.zeros((8, blocks * width), F32)
        return carry

    lax.fori_loop(used, chunks * depth_tiles, clear, 0)

    unit = (iota((width, width), 0) == iota((width, width), 1)).astype(F32).astype(BF16)

    def chunk_step(chunk, carry):
        at = pl.multiple_of(chunk * DEPTH, DEPTH)
        wide_s[...] = spread_s[pl.ds(at, DEPTH), :].astype(BF16)
        for p in range(blocks):
            turned = lax.dot_general(
                unit, wide_s[:, p * width : (p + 1) * width], NT, preferred_element_type=F32
            )
            turned = (0.0 - turned).astype(BF16)
            turned_s[p * width : (p + 1) * width] = turned
            if p < many:
                turned_s[(blocks + p) * width : (blocks + p + 1) * width] = turned

        def products(add):
            for q in range(0, blocks, 2):
                reach = many if q >= many else many - 1
                upper = (q + blocks - reach) % blocks
                value = jnp.dot(
                    turned_s[upper * width : (upper + reach + 2) * width],
                    wide_s[:, q * width : (q + 2) * width],
                    preferred_element_type=F32,
                )
                for r in range(reach + 2):
                    p = (upper + r) % blocks
                    for c in range(2):
                        d = reach - r + c
                        if 0 <= d <= many and (d < many or p < many):
                            part = value[r * width : (r + 1) * width, c * width : (c + 1) * width]
                            columns = slice(d * width, (d + 1) * width)
                            acc_s[p, :, columns] = acc_s[p, :, columns] + part if add else part

        @pl.when(chunk == 0)
        def _():
            products(False)

        @pl.when(chunk > 0)
        def _():
            products(True)

        return carry

    lax.fori_loop(0, chunks, chunk_step, 0)
    half = width // 2
    for n in range(blocks // 2):
        for odd, out_ref in ((0, keep_ref), (1, send_ref)):
            p = block ^ (jnp.where(block % 2 == 1 - odd, ODD[n], EVEN[n]) + odd)
            columns = pl.ds(pl.multiple_of(p * width, width), width)
            parts = [direct_s[0:width, columns] + acc_s[p, :, 0:width]]
            parts += [acc_s[p, :, d * width : (d + 1) * width] for d in range(1, many)]
            upper = pl.multiple_of((p // many) * half, half)
            parts.append(acc_s[p % many, pl.ds(upper, half), many * width :])
            row = direct_s[width : width + 1, columns]
            high = row.astype(BF16).astype(F32)
            sub = iota((16, width), 0)
            parts.append(jnp.where(sub == 0, high, jnp.where(sub == 1, row - high, 0.0)))
            out_ref[n, number] = jnp.concatenate(parts, axis=0).astype(BF16)


def assemble(ks, sub, inputs, g, blocks, regions):
    tracks, hits, width = g.shape
    lead = len(inputs) == 7
    rows = width * (blocks // 2) + width // 2 + 16
    longest = -(-(-(-tracks // PAIR) * 5 * PAIR) // DEPTH) * DEPTH
    rr = -(-regions // 8) * 8
    slots = -(-(tracks + regions * (PAIR - 1)) // 128) * 128
    shared = [
        jax.ShapeDtypeStruct((slots // GROUP * (5 * GROUP + 2) + GROUP * hits, GROUP * hits), F32),
        jax.ShapeDtypeStruct((8 + rr, slots), jnp.int32),
    ]
    out = jax.ShapeDtypeStruct((blocks // 2, len(ks), rows, width), BF16)
    vmem = pl.BlockSpec(memory_space=pltpu.VMEM)
    smem = pl.BlockSpec(memory_space=pltpu.SMEM)
    copies = [pltpu.SMEM(inputs[0].shape, jnp.int32)]
    copies += [pltpu.VMEM(value.shape, value.dtype) for value in inputs[1:]]
    copies += [
        pltpu.VMEM(g.shape, g.dtype),
        pltpu.SMEM(shared[1].shape, jnp.int32),
        pltpu.SemaphoreType.DMA((8,)),
    ]
    return pl.pallas_call(
        functools.partial(lead_kernel if lead else follow_kernel, ks, sub),
        in_specs=[pl.BlockSpec(memory_space=pltpu.HBM)] * 8 if lead else [vmem, smem, vmem],
        out_specs=[vmem] * (4 if lead else 2),
        out_shape=[out, out] + shared * lead,
        scratch_shapes=copies * lead
        + [
            pltpu.VMEM((2, GROUP * hits, width), BF16),
            pltpu.VMEM((width + 8, blocks * width), F32),
            pltpu.VMEM((longest, blocks * width), F32),
            pltpu.VMEM((DEPTH, blocks * width), BF16),
            pltpu.VMEM(((blocks + blocks // 2) * width, DEPTH), BF16),
            pltpu.VMEM((blocks, width, (blocks // 2 + 1) * width), F32),
        ],
        compiler_params=pltpu.CompilerParams(vmem_limit_bytes=(60 if lead else 28) * 1024 * 1024),
        cost_estimate=pl.CostEstimate(
            flops=10**9 * len(ks), bytes_accessed=4 * 10**6, transcendentals=0
        ),
        name="assemble",
    )(*inputs, g)


def finish_kernel(sub, own_ref, r1_ref, r2_ref, r3_ref, e_ref, out_ref, vec_ref):
    width = own_ref.shape[1]
    p = lax.axis_index("tile") // sub
    blocks = out_ref.shape[1] // width
    many = blocks // 2

    def put(column, value):
        column = pl.multiple_of(((column + blocks) % blocks) * width, width)
        out_ref[:, pl.ds(column, width)] = value

    for d in range(many):
        put(p + d, own_ref[d * width : (d + 1) * width, :])
    for d, ref in ((1, r1_ref), (2, r2_ref), (3, r3_ref)):
        put(p - d, ref[...].astype(F32).T)
    tail = many * width + width // 2
    mine = own_ref[many * width : tail, :]
    other = e_ref[...].astype(F32)

    @pl.when(p < many)
    def _():
        put(p + many, jnp.concatenate([mine, other], axis=0))

    @pl.when(p >= many)
    def _():
        put(p + many, jnp.concatenate([other, mine], axis=0).T)

    vec_ref[...] = own_ref[tail : tail + 1, :] + own_ref[tail + 1 : tail + 2, :]


def finish(sub, own, r1, r2, r3, ext, blocks):
    width = own.shape[1]
    vmem = pl.BlockSpec(memory_space=pltpu.VMEM)
    return pl.pallas_call(
        functools.partial(finish_kernel, sub),
        in_specs=[vmem] * 5,
        out_specs=[vmem, vmem],
        out_shape=[
            jax.ShapeDtypeStruct((width, blocks * width), F32),
            jax.ShapeDtypeStruct((1, width), F32),
        ],
        compiler_params=pltpu.CompilerParams(vmem_limit_bytes=8 * 1024 * 1024),
        name="finish",
    )(own, r1, r2, r3, ext)


def local(
    tiles, global_deriv, local_deriv, hit_weight, hit_resid, block_ids, hit_count, track_region,
    block_place,
):
    regions = lax.axis_size("region")
    tracks, hits, width = global_deriv.shape
    blocks = block_place.shape[0]
    sub = tiles // blocks
    tile = lax.axis_index("tile")
    inputs = (
        block_place,
        track_region.reshape(1, tracks),
        hit_count.reshape(1, tracks),
        local_deriv.transpose(1, 2, 0).reshape(-1, tracks),
        hit_weight.T,
        hit_resid.T,
        block_ids.T,
    )

    def swap(value, even, odd):
        pairs = [(t, t ^ (sub * (odd if t // sub % 2 else even))) for t in range(tiles)]
        return lax.ppermute(value, "tile", pairs)

    def across(value, k):
        return lax.ppermute(value.astype(BF16), "region", [(r, r ^ k) for r in range(regions)])

    def near(keep, send):
        bit = 1
        while bit < sub:
            pairs = [(t, t ^ bit) for t in range(tiles)]
            keep, send = (v + lax.ppermute(v, "tile", pairs) for v in (keep, send))
            bit *= 2
        return keep, swap(send, 1, 1)

    def both(pair, part):
        return pair[0][part].astype(F32) + pair[1][part].astype(F32)

    low, top = slice(0, blocks // 4), slice(blocks // 4, blocks // 2)
    def upper(pair):
        return swap(both(pair, top).astype(BF16), 2, 4)

    def lower(pair, more):
        value = both(pair, low) + more.astype(F32)
        return value[0], swap(value[1].astype(BF16), 4, 2)

    groups = [(k + 1, k) for k in range(regions - 2, 0, -2)] + [(1,), (0,)]
    def after(value, other):
        return lax.optimization_barrier((value, other))[0]

    last = len(groups) - 1
    totals = [None] * regions
    cores, firsts, seconds = ([None] * (last + 1) for _ in range(3))

    def settle(n):
        value = seconds[n][0] + seconds[n][1].astype(F32)
        for place, k in enumerate(groups[n]):
            totals[k] = value[place]

    for n, ks in enumerate(groups):
        keep, send, *made = assemble(ks, sub, inputs, global_deriv, blocks, regions)
        if n == 0:
            cores[0] = near(keep, send)
            operand = both(cores[0], top).astype(BF16)
            inputs = made[0], after(made[1], operand)
            firsts[0] = swap(operand, 2, 4)
        elif n < last - 1:
            inputs = inputs[0], after(inputs[1], send)
            cores[n] = near(keep, send)
            firsts[n] = swap(both(cores[n], top).astype(BF16), 2, 4)
            seconds[n] = lower(cores[n], firsts[n])
            settle(n)
        elif n < last:
            firsts[0] = after(firsts[0], send)
            value = both(cores[0], low) + firsts[0].astype(F32)
            operand = value[1].astype(BF16)
            inputs = inputs[0], after(inputs[1], (send, operand))
            seconds[0] = value[0], swap(operand, 4, 2)
            cores[n] = near(keep, send)
        else:
            cores[n - 1] = after(cores[n - 1], send)
            send = after(send, cores[n - 1][1])
            cores[n] = near(keep, send)
            seconds[0] = seconds[0][0], after(seconds[0][1], send)
            settle(0)
    firsts[last - 1] = upper(cores[last - 1])
    operand = both(cores[last], top).astype(BF16)
    firsts[last - 1] = after(firsts[last - 1], operand)
    value = both(cores[last - 1], low) + firsts[last - 1].astype(F32)
    half, more = value[0], value[1].astype(BF16)
    firsts[last] = swap(operand, 2, 4)
    seconds[last - 1] = half, after(swap(more, 4, 2), firsts[last])
    settle(last - 1)
    crossed = []
    for k in range(regions - 1, 1, -1):
        step = k & -k
        operand = totals[k].astype(BF16)
        if k == 2:
            firsts[last] = after(firsts[last], operand)
        value = across(operand, step)
        if k == 3:
            value = after(value, more)
        if k == step:
            crossed.append(value)
        else:
            totals[k - step] = totals[k - step] + value.astype(F32)
    seconds[last] = lower(cores[last], firsts[last])
    settle(last)
    own = totals[0]
    for value in crossed + [across(totals[1], 1)]:
        own = own + value.astype(F32)

    def onward(value, d):
        pairs = [
            (p * sub + s, ((p + d) % blocks) * sub + s) for p in range(blocks) for s in range(sub)
        ]
        return lax.ppermute(value.astype(BF16), "tile", pairs)

    matrix, vector = finish(
        sub,
        own,
        *(onward(own[d * width : (d + 1) * width], d) for d in range(1, blocks // 2)),
        onward(own[blocks // 2 * width : blocks // 2 * width + width // 2], blocks // 2),
        blocks,
    )
    if sub > 1:
        part = tile % sub
        rows = width // sub
        matrix = lax.dynamic_slice(matrix, (part * rows, 0), (rows, blocks * width))
        vector = lax.dynamic_slice(vector, (0, part * rows), (1, rows))
    return matrix[None], vector


def solution(mesh):
    return jax.shard_map(
        functools.partial(local, mesh.shape["tile"]),
        mesh=mesh,
        in_specs=(
            P(("region", "tile"), None, None),
            P(("region", "tile"), None, None),
            P(("region", "tile"), None),
            P(("region", "tile"), None),
            P(("region", "tile"), None),
            P(("region", "tile")),
            P(("region", "tile"), None),
            P(),
        ),
        out_specs=(P("region", "tile", None), P("region", "tile")),
        check_vma=False,
    )
```

```python
import functools
import jax
import jax.numpy as jnp
from jax import lax
from jax.experimental import pallas as pl
from jax.experimental.pallas import tpu as pltpu
from jax.sharding import PartitionSpec as P

F32 = jnp.float32
BF16 = jnp.bfloat16
GROUP = 8
PAIR = 2 * GROUP
DEPTH = 256

NT = (((1,), (1,)), ((), ()))


def iota(shape, axis):
    return lax.broadcasted_iota(jnp.int32, shape, axis)


def fit(ld, weight, resid, counts):
    hits = weight.shape[0]
    live = iota(weight.shape, 0) < counts.astype(jnp.int32)
    masked_w = jnp.where(live, weight, 0.0)
    weighted_l = [v * masked_w for v in ld]
    gamma = [[None] * 5 for _ in range(5)]
    for a in range(5):
        for b in range(a + 1):
            gamma[a][b] = jnp.sum(weighted_l[a] * ld[b], axis=0, keepdims=True)
            if a == b:
                gamma[a][b] = gamma[a][b] + 1.0
    beta = [jnp.sum(weighted_l[a] * resid, axis=0, keepdims=True) for a in range(5)]
    factor = [[None] * 5 for _ in range(5)]
    inverse = [None] * 5
    for j in range(5):
        center = gamma[j][j]
        for k in range(j):
            center = center - factor[j][k] * factor[j][k]
        factor[j][j] = jnp.sqrt(center)
        inverse[j] = 1.0 / factor[j][j]
        for i in range(j + 1, 5):
            offdiag = gamma[i][j]
            for k in range(j):
                offdiag = offdiag - factor[i][k] * factor[j][k]
            factor[i][j] = offdiag * inverse[j]
    solved, rhs = [], []
    for j in range(5):
        current, target = weighted_l[j], beta[j]
        for k in range(j):
            current = current - factor[j][k] * solved[k]
            target = target - factor[j][k] * rhs[k]
        solved.append(current * inverse[j])
        rhs.append(target * inverse[j])
    projection = solved[0] * rhs[0]
    for k in range(1, 5):
        projection = projection + solved[k] * rhs[k]
    return solved, masked_w * resid - projection, masked_w


def prepare(
    place_ref, region_ref, count_ref, ld_ref, weight_ref, resid_ref, ids_ref, shared_ref, table_ref
):
    tracks = region_ref.shape[1]
    slots = table_ref.shape[1]
    groups = slots // GROUP
    depth = shared_ref.shape[1]
    hits = depth // GROUP
    lanes_at, column_at = groups * 5 * GROUP, groups * (5 * GROUP + 2)
    blocks = place_ref.shape[0]
    rr = table_ref.shape[0] - 8
    member = (iota((rr, tracks), 0) == region_ref[...]).astype(F32)
    before = (iota((tracks, tracks), 0) < iota((tracks, tracks), 1)).astype(F32).astype(BF16)
    rank = jnp.dot(member.astype(BF16), before, preferred_element_type=F32)
    count = jnp.sum(member, axis=1, keepdims=True)
    room = (count.astype(jnp.int32) + (PAIR - 1)) & -PAIR
    room = jnp.broadcast_to(room.astype(F32), (rr, slots))
    lower = (iota((rr, rr), 1) < iota((rr, rr), 0)).astype(F32)
    start = jnp.zeros((rr, slots), F32)
    for g in range(rr):
        start = start + lower[:, g : g + 1] * room[g : g + 1, :]
    slot = jnp.sum(member * (rank + start[:, 0:1]), axis=0, keepdims=True)
    perm = (iota((slots, tracks), 0) == slot.astype(jnp.int32)).astype(F32).astype(BF16)
    numbers = jnp.where(
        iota((8, tracks), 0) == 0, iota((8, tracks), 1), jnp.broadcast_to(count_ref[...], (8, tracks))
    )

    def sort(value):
        return lax.dot_general(value, perm, NT, preferred_element_type=F32)

    numbers = sort(numbers.astype(F32).astype(BF16))
    table_ref[0:8, :] = numbers.astype(jnp.int32)
    table_ref[8:, :] = jnp.where(
        iota((rr, slots), 1) == 0, start.astype(jnp.int32), (start + room).astype(jnp.int32)
    )
    flat = sort(ld_ref[...])
    ld = [flat[c * hits : (c + 1) * hits] for c in range(5)]
    solved, hit_factor, masked_w = fit(
        ld, sort(weight_ref[...]), sort(resid_ref[...]), numbers[1:2]
    )
    ids = sort(ids_ref[...].astype(F32).astype(BF16))
    position = jnp.zeros_like(ids)
    for b in range(blocks):
        position = jnp.where(ids == float(b), place_ref[b].astype(F32), position)
    own = (iota((depth, slots), 0) // hits) == (iota((depth, slots), 1) % GROUP)

    def spread_out(value):
        return jnp.where(own, jnp.concatenate([value] * GROUP, axis=0), 0.0)

    grouping = (iota((groups, slots), 1) // GROUP == iota((groups, slots), 0)).astype(F32)
    for n, value in enumerate((masked_w, hit_factor)):
        shared_ref[lanes_at + n * groups : lanes_at + (n + 1) * groups, :] = lax.dot_general(
            grouping.astype(BF16), spread_out(value).astype(BF16), NT, preferred_element_type=F32
        )
    columns = 128
    grouping = (iota((columns, slots), 1) // GROUP == iota((columns, slots), 0)).astype(F32)
    shared_ref[column_at : column_at + depth, :columns] = lax.dot_general(
        spread_out(position).astype(BF16), grouping.astype(BF16), NT, preferred_element_type=F32
    )
    for c in range(5):
        value = spread_out(solved[c]).T
        for g in range(groups):
            at = (g * 5 + c) * GROUP
            shared_ref[at : at + GROUP, :] = value[g * GROUP : (g + 1) * GROUP, :]


def one_step(step, at, table_ref, shared_ref, g_ref, g_s, direct_s, spread_s):
    hits, width = g_ref.shape[1:]
    depth = GROUP * hits
    blocks = spread_s.shape[1] // width
    rows = 5 * GROUP
    head = width + 8
    groups = table_ref.shape[1] // GROUP
    lanes_at, column_at = groups * rows, groups * (rows + 2)
    column = shared_ref[column_at : column_at + depth, :128]
    lefts, values, positions = [], [], []
    for u in range(2):
        group = step * 2 + u
        for i in range(GROUP):
            g_s[u, i * hits : (i + 1) * hits, :] = g_ref[table_ref[0, group * GROUP + i]]
        g = g_s[u]
        chosen = jnp.full(column.shape, group, jnp.int32)
        position = jnp.take_along_axis(column, chosen, axis=1, mode="promise_in_bounds")
        turned = g.T.astype(F32)
        weighted = turned * shared_ref[pl.ds(lanes_at + group, 1), :]
        factor = jnp.where(iota((8, depth), 0) == 0, shared_ref[pl.ds(lanes_at + groups + group, 1), :], 0.0)
        scaled = shared_ref[pl.ds(pl.multiple_of(group * rows, GROUP), rows), :]
        high = scaled.astype(BF16).astype(F32)
        left = jnp.concatenate(
            [weighted, factor, high, scaled - high, jnp.zeros((8, depth), F32)], axis=0
        )
        lefts.append(left.astype(BF16))
        values.append(g)
        positions.append(position.astype(BF16))
    for p in range(0, blocks, 2):
        columns = slice(p * width, (p + 2) * width)
        direct = direct_s[:, columns]
        for u in range(2):
            right = jnp.concatenate(
                [
                    jnp.where(positions[u] == jnp.bfloat16(q), values[u], jnp.bfloat16(0))
                    for q in (p, p + 1)
                ],
                axis=1,
            )
            total = jnp.dot(lefts[u], right, preferred_element_type=F32)
            direct = direct + total[:head]
            spread_s[pl.ds(pl.multiple_of(at + u * rows, GROUP), rows), columns] = (
                total[head : head + rows] + total[head + rows : head + 2 * rows]
            )
        direct_s[:, columns] = direct


EVEN = (0, 4, 2, 6)
ODD = (0, 2, 4, 6)


def lead_kernel(ks, sub, *refs):
    small, g_hbm, (keep_ref, send_ref, shared_ref, table_ref) = refs[:7], refs[7], refs[8:12]
    local_small, g_ref, table_s, sems, scratch = refs[12:19], refs[19], refs[20], refs[21], refs[22:]
    copies = [
        pltpu.make_async_copy(source, target, sems.at[n])
        for n, (source, target) in enumerate([*zip(small, local_small), (g_hbm, g_ref)])
    ]
    for copy in copies:
        copy.start()
    for copy in copies[:-1]:
        copy.wait()
    prepare(*local_small, shared_ref, table_ref)
    copy = pltpu.make_async_copy(table_ref, table_s, sems.at[0])
    copy.start()
    copy.wait()
    copies[-1].wait()

    def region(n, carry):
        assemble_region(
            n, ks, sub, table_s, shared_ref, g_ref, keep_ref, send_ref, *scratch
        )
        return carry

    lax.fori_loop(0, len(ks), region, 0)


def follow_kernel(ks, sub, shared_ref, table_ref, g_ref, *refs):
    def region(n, carry):
        assemble_region(n, ks, sub, table_ref, shared_ref, g_ref, *refs)
        return carry

    if len(ks) == 1:
        region(0, 0)
    else:
        lax.fori_loop(0, len(ks), region, 0)


def assemble_region(
    number, ks, sub, table_ref, shared_ref, g_ref,
    keep_ref, send_ref, g_s, direct_s, spread_s, wide_s, turned_s, acc_s,
):
    k = jnp.where(number == 0, ks[0], ks[-1])
    width = g_ref.shape[2]
    blocks = spread_s.shape[1] // width
    many = blocks // 2
    region = lax.axis_index("region") ^ k
    block = lax.axis_index("tile") // sub
    first = table_ref[8 + region, 0] // PAIR
    steps = table_ref[8 + region, 1] // PAIR - first
    direct_s[...] = jnp.zeros_like(direct_s)

    def group_step(n, carry):
        one_step(
            first + n, n * (10 * GROUP), table_ref, shared_ref, g_ref, g_s, direct_s, spread_s
        )
        return carry

    lax.fori_loop(0, steps, group_step, 0)
    used = steps * 10
    depth_tiles = DEPTH // 8
    chunks = jnp.maximum((used + depth_tiles - 1) // depth_tiles, 1)

    def clear(tile, carry):
        spread_s[pl.ds(pl.multiple_of(tile * 8, 8), 8), :] = jnp.zeros((8, blocks * width), F32)
        return carry

    lax.fori_loop(used, chunks * depth_tiles, clear, 0)

    def chunk_step(chunk, carry):
        at = pl.multiple_of(chunk * DEPTH, DEPTH)
        wide_s[...] = spread_s[pl.ds(at, DEPTH), :].astype(BF16)
        for p in range(blocks):
            turned = -wide_s[:, p * width : (p + 1) * width].T
            turned_s[p * width : (p + 1) * width] = turned
            if p < many:
                turned_s[(blocks + p) * width : (blocks + p + 1) * width] = turned

        def products(add):
            for q in range(0, blocks, 2):
                reach = many if q >= many else many - 1
                upper = (q + blocks - reach) % blocks
                value = jnp.dot(
                    turned_s[upper * width : (upper + reach + 2) * width],
                    wide_s[:, q * width : (q + 2) * width],
                    preferred_element_type=F32,
                )
                for r in range(reach + 2):
                    p = (upper + r) % blocks
                    for c in range(2):
                        d = reach - r + c
                        if 0 <= d <= many and (d < many or p < many):
                            part = value[r * width : (r + 1) * width, c * width : (c + 1) * width]
                            columns = slice(d * width, (d + 1) * width)
                            acc_s[p, :, columns] = acc_s[p, :, columns] + part if add else part

        @pl.when(chunk == 0)
        def _():
            products(False)

        @pl.when(chunk > 0)
        def _():
            products(True)

        return carry

    lax.fori_loop(0, chunks, chunk_step, 0)
    half = width // 2
    for n in range(blocks // 2):
        for odd, out_ref in ((0, keep_ref), (1, send_ref)):
            p = block ^ (jnp.where(block % 2 == 1 - odd, ODD[n], EVEN[n]) + odd)
            columns = pl.ds(pl.multiple_of(p * width, width), width)
            parts = [direct_s[0:width, columns] + acc_s[p, :, 0:width]]
            parts += [acc_s[p, :, d * width : (d + 1) * width] for d in range(1, many)]
            upper = pl.multiple_of((p // many) * half, half)
            parts.append(acc_s[p % many, pl.ds(upper, half), many * width :])
            row = direct_s[width : width + 1, columns]
            high = row.astype(BF16).astype(F32)
            sub = iota((16, width), 0)
            parts.append(jnp.where(sub == 0, high, jnp.where(sub == 1, row - high, 0.0)))
            out_ref[n, number] = jnp.concatenate(parts, axis=0).astype(BF16)


def assemble(ks, sub, inputs, g, blocks, regions):
    tracks, hits, width = g.shape
    lead = len(inputs) == 7
    rows = width * (blocks // 2) + width // 2 + 16
    longest = -(-(-(-tracks // PAIR) * 5 * PAIR) // DEPTH) * DEPTH
    rr = -(-regions // 8) * 8
    slots = -(-(tracks + regions * (PAIR - 1)) // 128) * 128
    shared = [
        jax.ShapeDtypeStruct((slots // GROUP * (5 * GROUP + 2) + GROUP * hits, GROUP * hits), F32),
        jax.ShapeDtypeStruct((8 + rr, slots), jnp.int32),
    ]
    out = jax.ShapeDtypeStruct((blocks // 2, len(ks), rows, width), BF16)
    vmem = pl.BlockSpec(memory_space=pltpu.VMEM)
    smem = pl.BlockSpec(memory_space=pltpu.SMEM)
    copies = [pltpu.SMEM(inputs[0].shape, jnp.int32)]
    copies += [pltpu.VMEM(value.shape, value.dtype) for value in inputs[1:]]
    copies += [
        pltpu.VMEM(g.shape, g.dtype),
        pltpu.SMEM(shared[1].shape, jnp.int32),
        pltpu.SemaphoreType.DMA((8,)),
    ]
    return pl.pallas_call(
        functools.partial(lead_kernel if lead else follow_kernel, ks, sub),
        in_specs=[pl.BlockSpec(memory_space=pltpu.HBM)] * 8 if lead else [vmem, smem, vmem],
        out_specs=[vmem] * (4 if lead else 2),
        out_shape=[out, out] + shared * lead,
        scratch_shapes=copies * lead
        + [
            pltpu.VMEM((2, GROUP * hits, width), BF16),
            pltpu.VMEM((width + 8, blocks * width), F32),
            pltpu.VMEM((longest, blocks * width), F32),
            pltpu.VMEM((DEPTH, blocks * width), BF16),
            pltpu.VMEM(((blocks + blocks // 2) * width, DEPTH), BF16),
            pltpu.VMEM((blocks, width, (blocks // 2 + 1) * width), F32),
        ],
        compiler_params=pltpu.CompilerParams(vmem_limit_bytes=(60 if lead else 28) * 1024 * 1024),
        cost_estimate=pl.CostEstimate(
            flops=10**9 * len(ks), bytes_accessed=4 * 10**6, transcendentals=0
        ),
        name="assemble",
    )(*inputs, g)


def finish_kernel(sub, own_ref, r1_ref, r2_ref, r3_ref, e_ref, out_ref, vec_ref):
    width = own_ref.shape[1]
    p = lax.axis_index("tile") // sub
    blocks = out_ref.shape[1] // width
    many = blocks // 2

    def put(column, value):
        column = pl.multiple_of(((column + blocks) % blocks) * width, width)
        out_ref[:, pl.ds(column, width)] = value

    for d in range(many):
        put(p + d, own_ref[d * width : (d + 1) * width, :])
    for d, ref in ((1, r1_ref), (2, r2_ref), (3, r3_ref)):
        put(p - d, ref[...].astype(F32).T)
    tail = many * width + width // 2
    mine = own_ref[many * width : tail, :]
    other = e_ref[...].astype(F32)

    @pl.when(p < many)
    def _():
        put(p + many, jnp.concatenate([mine, other], axis=0))

    @pl.when(p >= many)
    def _():
        put(p + many, jnp.concatenate([other, mine], axis=0).T)

    vec_ref[...] = own_ref[tail : tail + 1, :] + own_ref[tail + 1 : tail + 2, :]


def finish(sub, own, r1, r2, r3, ext, blocks):
    width = own.shape[1]
    vmem = pl.BlockSpec(memory_space=pltpu.VMEM)
    return pl.pallas_call(
        functools.partial(finish_kernel, sub),
        in_specs=[vmem] * 5,
        out_specs=[vmem, vmem],
        out_shape=[
            jax.ShapeDtypeStruct((width, blocks * width), F32),
            jax.ShapeDtypeStruct((1, width), F32),
        ],
        compiler_params=pltpu.CompilerParams(vmem_limit_bytes=8 * 1024 * 1024),
        name="finish",
    )(own, r1, r2, r3, ext)


def local(
    tiles, global_deriv, local_deriv, hit_weight, hit_resid, block_ids, hit_count, track_region,
    block_place,
):
    regions = lax.axis_size("region")
    tracks, hits, width = global_deriv.shape
    blocks = block_place.shape[0]
    sub = tiles // blocks
    tile = lax.axis_index("tile")
    inputs = (
        block_place,
        track_region.reshape(1, tracks),
        hit_count.reshape(1, tracks),
        local_deriv.transpose(1, 2, 0).reshape(-1, tracks),
        hit_weight.T,
        hit_resid.T,
        block_ids.T,
    )

    def swap(value, even, odd):
        pairs = [(t, t ^ (sub * (odd if t // sub % 2 else even))) for t in range(tiles)]
        return lax.ppermute(value, "tile", pairs)

    def across(value, k):
        return lax.ppermute(value.astype(BF16), "region", [(r, r ^ k) for r in range(regions)])

    def near(keep, send):
        bit = 1
        while bit < sub:
            pairs = [(t, t ^ bit) for t in range(tiles)]
            keep, send = (v + lax.ppermute(v, "tile", pairs) for v in (keep, send))
            bit *= 2
        return keep, swap(send, 1, 1)

    def both(pair, part):
        return pair[0][part].astype(F32) + pair[1][part].astype(F32)

    low, top = slice(0, blocks // 4), slice(blocks // 4, blocks // 2)
    def upper(pair):
        return swap(both(pair, top).astype(BF16), 2, 4)

    def lower(pair, more):
        value = both(pair, low) + more.astype(F32)
        return value[0], swap(value[1].astype(BF16), 4, 2)

    groups = [(k + 1, k) for k in range(regions - 2, 0, -2)] + [(1,), (0,)]
    def after(value, other):
        return lax.optimization_barrier((value, other))[0]

    last = len(groups) - 1
    totals = [None] * regions
    cores, firsts, seconds = ([None] * (last + 1) for _ in range(3))

    def settle(n):
        value = seconds[n][0] + seconds[n][1].astype(F32)
        for place, k in enumerate(groups[n]):
            totals[k] = value[place]

    for n, ks in enumerate(groups):
        keep, send, *made = assemble(ks, sub, inputs, global_deriv, blocks, regions)
        if n == 0:
            inputs = tuple(made)
            cores[0] = near(keep, send)
            continue
        if n == 1:
            cores[0] = after(cores[0], send)
            operand = both(cores[0], top).astype(BF16)
            firsts[0] = swap(operand, 2, 4)
            send = after(send, operand)
        if n < last - 1:
            cores[n] = near(keep, send)
            firsts[n] = swap(both(cores[n], top).astype(BF16), 2, 4)
            seconds[n] = lower(cores[n], firsts[n])
            settle(n)
            inputs = inputs[0], after(inputs[1], send)
        elif n < last:
            inputs = inputs[0], after(inputs[1], send)
            cores[n] = near(keep, send)
        else:
            firsts[0] = after(firsts[0], send)
            seconds[0] = lower(cores[0], firsts[0])
            settle(0)
            cores[n - 1] = after(cores[n - 1], send)
            send = after(send, cores[n - 1][1])
            cores[n] = after(near(keep, send), seconds[0][1])
            cores[n - 1] = after(cores[n - 1], cores[n][1])
    firsts[last - 1] = upper(cores[last - 1])
    operand = both(cores[last], top).astype(BF16)
    firsts[last - 1] = after(firsts[last - 1], operand)
    value = both(cores[last - 1], low) + firsts[last - 1].astype(F32)
    half, more = value[0], value[1].astype(BF16)
    firsts[last] = swap(operand, 2, 4)
    seconds[last - 1] = half, after(swap(more, 4, 2), firsts[last])
    settle(last - 1)
    crossed = []
    for k in range(regions - 1, 1, -1):
        step = k & -k
        operand = totals[k].astype(BF16)
        if k == 2:
            firsts[last] = after(firsts[last], operand)
        value = across(operand, step)
        if k == 3:
            value = after(value, more)
        if k == step:
            crossed.append(value)
        else:
            totals[k - step] = totals[k - step] + value.astype(F32)
    seconds[last] = lower(cores[last], firsts[last])
    settle(last)
    own = totals[0]
    for value in crossed + [across(totals[1], 1)]:
        own = own + value.astype(F32)

    def onward(value, d):
        pairs = [
            (p * sub + s, ((p + d) % blocks) * sub + s) for p in range(blocks) for s in range(sub)
        ]
        return lax.ppermute(value.astype(BF16), "tile", pairs)

    matrix, vector = finish(
        sub,
        own,
        *(onward(own[d * width : (d + 1) * width], d) for d in range(1, blocks // 2)),
        onward(own[blocks // 2 * width : blocks // 2 * width + width // 2], blocks // 2),
        blocks,
    )
    if sub > 1:
        part = tile % sub
        rows = width // sub
        matrix = lax.dynamic_slice(matrix, (part * rows, 0), (rows, blocks * width))
        vector = lax.dynamic_slice(vector, (0, part * rows), (1, rows))
    return matrix[None], vector


def solution(mesh):
    return jax.shard_map(
        functools.partial(local, mesh.shape["tile"]),
        mesh=mesh,
        in_specs=(
            P(("region", "tile"), None, None),
            P(("region", "tile"), None, None),
            P(("region", "tile"), None),
            P(("region", "tile"), None),
            P(("region", "tile"), None),
            P(("region", "tile")),
            P(("region", "tile"), None),
            P(),
        ),
        out_specs=(P("region", "tile", None), P("region", "tile")),
        check_vma=False,
    )
```

```python
import functools
import jax
import jax.numpy as jnp
from jax import lax
from jax.experimental import pallas as pl
from jax.experimental.pallas import tpu as pltpu
from jax.sharding import PartitionSpec as P

F32 = jnp.float32
BF16 = jnp.bfloat16
GROUP = 8
PAIR = 2 * GROUP
DEPTH = 256

NT = (((1,), (1,)), ((), ()))


def iota(shape, axis):
    return lax.broadcasted_iota(jnp.int32, shape, axis)


def fit(ld, weight, resid, counts):
    hits = weight.shape[0]
    live = iota(weight.shape, 0) < counts.astype(jnp.int32)
    masked_w = jnp.where(live, weight, 0.0)
    weighted_l = [v * masked_w for v in ld]
    gamma = [[None] * 5 for _ in range(5)]
    for a in range(5):
        for b in range(a + 1):
            gamma[a][b] = jnp.sum(weighted_l[a] * ld[b], axis=0, keepdims=True)
            if a == b:
                gamma[a][b] = gamma[a][b] + 1.0
    beta = [jnp.sum(weighted_l[a] * resid, axis=0, keepdims=True) for a in range(5)]
    factor = [[None] * 5 for _ in range(5)]
    inverse = [None] * 5
    for j in range(5):
        center = gamma[j][j]
        for k in range(j):
            center = center - factor[j][k] * factor[j][k]
        factor[j][j] = jnp.sqrt(center)
        inverse[j] = 1.0 / factor[j][j]
        for i in range(j + 1, 5):
            offdiag = gamma[i][j]
            for k in range(j):
                offdiag = offdiag - factor[i][k] * factor[j][k]
            factor[i][j] = offdiag * inverse[j]
    solved, rhs = [], []
    for j in range(5):
        current, target = weighted_l[j], beta[j]
        for k in range(j):
            current = current - factor[j][k] * solved[k]
            target = target - factor[j][k] * rhs[k]
        solved.append(current * inverse[j])
        rhs.append(target * inverse[j])
    projection = solved[0] * rhs[0]
    for k in range(1, 5):
        projection = projection + solved[k] * rhs[k]
    return solved, masked_w * resid - projection, masked_w


def prepare(
    place_ref, region_ref, count_ref, ld_ref, weight_ref, resid_ref, ids_ref, shared_ref, table_ref
):
    tracks = region_ref.shape[1]
    slots = table_ref.shape[1]
    groups = slots // GROUP
    depth = shared_ref.shape[1]
    hits = depth // GROUP
    lanes_at, column_at = groups * 5 * GROUP, groups * (5 * GROUP + 2)
    blocks = place_ref.shape[0]
    rr = table_ref.shape[0] - 8
    member = (iota((rr, tracks), 0) == region_ref[...]).astype(F32)
    before = (iota((tracks, tracks), 0) < iota((tracks, tracks), 1)).astype(F32).astype(BF16)
    rank = jnp.dot(member.astype(BF16), before, preferred_element_type=F32)
    count = jnp.sum(member, axis=1, keepdims=True)
    room = (count.astype(jnp.int32) + (PAIR - 1)) & -PAIR
    room = jnp.broadcast_to(room.astype(F32), (rr, slots))
    lower = (iota((rr, rr), 1) < iota((rr, rr), 0)).astype(F32)
    start = jnp.zeros((rr, slots), F32)
    for g in range(rr):
        start = start + lower[:, g : g + 1] * room[g : g + 1, :]
    slot = jnp.sum(member * (rank + start[:, 0:1]), axis=0, keepdims=True)
    perm = (iota((slots, tracks), 0) == slot.astype(jnp.int32)).astype(F32).astype(BF16)
    numbers = jnp.where(
        iota((8, tracks), 0) == 0, iota((8, tracks), 1), jnp.broadcast_to(count_ref[...], (8, tracks))
    )

    def sort(value):
        return lax.dot_general(value, perm, NT, preferred_element_type=F32)

    numbers = sort(numbers.astype(F32).astype(BF16))
    table_ref[0:8, :] = numbers.astype(jnp.int32)
    table_ref[8:, :] = jnp.where(
        iota((rr, slots), 1) == 0, start.astype(jnp.int32), (start + room).astype(jnp.int32)
    )
    flat = sort(ld_ref[...])
    ld = [flat[c * hits : (c + 1) * hits] for c in range(5)]
    solved, hit_factor, masked_w = fit(
        ld, sort(weight_ref[...]), sort(resid_ref[...]), numbers[1:2]
    )
    ids = sort(ids_ref[...].astype(F32).astype(BF16))
    position = jnp.zeros_like(ids)
    for b in range(blocks):
        position = jnp.where(ids == float(b), place_ref[b].astype(F32), position)
    own = (iota((depth, slots), 0) // hits) == (iota((depth, slots), 1) % GROUP)

    def spread_out(value):
        return jnp.where(own, jnp.concatenate([value] * GROUP, axis=0), 0.0)

    grouping = (iota((groups, slots), 1) // GROUP == iota((groups, slots), 0)).astype(F32)
    for n, value in enumerate((masked_w, hit_factor)):
        shared_ref[lanes_at + n * groups : lanes_at + (n + 1) * groups, :] = lax.dot_general(
            grouping.astype(BF16), spread_out(value).astype(BF16), NT, preferred_element_type=F32
        )
    columns = 128
    grouping = (iota((columns, slots), 1) // GROUP == iota((columns, slots), 0)).astype(F32)
    shared_ref[column_at : column_at + depth, :columns] = lax.dot_general(
        spread_out(position).astype(BF16), grouping.astype(BF16), NT, preferred_element_type=F32
    )
    for c in range(5):
        value = spread_out(solved[c]).T
        for g in range(groups):
            at = (g * 5 + c) * GROUP
            shared_ref[at : at + GROUP, :] = value[g * GROUP : (g + 1) * GROUP, :]


def one_step(step, at, table_ref, shared_ref, g_ref, g_s, direct_s, spread_s):
    hits, width = g_ref.shape[1:]
    depth = GROUP * hits
    blocks = spread_s.shape[1] // width
    rows = 5 * GROUP
    head = width + 8
    groups = table_ref.shape[1] // GROUP
    lanes_at, column_at = groups * rows, groups * (rows + 2)
    column = shared_ref[column_at : column_at + depth, :128]
    lefts, values, positions = [], [], []
    for u in range(2):
        group = step * 2 + u
        for i in range(GROUP):
            g_s[u, i * hits : (i + 1) * hits, :] = g_ref[table_ref[0, group * GROUP + i]]
        g = g_s[u]
        chosen = jnp.full(column.shape, group, jnp.int32)
        position = jnp.take_along_axis(column, chosen, axis=1, mode="promise_in_bounds")
        turned = g.T.astype(F32)
        weighted = turned * shared_ref[pl.ds(lanes_at + group, 1), :]
        factor = jnp.where(iota((8, depth), 0) == 0, shared_ref[pl.ds(lanes_at + groups + group, 1), :], 0.0)
        scaled = shared_ref[pl.ds(pl.multiple_of(group * rows, GROUP), rows), :]
        high = scaled.astype(BF16).astype(F32)
        left = jnp.concatenate(
            [weighted, factor, high, scaled - high, jnp.zeros((8, depth), F32)], axis=0
        )
        lefts.append(left.astype(BF16))
        values.append(g)
        positions.append(position.astype(BF16))
    for p in range(0, blocks, 2):
        columns = slice(p * width, (p + 2) * width)
        direct = direct_s[:, columns]
        for u in range(2):
            right = jnp.concatenate(
                [
                    jnp.where(positions[u] == jnp.bfloat16(q), values[u], jnp.bfloat16(0))
                    for q in (p, p + 1)
                ],
                axis=1,
            )
            total = jnp.dot(lefts[u], right, preferred_element_type=F32)
            direct = direct + total[:head]
            spread_s[pl.ds(pl.multiple_of(at + u * rows, GROUP), rows), columns] = (
                total[head : head + rows] + total[head + rows : head + 2 * rows]
            )
        direct_s[:, columns] = direct


EVEN = (0, 4, 2, 6)
ODD = (0, 2, 4, 6)


def lead_kernel(ks, sub, *refs):
    small, g_hbm, (keep_ref, send_ref, shared_ref, table_ref) = refs[:7], refs[7], refs[8:12]
    local_small, g_ref, table_s, sems, scratch = refs[12:19], refs[19], refs[20], refs[21], refs[22:]
    copies = [
        pltpu.make_async_copy(source, target, sems.at[n])
        for n, (source, target) in enumerate([*zip(small, local_small), (g_hbm, g_ref)])
    ]
    for copy in copies:
        copy.start()
    for copy in copies[:-1]:
        copy.wait()
    prepare(*local_small, shared_ref, table_ref)
    copy = pltpu.make_async_copy(table_ref, table_s, sems.at[0])
    copy.start()
    copy.wait()
    copies[-1].wait()

    def region(n, carry):
        assemble_region(
            n, ks, sub, table_s, shared_ref, g_ref, keep_ref, send_ref, *scratch
        )
        return carry

    lax.fori_loop(0, len(ks), region, 0)


def follow_kernel(ks, sub, shared_ref, table_ref, g_ref, *refs):
    def region(n, carry):
        assemble_region(n, ks, sub, table_ref, shared_ref, g_ref, *refs)
        return carry

    if len(ks) == 1:
        region(0, 0)
    else:
        lax.fori_loop(0, len(ks), region, 0)


def assemble_region(
    number, ks, sub, table_ref, shared_ref, g_ref,
    keep_ref, send_ref, g_s, direct_s, spread_s, wide_s, turned_s, acc_s,
):
    k = jnp.where(number == 0, ks[0], ks[-1])
    width = g_ref.shape[2]
    blocks = spread_s.shape[1] // width
    many = blocks // 2
    region = lax.axis_index("region") ^ k
    block = lax.axis_index("tile") // sub
    first = table_ref[8 + region, 0] // PAIR
    steps = table_ref[8 + region, 1] // PAIR - first
    direct_s[...] = jnp.zeros_like(direct_s)

    def group_step(n, carry):
        one_step(
            first + n, n * (10 * GROUP), table_ref, shared_ref, g_ref, g_s, direct_s, spread_s
        )
        return carry

    lax.fori_loop(0, steps, group_step, 0)
    used = steps * 10
    depth_tiles = DEPTH // 8
    chunks = jnp.maximum((used + depth_tiles - 1) // depth_tiles, 1)

    def clear(tile, carry):
        spread_s[pl.ds(pl.multiple_of(tile * 8, 8), 8), :] = jnp.zeros((8, blocks * width), F32)
        return carry

    lax.fori_loop(used, chunks * depth_tiles, clear, 0)

    def chunk_step(chunk, carry):
        at = pl.multiple_of(chunk * DEPTH, DEPTH)
        wide_s[...] = spread_s[pl.ds(at, DEPTH), :].astype(BF16)
        for p in range(blocks):
            turned = -wide_s[:, p * width : (p + 1) * width].T
            turned_s[p * width : (p + 1) * width] = turned
            if p < many:
                turned_s[(blocks + p) * width : (blocks + p + 1) * width] = turned

        def products(add):
            for q in range(0, blocks, 2):
                reach = many if q >= many else many - 1
                upper = (q + blocks - reach) % blocks
                value = jnp.dot(
                    turned_s[upper * width : (upper + reach + 2) * width],
                    wide_s[:, q * width : (q + 2) * width],
                    preferred_element_type=F32,
                )
                for r in range(reach + 2):
                    p = (upper + r) % blocks
                    for c in range(2):
                        d = reach - r + c
                        if 0 <= d <= many and (d < many or p < many):
                            part = value[r * width : (r + 1) * width, c * width : (c + 1) * width]
                            columns = slice(d * width, (d + 1) * width)
                            acc_s[p, :, columns] = acc_s[p, :, columns] + part if add else part

        @pl.when(chunk == 0)
        def _():
            products(False)

        @pl.when(chunk > 0)
        def _():
            products(True)

        return carry

    lax.fori_loop(0, chunks, chunk_step, 0)
    half = width // 2
    for n in range(blocks // 2):
        for odd, out_ref in ((0, keep_ref), (1, send_ref)):
            p = block ^ (jnp.where(block % 2 == 1 - odd, ODD[n], EVEN[n]) + odd)
            columns = pl.ds(pl.multiple_of(p * width, width), width)
            parts = [direct_s[0:width, columns] + acc_s[p, :, 0:width]]
            parts += [acc_s[p, :, d * width : (d + 1) * width] for d in range(1, many)]
            upper = pl.multiple_of((p // many) * half, half)
            parts.append(acc_s[p % many, pl.ds(upper, half), many * width :])
            row = direct_s[width : width + 1, columns]
            high = row.astype(BF16).astype(F32)
            sub = iota((16, width), 0)
            parts.append(jnp.where(sub == 0, high, jnp.where(sub == 1, row - high, 0.0)))
            out_ref[n, number] = jnp.concatenate(parts, axis=0).astype(BF16)


def assemble(ks, sub, inputs, g, blocks, regions):
    tracks, hits, width = g.shape
    lead = len(inputs) == 7
    rows = width * (blocks // 2) + width // 2 + 16
    longest = -(-(-(-tracks // PAIR) * 5 * PAIR) // DEPTH) * DEPTH
    rr = -(-regions // 8) * 8
    slots = -(-(tracks + regions * (PAIR - 1)) // 128) * 128
    shared = [
        jax.ShapeDtypeStruct((slots // GROUP * (5 * GROUP + 2) + GROUP * hits, GROUP * hits), F32),
        jax.ShapeDtypeStruct((8 + rr, slots), jnp.int32),
    ]
    out = jax.ShapeDtypeStruct((blocks // 2, len(ks), rows, width), BF16)
    vmem = pl.BlockSpec(memory_space=pltpu.VMEM)
    smem = pl.BlockSpec(memory_space=pltpu.SMEM)
    copies = [pltpu.SMEM(inputs[0].shape, jnp.int32)]
    copies += [pltpu.VMEM(value.shape, value.dtype) for value in inputs[1:]]
    copies += [
        pltpu.VMEM(g.shape, g.dtype),
        pltpu.SMEM(shared[1].shape, jnp.int32),
        pltpu.SemaphoreType.DMA((8,)),
    ]
    return pl.pallas_call(
        functools.partial(lead_kernel if lead else follow_kernel, ks, sub),
        in_specs=[pl.BlockSpec(memory_space=pltpu.HBM)] * 8 if lead else [vmem, smem, vmem],
        out_specs=[vmem] * (4 if lead else 2),
        out_shape=[out, out] + shared * lead,
        scratch_shapes=copies * lead
        + [
            pltpu.VMEM((2, GROUP * hits, width), BF16),
            pltpu.VMEM((width + 8, blocks * width), F32),
            pltpu.VMEM((longest, blocks * width), F32),
            pltpu.VMEM((DEPTH, blocks * width), BF16),
            pltpu.VMEM(((blocks + blocks // 2) * width, DEPTH), BF16),
            pltpu.VMEM((blocks, width, (blocks // 2 + 1) * width), F32),
        ],
        compiler_params=pltpu.CompilerParams(vmem_limit_bytes=(60 if lead else 28) * 1024 * 1024),
        cost_estimate=pl.CostEstimate(
            flops=10**9 * len(ks), bytes_accessed=4 * 10**6, transcendentals=0
        ),
        name="assemble",
    )(*inputs, g)


def finish_kernel(sub, own_ref, r1_ref, r2_ref, r3_ref, e_ref, out_ref, vec_ref):
    width = own_ref.shape[1]
    p = lax.axis_index("tile") // sub
    blocks = out_ref.shape[1] // width
    many = blocks // 2

    def put(column, value):
        column = pl.multiple_of(((column + blocks) % blocks) * width, width)
        out_ref[:, pl.ds(column, width)] = value

    for d in range(many):
        put(p + d, own_ref[d * width : (d + 1) * width, :])
    for d, ref in ((1, r1_ref), (2, r2_ref), (3, r3_ref)):
        put(p - d, ref[...].astype(F32).T)
    tail = many * width + width // 2
    mine = own_ref[many * width : tail, :]
    other = e_ref[...].astype(F32)

    @pl.when(p < many)
    def _():
        put(p + many, jnp.concatenate([mine, other], axis=0))

    @pl.when(p >= many)
    def _():
        put(p + many, jnp.concatenate([other, mine], axis=0).T)

    vec_ref[...] = own_ref[tail : tail + 1, :] + own_ref[tail + 1 : tail + 2, :]


def finish(sub, own, r1, r2, r3, ext, blocks):
    width = own.shape[1]
    vmem = pl.BlockSpec(memory_space=pltpu.VMEM)
    return pl.pallas_call(
        functools.partial(finish_kernel, sub),
        in_specs=[vmem] * 5,
        out_specs=[vmem, vmem],
        out_shape=[
            jax.ShapeDtypeStruct((width, blocks * width), F32),
            jax.ShapeDtypeStruct((1, width), F32),
        ],
        compiler_params=pltpu.CompilerParams(vmem_limit_bytes=8 * 1024 * 1024),
        name="finish",
    )(own, r1, r2, r3, ext)


def local(
    tiles, global_deriv, local_deriv, hit_weight, hit_resid, block_ids, hit_count, track_region,
    block_place,
):
    regions = lax.axis_size("region")
    tracks, hits, width = global_deriv.shape
    blocks = block_place.shape[0]
    sub = tiles // blocks
    tile = lax.axis_index("tile")
    inputs = (
        block_place,
        track_region.reshape(1, tracks),
        hit_count.reshape(1, tracks),
        local_deriv.transpose(1, 2, 0).reshape(-1, tracks),
        hit_weight.T,
        hit_resid.T,
        block_ids.T,
    )

    def swap(value, even, odd):
        pairs = [(t, t ^ (sub * (odd if t // sub % 2 else even))) for t in range(tiles)]
        return lax.ppermute(value, "tile", pairs)

    def across(value, k):
        return lax.ppermute(value.astype(BF16), "region", [(r, r ^ k) for r in range(regions)])

    def near(keep, send):
        bit = 1
        while bit < sub:
            pairs = [(t, t ^ bit) for t in range(tiles)]
            keep, send = (v + lax.ppermute(v, "tile", pairs) for v in (keep, send))
            bit *= 2
        return keep, swap(send, 1, 1)

    def both(pair, part):
        return pair[0][part].astype(F32) + pair[1][part].astype(F32)

    low, top = slice(0, blocks // 4), slice(blocks // 4, blocks // 2)
    def after(value, other):
        return value if other is None else lax.optimization_barrier((value, other))[0]

    cores, firsts, seconds = ([None] * regions for _ in range(3))
    incoming = [[] for _ in range(regions)]
    own = None
    for slot in range(regions + 3):
        done, operands = None, []
        if slot < regions:
            k = regions - 1 - slot
            keep, send, *made = assemble((k,), sub, inputs, global_deriv, blocks, regions)
            inputs = tuple(made) if made else inputs
            done = send
        elif slot == regions:
            done = both(cores[0], top)[:, 0].astype(BF16)
        k = regions - 1 - (slot - 3)
        if 0 <= k < regions:
            total = seconds[k][0] + after(seconds[k][1], done).astype(F32)
            for value in incoming[k]:
                total = total + value.astype(F32)
            if k:
                operands.append(total.astype(BF16))
                incoming[k - (k & -k)].append(across(operands[-1], k & -k))
            else:
                own = total
        k -= 1
        if 0 <= k < regions:
            total = both(cores[k], low)[:, 0] + after(firsts[k], done).astype(F32)
            operands.append(total[1].astype(BF16))
            seconds[k] = total[0], swap(operands[-1], 4, 2)
        k -= 1
        if 0 <= k < regions:
            if slot < regions:
                cores[k] = after(cores[k], done)
            operands.append(both(cores[k], top)[:, 0].astype(BF16))
            firsts[k] = swap(operands[-1], 2, 4)
        if slot < regions:
            inputs = inputs[0], after(inputs[1], (send, operands))
            cores[k - 1] = near(keep, send)

    def onward(value, d):
        pairs = [
            (p * sub + s, ((p + d) % blocks) * sub + s) for p in range(blocks) for s in range(sub)
        ]
        return lax.ppermute(value.astype(BF16), "tile", pairs)

    matrix, vector = finish(
        sub,
        own,
        *(onward(own[d * width : (d + 1) * width], d) for d in range(1, blocks // 2)),
        onward(own[blocks // 2 * width : blocks // 2 * width + width // 2], blocks // 2),
        blocks,
    )
    if sub > 1:
        part = tile % sub
        rows = width // sub
        matrix = lax.dynamic_slice(matrix, (part * rows, 0), (rows, blocks * width))
        vector = lax.dynamic_slice(vector, (0, part * rows), (1, rows))
    return matrix[None], vector


def solution(mesh):
    return jax.shard_map(
        functools.partial(local, mesh.shape["tile"]),
        mesh=mesh,
        in_specs=(
            P(("region", "tile"), None, None),
            P(("region", "tile"), None, None),
            P(("region", "tile"), None),
            P(("region", "tile"), None),
            P(("region", "tile"), None),
            P(("region", "tile")),
            P(("region", "tile"), None),
            P(),
        ),
        out_specs=(P("region", "tile", None), P("region", "tile")),
        check_vma=False,
    )
```

```python
import functools
import jax
import jax.numpy as jnp
from jax import lax
from jax.experimental import pallas as pl
from jax.experimental.pallas import tpu as pltpu
from jax.sharding import PartitionSpec as P

F32 = jnp.float32
BF16 = jnp.bfloat16
GROUP = 8
PAIR = 2 * GROUP
DEPTH = 256

NT = (((1,), (1,)), ((), ()))


def iota(shape, axis):
    return lax.broadcasted_iota(jnp.int32, shape, axis)


def fit(ld, weight, resid, counts):
    hits = weight.shape[0]
    live = iota(weight.shape, 0) < counts.astype(jnp.int32)
    masked_w = jnp.where(live, weight, 0.0)
    weighted_l = [v * masked_w for v in ld]
    gamma = [[None] * 5 for _ in range(5)]
    for a in range(5):
        for b in range(a + 1):
            gamma[a][b] = jnp.sum(weighted_l[a] * ld[b], axis=0, keepdims=True)
            if a == b:
                gamma[a][b] = gamma[a][b] + 1.0
    beta = [jnp.sum(weighted_l[a] * resid, axis=0, keepdims=True) for a in range(5)]
    factor = [[None] * 5 for _ in range(5)]
    inverse = [None] * 5
    for j in range(5):
        center = gamma[j][j]
        for k in range(j):
            center = center - factor[j][k] * factor[j][k]
        factor[j][j] = jnp.sqrt(center)
        inverse[j] = 1.0 / factor[j][j]
        for i in range(j + 1, 5):
            offdiag = gamma[i][j]
            for k in range(j):
                offdiag = offdiag - factor[i][k] * factor[j][k]
            factor[i][j] = offdiag * inverse[j]
    solved, rhs = [], []
    for j in range(5):
        current, target = weighted_l[j], beta[j]
        for k in range(j):
            current = current - factor[j][k] * solved[k]
            target = target - factor[j][k] * rhs[k]
        solved.append(current * inverse[j])
        rhs.append(target * inverse[j])
    projection = solved[0] * rhs[0]
    for k in range(1, 5):
        projection = projection + solved[k] * rhs[k]
    return solved, masked_w * resid - projection, masked_w


def prepare(
    place_ref, region_ref, count_ref, ld_ref, weight_ref, resid_ref, ids_ref, shared_ref, table_ref
):
    tracks = region_ref.shape[1]
    slots = table_ref.shape[1]
    groups = slots // GROUP
    depth = shared_ref.shape[1]
    hits = depth // GROUP
    lanes_at, column_at = groups * 5 * GROUP, groups * (5 * GROUP + 2)
    blocks = place_ref.shape[0]
    rr = table_ref.shape[0] - 8
    member = (iota((rr, tracks), 0) == region_ref[...]).astype(F32)
    before = (iota((tracks, tracks), 0) < iota((tracks, tracks), 1)).astype(F32).astype(BF16)
    rank = jnp.dot(member.astype(BF16), before, preferred_element_type=F32)
    count = jnp.sum(member, axis=1, keepdims=True)
    room = (count.astype(jnp.int32) + (PAIR - 1)) & -PAIR
    room = jnp.broadcast_to(room.astype(F32), (rr, slots))
    lower = (iota((rr, rr), 1) < iota((rr, rr), 0)).astype(F32)
    start = jnp.zeros((rr, slots), F32)
    for g in range(rr):
        start = start + lower[:, g : g + 1] * room[g : g + 1, :]
    slot = jnp.sum(member * (rank + start[:, 0:1]), axis=0, keepdims=True)
    perm = (iota((slots, tracks), 0) == slot.astype(jnp.int32)).astype(F32).astype(BF16)
    numbers = jnp.where(
        iota((8, tracks), 0) == 0, iota((8, tracks), 1), jnp.broadcast_to(count_ref[...], (8, tracks))
    )

    def sort(value):
        return lax.dot_general(value, perm, NT, preferred_element_type=F32)

    numbers = sort(numbers.astype(F32).astype(BF16))
    table_ref[0:8, :] = numbers.astype(jnp.int32)
    table_ref[8:, :] = jnp.where(
        iota((rr, slots), 1) == 0, start.astype(jnp.int32), (start + room).astype(jnp.int32)
    )
    flat = sort(ld_ref[...])
    ld = [flat[c * hits : (c + 1) * hits] for c in range(5)]
    solved, hit_factor, masked_w = fit(
        ld, sort(weight_ref[...]), sort(resid_ref[...]), numbers[1:2]
    )
    ids = sort(ids_ref[...].astype(F32).astype(BF16))
    position = jnp.zeros_like(ids)
    for b in range(blocks):
        position = jnp.where(ids == float(b), place_ref[b].astype(F32), position)
    own = (iota((depth, slots), 0) // hits) == (iota((depth, slots), 1) % GROUP)

    def spread_out(value):
        return jnp.where(own, jnp.concatenate([value] * GROUP, axis=0), 0.0)

    grouping = (iota((groups, slots), 1) // GROUP == iota((groups, slots), 0)).astype(F32)
    for n, value in enumerate((masked_w, hit_factor)):
        shared_ref[lanes_at + n * groups : lanes_at + (n + 1) * groups, :] = lax.dot_general(
            grouping.astype(BF16), spread_out(value).astype(BF16), NT, preferred_element_type=F32
        )
    columns = 128
    grouping = (iota((columns, slots), 1) // GROUP == iota((columns, slots), 0)).astype(F32)
    shared_ref[column_at : column_at + depth, :columns] = lax.dot_general(
        spread_out(position).astype(BF16), grouping.astype(BF16), NT, preferred_element_type=F32
    )
    for c in range(5):
        value = spread_out(solved[c]).T
        for g in range(groups):
            at = (g * 5 + c) * GROUP
            shared_ref[at : at + GROUP, :] = value[g * GROUP : (g + 1) * GROUP, :]


def one_step(step, at, table_ref, shared_ref, g_ref, g_s, direct_s, spread_s):
    hits, width = g_ref.shape[1:]
    depth = GROUP * hits
    blocks = spread_s.shape[1] // width
    rows = 5 * GROUP
    head = width + 8
    groups = table_ref.shape[1] // GROUP
    lanes_at, column_at = groups * rows, groups * (rows + 2)
    column = shared_ref[column_at : column_at + depth, :128]
    lefts, values, positions = [], [], []
    for u in range(2):
        group = step * 2 + u
        for i in range(GROUP):
            g_s[u, i * hits : (i + 1) * hits, :] = g_ref[table_ref[0, group * GROUP + i]]
        g = g_s[u]
        chosen = jnp.full(column.shape, group, jnp.int32)
        position = jnp.take_along_axis(column, chosen, axis=1, mode="promise_in_bounds")
        turned = g.T.astype(F32)
        weighted = turned * shared_ref[pl.ds(lanes_at + group, 1), :]
        factor = jnp.where(iota((8, depth), 0) == 0, shared_ref[pl.ds(lanes_at + groups + group, 1), :], 0.0)
        scaled = shared_ref[pl.ds(pl.multiple_of(group * rows, GROUP), rows), :]
        high = scaled.astype(BF16).astype(F32)
        left = jnp.concatenate(
            [weighted, factor, high, scaled - high, jnp.zeros((8, depth), F32)], axis=0
        )
        lefts.append(left.astype(BF16))
        values.append(g)
        positions.append(position.astype(BF16))
    for p in range(0, blocks, 2):
        columns = slice(p * width, (p + 2) * width)
        direct = direct_s[:, columns]
        for u in range(2):
            right = jnp.concatenate(
                [
                    jnp.where(positions[u] == jnp.bfloat16(q), values[u], jnp.bfloat16(0))
                    for q in (p, p + 1)
                ],
                axis=1,
            )
            total = jnp.dot(lefts[u], right, preferred_element_type=F32)
            direct = direct + total[:head]
            spread_s[pl.ds(pl.multiple_of(at + u * rows, GROUP), rows), columns] = (
                total[head : head + rows] + total[head + rows : head + 2 * rows]
            )
        direct_s[:, columns] = direct


EVEN = (0, 4, 2, 6)
ODD = (0, 2, 4, 6)


def lead_kernel(ks, sub, *refs):
    small, g_hbm, (keep_ref, send_ref, shared_ref, table_ref) = refs[:7], refs[7], refs[8:12]
    local_small, g_ref, table_s, sems, scratch = refs[12:19], refs[19], refs[20], refs[21], refs[22:]
    copies = [
        pltpu.make_async_copy(source, target, sems.at[n])
        for n, (source, target) in enumerate([*zip(small, local_small), (g_hbm, g_ref)])
    ]
    for copy in copies:
        copy.start()
    for copy in copies[:-1]:
        copy.wait()
    prepare(*local_small, shared_ref, table_ref)
    copy = pltpu.make_async_copy(table_ref, table_s, sems.at[0])
    copy.start()
    copy.wait()
    copies[-1].wait()

    def region(n, carry):
        assemble_region(
            n, ks, sub, table_s, shared_ref, g_ref, keep_ref, send_ref, *scratch
        )
        return carry

    lax.fori_loop(0, len(ks), region, 0)


def follow_kernel(ks, sub, shared_ref, table_ref, g_ref, *refs):
    def region(n, carry):
        assemble_region(n, ks, sub, table_ref, shared_ref, g_ref, *refs)
        return carry

    if len(ks) == 1:
        region(0, 0)
    else:
        lax.fori_loop(0, len(ks), region, 0)


def assemble_region(
    number, ks, sub, table_ref, shared_ref, g_ref,
    keep_ref, send_ref, g_s, direct_s, spread_s, wide_s, turned_s, acc_s,
):
    k = jnp.where(number == 0, ks[0], ks[-1])
    width = g_ref.shape[2]
    blocks = spread_s.shape[1] // width
    many = blocks // 2
    region = lax.axis_index("region") ^ k
    block = lax.axis_index("tile") // sub
    first = table_ref[8 + region, 0] // PAIR
    steps = table_ref[8 + region, 1] // PAIR - first
    direct_s[...] = jnp.zeros_like(direct_s)

    def group_step(n, carry):
        one_step(
            first + n, n * (10 * GROUP), table_ref, shared_ref, g_ref, g_s, direct_s, spread_s
        )
        return carry

    lax.fori_loop(0, steps, group_step, 0)
    used = steps * 10
    depth_tiles = DEPTH // 8
    chunks = jnp.maximum((used + depth_tiles - 1) // depth_tiles, 1)

    def clear(tile, carry):
        spread_s[pl.ds(pl.multiple_of(tile * 8, 8), 8), :] = jnp.zeros((8, blocks * width), F32)
        return carry

    lax.fori_loop(used, chunks * depth_tiles, clear, 0)

    def chunk_step(chunk, carry):
        at = pl.multiple_of(chunk * DEPTH, DEPTH)
        wide_s[...] = spread_s[pl.ds(at, DEPTH), :].astype(BF16)
        for p in range(blocks):
            turned = -wide_s[:, p * width : (p + 1) * width].T
            turned_s[p * width : (p + 1) * width] = turned
            if p < many:
                turned_s[(blocks + p) * width : (blocks + p + 1) * width] = turned

        def products(add):
            for q in range(0, blocks, 2):
                reach = many if q >= many else many - 1
                upper = (q + blocks - reach) % blocks
                value = jnp.dot(
                    turned_s[upper * width : (upper + reach + 2) * width],
                    wide_s[:, q * width : (q + 2) * width],
                    preferred_element_type=F32,
                )
                for r in range(reach + 2):
                    p = (upper + r) % blocks
                    for c in range(2):
                        d = reach - r + c
                        if 0 <= d <= many and (d < many or p < many):
                            part = value[r * width : (r + 1) * width, c * width : (c + 1) * width]
                            columns = slice(d * width, (d + 1) * width)
                            acc_s[p, :, columns] = acc_s[p, :, columns] + part if add else part

        @pl.when(chunk == 0)
        def _():
            products(False)

        @pl.when(chunk > 0)
        def _():
            products(True)

        return carry

    lax.fori_loop(0, chunks, chunk_step, 0)
    half = width // 2
    for n in range(blocks // 2):
        for odd, out_ref in ((0, keep_ref), (1, send_ref)):
            p = block ^ (jnp.where(block % 2 == 1 - odd, ODD[n], EVEN[n]) + odd)
            columns = pl.ds(pl.multiple_of(p * width, width), width)
            parts = [direct_s[0:width, columns] + acc_s[p, :, 0:width]]
            parts += [acc_s[p, :, d * width : (d + 1) * width] for d in range(1, many)]
            upper = pl.multiple_of((p // many) * half, half)
            parts.append(acc_s[p % many, pl.ds(upper, half), many * width :])
            row = direct_s[width : width + 1, columns]
            high = row.astype(BF16).astype(F32)
            sub = iota((16, width), 0)
            parts.append(jnp.where(sub == 0, high, jnp.where(sub == 1, row - high, 0.0)))
            out_ref[n, number] = jnp.concatenate(parts, axis=0).astype(BF16)


def assemble(ks, sub, inputs, g, blocks, regions):
    tracks, hits, width = g.shape
    lead = len(inputs) == 7
    rows = width * (blocks // 2) + width // 2 + 16
    longest = -(-(-(-tracks // PAIR) * 5 * PAIR) // DEPTH) * DEPTH
    rr = -(-regions // 8) * 8
    slots = -(-(tracks + regions * (PAIR - 1)) // 128) * 128
    shared = [
        jax.ShapeDtypeStruct((slots // GROUP * (5 * GROUP + 2) + GROUP * hits, GROUP * hits), F32),
        jax.ShapeDtypeStruct((8 + rr, slots), jnp.int32),
    ]
    out = jax.ShapeDtypeStruct((blocks // 2, len(ks), rows, width), BF16)
    vmem = pl.BlockSpec(memory_space=pltpu.VMEM)
    smem = pl.BlockSpec(memory_space=pltpu.SMEM)
    copies = [pltpu.SMEM(inputs[0].shape, jnp.int32)]
    copies += [pltpu.VMEM(value.shape, value.dtype) for value in inputs[1:]]
    copies += [
        pltpu.VMEM(g.shape, g.dtype),
        pltpu.SMEM(shared[1].shape, jnp.int32),
        pltpu.SemaphoreType.DMA((8,)),
    ]
    return pl.pallas_call(
        functools.partial(lead_kernel if lead else follow_kernel, ks, sub),
        in_specs=[pl.BlockSpec(memory_space=pltpu.HBM)] * 8 if lead else [vmem, smem, vmem],
        out_specs=[vmem] * (4 if lead else 2),
        out_shape=[out, out] + shared * lead,
        scratch_shapes=copies * lead
        + [
            pltpu.VMEM((2, GROUP * hits, width), BF16),
            pltpu.VMEM((width + 8, blocks * width), F32),
            pltpu.VMEM((longest, blocks * width), F32),
            pltpu.VMEM((DEPTH, blocks * width), BF16),
            pltpu.VMEM(((blocks + blocks // 2) * width, DEPTH), BF16),
            pltpu.VMEM((blocks, width, (blocks // 2 + 1) * width), F32),
        ],
        compiler_params=pltpu.CompilerParams(vmem_limit_bytes=(60 if lead else 28) * 1024 * 1024),
        cost_estimate=pl.CostEstimate(
            flops=10**9 * len(ks), bytes_accessed=4 * 10**6, transcendentals=0
        ),
        name="assemble",
    )(*inputs, g)


def finish_kernel(sub, own_ref, r1_ref, r2_ref, r3_ref, e_ref, out_ref, vec_ref):
    width = own_ref.shape[1]
    p = lax.axis_index("tile") // sub
    blocks = out_ref.shape[1] // width
    many = blocks // 2

    def put(column, value):
        column = pl.multiple_of(((column + blocks) % blocks) * width, width)
        out_ref[:, pl.ds(column, width)] = value

    for d in range(many):
        put(p + d, own_ref[d * width : (d + 1) * width, :])
    for d, ref in ((1, r1_ref), (2, r2_ref), (3, r3_ref)):
        put(p - d, ref[...].astype(F32).T)
    tail = many * width + width // 2
    mine = own_ref[many * width : tail, :]
    other = e_ref[...].astype(F32)

    @pl.when(p < many)
    def _():
        put(p + many, jnp.concatenate([mine, other], axis=0))

    @pl.when(p >= many)
    def _():
        put(p + many, jnp.concatenate([other, mine], axis=0).T)

    vec_ref[...] = own_ref[tail : tail + 1, :] + own_ref[tail + 1 : tail + 2, :]


def finish(sub, own, r1, r2, r3, ext, blocks):
    width = own.shape[1]
    vmem = pl.BlockSpec(memory_space=pltpu.VMEM)
    return pl.pallas_call(
        functools.partial(finish_kernel, sub),
        in_specs=[vmem] * 5,
        out_specs=[vmem, vmem],
        out_shape=[
            jax.ShapeDtypeStruct((width, blocks * width), F32),
            jax.ShapeDtypeStruct((1, width), F32),
        ],
        compiler_params=pltpu.CompilerParams(vmem_limit_bytes=8 * 1024 * 1024),
        name="finish",
    )(own, r1, r2, r3, ext)


def local(
    tiles, global_deriv, local_deriv, hit_weight, hit_resid, block_ids, hit_count, track_region,
    block_place,
):
    regions = lax.axis_size("region")
    tracks, hits, width = global_deriv.shape
    blocks = block_place.shape[0]
    sub = tiles // blocks
    tile = lax.axis_index("tile")
    inputs = (
        block_place,
        track_region.reshape(1, tracks),
        hit_count.reshape(1, tracks),
        local_deriv.transpose(1, 2, 0).reshape(-1, tracks),
        hit_weight.T,
        hit_resid.T,
        block_ids.T,
    )

    def swap(value, even, odd):
        pairs = [(t, t ^ (sub * (odd if t // sub % 2 else even))) for t in range(tiles)]
        return lax.ppermute(value, "tile", pairs)

    def across(value, k):
        return lax.ppermute(value.astype(BF16), "region", [(r, r ^ k) for r in range(regions)])

    def near(keep, send):
        bit = 1
        while bit < sub:
            pairs = [(t, t ^ bit) for t in range(tiles)]
            keep, send = (v + lax.ppermute(v, "tile", pairs) for v in (keep, send))
            bit *= 2
        return keep, swap(send, 1, 1)

    def both(pair, part):
        return pair[0][part].astype(F32) + pair[1][part].astype(F32)

    low, top = slice(0, blocks // 4), slice(blocks // 4, blocks // 2)
    def after(value, other):
        return value if other is None else lax.optimization_barrier((value, other))[0]

    cores, firsts, seconds = ([None] * regions for _ in range(3))
    crossed, own = [], None
    for slot in range(regions + 3):
        done, operands, ready = None, [], None
        if slot < regions:
            k = regions - 1 - slot
            keep, send, *made = assemble((k,), sub, inputs, global_deriv, blocks, regions)
            inputs = tuple(made) if made else inputs
            done = send
        elif slot == regions:
            done = both(cores[0], top)[:, 0].astype(BF16)
        k = regions - 1 - (slot - 3)
        if 0 <= k < regions:
            ready = seconds[k][0] + after(seconds[k][1], done).astype(F32)
            if k == 0:
                own = ready
        k -= 1
        if 0 <= k < regions:
            total = both(cores[k], low)[:, 0] + after(firsts[k], done).astype(F32)
            operands.append(total[1].astype(BF16))
            seconds[k] = total[0], swap(operands[-1], 4, 2)
        k -= 1
        if 0 <= k < regions:
            if slot < regions:
                cores[k] = after(cores[k], done)
            operands.append(both(cores[k], top)[:, 0].astype(BF16))
            firsts[k] = swap(operands[-1], 2, 4)
        k = regions - 1 - (slot - 3)
        if 0 < k < regions:
            value = ready.astype(BF16)
            if k == 1:
                value = after(value, operands)
            operands.append(value)
            crossed.append(across(value, k))
        if slot < regions:
            inputs = inputs[0], after(inputs[1], (send, operands))
            k = regions - 1 - slot
            cores[k] = near(keep, send)
    for value in crossed:
        own = own + value.astype(F32)

    def onward(value, d):
        pairs = [
            (p * sub + s, ((p + d) % blocks) * sub + s) for p in range(blocks) for s in range(sub)
        ]
        return lax.ppermute(value.astype(BF16), "tile", pairs)

    matrix, vector = finish(
        sub,
        own,
        *(onward(own[d * width : (d + 1) * width], d) for d in range(1, blocks // 2)),
        onward(own[blocks // 2 * width : blocks // 2 * width + width // 2], blocks // 2),
        blocks,
    )
    if sub > 1:
        part = tile % sub
        rows = width // sub
        matrix = lax.dynamic_slice(matrix, (part * rows, 0), (rows, blocks * width))
        vector = lax.dynamic_slice(vector, (0, part * rows), (1, rows))
    return matrix[None], vector


def solution(mesh):
    return jax.shard_map(
        functools.partial(local, mesh.shape["tile"]),
        mesh=mesh,
        in_specs=(
            P(("region", "tile"), None, None),
            P(("region", "tile"), None, None),
            P(("region", "tile"), None),
            P(("region", "tile"), None),
            P(("region", "tile"), None),
            P(("region", "tile")),
            P(("region", "tile"), None),
            P(),
        ),
        out_specs=(P("region", "tile", None), P("region", "tile")),
        check_vma=False,
    )
```

```python
import functools
import jax
import jax.numpy as jnp
from jax import lax
from jax.experimental import pallas as pl
from jax.experimental.pallas import tpu as pltpu
from jax.sharding import PartitionSpec as P

F32 = jnp.float32
BF16 = jnp.bfloat16
GROUP = 8
PAIR = 2 * GROUP
DEPTH = 256

NT = (((1,), (1,)), ((), ()))


def iota(shape, axis):
    return lax.broadcasted_iota(jnp.int32, shape, axis)


def fit(ld, weight, resid, counts):
    hits = weight.shape[0]
    live = iota(weight.shape, 0) < counts.astype(jnp.int32)
    masked_w = jnp.where(live, weight, 0.0)
    weighted_l = [v * masked_w for v in ld]
    gamma = [[None] * 5 for _ in range(5)]
    for a in range(5):
        for b in range(a + 1):
            gamma[a][b] = jnp.sum(weighted_l[a] * ld[b], axis=0, keepdims=True)
            if a == b:
                gamma[a][b] = gamma[a][b] + 1.0
    beta = [jnp.sum(weighted_l[a] * resid, axis=0, keepdims=True) for a in range(5)]
    factor = [[None] * 5 for _ in range(5)]
    inverse = [None] * 5
    for j in range(5):
        center = gamma[j][j]
        for k in range(j):
            center = center - factor[j][k] * factor[j][k]
        factor[j][j] = jnp.sqrt(center)
        inverse[j] = 1.0 / factor[j][j]
        for i in range(j + 1, 5):
            offdiag = gamma[i][j]
            for k in range(j):
                offdiag = offdiag - factor[i][k] * factor[j][k]
            factor[i][j] = offdiag * inverse[j]
    solved, rhs = [], []
    for j in range(5):
        current, target = weighted_l[j], beta[j]
        for k in range(j):
            current = current - factor[j][k] * solved[k]
            target = target - factor[j][k] * rhs[k]
        solved.append(current * inverse[j])
        rhs.append(target * inverse[j])
    projection = solved[0] * rhs[0]
    for k in range(1, 5):
        projection = projection + solved[k] * rhs[k]
    return solved, masked_w * resid - projection, masked_w


def prepare(
    place_ref, region_ref, count_ref, ld_ref, weight_ref, resid_ref, ids_ref, shared_ref, table_ref
):
    tracks = region_ref.shape[1]
    slots = table_ref.shape[1]
    groups = slots // GROUP
    depth = shared_ref.shape[1]
    hits = depth // GROUP
    lanes_at, column_at = groups * 5 * GROUP, groups * (5 * GROUP + 2)
    blocks = place_ref.shape[0]
    rr = table_ref.shape[0] - 8
    member = (iota((rr, tracks), 0) == region_ref[...]).astype(F32)
    before = (iota((tracks, tracks), 0) < iota((tracks, tracks), 1)).astype(F32).astype(BF16)
    rank = jnp.dot(member.astype(BF16), before, preferred_element_type=F32)
    count = jnp.sum(member, axis=1, keepdims=True)
    room = (count.astype(jnp.int32) + (PAIR - 1)) & -PAIR
    room = jnp.broadcast_to(room.astype(F32), (rr, slots))
    lower = (iota((rr, rr), 1) < iota((rr, rr), 0)).astype(F32)
    start = jnp.zeros((rr, slots), F32)
    for g in range(rr):
        start = start + lower[:, g : g + 1] * room[g : g + 1, :]
    slot = jnp.sum(member * (rank + start[:, 0:1]), axis=0, keepdims=True)
    perm = (iota((slots, tracks), 0) == slot.astype(jnp.int32)).astype(F32).astype(BF16)
    numbers = jnp.where(
        iota((8, tracks), 0) == 0, iota((8, tracks), 1), jnp.broadcast_to(count_ref[...], (8, tracks))
    )

    def sort(value):
        return lax.dot_general(value, perm, NT, preferred_element_type=F32)

    numbers = sort(numbers.astype(F32).astype(BF16))
    table_ref[0:8, :] = numbers.astype(jnp.int32)
    table_ref[8:, :] = jnp.where(
        iota((rr, slots), 1) == 0, start.astype(jnp.int32), (start + room).astype(jnp.int32)
    )
    flat = sort(ld_ref[...])
    ld = [flat[c * hits : (c + 1) * hits] for c in range(5)]
    solved, hit_factor, masked_w = fit(
        ld, sort(weight_ref[...]), sort(resid_ref[...]), numbers[1:2]
    )
    ids = sort(ids_ref[...].astype(F32).astype(BF16))
    position = jnp.zeros_like(ids)
    for b in range(blocks):
        position = jnp.where(ids == float(b), place_ref[b].astype(F32), position)
    own = (iota((depth, slots), 0) // hits) == (iota((depth, slots), 1) % GROUP)

    def spread_out(value):
        return jnp.where(own, jnp.concatenate([value] * GROUP, axis=0), 0.0)

    grouping = (iota((groups, slots), 1) // GROUP == iota((groups, slots), 0)).astype(F32)
    for n, value in enumerate((masked_w, hit_factor)):
        shared_ref[lanes_at + n * groups : lanes_at + (n + 1) * groups, :] = lax.dot_general(
            grouping.astype(BF16), spread_out(value).astype(BF16), NT, preferred_element_type=F32
        )
    columns = 128
    grouping = (iota((columns, slots), 1) // GROUP == iota((columns, slots), 0)).astype(F32)
    shared_ref[column_at : column_at + depth, :columns] = lax.dot_general(
        spread_out(position).astype(BF16), grouping.astype(BF16), NT, preferred_element_type=F32
    )
    for c in range(5):
        value = spread_out(solved[c]).T
        for g in range(groups):
            at = (g * 5 + c) * GROUP
            shared_ref[at : at + GROUP, :] = value[g * GROUP : (g + 1) * GROUP, :]


def one_step(step, at, table_ref, shared_ref, g_ref, g_s, direct_s, spread_s):
    hits, width = g_ref.shape[1:]
    depth = GROUP * hits
    blocks = spread_s.shape[1] // width
    rows = 5 * GROUP
    head = width + 8
    groups = table_ref.shape[1] // GROUP
    lanes_at, column_at = groups * rows, groups * (rows + 2)
    column = shared_ref[column_at : column_at + depth, :128]
    lefts, values, positions = [], [], []
    for u in range(2):
        group = step * 2 + u
        for i in range(GROUP):
            g_s[u, i * hits : (i + 1) * hits, :] = g_ref[table_ref[0, group * GROUP + i]]
        g = g_s[u]
        chosen = jnp.full(column.shape, group, jnp.int32)
        position = jnp.take_along_axis(column, chosen, axis=1, mode="promise_in_bounds")
        turned = g.T.astype(F32)
        weighted = turned * shared_ref[pl.ds(lanes_at + group, 1), :]
        factor = jnp.where(iota((8, depth), 0) == 0, shared_ref[pl.ds(lanes_at + groups + group, 1), :], 0.0)
        scaled = shared_ref[pl.ds(pl.multiple_of(group * rows, GROUP), rows), :]
        high = scaled.astype(BF16).astype(F32)
        left = jnp.concatenate(
            [weighted, factor, high, scaled - high, jnp.zeros((8, depth), F32)], axis=0
        )
        lefts.append(left.astype(BF16))
        values.append(g)
        positions.append(position.astype(BF16))
    for p in range(0, blocks, 2):
        columns = slice(p * width, (p + 2) * width)
        direct = direct_s[:, columns]
        for u in range(2):
            right = jnp.concatenate(
                [
                    jnp.where(positions[u] == jnp.bfloat16(q), values[u], jnp.bfloat16(0))
                    for q in (p, p + 1)
                ],
                axis=1,
            )
            total = jnp.dot(lefts[u], right, preferred_element_type=F32)
            direct = direct + total[:head]
            spread_s[pl.ds(pl.multiple_of(at + u * rows, GROUP), rows), columns] = (
                total[head : head + rows] + total[head + rows : head + 2 * rows]
            )
        direct_s[:, columns] = direct


EVEN = (0, 4, 2, 6)
ODD = (0, 2, 4, 6)


def lead_kernel(ks, sub, *refs):
    small, g_hbm, (keep_ref, send_ref, shared_ref, table_ref) = refs[:7], refs[7], refs[8:12]
    local_small, g_ref, table_s, sems, scratch = refs[12:19], refs[19], refs[20], refs[21], refs[22:]
    copies = [
        pltpu.make_async_copy(source, target, sems.at[n])
        for n, (source, target) in enumerate([*zip(small, local_small), (g_hbm, g_ref)])
    ]
    for copy in copies:
        copy.start()
    for copy in copies[:-1]:
        copy.wait()
    prepare(*local_small, shared_ref, table_ref)
    copy = pltpu.make_async_copy(table_ref, table_s, sems.at[0])
    copy.start()
    copy.wait()
    copies[-1].wait()

    def region(n, carry):
        assemble_region(
            n, ks, sub, table_s, shared_ref, g_ref, keep_ref, send_ref, *scratch
        )
        return carry

    lax.fori_loop(0, len(ks), region, 0)


def follow_kernel(ks, sub, shared_ref, table_ref, g_ref, *refs):
    def region(n, carry):
        assemble_region(n, ks, sub, table_ref, shared_ref, g_ref, *refs)
        return carry

    if len(ks) == 1:
        region(0, 0)
    else:
        lax.fori_loop(0, len(ks), region, 0)


def assemble_region(
    number, ks, sub, table_ref, shared_ref, g_ref,
    keep_ref, send_ref, g_s, direct_s, spread_s, wide_s, turned_s, acc_s,
):
    k = jnp.where(number == 0, ks[0], ks[-1])
    width = g_ref.shape[2]
    blocks = spread_s.shape[1] // width
    many = blocks // 2
    region = lax.axis_index("region") ^ k
    block = lax.axis_index("tile") // sub
    first = table_ref[8 + region, 0] // PAIR
    steps = table_ref[8 + region, 1] // PAIR - first
    direct_s[...] = jnp.zeros_like(direct_s)

    def group_step(n, carry):
        one_step(
            first + n, n * (10 * GROUP), table_ref, shared_ref, g_ref, g_s, direct_s, spread_s
        )
        return carry

    lax.fori_loop(0, steps, group_step, 0)
    used = steps * 10
    depth_tiles = DEPTH // 8
    chunks = jnp.maximum((used + depth_tiles - 1) // depth_tiles, 1)

    def clear(tile, carry):
        spread_s[pl.ds(pl.multiple_of(tile * 8, 8), 8), :] = jnp.zeros((8, blocks * width), F32)
        return carry

    lax.fori_loop(used, chunks * depth_tiles, clear, 0)

    def chunk_step(chunk, carry):
        at = pl.multiple_of(chunk * DEPTH, DEPTH)
        wide_s[...] = spread_s[pl.ds(at, DEPTH), :].astype(BF16)
        for p in range(blocks):
            turned = -wide_s[:, p * width : (p + 1) * width].T
            turned_s[p * width : (p + 1) * width] = turned
            if p < many:
                turned_s[(blocks + p) * width : (blocks + p + 1) * width] = turned

        def products(add):
            for q in range(0, blocks, 2):
                reach = many if q >= many else many - 1
                upper = (q + blocks - reach) % blocks
                value = jnp.dot(
                    turned_s[upper * width : (upper + reach + 2) * width],
                    wide_s[:, q * width : (q + 2) * width],
                    preferred_element_type=F32,
                )
                for r in range(reach + 2):
                    p = (upper + r) % blocks
                    for c in range(2):
                        d = reach - r + c
                        if 0 <= d <= many and (d < many or p < many):
                            part = value[r * width : (r + 1) * width, c * width : (c + 1) * width]
                            columns = slice(d * width, (d + 1) * width)
                            acc_s[p, :, columns] = acc_s[p, :, columns] + part if add else part

        @pl.when(chunk == 0)
        def _():
            products(False)

        @pl.when(chunk > 0)
        def _():
            products(True)

        return carry

    lax.fori_loop(0, chunks, chunk_step, 0)
    half = width // 2
    for n in range(blocks // 2):
        for odd, out_ref in ((0, keep_ref), (1, send_ref)):
            p = block ^ (jnp.where(block % 2 == 1 - odd, ODD[n], EVEN[n]) + odd)
            columns = pl.ds(pl.multiple_of(p * width, width), width)
            parts = [direct_s[0:width, columns] + acc_s[p, :, 0:width]]
            parts += [acc_s[p, :, d * width : (d + 1) * width] for d in range(1, many)]
            upper = pl.multiple_of((p // many) * half, half)
            parts.append(acc_s[p % many, pl.ds(upper, half), many * width :])
            row = direct_s[width : width + 1, columns]
            high = row.astype(BF16).astype(F32)
            sub = iota((16, width), 0)
            parts.append(jnp.where(sub == 0, high, jnp.where(sub == 1, row - high, 0.0)))
            out_ref[n, number] = jnp.concatenate(parts, axis=0).astype(BF16)


def assemble(ks, sub, inputs, g, blocks, regions):
    tracks, hits, width = g.shape
    lead = len(inputs) == 7
    rows = width * (blocks // 2) + width // 2 + 16
    longest = -(-(-(-tracks // PAIR) * 5 * PAIR) // DEPTH) * DEPTH
    rr = -(-regions // 8) * 8
    slots = -(-(tracks + regions * (PAIR - 1)) // 128) * 128
    shared = [
        jax.ShapeDtypeStruct((slots // GROUP * (5 * GROUP + 2) + GROUP * hits, GROUP * hits), F32),
        jax.ShapeDtypeStruct((8 + rr, slots), jnp.int32),
    ]
    out = jax.ShapeDtypeStruct((blocks // 2, len(ks), rows, width), BF16)
    vmem = pl.BlockSpec(memory_space=pltpu.VMEM)
    smem = pl.BlockSpec(memory_space=pltpu.SMEM)
    copies = [pltpu.SMEM(inputs[0].shape, jnp.int32)]
    copies += [pltpu.VMEM(value.shape, value.dtype) for value in inputs[1:]]
    copies += [
        pltpu.VMEM(g.shape, g.dtype),
        pltpu.SMEM(shared[1].shape, jnp.int32),
        pltpu.SemaphoreType.DMA((8,)),
    ]
    return pl.pallas_call(
        functools.partial(lead_kernel if lead else follow_kernel, ks, sub),
        in_specs=[pl.BlockSpec(memory_space=pltpu.HBM)] * 8 if lead else [vmem, smem, vmem],
        out_specs=[vmem] * (4 if lead else 2),
        out_shape=[out, out] + shared * lead,
        scratch_shapes=copies * lead
        + [
            pltpu.VMEM((2, GROUP * hits, width), BF16),
            pltpu.VMEM((width + 8, blocks * width), F32),
            pltpu.VMEM((longest, blocks * width), F32),
            pltpu.VMEM((DEPTH, blocks * width), BF16),
            pltpu.VMEM(((blocks + blocks // 2) * width, DEPTH), BF16),
            pltpu.VMEM((blocks, width, (blocks // 2 + 1) * width), F32),
        ],
        compiler_params=pltpu.CompilerParams(vmem_limit_bytes=(60 if lead else 28) * 1024 * 1024),
        cost_estimate=pl.CostEstimate(
            flops=10**9 * len(ks), bytes_accessed=4 * 10**6, transcendentals=0
        ),
        name="assemble",
    )(*inputs, g)


def finish_kernel(sub, own_ref, r1_ref, r2_ref, r3_ref, e_ref, out_ref, vec_ref):
    width = own_ref.shape[1]
    p = lax.axis_index("tile") // sub
    blocks = out_ref.shape[1] // width
    many = blocks // 2

    def put(column, value):
        column = pl.multiple_of(((column + blocks) % blocks) * width, width)
        out_ref[:, pl.ds(column, width)] = value

    for d in range(many):
        put(p + d, own_ref[d * width : (d + 1) * width, :])
    for d, ref in ((1, r1_ref), (2, r2_ref), (3, r3_ref)):
        put(p - d, ref[...].astype(F32).T)
    tail = many * width + width // 2
    mine = own_ref[many * width : tail, :]
    other = e_ref[...].astype(F32)

    @pl.when(p < many)
    def _():
        put(p + many, jnp.concatenate([mine, other], axis=0))

    @pl.when(p >= many)
    def _():
        put(p + many, jnp.concatenate([other, mine], axis=0).T)

    vec_ref[...] = own_ref[tail : tail + 1, :] + own_ref[tail + 1 : tail + 2, :]


def finish(sub, own, r1, r2, r3, ext, blocks):
    width = own.shape[1]
    vmem = pl.BlockSpec(memory_space=pltpu.VMEM)
    return pl.pallas_call(
        functools.partial(finish_kernel, sub),
        in_specs=[vmem] * 5,
        out_specs=[vmem, vmem],
        out_shape=[
            jax.ShapeDtypeStruct((width, blocks * width), F32),
            jax.ShapeDtypeStruct((1, width), F32),
        ],
        compiler_params=pltpu.CompilerParams(vmem_limit_bytes=8 * 1024 * 1024),
        name="finish",
    )(own, r1, r2, r3, ext)


def local(
    tiles, global_deriv, local_deriv, hit_weight, hit_resid, block_ids, hit_count, track_region,
    block_place,
):
    regions = lax.axis_size("region")
    tracks, hits, width = global_deriv.shape
    blocks = block_place.shape[0]
    sub = tiles // blocks
    tile = lax.axis_index("tile")
    inputs = (
        block_place,
        track_region.reshape(1, tracks),
        hit_count.reshape(1, tracks),
        local_deriv.transpose(1, 2, 0).reshape(-1, tracks),
        hit_weight.T,
        hit_resid.T,
        block_ids.T,
    )

    def swap(value, even, odd):
        pairs = [(t, t ^ (sub * (odd if t // sub % 2 else even))) for t in range(tiles)]
        return lax.ppermute(value, "tile", pairs)

    def across(value, k):
        return lax.ppermute(value.astype(BF16), "region", [(r, r ^ k) for r in range(regions)])

    def near(keep, send):
        bit = 1
        while bit < sub:
            pairs = [(t, t ^ bit) for t in range(tiles)]
            keep, send = (v + lax.ppermute(v, "tile", pairs) for v in (keep, send))
            bit *= 2
        return keep, swap(send, 1, 1)

    def both(pair, part):
        return pair[0][part].astype(F32) + pair[1][part].astype(F32)

    low, top = slice(0, blocks // 4), slice(blocks // 4, blocks // 2)
    def after(value, other):
        return value if other is None else lax.optimization_barrier((value, other))[0]

    cores, firsts, seconds = ([None] * regions for _ in range(3))
    crossed, own = [], None
    for slot in range(regions + 3):
        done, operands, ready = None, [], None
        if slot < regions:
            k = regions - 1 - slot
            keep, send, *made = assemble((k,), sub, inputs, global_deriv, blocks, regions)
            inputs = tuple(made) if made else inputs
            done = send
        elif slot == regions:
            done = both(cores[0], top)[:, 0].astype(BF16)
            value = after(waiting[0], done)
            crossed.append(across(value, waiting[1]))
            done = done, value
        k = regions - 1 - (slot - 3)
        if 0 <= k < regions:
            ready = seconds[k][0] + after(seconds[k][1], done).astype(F32)
            if k == 0:
                own = ready
        k -= 1
        if 0 <= k < regions:
            total = both(cores[k], low)[:, 0] + after(firsts[k], done).astype(F32)
            operands.append(total[1].astype(BF16))
            seconds[k] = total[0], swap(operands[-1], 4, 2)
        k -= 1
        if 0 <= k < regions:
            if slot < regions:
                cores[k] = after(cores[k], done)
            operands.append(both(cores[k], top)[:, 0].astype(BF16))
            firsts[k] = swap(operands[-1], 2, 4)
        k = regions - 1 - (slot - 3)
        if 0 < k < regions:
            if slot == regions - 1:
                waiting = ready.astype(BF16), k
            else:
                operands.append(ready.astype(BF16))
                crossed.append(across(operands[-1], k))
        if slot < regions:
            inputs = inputs[0], after(inputs[1], (send, operands))
            k = regions - 1 - slot
            cores[k] = near(keep, send)
    for value in crossed:
        own = own + value.astype(F32)

    def onward(value, d):
        pairs = [
            (p * sub + s, ((p + d) % blocks) * sub + s) for p in range(blocks) for s in range(sub)
        ]
        return lax.ppermute(value.astype(BF16), "tile", pairs)

    matrix, vector = finish(
        sub,
        own,
        *(onward(own[d * width : (d + 1) * width], d) for d in range(1, blocks // 2)),
        onward(own[blocks // 2 * width : blocks // 2 * width + width // 2], blocks // 2),
        blocks,
    )
    if sub > 1:
        part = tile % sub
        rows = width // sub
        matrix = lax.dynamic_slice(matrix, (part * rows, 0), (rows, blocks * width))
        vector = lax.dynamic_slice(vector, (0, part * rows), (1, rows))
    return matrix[None], vector


def solution(mesh):
    return jax.shard_map(
        functools.partial(local, mesh.shape["tile"]),
        mesh=mesh,
        in_specs=(
            P(("region", "tile"), None, None),
            P(("region", "tile"), None, None),
            P(("region", "tile"), None),
            P(("region", "tile"), None),
            P(("region", "tile"), None),
            P(("region", "tile")),
            P(("region", "tile"), None),
            P(),
        ),
        out_specs=(P("region", "tile", None), P("region", "tile")),
        check_vma=False,
    )
```

```python
import functools
import jax
import jax.numpy as jnp
from jax import lax
from jax.experimental import pallas as pl
from jax.experimental.pallas import tpu as pltpu
from jax.sharding import PartitionSpec as P

F32 = jnp.float32
BF16 = jnp.bfloat16
GROUP = 8
PAIR = 2 * GROUP
DEPTH = 256

NT = (((1,), (1,)), ((), ()))


def iota(shape, axis):
    return lax.broadcasted_iota(jnp.int32, shape, axis)


def fit(ld, weight, resid, counts):
    hits = weight.shape[0]
    live = iota(weight.shape, 0) < counts.astype(jnp.int32)
    masked_w = jnp.where(live, weight, 0.0)
    weighted_l = [v * masked_w for v in ld]
    gamma = [[None] * 5 for _ in range(5)]
    for a in range(5):
        for b in range(a + 1):
            gamma[a][b] = jnp.sum(weighted_l[a] * ld[b], axis=0, keepdims=True)
            if a == b:
                gamma[a][b] = gamma[a][b] + 1.0
    beta = [jnp.sum(weighted_l[a] * resid, axis=0, keepdims=True) for a in range(5)]
    factor = [[None] * 5 for _ in range(5)]
    inverse = [None] * 5
    for j in range(5):
        center = gamma[j][j]
        for k in range(j):
            center = center - factor[j][k] * factor[j][k]
        factor[j][j] = jnp.sqrt(center)
        inverse[j] = 1.0 / factor[j][j]
        for i in range(j + 1, 5):
            offdiag = gamma[i][j]
            for k in range(j):
                offdiag = offdiag - factor[i][k] * factor[j][k]
            factor[i][j] = offdiag * inverse[j]
    solved, rhs = [], []
    for j in range(5):
        current, target = weighted_l[j], beta[j]
        for k in range(j):
            current = current - factor[j][k] * solved[k]
            target = target - factor[j][k] * rhs[k]
        solved.append(current * inverse[j])
        rhs.append(target * inverse[j])
    projection = solved[0] * rhs[0]
    for k in range(1, 5):
        projection = projection + solved[k] * rhs[k]
    return solved, masked_w * resid - projection, masked_w


def prepare(
    place_ref, region_ref, count_ref, ld_ref, weight_ref, resid_ref, ids_ref, shared_ref, table_ref
):
    tracks = region_ref.shape[1]
    slots = table_ref.shape[1]
    groups = slots // GROUP
    depth = shared_ref.shape[1]
    hits = depth // GROUP
    lanes_at, column_at = groups * 5 * GROUP, groups * (5 * GROUP + 2)
    blocks = place_ref.shape[0]
    rr = table_ref.shape[0] - 8
    member = (iota((rr, tracks), 0) == region_ref[...]).astype(F32)
    before = (iota((tracks, tracks), 0) < iota((tracks, tracks), 1)).astype(F32).astype(BF16)
    rank = jnp.dot(member.astype(BF16), before, preferred_element_type=F32)
    count = jnp.sum(member, axis=1, keepdims=True)
    room = (count.astype(jnp.int32) + (PAIR - 1)) & -PAIR
    room = jnp.broadcast_to(room.astype(F32), (rr, slots))
    lower = (iota((rr, rr), 1) < iota((rr, rr), 0)).astype(F32)
    start = jnp.zeros((rr, slots), F32)
    for g in range(rr):
        start = start + lower[:, g : g + 1] * room[g : g + 1, :]
    slot = jnp.sum(member * (rank + start[:, 0:1]), axis=0, keepdims=True)
    perm = (iota((slots, tracks), 0) == slot.astype(jnp.int32)).astype(F32).astype(BF16)
    numbers = jnp.where(
        iota((8, tracks), 0) == 0, iota((8, tracks), 1), jnp.broadcast_to(count_ref[...], (8, tracks))
    )

    def sort(value):
        return lax.dot_general(value, perm, NT, preferred_element_type=F32)

    numbers = sort(numbers.astype(F32).astype(BF16))
    table_ref[0:8, :] = numbers.astype(jnp.int32)
    table_ref[8:, :] = jnp.where(
        iota((rr, slots), 1) == 0, start.astype(jnp.int32), (start + room).astype(jnp.int32)
    )
    flat = sort(ld_ref[...])
    ld = [flat[c * hits : (c + 1) * hits] for c in range(5)]
    solved, hit_factor, masked_w = fit(
        ld, sort(weight_ref[...]), sort(resid_ref[...]), numbers[1:2]
    )
    ids = sort(ids_ref[...].astype(F32).astype(BF16))
    position = jnp.zeros_like(ids)
    for b in range(blocks):
        position = jnp.where(ids == float(b), place_ref[b].astype(F32), position)
    own = (iota((depth, slots), 0) // hits) == (iota((depth, slots), 1) % GROUP)

    def spread_out(value):
        return jnp.where(own, jnp.concatenate([value] * GROUP, axis=0), 0.0)

    grouping = (iota((groups, slots), 1) // GROUP == iota((groups, slots), 0)).astype(F32)
    for n, value in enumerate((masked_w, hit_factor)):
        shared_ref[lanes_at + n * groups : lanes_at + (n + 1) * groups, :] = lax.dot_general(
            grouping.astype(BF16), spread_out(value).astype(BF16), NT, preferred_element_type=F32
        )
    columns = 128
    grouping = (iota((columns, slots), 1) // GROUP == iota((columns, slots), 0)).astype(F32)
    shared_ref[column_at : column_at + depth, :columns] = lax.dot_general(
        spread_out(position).astype(BF16), grouping.astype(BF16), NT, preferred_element_type=F32
    )
    for c in range(5):
        value = spread_out(solved[c]).T
        for g in range(groups):
            at = (g * 5 + c) * GROUP
            shared_ref[at : at + GROUP, :] = value[g * GROUP : (g + 1) * GROUP, :]


def one_step(step, at, table_ref, shared_ref, g_ref, g_s, direct_s, spread_s):
    hits, width = g_ref.shape[1:]
    depth = GROUP * hits
    blocks = spread_s.shape[1] // width
    rows = 5 * GROUP
    head = width + 8
    groups = table_ref.shape[1] // GROUP
    lanes_at, column_at = groups * rows, groups * (rows + 2)
    column = shared_ref[column_at : column_at + depth, :128]
    lefts, values, positions = [], [], []
    for u in range(2):
        group = step * 2 + u
        for i in range(GROUP):
            g_s[u, i * hits : (i + 1) * hits, :] = g_ref[table_ref[0, group * GROUP + i]]
        g = g_s[u]
        chosen = jnp.full(column.shape, group, jnp.int32)
        position = jnp.take_along_axis(column, chosen, axis=1, mode="promise_in_bounds")
        turned = g.T.astype(F32)
        weighted = turned * shared_ref[pl.ds(lanes_at + group, 1), :]
        factor = jnp.where(iota((8, depth), 0) == 0, shared_ref[pl.ds(lanes_at + groups + group, 1), :], 0.0)
        scaled = shared_ref[pl.ds(pl.multiple_of(group * rows, GROUP), rows), :]
        high = scaled.astype(BF16).astype(F32)
        left = jnp.concatenate(
            [weighted, factor, high, scaled - high, jnp.zeros((8, depth), F32)], axis=0
        )
        lefts.append(left.astype(BF16))
        values.append(g)
        positions.append(position.astype(BF16))
    for p in range(0, blocks, 2):
        columns = slice(p * width, (p + 2) * width)
        direct = direct_s[:, columns]
        for u in range(2):
            right = jnp.concatenate(
                [
                    jnp.where(positions[u] == jnp.bfloat16(q), values[u], jnp.bfloat16(0))
                    for q in (p, p + 1)
                ],
                axis=1,
            )
            total = jnp.dot(lefts[u], right, preferred_element_type=F32)
            direct = direct + total[:head]
            spread_s[pl.ds(pl.multiple_of(at + u * rows, GROUP), rows), columns] = (
                total[head : head + rows] + total[head + rows : head + 2 * rows]
            )
        direct_s[:, columns] = direct


EVEN = (0, 4, 2, 6)
ODD = (0, 2, 4, 6)


def lead_kernel(ks, sub, *refs):
    small, g_hbm, (keep_ref, send_ref, shared_ref, table_ref) = refs[:7], refs[7], refs[8:12]
    local_small, g_ref, table_s, sems, scratch = refs[12:19], refs[19], refs[20], refs[21], refs[22:]
    copies = [
        pltpu.make_async_copy(source, target, sems.at[n])
        for n, (source, target) in enumerate([*zip(small, local_small), (g_hbm, g_ref)])
    ]
    for copy in copies:
        copy.start()
    for copy in copies[:-1]:
        copy.wait()
    prepare(*local_small, shared_ref, table_ref)
    copy = pltpu.make_async_copy(table_ref, table_s, sems.at[0])
    copy.start()
    copy.wait()
    copies[-1].wait()

    def region(n, carry):
        assemble_region(
            n, ks, sub, table_s, shared_ref, g_ref, keep_ref, send_ref, *scratch
        )
        return carry

    lax.fori_loop(0, len(ks), region, 0)


def follow_kernel(ks, sub, shared_ref, table_ref, g_ref, *refs):
    def region(n, carry):
        assemble_region(n, ks, sub, table_ref, shared_ref, g_ref, *refs)
        return carry

    if len(ks) == 1:
        region(0, 0)
    else:
        lax.fori_loop(0, len(ks), region, 0)


def assemble_region(
    number, ks, sub, table_ref, shared_ref, g_ref,
    keep_ref, send_ref, g_s, direct_s, spread_s, wide_s, turned_s, acc_s,
):
    k = jnp.where(number == 0, ks[0], ks[-1])
    width = g_ref.shape[2]
    blocks = spread_s.shape[1] // width
    many = blocks // 2
    region = lax.axis_index("region") ^ k
    block = lax.axis_index("tile") // sub
    first = table_ref[8 + region, 0] // PAIR
    steps = table_ref[8 + region, 1] // PAIR - first
    direct_s[...] = jnp.zeros_like(direct_s)

    def group_step(n, carry):
        one_step(
            first + n, n * (10 * GROUP), table_ref, shared_ref, g_ref, g_s, direct_s, spread_s
        )
        return carry

    lax.fori_loop(0, steps, group_step, 0)
    used = steps * 10
    depth_tiles = DEPTH // 8
    chunks = jnp.maximum((used + depth_tiles - 1) // depth_tiles, 1)

    def clear(tile, carry):
        spread_s[pl.ds(pl.multiple_of(tile * 8, 8), 8), :] = jnp.zeros((8, blocks * width), F32)
        return carry

    lax.fori_loop(used, chunks * depth_tiles, clear, 0)

    def chunk_step(chunk, carry):
        at = pl.multiple_of(chunk * DEPTH, DEPTH)
        wide_s[...] = spread_s[pl.ds(at, DEPTH), :].astype(BF16)
        for p in range(blocks):
            turned = -wide_s[:, p * width : (p + 1) * width].T
            turned_s[p * width : (p + 1) * width] = turned
            if p < many:
                turned_s[(blocks + p) * width : (blocks + p + 1) * width] = turned

        def products(add):
            for q in range(0, blocks, 2):
                reach = many if q >= many else many - 1
                upper = (q + blocks - reach) % blocks
                value = jnp.dot(
                    turned_s[upper * width : (upper + reach + 2) * width],
                    wide_s[:, q * width : (q + 2) * width],
                    preferred_element_type=F32,
                )
                for r in range(reach + 2):
                    p = (upper + r) % blocks
                    for c in range(2):
                        d = reach - r + c
                        if 0 <= d <= many and (d < many or p < many):
                            part = value[r * width : (r + 1) * width, c * width : (c + 1) * width]
                            columns = slice(d * width, (d + 1) * width)
                            acc_s[p, :, columns] = acc_s[p, :, columns] + part if add else part

        @pl.when(chunk == 0)
        def _():
            products(False)

        @pl.when(chunk > 0)
        def _():
            products(True)

        return carry

    lax.fori_loop(0, chunks, chunk_step, 0)
    half = width // 2
    for n in range(blocks // 2):
        for odd, out_ref in ((0, keep_ref), (1, send_ref)):
            p = block ^ (jnp.where(block % 2 == 1 - odd, ODD[n], EVEN[n]) + odd)
            columns = pl.ds(pl.multiple_of(p * width, width), width)
            parts = [direct_s[0:width, columns] + acc_s[p, :, 0:width]]
            for d in range(1, many):
                parts.append(acc_s[p, :half, d * width : (d + 1) * width])
            upper = pl.multiple_of((p // many) * half, half)
            parts.append(acc_s[p % many, pl.ds(upper, half), many * width :])
            for d in range(1, many):
                other = (p + blocks - d) % blocks
                parts.append(acc_s[other, half:, d * width : (d + 1) * width])
            row = direct_s[width : width + 1, columns]
            high = row.astype(BF16).astype(F32)
            sub = iota((16, width), 0)
            parts.append(jnp.where(sub == 0, high, jnp.where(sub == 1, row - high, 0.0)))
            out_ref[n, number] = jnp.concatenate(parts, axis=0).astype(BF16)


def assemble(ks, sub, inputs, g, blocks, regions):
    tracks, hits, width = g.shape
    lead = len(inputs) == 7
    rows = width * (blocks // 2) + width // 2 + 16
    longest = -(-(-(-tracks // PAIR) * 5 * PAIR) // DEPTH) * DEPTH
    rr = -(-regions // 8) * 8
    slots = -(-(tracks + regions * (PAIR - 1)) // 128) * 128
    shared = [
        jax.ShapeDtypeStruct((slots // GROUP * (5 * GROUP + 2) + GROUP * hits, GROUP * hits), F32),
        jax.ShapeDtypeStruct((8 + rr, slots), jnp.int32),
    ]
    out = jax.ShapeDtypeStruct((blocks // 2, len(ks), rows, width), BF16)
    vmem = pl.BlockSpec(memory_space=pltpu.VMEM)
    smem = pl.BlockSpec(memory_space=pltpu.SMEM)
    copies = [pltpu.SMEM(inputs[0].shape, jnp.int32)]
    copies += [pltpu.VMEM(value.shape, value.dtype) for value in inputs[1:]]
    copies += [
        pltpu.VMEM(g.shape, g.dtype),
        pltpu.SMEM(shared[1].shape, jnp.int32),
        pltpu.SemaphoreType.DMA((8,)),
    ]
    return pl.pallas_call(
        functools.partial(lead_kernel if lead else follow_kernel, ks, sub),
        in_specs=[pl.BlockSpec(memory_space=pltpu.HBM)] * 8 if lead else [vmem, smem, vmem],
        out_specs=[vmem] * (4 if lead else 2),
        out_shape=[out, out] + shared * lead,
        scratch_shapes=copies * lead
        + [
            pltpu.VMEM((2, GROUP * hits, width), BF16),
            pltpu.VMEM((width + 8, blocks * width), F32),
            pltpu.VMEM((longest, blocks * width), F32),
            pltpu.VMEM((DEPTH, blocks * width), BF16),
            pltpu.VMEM(((blocks + blocks // 2) * width, DEPTH), BF16),
            pltpu.VMEM((blocks, width, (blocks // 2 + 1) * width), F32),
        ],
        compiler_params=pltpu.CompilerParams(vmem_limit_bytes=(60 if lead else 28) * 1024 * 1024),
        cost_estimate=pl.CostEstimate(
            flops=10**9 * len(ks), bytes_accessed=4 * 10**6, transcendentals=0
        ),
        name="assemble",
    )(*inputs, g)


def gather_kernel(sub, own_ref, *refs):
    crossed, (total_ref, send_ref) = refs[:-2], refs[-2:]
    width = own_ref.shape[1]
    half = width // 2
    blocks = send_ref.shape[0]
    p = lax.axis_index("tile") // sub
    total = own_ref[...]
    for ref in crossed:
        total = total + ref[...].astype(F32)
    total_ref[...] = total
    send_ref[p] = jnp.zeros(send_ref.shape[1:], BF16)
    for n, d in enumerate(distances(blocks)):
        at = width + n * half
        send_ref[(p + blocks + d) % blocks] = total[at : at + half].astype(BF16)


def distances(blocks):
    return [*range(1, blocks // 2 + 1), *range(-1, -(blocks // 2), -1)]


def finish_kernel(sub, own_ref, got_ref, out_ref, vec_ref):
    width = own_ref.shape[1]
    half = width // 2
    p = lax.axis_index("tile") // sub
    blocks = out_ref.shape[1] // width
    many = blocks // 2

    def put(place, value):
        out_ref[:, pl.ds(pl.multiple_of(place * width, width), width)] = value

    put(p, own_ref[0:width, :])
    for n, d in enumerate(distances(blocks)):
        at = width + n * half
        place = (p + blocks + d) % blocks
        mine, other = own_ref[at : at + half, :], got_ref[place].astype(F32)
        if 0 < d < many:
            put(place, jnp.concatenate([mine, other], axis=0))
        elif d < 0:
            put(place, jnp.concatenate([other, mine], axis=0).T)
        else:

            @pl.when(p < many)
            def _():
                put(place, jnp.concatenate([mine, other], axis=0))

            @pl.when(p >= many)
            def _():
                put(place, jnp.concatenate([other, mine], axis=0).T)

    tail = width + (blocks - 1) * half
    vec_ref[...] = own_ref[tail : tail + 1, :] + own_ref[tail + 1 : tail + 2, :]


def small_call(kernel, out_shape, name, *values):
    vmem = pl.BlockSpec(memory_space=pltpu.VMEM)
    return pl.pallas_call(
        kernel,
        in_specs=[vmem] * len(values),
        out_specs=[vmem] * len(out_shape),
        out_shape=out_shape,
        compiler_params=pltpu.CompilerParams(vmem_limit_bytes=8 * 1024 * 1024),
        name=name,
    )(*values)


def local(
    tiles, global_deriv, local_deriv, hit_weight, hit_resid, block_ids, hit_count, track_region,
    block_place,
):
    regions = lax.axis_size("region")
    tracks, hits, width = global_deriv.shape
    blocks = block_place.shape[0]
    sub = tiles // blocks
    tile = lax.axis_index("tile")
    inputs = (
        block_place,
        track_region.reshape(1, tracks),
        hit_count.reshape(1, tracks),
        local_deriv.transpose(1, 2, 0).reshape(-1, tracks),
        hit_weight.T,
        hit_resid.T,
        block_ids.T,
    )

    def swap(value, even, odd):
        pairs = [(t, t ^ (sub * (odd if t // sub % 2 else even))) for t in range(tiles)]
        return lax.ppermute(value, "tile", pairs)

    def across(value, k):
        return lax.ppermute(value.astype(BF16), "region", [(r, r ^ k) for r in range(regions)])

    def near(keep, send):
        bit = 1
        while bit < sub:
            pairs = [(t, t ^ bit) for t in range(tiles)]
            keep, send = (v + lax.ppermute(v, "tile", pairs) for v in (keep, send))
            bit *= 2
        return keep, swap(send, 1, 1)

    def both(pair, part):
        return pair[0][part].astype(F32) + pair[1][part].astype(F32)

    low, top = slice(0, blocks // 4), slice(blocks // 4, blocks // 2)
    def after(value, other):
        return value if other is None else lax.optimization_barrier((value, other))[0]

    cores, firsts, seconds = ([None] * regions for _ in range(3))
    incoming = [[] for _ in range(regions)]
    own = None
    for slot in range(regions + 3):
        done, operands = None, []
        if slot < regions:
            k = regions - 1 - slot
            keep, send, *made = assemble((k,), sub, inputs, global_deriv, blocks, regions)
            inputs = tuple(made) if made else inputs
            done = send
        elif slot == regions:
            done = both(cores[0], top)[:, 0].astype(BF16)
        k = regions - 1 - (slot - 3)
        if 0 <= k < regions:
            total = seconds[k][0] + after(seconds[k][1], done).astype(F32)
            if k:
                for value in incoming[k]:
                    total = total + value.astype(F32)
                operands.append(total.astype(BF16))
                incoming[k - (k & -k)].append(across(operands[-1], k & -k))
            else:
                own = total
        k -= 1
        if 0 <= k < regions:
            total = both(cores[k], low)[:, 0] + after(firsts[k], done).astype(F32)
            operands.append(total[1].astype(BF16))
            seconds[k] = total[0], swap(operands[-1], 4, 2)
        k -= 1
        if 0 <= k < regions:
            if slot < regions:
                cores[k] = after(cores[k], done)
            operands.append(both(cores[k], top)[:, 0].astype(BF16))
            firsts[k] = swap(operands[-1], 2, 4)
        if slot < regions:
            inputs = inputs[0], after(inputs[1], (send, operands))
            cores[k - 1] = near(keep, send)

    crossed = incoming[0]
    own, send = small_call(
        functools.partial(gather_kernel, sub),
        [
            jax.ShapeDtypeStruct(own.shape, F32),
            jax.ShapeDtypeStruct((blocks, width // 2, width), BF16),
        ],
        "gather",
        own,
        *crossed,
    )
    across_tiles = [[b * sub + n for b in range(blocks)] for n in range(sub)]
    got = lax.all_to_all(
        send, "tile", 0, 0, axis_index_groups=across_tiles if sub > 1 else None, tiled=True
    )
    matrix, vector = small_call(
        functools.partial(finish_kernel, sub),
        [
            jax.ShapeDtypeStruct((width, blocks * width), F32),
            jax.ShapeDtypeStruct((1, width), F32),
        ],
        "finish",
        own,
        got,
    )
    if sub > 1:
        part = tile % sub
        rows = width // sub
        matrix = lax.dynamic_slice(matrix, (part * rows, 0), (rows, blocks * width))
        vector = lax.dynamic_slice(vector, (0, part * rows), (1, rows))
    return matrix[None], vector


def solution(mesh):
    return jax.shard_map(
        functools.partial(local, mesh.shape["tile"]),
        mesh=mesh,
        in_specs=(
            P(("region", "tile"), None, None),
            P(("region", "tile"), None, None),
            P(("region", "tile"), None),
            P(("region", "tile"), None),
            P(("region", "tile"), None),
            P(("region", "tile")),
            P(("region", "tile"), None),
            P(),
        ),
        out_specs=(P("region", "tile", None), P("region", "tile")),
        check_vma=False,
    )
```

```python
import functools
import jax
import jax.numpy as jnp
from jax import lax
from jax.experimental import pallas as pl
from jax.experimental.pallas import tpu as pltpu
from jax.sharding import PartitionSpec as P

F32 = jnp.float32
BF16 = jnp.bfloat16
GROUP = 8
PAIR = 2 * GROUP
DEPTH = 256

NT = (((1,), (1,)), ((), ()))


def iota(shape, axis):
    return lax.broadcasted_iota(jnp.int32, shape, axis)


def fit(ld, weight, resid, counts):
    hits = weight.shape[0]
    live = iota(weight.shape, 0) < counts.astype(jnp.int32)
    masked_w = jnp.where(live, weight, 0.0)
    weighted_l = [v * masked_w for v in ld]
    gamma = [[None] * 5 for _ in range(5)]
    for a in range(5):
        for b in range(a + 1):
            gamma[a][b] = jnp.sum(weighted_l[a] * ld[b], axis=0, keepdims=True)
            if a == b:
                gamma[a][b] = gamma[a][b] + 1.0
    beta = [jnp.sum(weighted_l[a] * resid, axis=0, keepdims=True) for a in range(5)]
    factor = [[None] * 5 for _ in range(5)]
    inverse = [None] * 5
    for j in range(5):
        center = gamma[j][j]
        for k in range(j):
            center = center - factor[j][k] * factor[j][k]
        factor[j][j] = jnp.sqrt(center)
        inverse[j] = 1.0 / factor[j][j]
        for i in range(j + 1, 5):
            offdiag = gamma[i][j]
            for k in range(j):
                offdiag = offdiag - factor[i][k] * factor[j][k]
            factor[i][j] = offdiag * inverse[j]
    solved, rhs = [], []
    for j in range(5):
        current, target = weighted_l[j], beta[j]
        for k in range(j):
            current = current - factor[j][k] * solved[k]
            target = target - factor[j][k] * rhs[k]
        solved.append(current * inverse[j])
        rhs.append(target * inverse[j])
    projection = solved[0] * rhs[0]
    for k in range(1, 5):
        projection = projection + solved[k] * rhs[k]
    return solved, masked_w * resid - projection, masked_w


def prepare(
    place_ref, region_ref, count_ref, ld_ref, weight_ref, resid_ref, ids_ref, shared_ref, table_ref
):
    tracks = region_ref.shape[1]
    slots = table_ref.shape[1]
    groups = slots // GROUP
    depth = shared_ref.shape[1]
    hits = depth // GROUP
    lanes_at, column_at = groups * 5 * GROUP, groups * (5 * GROUP + 2)
    blocks = place_ref.shape[0]
    rr = table_ref.shape[0] - 8
    member = (iota((rr, tracks), 0) == region_ref[...]).astype(F32)
    before = (iota((tracks, tracks), 0) < iota((tracks, tracks), 1)).astype(F32).astype(BF16)
    rank = jnp.dot(member.astype(BF16), before, preferred_element_type=F32)
    count = jnp.sum(member, axis=1, keepdims=True)
    room = (count.astype(jnp.int32) + (PAIR - 1)) & -PAIR
    room = jnp.broadcast_to(room.astype(F32), (rr, slots))
    lower = (iota((rr, rr), 1) < iota((rr, rr), 0)).astype(F32)
    start = jnp.zeros((rr, slots), F32)
    for g in range(rr):
        start = start + lower[:, g : g + 1] * room[g : g + 1, :]
    slot = jnp.sum(member * (rank + start[:, 0:1]), axis=0, keepdims=True)
    perm = (iota((slots, tracks), 0) == slot.astype(jnp.int32)).astype(F32).astype(BF16)
    numbers = jnp.where(
        iota((8, tracks), 0) == 0, iota((8, tracks), 1), jnp.broadcast_to(count_ref[...], (8, tracks))
    )

    def sort(value):
        return lax.dot_general(value, perm, NT, preferred_element_type=F32)

    numbers = sort(numbers.astype(F32).astype(BF16))
    table_ref[0:8, :] = numbers.astype(jnp.int32)
    table_ref[8:, :] = jnp.where(
        iota((rr, slots), 1) == 0, start.astype(jnp.int32), (start + room).astype(jnp.int32)
    )
    flat = sort(ld_ref[...])
    ld = [flat[c * hits : (c + 1) * hits] for c in range(5)]
    solved, hit_factor, masked_w = fit(
        ld, sort(weight_ref[...]), sort(resid_ref[...]), numbers[1:2]
    )
    ids = sort(ids_ref[...].astype(F32).astype(BF16))
    position = jnp.zeros_like(ids)
    for b in range(blocks):
        position = jnp.where(ids == float(b), place_ref[b].astype(F32), position)
    own = (iota((depth, slots), 0) // hits) == (iota((depth, slots), 1) % GROUP)

    def spread_out(value):
        return jnp.where(own, jnp.concatenate([value] * GROUP, axis=0), 0.0)

    grouping = (iota((groups, slots), 1) // GROUP == iota((groups, slots), 0)).astype(F32)
    for n, value in enumerate((masked_w, hit_factor)):
        shared_ref[lanes_at + n * groups : lanes_at + (n + 1) * groups, :] = lax.dot_general(
            grouping.astype(BF16), spread_out(value).astype(BF16), NT, preferred_element_type=F32
        )
    columns = 128
    grouping = (iota((columns, slots), 1) // GROUP == iota((columns, slots), 0)).astype(F32)
    shared_ref[column_at : column_at + depth, :columns] = lax.dot_general(
        spread_out(position).astype(BF16), grouping.astype(BF16), NT, preferred_element_type=F32
    )
    for c in range(5):
        value = spread_out(solved[c]).T
        for g in range(groups):
            at = (g * 5 + c) * GROUP
            shared_ref[at : at + GROUP, :] = value[g * GROUP : (g + 1) * GROUP, :]


def one_step(step, at, table_ref, shared_ref, g_ref, g_s, direct_s, spread_s):
    hits, width = g_ref.shape[1:]
    depth = GROUP * hits
    blocks = spread_s.shape[1] // width
    rows = 5 * GROUP
    head = width + 8
    groups = table_ref.shape[1] // GROUP
    lanes_at, column_at = groups * rows, groups * (rows + 2)
    column = shared_ref[column_at : column_at + depth, :128]
    lefts, values, positions = [], [], []
    for u in range(2):
        group = step * 2 + u
        for i in range(GROUP):
            g_s[u, i * hits : (i + 1) * hits, :] = g_ref[table_ref[0, group * GROUP + i]]
        g = g_s[u]
        chosen = jnp.full(column.shape, group, jnp.int32)
        position = jnp.take_along_axis(column, chosen, axis=1, mode="promise_in_bounds")
        turned = g.T.astype(F32)
        weighted = turned * shared_ref[pl.ds(lanes_at + group, 1), :]
        factor = jnp.where(iota((8, depth), 0) == 0, shared_ref[pl.ds(lanes_at + groups + group, 1), :], 0.0)
        scaled = shared_ref[pl.ds(pl.multiple_of(group * rows, GROUP), rows), :]
        high = scaled.astype(BF16).astype(F32)
        left = jnp.concatenate(
            [weighted, factor, high, scaled - high, jnp.zeros((8, depth), F32)], axis=0
        )
        lefts.append(left.astype(BF16))
        values.append(g)
        positions.append(position.astype(BF16))
    for p in range(0, blocks, 2):
        columns = slice(p * width, (p + 2) * width)
        direct = direct_s[:, columns]
        for u in range(2):
            right = jnp.concatenate(
                [
                    jnp.where(positions[u] == jnp.bfloat16(q), values[u], jnp.bfloat16(0))
                    for q in (p, p + 1)
                ],
                axis=1,
            )
            total = jnp.dot(lefts[u], right, preferred_element_type=F32)
            direct = direct + total[:head]
            spread_s[pl.ds(pl.multiple_of(at + u * rows, GROUP), rows), columns] = (
                total[head : head + rows] + total[head + rows : head + 2 * rows]
            )
        direct_s[:, columns] = direct


EVEN = (0, 4, 2, 6)
ODD = (0, 2, 4, 6)


def lead_kernel(ks, sub, *refs):
    small, g_hbm, (keep_ref, send_ref, shared_ref, table_ref) = refs[:7], refs[7], refs[8:12]
    local_small, g_ref, table_s, sems, scratch = refs[12:19], refs[19], refs[20], refs[21], refs[22:]
    copies = [
        pltpu.make_async_copy(source, target, sems.at[n])
        for n, (source, target) in enumerate([*zip(small, local_small), (g_hbm, g_ref)])
    ]
    for copy in copies:
        copy.start()
    for copy in copies[:-1]:
        copy.wait()
    prepare(*local_small, shared_ref, table_ref)
    copy = pltpu.make_async_copy(table_ref, table_s, sems.at[0])
    copy.start()
    copy.wait()
    copies[-1].wait()

    def region(n, carry):
        assemble_region(
            n, ks, sub, table_s, shared_ref, g_ref, keep_ref, send_ref, *scratch
        )
        return carry

    lax.fori_loop(0, len(ks), region, 0)


def follow_kernel(ks, sub, shared_ref, table_ref, g_ref, *refs):
    def region(n, carry):
        assemble_region(n, ks, sub, table_ref, shared_ref, g_ref, *refs)
        return carry

    if len(ks) == 1:
        region(0, 0)
    else:
        lax.fori_loop(0, len(ks), region, 0)


def assemble_region(
    number, ks, sub, table_ref, shared_ref, g_ref,
    keep_ref, send_ref, g_s, direct_s, spread_s, wide_s, turned_s, acc_s,
):
    k = jnp.where(number == 0, ks[0], ks[-1])
    width = g_ref.shape[2]
    blocks = spread_s.shape[1] // width
    many = blocks // 2
    region = lax.axis_index("region") ^ k
    block = lax.axis_index("tile") // sub
    first = table_ref[8 + region, 0] // PAIR
    steps = table_ref[8 + region, 1] // PAIR - first
    direct_s[...] = jnp.zeros_like(direct_s)

    def group_step(n, carry):
        one_step(
            first + n, n * (10 * GROUP), table_ref, shared_ref, g_ref, g_s, direct_s, spread_s
        )
        return carry

    lax.fori_loop(0, steps, group_step, 0)
    used = steps * 10
    depth_tiles = DEPTH // 8
    chunks = jnp.maximum((used + depth_tiles - 1) // depth_tiles, 1)

    def clear(tile, carry):
        spread_s[pl.ds(pl.multiple_of(tile * 8, 8), 8), :] = jnp.zeros((8, blocks * width), F32)
        return carry

    lax.fori_loop(used, chunks * depth_tiles, clear, 0)

    def chunk_step(chunk, carry):
        at = pl.multiple_of(chunk * DEPTH, DEPTH)
        wide_s[...] = spread_s[pl.ds(at, DEPTH), :].astype(BF16)
        for p in range(blocks):
            turned = -wide_s[:, p * width : (p + 1) * width].T
            turned_s[p * width : (p + 1) * width] = turned
            if p < many:
                turned_s[(blocks + p) * width : (blocks + p + 1) * width] = turned

        def products(add):
            for q in range(0, blocks, 2):
                reach = many if q >= many else many - 1
                upper = (q + blocks - reach) % blocks
                value = jnp.dot(
                    turned_s[upper * width : (upper + reach + 2) * width],
                    wide_s[:, q * width : (q + 2) * width],
                    preferred_element_type=F32,
                )
                for r in range(reach + 2):
                    p = (upper + r) % blocks
                    for c in range(2):
                        d = reach - r + c
                        if 0 <= d <= many and (d < many or p < many):
                            part = value[r * width : (r + 1) * width, c * width : (c + 1) * width]
                            columns = slice(d * width, (d + 1) * width)
                            acc_s[p, :, columns] = acc_s[p, :, columns] + part if add else part

        @pl.when(chunk == 0)
        def _():
            products(False)

        @pl.when(chunk > 0)
        def _():
            products(True)

        return carry

    lax.fori_loop(0, chunks, chunk_step, 0)
    half = width // 2
    for n in range(blocks // 2):
        for odd, out_ref in ((0, keep_ref), (1, send_ref)):
            p = block ^ (jnp.where(block % 2 == 1 - odd, ODD[n], EVEN[n]) + odd)
            columns = pl.ds(pl.multiple_of(p * width, width), width)
            parts = [direct_s[0:width, columns] + acc_s[p, :, 0:width]]
            parts += [acc_s[p, :, d * width : (d + 1) * width] for d in range(1, many)]
            upper = pl.multiple_of((p // many) * half, half)
            parts.append(acc_s[p % many, pl.ds(upper, half), many * width :])
            row = direct_s[width : width + 1, columns]
            high = row.astype(BF16).astype(F32)
            sub = iota((16, width), 0)
            parts.append(jnp.where(sub == 0, high, jnp.where(sub == 1, row - high, 0.0)))
            out_ref[n, number] = jnp.concatenate(parts, axis=0).astype(BF16)


def assemble(ks, sub, inputs, g, blocks, regions):
    tracks, hits, width = g.shape
    lead = len(inputs) == 7
    rows = width * (blocks // 2) + width // 2 + 16
    longest = -(-(-(-tracks // PAIR) * 5 * PAIR) // DEPTH) * DEPTH
    rr = -(-regions // 8) * 8
    slots = -(-(tracks + regions * (PAIR - 1)) // 128) * 128
    shared = [
        jax.ShapeDtypeStruct((slots // GROUP * (5 * GROUP + 2) + GROUP * hits, GROUP * hits), F32),
        jax.ShapeDtypeStruct((8 + rr, slots), jnp.int32),
    ]
    out = jax.ShapeDtypeStruct((blocks // 2, len(ks), rows, width), BF16)
    vmem = pl.BlockSpec(memory_space=pltpu.VMEM)
    smem = pl.BlockSpec(memory_space=pltpu.SMEM)
    copies = [pltpu.SMEM(inputs[0].shape, jnp.int32)]
    copies += [pltpu.VMEM(value.shape, value.dtype) for value in inputs[1:]]
    copies += [
        pltpu.VMEM(g.shape, g.dtype),
        pltpu.SMEM(shared[1].shape, jnp.int32),
        pltpu.SemaphoreType.DMA((8,)),
    ]
    return pl.pallas_call(
        functools.partial(lead_kernel if lead else follow_kernel, ks, sub),
        in_specs=[pl.BlockSpec(memory_space=pltpu.HBM)] * 8 if lead else [vmem, smem, vmem],
        out_specs=[vmem] * (4 if lead else 2),
        out_shape=[out, out] + shared * lead,
        scratch_shapes=copies * lead
        + [
            pltpu.VMEM((2, GROUP * hits, width), BF16),
            pltpu.VMEM((width + 8, blocks * width), F32),
            pltpu.VMEM((longest, blocks * width), F32),
            pltpu.VMEM((DEPTH, blocks * width), BF16),
            pltpu.VMEM(((blocks + blocks // 2) * width, DEPTH), BF16),
            pltpu.VMEM((blocks, width, (blocks // 2 + 1) * width), F32),
        ],
        compiler_params=pltpu.CompilerParams(vmem_limit_bytes=(60 if lead else 28) * 1024 * 1024),
        cost_estimate=pl.CostEstimate(
            flops=10**9 * len(ks), bytes_accessed=4 * 10**6, transcendentals=0
        ),
        name="assemble",
    )(*inputs, g)


def finish_kernel(sub, own_ref, r1_ref, r2_ref, r3_ref, e_ref, out_ref, vec_ref):
    width = own_ref.shape[1]
    p = lax.axis_index("tile") // sub
    blocks = out_ref.shape[1] // width
    many = blocks // 2

    def put(column, value):
        column = pl.multiple_of(((column + blocks) % blocks) * width, width)
        out_ref[:, pl.ds(column, width)] = value

    for d in range(many):
        put(p + d, own_ref[d * width : (d + 1) * width, :])
    for d, ref in ((1, r1_ref), (2, r2_ref), (3, r3_ref)):
        put(p - d, ref[...].astype(F32).T)
    tail = many * width + width // 2
    mine = own_ref[many * width : tail, :]
    other = e_ref[...].astype(F32)

    @pl.when(p < many)
    def _():
        put(p + many, jnp.concatenate([mine, other], axis=0))

    @pl.when(p >= many)
    def _():
        put(p + many, jnp.concatenate([other, mine], axis=0).T)

    vec_ref[...] = own_ref[tail : tail + 1, :] + own_ref[tail + 1 : tail + 2, :]


def gather_kernel(number, own_ref, *refs):
    crossed, total_ref, sends = refs[:number], refs[number], refs[number + 1 :]
    width = own_ref.shape[1]
    total = own_ref[...]
    for ref in crossed:
        total = total + ref[...].astype(F32)
    total_ref[...] = total
    for n, ref in enumerate(sends):
        at = (n + 1) * width
        ref[...] = total[at : at + ref.shape[0]].astype(BF16)


def gather(own, crossed, blocks):
    width = own.shape[1]
    vmem = pl.BlockSpec(memory_space=pltpu.VMEM)
    rows = [width] * (blocks // 2 - 1) + [width // 2]
    return pl.pallas_call(
        functools.partial(gather_kernel, len(crossed)),
        in_specs=[vmem] * (1 + len(crossed)),
        out_specs=[vmem] * (1 + len(rows)),
        out_shape=[jax.ShapeDtypeStruct(own.shape, F32)]
        + [jax.ShapeDtypeStruct((n, width), BF16) for n in rows],
        compiler_params=pltpu.CompilerParams(vmem_limit_bytes=8 * 1024 * 1024),
        name="gather",
    )(own, *crossed)


def finish(sub, own, r1, r2, r3, ext, blocks):
    width = own.shape[1]
    vmem = pl.BlockSpec(memory_space=pltpu.VMEM)
    return pl.pallas_call(
        functools.partial(finish_kernel, sub),
        in_specs=[vmem] * 5,
        out_specs=[vmem, vmem],
        out_shape=[
            jax.ShapeDtypeStruct((width, blocks * width), F32),
            jax.ShapeDtypeStruct((1, width), F32),
        ],
        compiler_params=pltpu.CompilerParams(vmem_limit_bytes=8 * 1024 * 1024),
        name="finish",
    )(own, r1, r2, r3, ext)


def local(
    tiles, global_deriv, local_deriv, hit_weight, hit_resid, block_ids, hit_count, track_region,
    block_place,
):
    regions = lax.axis_size("region")
    tracks, hits, width = global_deriv.shape
    blocks = block_place.shape[0]
    sub = tiles // blocks
    tile = lax.axis_index("tile")
    inputs = (
        block_place,
        track_region.reshape(1, tracks),
        hit_count.reshape(1, tracks),
        local_deriv.transpose(1, 2, 0).reshape(-1, tracks),
        hit_weight.T,
        hit_resid.T,
        block_ids.T,
    )

    def swap(value, even, odd):
        pairs = [(t, t ^ (sub * (odd if t // sub % 2 else even))) for t in range(tiles)]
        return lax.ppermute(value, "tile", pairs)

    def across(value, k):
        return lax.ppermute(value.astype(BF16), "region", [(r, r ^ k) for r in range(regions)])

    def near(keep, send):
        bit = 1
        while bit < sub:
            pairs = [(t, t ^ bit) for t in range(tiles)]
            keep, send = (v + lax.ppermute(v, "tile", pairs) for v in (keep, send))
            bit *= 2
        return keep, swap(send, 1, 1)

    def both(pair, part):
        return pair[0][part].astype(F32) + pair[1][part].astype(F32)

    low, top = slice(0, blocks // 4), slice(blocks // 4, blocks // 2)
    def after(value, other):
        return value if other is None else lax.optimization_barrier((value, other))[0]

    cores, firsts, seconds = ([None] * regions for _ in range(3))
    incoming = [[] for _ in range(regions)]
    own = None
    for slot in range(regions + 3):
        done, operands = None, []
        if slot < regions:
            k = regions - 1 - slot
            keep, send, *made = assemble((k,), sub, inputs, global_deriv, blocks, regions)
            inputs = tuple(made) if made else inputs
            done = send
        elif slot == regions:
            done = both(cores[0], top)[:, 0].astype(BF16)
        k = regions - 1 - (slot - 3)

        def lowered(k, done):
            total = both(cores[k], low)[:, 0] + after(firsts[k], done).astype(F32)
            seconds[k] = total[0], swap(total[1].astype(BF16), 4, 2)
            return total[1].astype(BF16)

        if slot > regions and k > 0:
            done = lowered(k - 1, done)
        if 0 <= k < regions:
            total = seconds[k][0] + after(seconds[k][1], done).astype(F32)
            if k:
                for value in incoming[k]:
                    total = total + value.astype(F32)
                operands.append(total.astype(BF16))
                incoming[k - (k & -k)].append(across(operands[-1], k & -k))
            else:
                own = total
        k -= 1
        if 0 <= k < regions and slot <= regions:
            operands.append(lowered(k, (done, operands) if slot == regions else done))
        k -= 1
        if 0 <= k < regions:
            if slot < regions:
                cores[k] = after(cores[k], (done, operands) if slot == regions - 1 else done)
            operands.append(both(cores[k], top)[:, 0].astype(BF16))
            firsts[k] = swap(operands[-1], 2, 4)
        if slot < regions:
            inputs = inputs[0], after(inputs[1], (send, operands))
            cores[k - 1] = near(keep, send)

    def onward(value, d):
        pairs = [
            (p * sub + s, ((p + d) % blocks) * sub + s) for p in range(blocks) for s in range(sub)
        ]
        return lax.ppermute(value, "tile", pairs)

    own, *sends = gather(own, incoming[0], blocks)
    matrix, vector = finish(sub, own, *(onward(v, d + 1) for d, v in enumerate(sends)), blocks)
    if sub > 1:
        part = tile % sub
        rows = width // sub
        matrix = lax.dynamic_slice(matrix, (part * rows, 0), (rows, blocks * width))
        vector = lax.dynamic_slice(vector, (0, part * rows), (1, rows))
    return matrix[None], vector


def solution(mesh):
    return jax.shard_map(
        functools.partial(local, mesh.shape["tile"]),
        mesh=mesh,
        in_specs=(
            P(("region", "tile"), None, None),
            P(("region", "tile"), None, None),
            P(("region", "tile"), None),
            P(("region", "tile"), None),
            P(("region", "tile"), None),
            P(("region", "tile")),
            P(("region", "tile"), None),
            P(),
        ),
        out_specs=(P("region", "tile", None), P("region", "tile")),
        check_vma=False,
    )
```

```python
import functools
import jax
import jax.numpy as jnp
from jax import lax
from jax.experimental import pallas as pl
from jax.experimental.pallas import tpu as pltpu
from jax.sharding import PartitionSpec as P

F32 = jnp.float32
BF16 = jnp.bfloat16
GROUP = 8
PAIR = 2 * GROUP
DEPTH = 256

NT = (((1,), (1,)), ((), ()))


def iota(shape, axis):
    return lax.broadcasted_iota(jnp.int32, shape, axis)


def fit(ld, weight, resid, counts):
    hits = weight.shape[0]
    live = iota(weight.shape, 0) < counts.astype(jnp.int32)
    masked_w = jnp.where(live, weight, 0.0)
    weighted_l = [v * masked_w for v in ld]
    gamma = [[None] * 5 for _ in range(5)]
    for a in range(5):
        for b in range(a + 1):
            gamma[a][b] = jnp.sum(weighted_l[a] * ld[b], axis=0, keepdims=True)
            if a == b:
                gamma[a][b] = gamma[a][b] + 1.0
    beta = [jnp.sum(weighted_l[a] * resid, axis=0, keepdims=True) for a in range(5)]
    factor = [[None] * 5 for _ in range(5)]
    inverse = [None] * 5
    for j in range(5):
        center = gamma[j][j]
        for k in range(j):
            center = center - factor[j][k] * factor[j][k]
        factor[j][j] = jnp.sqrt(center)
        inverse[j] = 1.0 / factor[j][j]
        for i in range(j + 1, 5):
            offdiag = gamma[i][j]
            for k in range(j):
                offdiag = offdiag - factor[i][k] * factor[j][k]
            factor[i][j] = offdiag * inverse[j]
    solved, rhs = [], []
    for j in range(5):
        current, target = weighted_l[j], beta[j]
        for k in range(j):
            current = current - factor[j][k] * solved[k]
            target = target - factor[j][k] * rhs[k]
        solved.append(current * inverse[j])
        rhs.append(target * inverse[j])
    projection = solved[0] * rhs[0]
    for k in range(1, 5):
        projection = projection + solved[k] * rhs[k]
    return solved, masked_w * resid - projection, masked_w


def prepare(
    place_ref, region_ref, count_ref, ld_ref, weight_ref, resid_ref, ids_ref, shared_ref, table_ref
):
    tracks = region_ref.shape[1]
    slots = table_ref.shape[1]
    groups = slots // GROUP
    depth = shared_ref.shape[1]
    hits = depth // GROUP
    lanes_at, column_at = groups * 5 * GROUP, groups * (5 * GROUP + 2)
    blocks = place_ref.shape[0]
    rr = table_ref.shape[0] - 8
    member = (iota((rr, tracks), 0) == region_ref[...]).astype(F32)
    before = (iota((tracks, tracks), 0) < iota((tracks, tracks), 1)).astype(F32).astype(BF16)
    rank = jnp.dot(member.astype(BF16), before, preferred_element_type=F32)
    count = jnp.sum(member, axis=1, keepdims=True)
    room = (count.astype(jnp.int32) + (PAIR - 1)) & -PAIR
    room = jnp.broadcast_to(room.astype(F32), (rr, slots))
    lower = (iota((rr, rr), 1) < iota((rr, rr), 0)).astype(F32)
    start = jnp.zeros((rr, slots), F32)
    for g in range(rr):
        start = start + lower[:, g : g + 1] * room[g : g + 1, :]
    slot = jnp.sum(member * (rank + start[:, 0:1]), axis=0, keepdims=True)
    perm = (iota((slots, tracks), 0) == slot.astype(jnp.int32)).astype(F32).astype(BF16)
    numbers = jnp.where(
        iota((8, tracks), 0) == 0, iota((8, tracks), 1), jnp.broadcast_to(count_ref[...], (8, tracks))
    )

    def sort(value):
        return lax.dot_general(value, perm, NT, preferred_element_type=F32)

    numbers = sort(numbers.astype(F32).astype(BF16))
    table_ref[0:8, :] = numbers.astype(jnp.int32)
    table_ref[8:, :] = jnp.where(
        iota((rr, slots), 1) == 0, start.astype(jnp.int32), (start + room).astype(jnp.int32)
    )
    flat = sort(ld_ref[...])
    ld = [flat[c * hits : (c + 1) * hits] for c in range(5)]
    solved, hit_factor, masked_w = fit(
        ld, sort(weight_ref[...]), sort(resid_ref[...]), numbers[1:2]
    )
    ids = sort(ids_ref[...].astype(F32).astype(BF16))
    position = jnp.zeros_like(ids)
    for b in range(blocks):
        position = jnp.where(ids == float(b), place_ref[b].astype(F32), position)
    own = (iota((depth, slots), 0) // hits) == (iota((depth, slots), 1) % GROUP)

    def spread_out(value):
        return jnp.where(own, jnp.concatenate([value] * GROUP, axis=0), 0.0)

    grouping = (iota((groups, slots), 1) // GROUP == iota((groups, slots), 0)).astype(F32)
    for n, value in enumerate((masked_w, hit_factor)):
        shared_ref[lanes_at + n * groups : lanes_at + (n + 1) * groups, :] = lax.dot_general(
            grouping.astype(BF16), spread_out(value).astype(BF16), NT, preferred_element_type=F32
        )
    columns = 128
    grouping = (iota((columns, slots), 1) // GROUP == iota((columns, slots), 0)).astype(F32)
    shared_ref[column_at : column_at + depth, :columns] = lax.dot_general(
        spread_out(position).astype(BF16), grouping.astype(BF16), NT, preferred_element_type=F32
    )
    for c in range(5):
        value = spread_out(solved[c]).T
        for g in range(groups):
            at = (g * 5 + c) * GROUP
            shared_ref[at : at + GROUP, :] = value[g * GROUP : (g + 1) * GROUP, :]


def one_step(step, at, table_ref, shared_ref, g_ref, g_s, direct_s, spread_s):
    hits, width = g_ref.shape[1:]
    depth = GROUP * hits
    blocks = spread_s.shape[1] // width
    rows = 5 * GROUP
    head = width + 8
    groups = table_ref.shape[1] // GROUP
    lanes_at, column_at = groups * rows, groups * (rows + 2)
    column = shared_ref[column_at : column_at + depth, :128]
    lefts, values, positions = [], [], []
    for u in range(2):
        group = step * 2 + u
        for i in range(GROUP):
            g_s[u, i * hits : (i + 1) * hits, :] = g_ref[table_ref[0, group * GROUP + i]]
        g = g_s[u]
        chosen = jnp.full(column.shape, group, jnp.int32)
        position = jnp.take_along_axis(column, chosen, axis=1, mode="promise_in_bounds")
        turned = g.T.astype(F32)
        weighted = turned * shared_ref[pl.ds(lanes_at + group, 1), :]
        factor = jnp.where(iota((8, depth), 0) == 0, shared_ref[pl.ds(lanes_at + groups + group, 1), :], 0.0)
        scaled = shared_ref[pl.ds(pl.multiple_of(group * rows, GROUP), rows), :]
        high = scaled.astype(BF16).astype(F32)
        left = jnp.concatenate(
            [weighted, factor, high, scaled - high, jnp.zeros((8, depth), F32)], axis=0
        )
        lefts.append(left.astype(BF16))
        values.append(g)
        positions.append(position.astype(BF16))
    for p in range(0, blocks, 2):
        columns = slice(p * width, (p + 2) * width)
        direct = direct_s[:, columns]
        for u in range(2):
            right = jnp.concatenate(
                [
                    jnp.where(positions[u] == jnp.bfloat16(q), values[u], jnp.bfloat16(0))
                    for q in (p, p + 1)
                ],
                axis=1,
            )
            total = jnp.dot(lefts[u], right, preferred_element_type=F32)
            direct = direct + total[:head]
            spread_s[pl.ds(pl.multiple_of(at + u * rows, GROUP), rows), columns] = (
                total[head : head + rows] + total[head + rows : head + 2 * rows]
            )
        direct_s[:, columns] = direct


EVEN = (0, 4, 2, 6)
ODD = (0, 2, 4, 6)


def lead_kernel(ks, sub, *refs):
    small, g_hbm, (keep_ref, send_ref, shared_ref, table_ref) = refs[:7], refs[7], refs[8:12]
    local_small, g_ref, table_s, sems, scratch = refs[12:19], refs[19], refs[20], refs[21], refs[22:]
    copies = [
        pltpu.make_async_copy(source, target, sems.at[n])
        for n, (source, target) in enumerate([*zip(small, local_small), (g_hbm, g_ref)])
    ]
    for copy in copies:
        copy.start()
    for copy in copies[:-1]:
        copy.wait()
    prepare(*local_small, shared_ref, table_ref)
    copy = pltpu.make_async_copy(table_ref, table_s, sems.at[0])
    copy.start()
    copy.wait()
    copies[-1].wait()

    def region(n, carry):
        assemble_region(
            n, ks, sub, table_s, shared_ref, g_ref, keep_ref, send_ref, *scratch
        )
        return carry

    lax.fori_loop(0, len(ks), region, 0)


def follow_kernel(ks, sub, shared_ref, table_ref, g_ref, *refs):
    def region(n, carry):
        assemble_region(n, ks, sub, table_ref, shared_ref, g_ref, *refs)
        return carry

    if len(ks) == 1:
        region(0, 0)
    else:
        lax.fori_loop(0, len(ks), region, 0)


def assemble_region(
    number, ks, sub, table_ref, shared_ref, g_ref,
    keep_ref, send_ref, g_s, direct_s, spread_s, wide_s, turned_s, acc_s,
):
    k = jnp.where(number == 0, ks[0], ks[-1])
    width = g_ref.shape[2]
    blocks = spread_s.shape[1] // width
    many = blocks // 2
    region = lax.axis_index("region") ^ k
    block = lax.axis_index("tile") // sub
    first = table_ref[8 + region, 0] // PAIR
    steps = table_ref[8 + region, 1] // PAIR - first
    direct_s[...] = jnp.zeros_like(direct_s)

    def group_step(n, carry):
        one_step(
            first + n, n * (10 * GROUP), table_ref, shared_ref, g_ref, g_s, direct_s, spread_s
        )
        return carry

    lax.fori_loop(0, steps, group_step, 0)
    used = steps * 10
    depth_tiles = DEPTH // 8
    chunks = jnp.maximum((used + depth_tiles - 1) // depth_tiles, 1)

    def clear(tile, carry):
        spread_s[pl.ds(pl.multiple_of(tile * 8, 8), 8), :] = jnp.zeros((8, blocks * width), F32)
        return carry

    lax.fori_loop(used, chunks * depth_tiles, clear, 0)

    def chunk_step(chunk, carry):
        at = pl.multiple_of(chunk * DEPTH, DEPTH)
        wide_s[...] = spread_s[pl.ds(at, DEPTH), :].astype(BF16)
        for p in range(blocks):
            turned = -wide_s[:, p * width : (p + 1) * width].T
            turned_s[p * width : (p + 1) * width] = turned
            if p < many:
                turned_s[(blocks + p) * width : (blocks + p + 1) * width] = turned

        def products(add):
            for q in range(0, blocks, 2):
                reach = many if q >= many else many - 1
                upper = (q + blocks - reach) % blocks
                value = jnp.dot(
                    turned_s[upper * width : (upper + reach + 2) * width],
                    wide_s[:, q * width : (q + 2) * width],
                    preferred_element_type=F32,
                )
                for r in range(reach + 2):
                    p = (upper + r) % blocks
                    for c in range(2):
                        d = reach - r + c
                        if 0 <= d <= many and (d < many or p < many):
                            part = value[r * width : (r + 1) * width, c * width : (c + 1) * width]
                            columns = slice(d * width, (d + 1) * width)
                            acc_s[p, :, columns] = acc_s[p, :, columns] + part if add else part

        @pl.when(chunk == 0)
        def _():
            products(False)

        @pl.when(chunk > 0)
        def _():
            products(True)

        return carry

    lax.fori_loop(0, chunks, chunk_step, 0)
    half = width // 2
    for n in range(blocks // 2):
        for odd, out_ref in ((0, keep_ref), (1, send_ref)):
            p = block ^ (jnp.where(block % 2 == 1 - odd, ODD[n], EVEN[n]) + odd)
            columns = pl.ds(pl.multiple_of(p * width, width), width)
            parts = [direct_s[0:width, columns] + acc_s[p, :, 0:width]]
            parts += [acc_s[p, :, d * width : (d + 1) * width] for d in range(1, many)]
            upper = pl.multiple_of((p // many) * half, half)
            parts.append(acc_s[p % many, pl.ds(upper, half), many * width :])
            row = direct_s[width : width + 1, columns]
            high = row.astype(BF16).astype(F32)
            sub = iota((16, width), 0)
            parts.append(jnp.where(sub == 0, high, jnp.where(sub == 1, row - high, 0.0)))
            out_ref[n, number] = jnp.concatenate(parts, axis=0).astype(BF16)


def assemble(ks, sub, inputs, g, blocks, regions):
    tracks, hits, width = g.shape
    lead = len(inputs) == 7
    rows = width * (blocks // 2) + width // 2 + 16
    longest = -(-(-(-tracks // PAIR) * 5 * PAIR) // DEPTH) * DEPTH
    rr = -(-regions // 8) * 8
    slots = -(-(tracks + regions * (PAIR - 1)) // 128) * 128
    shared = [
        jax.ShapeDtypeStruct((slots // GROUP * (5 * GROUP + 2) + GROUP * hits, GROUP * hits), F32),
        jax.ShapeDtypeStruct((8 + rr, slots), jnp.int32),
    ]
    out = jax.ShapeDtypeStruct((blocks // 2, len(ks), rows, width), BF16)
    vmem = pl.BlockSpec(memory_space=pltpu.VMEM)
    smem = pl.BlockSpec(memory_space=pltpu.SMEM)
    copies = [pltpu.SMEM(inputs[0].shape, jnp.int32)]
    copies += [pltpu.VMEM(value.shape, value.dtype) for value in inputs[1:]]
    copies += [
        pltpu.VMEM(g.shape, g.dtype),
        pltpu.SMEM(shared[1].shape, jnp.int32),
        pltpu.SemaphoreType.DMA((8,)),
    ]
    return pl.pallas_call(
        functools.partial(lead_kernel if lead else follow_kernel, ks, sub),
        in_specs=[pl.BlockSpec(memory_space=pltpu.HBM)] * 8 if lead else [vmem, smem, vmem],
        out_specs=[vmem] * (4 if lead else 2),
        out_shape=[out, out] + shared * lead,
        scratch_shapes=copies * lead
        + [
            pltpu.VMEM((2, GROUP * hits, width), BF16),
            pltpu.VMEM((width + 8, blocks * width), F32),
            pltpu.VMEM((longest, blocks * width), F32),
            pltpu.VMEM((DEPTH, blocks * width), BF16),
            pltpu.VMEM(((blocks + blocks // 2) * width, DEPTH), BF16),
            pltpu.VMEM((blocks, width, (blocks // 2 + 1) * width), F32),
        ],
        compiler_params=pltpu.CompilerParams(vmem_limit_bytes=(60 if lead else 28) * 1024 * 1024),
        cost_estimate=pl.CostEstimate(
            flops=10**9 * len(ks), bytes_accessed=4 * 10**6, transcendentals=0
        ),
        name="assemble",
    )(*inputs, g)


def finish_kernel(sub, own_ref, r1_ref, r2_ref, r3_ref, e_ref, out_ref, vec_ref):
    width = own_ref.shape[1]
    p = lax.axis_index("tile") // sub
    blocks = out_ref.shape[1] // width
    many = blocks // 2

    def put(column, value):
        column = pl.multiple_of(((column + blocks) % blocks) * width, width)
        out_ref[:, pl.ds(column, width)] = value

    for d in range(many):
        put(p + d, own_ref[d * width : (d + 1) * width, :])
    for d, ref in ((1, r1_ref), (2, r2_ref), (3, r3_ref)):
        put(p - d, ref[...].astype(F32).T)
    tail = many * width + width // 2
    mine = own_ref[many * width : tail, :]
    other = e_ref[...].astype(F32)

    @pl.when(p < many)
    def _():
        put(p + many, jnp.concatenate([mine, other], axis=0))

    @pl.when(p >= many)
    def _():
        put(p + many, jnp.concatenate([other, mine], axis=0).T)

    vec_ref[...] = own_ref[tail : tail + 1, :] + own_ref[tail + 1 : tail + 2, :]


def gather_kernel(number, own_ref, *refs):
    crossed, total_ref, sends = refs[:number], refs[number], refs[number + 1 :]
    width = own_ref.shape[1]
    total = own_ref[...]
    for ref in crossed:
        total = total + ref[...].astype(F32)
    total_ref[...] = total
    for n, ref in enumerate(sends):
        at = (n + 1) * width
        ref[...] = total[at : at + ref.shape[0]].astype(BF16)


def gather(own, crossed, blocks):
    width = own.shape[1]
    vmem = pl.BlockSpec(memory_space=pltpu.VMEM)
    rows = [width] * (blocks // 2 - 1) + [width // 2]
    return pl.pallas_call(
        functools.partial(gather_kernel, len(crossed)),
        in_specs=[vmem] * (1 + len(crossed)),
        out_specs=[vmem] * (1 + len(rows)),
        out_shape=[jax.ShapeDtypeStruct(own.shape, F32)]
        + [jax.ShapeDtypeStruct((n, width), BF16) for n in rows],
        compiler_params=pltpu.CompilerParams(vmem_limit_bytes=8 * 1024 * 1024),
        name="gather",
    )(own, *crossed)


def finish(sub, own, r1, r2, r3, ext, blocks):
    width = own.shape[1]
    vmem = pl.BlockSpec(memory_space=pltpu.VMEM)
    return pl.pallas_call(
        functools.partial(finish_kernel, sub),
        in_specs=[vmem] * 5,
        out_specs=[vmem, vmem],
        out_shape=[
            jax.ShapeDtypeStruct((width, blocks * width), F32),
            jax.ShapeDtypeStruct((1, width), F32),
        ],
        compiler_params=pltpu.CompilerParams(vmem_limit_bytes=8 * 1024 * 1024),
        name="finish",
    )(own, r1, r2, r3, ext)


def local(
    tiles, global_deriv, local_deriv, hit_weight, hit_resid, block_ids, hit_count, track_region,
    block_place,
):
    regions = lax.axis_size("region")
    tracks, hits, width = global_deriv.shape
    blocks = block_place.shape[0]
    sub = tiles // blocks
    tile = lax.axis_index("tile")
    inputs = (
        block_place,
        track_region.reshape(1, tracks),
        hit_count.reshape(1, tracks),
        local_deriv.transpose(1, 2, 0).reshape(-1, tracks),
        hit_weight.T,
        hit_resid.T,
        block_ids.T,
    )

    def swap(value, even, odd):
        pairs = [(t, t ^ (sub * (odd if t // sub % 2 else even))) for t in range(tiles)]
        return lax.ppermute(value, "tile", pairs)

    def across(value, k):
        return lax.ppermute(value.astype(BF16), "region", [(r, r ^ k) for r in range(regions)])

    def near(keep, send):
        bit = 1
        while bit < sub:
            pairs = [(t, t ^ bit) for t in range(tiles)]
            keep, send = (v + lax.ppermute(v, "tile", pairs) for v in (keep, send))
            bit *= 2
        return keep, swap(send, 1, 1)

    def both(pair, part):
        return pair[0][part].astype(F32) + pair[1][part].astype(F32)

    low, top = slice(0, blocks // 4), slice(blocks // 4, blocks // 2)
    def after(value, other):
        return value if other is None else lax.optimization_barrier((value, other))[0]

    cores, firsts, seconds = ([None] * regions for _ in range(3))
    incoming = [[] for _ in range(regions)]
    own = None
    for slot in range(regions + 3):
        done, operands = None, []
        if slot < regions:
            k = regions - 1 - slot
            keep, send, *made = assemble((k,), sub, inputs, global_deriv, blocks, regions)
            inputs = tuple(made) if made else inputs
            done = send
        elif slot == regions:
            cores[0] = after(cores[0], seconds[2][1])
            done = both(cores[0], top)[:, 0].astype(BF16)
        k = regions - 1 - (slot - 3)

        def lowered(k, done):
            total = both(cores[k], low)[:, 0] + after(firsts[k], done).astype(F32)
            seconds[k] = total[0], swap(total[1].astype(BF16), 4, 2)
            return total[1].astype(BF16)

        if slot > regions and k > 0:
            lowered(k - 1, done)
        if 0 <= k < regions:
            total = seconds[k][0] + after(seconds[k][1], done).astype(F32)
            if k:
                for value in incoming[k]:
                    total = total + value.astype(F32)
                operands.append(total.astype(BF16))
                incoming[k - (k & -k)].append(across(operands[-1], k & -k))
            else:
                own = total
        k -= 1
        if 0 <= k < regions and slot <= regions:
            operands.append(lowered(k, (done, operands) if slot == regions else done))
        k -= 1
        if 0 <= k < regions:
            if slot < regions:
                cores[k] = after(cores[k], (done, operands) if slot == regions - 1 else done)
            operands.append(both(cores[k], top)[:, 0].astype(BF16))
            firsts[k] = swap(operands[-1], 2, 4)
        if slot < regions:
            inputs = inputs[0], after(inputs[1], (send, operands))
            cores[k - 1] = near(keep, send)

    def onward(value, d):
        pairs = [
            (p * sub + s, ((p + d) % blocks) * sub + s) for p in range(blocks) for s in range(sub)
        ]
        return lax.ppermute(value, "tile", pairs)

    own, *sends = gather(own, incoming[0], blocks)
    matrix, vector = finish(sub, own, *(onward(v, d + 1) for d, v in enumerate(sends)), blocks)
    if sub > 1:
        part = tile % sub
        rows = width // sub
        matrix = lax.dynamic_slice(matrix, (part * rows, 0), (rows, blocks * width))
        vector = lax.dynamic_slice(vector, (0, part * rows), (1, rows))
    return matrix[None], vector


def solution(mesh):
    return jax.shard_map(
        functools.partial(local, mesh.shape["tile"]),
        mesh=mesh,
        in_specs=(
            P(("region", "tile"), None, None),
            P(("region", "tile"), None, None),
            P(("region", "tile"), None),
            P(("region", "tile"), None),
            P(("region", "tile"), None),
            P(("region", "tile")),
            P(("region", "tile"), None),
            P(),
        ),
        out_specs=(P("region", "tile", None), P("region", "tile")),
        check_vma=False,
    )
```

```python
import functools
import jax
import jax.numpy as jnp
from jax import lax
from jax.experimental import pallas as pl
from jax.experimental.pallas import tpu as pltpu
from jax.sharding import PartitionSpec as P

F32 = jnp.float32
BF16 = jnp.bfloat16
GROUP = 8
PAIR = 2 * GROUP
DEPTH = 256

NT = (((1,), (1,)), ((), ()))


def iota(shape, axis):
    return lax.broadcasted_iota(jnp.int32, shape, axis)


def fit(ld, weight, resid, counts):
    hits = weight.shape[0]
    live = iota(weight.shape, 0) < counts.astype(jnp.int32)
    masked_w = jnp.where(live, weight, 0.0)
    weighted_l = [v * masked_w for v in ld]
    gamma = [[None] * 5 for _ in range(5)]
    for a in range(5):
        for b in range(a + 1):
            gamma[a][b] = jnp.sum(weighted_l[a] * ld[b], axis=0, keepdims=True)
            if a == b:
                gamma[a][b] = gamma[a][b] + 1.0
    beta = [jnp.sum(weighted_l[a] * resid, axis=0, keepdims=True) for a in range(5)]
    factor = [[None] * 5 for _ in range(5)]
    inverse = [None] * 5
    for j in range(5):
        center = gamma[j][j]
        for k in range(j):
            center = center - factor[j][k] * factor[j][k]
        factor[j][j] = jnp.sqrt(center)
        inverse[j] = 1.0 / factor[j][j]
        for i in range(j + 1, 5):
            offdiag = gamma[i][j]
            for k in range(j):
                offdiag = offdiag - factor[i][k] * factor[j][k]
            factor[i][j] = offdiag * inverse[j]
    solved, rhs = [], []
    for j in range(5):
        current, target = weighted_l[j], beta[j]
        for k in range(j):
            current = current - factor[j][k] * solved[k]
            target = target - factor[j][k] * rhs[k]
        solved.append(current * inverse[j])
        rhs.append(target * inverse[j])
    projection = solved[0] * rhs[0]
    for k in range(1, 5):
        projection = projection + solved[k] * rhs[k]
    return solved, masked_w * resid - projection, masked_w


def prepare(
    place_ref, region_ref, count_ref, ld_ref, weight_ref, resid_ref, ids_ref, shared_ref, table_ref,
    table_copy,
):
    tracks = region_ref.shape[1]
    slots = table_ref.shape[1]
    groups = slots // GROUP
    hits = weight_ref.shape[0]
    depth = hits * GROUP
    lanes_at, column_at = groups * 5 * GROUP, groups * (5 * GROUP + 4)
    blocks = place_ref.shape[0]
    rr = table_ref.shape[0] - 8
    member = (iota((rr, tracks), 0) == region_ref[...]).astype(F32)
    before = (iota((tracks, tracks), 0) < iota((tracks, tracks), 1)).astype(F32).astype(BF16)
    rank = jnp.dot(member.astype(BF16), before, preferred_element_type=F32)
    count = jnp.sum(member, axis=1, keepdims=True)
    room = (count.astype(jnp.int32) + (PAIR - 1)) & -PAIR
    room = jnp.broadcast_to(room.astype(F32), (rr, slots))
    lower = (iota((rr, rr), 1) < iota((rr, rr), 0)).astype(F32)
    start = jnp.zeros((rr, slots), F32)
    for g in range(rr):
        start = start + lower[:, g : g + 1] * room[g : g + 1, :]
    slot = jnp.sum(member * (rank + start[:, 0:1]), axis=0, keepdims=True)
    perm = (iota((slots, tracks), 0) == slot.astype(jnp.int32)).astype(F32).astype(BF16)
    numbers = jnp.where(
        iota((8, tracks), 0) == 0, iota((8, tracks), 1), jnp.broadcast_to(count_ref[...], (8, tracks))
    )

    def sort(value):
        return lax.dot_general(value, perm, NT, preferred_element_type=F32)

    numbers = sort(numbers.astype(F32).astype(BF16))
    table_ref[0:8, :] = numbers.astype(jnp.int32)
    table_ref[8:, :] = jnp.where(
        iota((rr, slots), 1) == 0, start.astype(jnp.int32), (start + room).astype(jnp.int32)
    )
    table_copy.start()
    flat = sort(ld_ref[...])
    ld = [flat[c * hits : (c + 1) * hits] for c in range(5)]
    solved, hit_factor, masked_w = fit(
        ld, sort(weight_ref[...]), sort(resid_ref[...]), numbers[1:2]
    )
    ids = sort(ids_ref[...].astype(F32).astype(BF16))
    position = jnp.zeros_like(ids)
    for b in range(blocks):
        position = jnp.where(ids == float(b), place_ref[b].astype(F32), position)
    own = (iota((depth, slots), 0) // hits) == (iota((depth, slots), 1) % GROUP)

    def spread_out(value):
        return jnp.where(own, jnp.concatenate([value] * GROUP, axis=0), 0.0)

    grouping = (iota((groups, slots), 1) // GROUP == iota((groups, slots), 0)).astype(F32)
    for n, value in enumerate((masked_w, hit_factor)):
        value = lax.dot_general(
            grouping.astype(BF16), spread_out(value).astype(BF16), NT, preferred_element_type=F32
        )
        for half in range(2):
            at = lanes_at + (2 * n + half) * groups
            shared_ref[at : at + groups, :] = value[:, half * depth // 2 : (half + 1) * depth // 2]
    columns = 128
    grouping = (iota((columns, slots), 1) // GROUP == iota((columns, slots), 0)).astype(F32)
    shared_ref[column_at : column_at + depth, :columns] = lax.dot_general(
        spread_out(position).astype(BF16), grouping.astype(BF16), NT, preferred_element_type=F32
    )
    own = (iota((depth // 2, slots), 0) // hits) == (iota((depth // 2, slots), 1) % (GROUP // 2))
    for c in range(5):
        value = jnp.where(own, jnp.concatenate([solved[c]] * (GROUP // 2), axis=0), 0.0).T
        for g in range(groups):
            at = (g * 5 + c) * GROUP
            shared_ref[at : at + GROUP, :] = value[g * GROUP : (g + 1) * GROUP, :]


def one_step(step, at, table_ref, shared_ref, g_ref, g_s, direct_s, spread_s):
    hits, width = g_ref.shape[1:]
    depth = GROUP * hits
    blocks = spread_s.shape[1] // width
    rows = 5 * GROUP
    head = width + 8
    groups = table_ref.shape[1] // GROUP
    lanes_at, column_at = groups * rows, groups * (rows + 4)
    column = shared_ref[column_at : column_at + depth, :]
    early = iota((rows, depth // 2), 0) % GROUP < GROUP // 2

    def lanes(which, group):
        return jnp.concatenate(
            [
                shared_ref[pl.ds(lanes_at + (2 * which + half) * groups + group, 1), :]
                for half in range(2)
            ],
            axis=1,
        )

    lefts, values, positions = [], [], []
    for u in range(2):
        group = step * 2 + u
        for i in range(GROUP):
            g_s[u, i * hits : (i + 1) * hits, :] = g_ref[table_ref[0, group * GROUP + i]]
        g = g_s[u]
        chosen = jnp.full(column.shape, group, jnp.int32)
        position = jnp.take_along_axis(column, chosen, axis=1, mode="promise_in_bounds")
        turned = g.T.astype(F32)
        weighted = turned * lanes(0, group)
        factor = jnp.where(iota((8, depth), 0) == 0, lanes(1, group), 0.0)
        scaled = shared_ref[pl.ds(pl.multiple_of(group * rows, GROUP), rows), :]
        scaled = jnp.concatenate(
            [jnp.where(early, scaled, 0.0), jnp.where(early, 0.0, scaled)], axis=1
        )
        high = scaled.astype(BF16).astype(F32)
        left = jnp.concatenate(
            [weighted, factor, high, scaled - high, jnp.zeros((8, depth), F32)], axis=0
        )
        lefts.append(left.astype(BF16))
        values.append(g)
        positions.append(position.astype(BF16))
    for p in range(0, blocks, 2):
        columns = slice(p * width, (p + 2) * width)
        direct = direct_s[:, columns]
        for u in range(2):
            right = jnp.concatenate(
                [
                    jnp.where(positions[u] == jnp.bfloat16(q), values[u], jnp.bfloat16(0))
                    for q in (p, p + 1)
                ],
                axis=1,
            )
            total = jnp.dot(lefts[u], right, preferred_element_type=F32)
            direct = direct + total[:head]
            spread_s[pl.ds(pl.multiple_of(at + u * rows, GROUP), rows), columns] = (
                total[head : head + rows] + total[head + rows : head + 2 * rows]
            )
        direct_s[:, columns] = direct


EVEN = (0, 4, 2, 6)
ODD = (0, 2, 4, 6)


def lead_kernel(ks, sub, *refs):
    small, g_hbm, (keep_ref, send_ref, shared_ref, table_ref) = refs[:7], refs[7], refs[8:12]
    local_small, g_ref, table_s, sems, scratch = refs[12:19], refs[19], refs[20], refs[21], refs[22:]
    copies = [
        pltpu.make_async_copy(source, target, sems.at[n])
        for n, (source, target) in enumerate([*zip(small, local_small), (g_hbm, g_ref)])
    ]
    for copy in copies:
        copy.start()
    for copy in copies[:-1]:
        copy.wait()
    table_copy = pltpu.make_async_copy(table_ref, table_s, sems.at[0])
    prepare(*local_small, shared_ref, table_ref, table_copy)
    table_copy.wait()
    copies[-1].wait()

    def region(n, carry):
        assemble_region(
            n, ks, sub, table_s, shared_ref, g_ref, keep_ref, send_ref, *scratch
        )
        return carry

    lax.fori_loop(0, len(ks), region, 0)


def follow_kernel(ks, sub, shared_ref, table_ref, g_ref, *refs):
    def region(n, carry):
        assemble_region(n, ks, sub, table_ref, shared_ref, g_ref, *refs)
        return carry

    if len(ks) == 1:
        region(0, 0)
    else:
        lax.fori_loop(0, len(ks), region, 0)


def assemble_region(
    number, ks, sub, table_ref, shared_ref, g_ref,
    keep_ref, send_ref, g_s, direct_s, spread_s, wide_s, turned_s, acc_s,
):
    k = jnp.where(number == 0, ks[0], ks[-1])
    width = g_ref.shape[2]
    blocks = spread_s.shape[1] // width
    many = blocks // 2
    region = lax.axis_index("region") ^ k
    block = lax.axis_index("tile") // sub
    first = table_ref[8 + region, 0] // PAIR
    steps = table_ref[8 + region, 1] // PAIR - first
    direct_s[...] = jnp.zeros_like(direct_s)

    def group_step(n, carry):
        one_step(
            first + n, n * (10 * GROUP), table_ref, shared_ref, g_ref, g_s, direct_s, spread_s
        )
        return carry

    lax.fori_loop(0, steps, group_step, 0)
    used = steps * 10
    depth_tiles = DEPTH // 8
    chunks = jnp.maximum((used + depth_tiles - 1) // depth_tiles, 1)

    def clear(tile, carry):
        spread_s[pl.ds(pl.multiple_of(tile * 8, 8), 8), :] = jnp.zeros((8, blocks * width), F32)
        return carry

    lax.fori_loop(used, chunks * depth_tiles, clear, 0)

    def chunk_step(chunk, carry):
        at = pl.multiple_of(chunk * DEPTH, DEPTH)
        wide_s[...] = spread_s[pl.ds(at, DEPTH), :].astype(BF16)
        for p in range(blocks):
            turned = -wide_s[:, p * width : (p + 1) * width].T
            turned_s[p * width : (p + 1) * width] = turned
            if p < many:
                turned_s[(blocks + p) * width : (blocks + p + 1) * width] = turned

        def products(add):
            for q in range(0, blocks, 2):
                reach = many if q >= many else many - 1
                upper = (q + blocks - reach) % blocks
                value = jnp.dot(
                    turned_s[upper * width : (upper + reach + 2) * width],
                    wide_s[:, q * width : (q + 2) * width],
                    preferred_element_type=F32,
                )
                for r in range(reach + 2):
                    p = (upper + r) % blocks
                    for c in range(2):
                        d = reach - r + c
                        if 0 <= d <= many and (d < many or p < many):
                            part = value[r * width : (r + 1) * width, c * width : (c + 1) * width]
                            columns = slice(d * width, (d + 1) * width)
                            acc_s[p, :, columns] = acc_s[p, :, columns] + part if add else part

        @pl.when(chunk == 0)
        def _():
            products(False)

        @pl.when(chunk > 0)
        def _():
            products(True)

        return carry

    lax.fori_loop(0, chunks, chunk_step, 0)
    half = width // 2
    for n in range(blocks // 2):
        for odd, out_ref in ((0, keep_ref), (1, send_ref)):
            p = block ^ (jnp.where(block % 2 == 1 - odd, ODD[n], EVEN[n]) + odd)
            columns = pl.ds(pl.multiple_of(p * width, width), width)
            parts = [direct_s[0:width, columns] + acc_s[p, :, 0:width]]
            parts += [acc_s[p, :, d * width : (d + 1) * width] for d in range(1, many)]
            upper = pl.multiple_of((p // many) * half, half)
            parts.append(acc_s[p % many, pl.ds(upper, half), many * width :])
            row = direct_s[width : width + 1, columns]
            high = row.astype(BF16).astype(F32)
            sub = iota((16, width), 0)
            parts.append(jnp.where(sub == 0, high, jnp.where(sub == 1, row - high, 0.0)))
            out_ref[n, number] = jnp.concatenate(parts, axis=0).astype(BF16)


def assemble(ks, sub, inputs, g, blocks, regions):
    tracks, hits, width = g.shape
    lead = len(inputs) == 7
    rows = width * (blocks // 2) + width // 2 + 16
    longest = -(-(-(-tracks // PAIR) * 5 * PAIR) // DEPTH) * DEPTH
    rr = -(-regions // 8) * 8
    slots = -(-(tracks + regions * (PAIR - 1)) // 128) * 128
    shared = [
        jax.ShapeDtypeStruct(
            (slots // GROUP * (5 * GROUP + 4) + GROUP * hits, GROUP * hits // 2), F32
        ),
        jax.ShapeDtypeStruct((8 + rr, slots), jnp.int32),
    ]
    out = jax.ShapeDtypeStruct((blocks // 2, len(ks), rows, width), BF16)
    vmem = pl.BlockSpec(memory_space=pltpu.VMEM)
    smem = pl.BlockSpec(memory_space=pltpu.SMEM)
    copies = [pltpu.SMEM(inputs[0].shape, jnp.int32)]
    copies += [pltpu.VMEM(value.shape, value.dtype) for value in inputs[1:]]
    copies += [
        pltpu.VMEM(g.shape, g.dtype),
        pltpu.SMEM(shared[1].shape, jnp.int32),
        pltpu.SemaphoreType.DMA((8,)),
    ]
    return pl.pallas_call(
        functools.partial(lead_kernel if lead else follow_kernel, ks, sub),
        in_specs=[pl.BlockSpec(memory_space=pltpu.HBM)] * 8 if lead else [vmem, smem, vmem],
        out_specs=[vmem] * (4 if lead else 2),
        out_shape=[out, out] + shared * lead,
        scratch_shapes=copies * lead
        + [
            pltpu.VMEM((2, GROUP * hits, width), BF16),
            pltpu.VMEM((width + 8, blocks * width), F32),
            pltpu.VMEM((longest, blocks * width), F32),
            pltpu.VMEM((DEPTH, blocks * width), BF16),
            pltpu.VMEM(((blocks + blocks // 2) * width, DEPTH), BF16),
            pltpu.VMEM((blocks, width, (blocks // 2 + 1) * width), F32),
        ],
        compiler_params=pltpu.CompilerParams(vmem_limit_bytes=(60 if lead else 28) * 1024 * 1024),
        cost_estimate=pl.CostEstimate(
            flops=10**9 * len(ks), bytes_accessed=4 * 10**6, transcendentals=0
        ),
        name="assemble",
    )(*inputs, g)


def finish_kernel(sub, own_ref, r1_ref, r2_ref, r3_ref, e_ref, out_ref, vec_ref):
    width = own_ref.shape[1]
    p = lax.axis_index("tile") // sub
    blocks = out_ref.shape[1] // width
    many = blocks // 2

    def put(column, value):
        column = pl.multiple_of(((column + blocks) % blocks) * width, width)
        out_ref[:, pl.ds(column, width)] = value

    for d in range(many):
        put(p + d, own_ref[d * width : (d + 1) * width, :])
    for d, ref in ((1, r1_ref), (2, r2_ref), (3, r3_ref)):
        put(p - d, ref[...].astype(F32).T)
    tail = many * width + width // 2
    mine = own_ref[many * width : tail, :]
    other = e_ref[...].astype(F32)

    @pl.when(p < many)
    def _():
        put(p + many, jnp.concatenate([mine, other], axis=0))

    @pl.when(p >= many)
    def _():
        put(p + many, jnp.concatenate([other, mine], axis=0).T)

    vec_ref[...] = own_ref[tail : tail + 1, :] + own_ref[tail + 1 : tail + 2, :]


def gather_kernel(number, own_ref, *refs):
    crossed, total_ref, sends = refs[:number], refs[number], refs[number + 1 :]
    width = own_ref.shape[1]
    total = own_ref[...]
    for ref in crossed:
        total = total + ref[...].astype(F32)
    total_ref[...] = total
    for n, ref in enumerate(sends):
        at = (n + 1) * width
        ref[...] = total[at : at + ref.shape[0]].astype(BF16)


def gather(own, crossed, blocks):
    width = own.shape[1]
    vmem = pl.BlockSpec(memory_space=pltpu.VMEM)
    rows = [width] * (blocks // 2 - 1) + [width // 2]
    return pl.pallas_call(
        functools.partial(gather_kernel, len(crossed)),
        in_specs=[vmem] * (1 + len(crossed)),
        out_specs=[vmem] * (1 + len(rows)),
        out_shape=[jax.ShapeDtypeStruct(own.shape, F32)]
        + [jax.ShapeDtypeStruct((n, width), BF16) for n in rows],
        compiler_params=pltpu.CompilerParams(vmem_limit_bytes=8 * 1024 * 1024),
        name="gather",
    )(own, *crossed)


def finish(sub, own, r1, r2, r3, ext, blocks):
    width = own.shape[1]
    vmem = pl.BlockSpec(memory_space=pltpu.VMEM)
    return pl.pallas_call(
        functools.partial(finish_kernel, sub),
        in_specs=[vmem] * 5,
        out_specs=[vmem, vmem],
        out_shape=[
            jax.ShapeDtypeStruct((width, blocks * width), F32),
            jax.ShapeDtypeStruct((1, width), F32),
        ],
        compiler_params=pltpu.CompilerParams(vmem_limit_bytes=8 * 1024 * 1024),
        name="finish",
    )(own, r1, r2, r3, ext)


def local(
    tiles, global_deriv, local_deriv, hit_weight, hit_resid, block_ids, hit_count, track_region,
    block_place,
):
    regions = lax.axis_size("region")
    tracks, hits, width = global_deriv.shape
    blocks = block_place.shape[0]
    sub = tiles // blocks
    tile = lax.axis_index("tile")
    inputs = (
        block_place,
        track_region.reshape(1, tracks),
        hit_count.reshape(1, tracks),
        local_deriv.transpose(1, 2, 0).reshape(-1, tracks),
        hit_weight.T,
        hit_resid.T,
        block_ids.T,
    )

    def swap(value, even, odd):
        pairs = [(t, t ^ (sub * (odd if t // sub % 2 else even))) for t in range(tiles)]
        return lax.ppermute(value, "tile", pairs)

    def across(value, k):
        return lax.ppermute(value.astype(BF16), "region", [(r, r ^ k) for r in range(regions)])

    def near(keep, send):
        bit = 1
        while bit < sub:
            pairs = [(t, t ^ bit) for t in range(tiles)]
            keep, send = (v + lax.ppermute(v, "tile", pairs) for v in (keep, send))
            bit *= 2
        return keep, swap(send, 1, 1)

    def both(pair, part):
        return pair[0][part].astype(F32) + pair[1][part].astype(F32)

    low, top = slice(0, blocks // 4), slice(blocks // 4, blocks // 2)
    def after(value, other):
        return value if other is None else lax.optimization_barrier((value, other))[0]

    cores, firsts, seconds = ([None] * regions for _ in range(3))
    incoming = [[] for _ in range(regions)]
    own = None
    for slot in range(regions + 3):
        done, operands = None, []
        if slot < regions:
            k = regions - 1 - slot
            keep, send, *made = assemble((k,), sub, inputs, global_deriv, blocks, regions)
            inputs = tuple(made) if made else inputs
            done = send
        elif slot == regions:
            done = both(cores[0], top)[:, 0].astype(BF16)
        k = regions - 1 - (slot - 3)

        def lowered(k, done):
            total = both(cores[k], low)[:, 0] + after(firsts[k], done).astype(F32)
            seconds[k] = total[0], swap(total[1].astype(BF16), 4, 2)
            return total[1].astype(BF16)

        if slot > regions and k > 0:
            done = lowered(k - 1, done)
        if 0 <= k < regions:
            total = seconds[k][0] + after(seconds[k][1], done).astype(F32)
            if k:
                for value in incoming[k]:
                    total = total + value.astype(F32)
                operands.append(total.astype(BF16))
                incoming[k - (k & -k)].append(across(operands[-1], k & -k))
            else:
                own = total
        k -= 1
        if 0 <= k < regions and slot <= regions:
            operands.append(lowered(k, (done, operands) if slot == regions else done))
        k -= 1
        if 0 <= k < regions:
            if slot < regions:
                cores[k] = after(cores[k], (done, operands) if slot == regions - 1 else done)
            operands.append(both(cores[k], top)[:, 0].astype(BF16))
            firsts[k] = swap(operands[-1], 2, 4)
        if slot < regions:
            inputs = inputs[0], after(inputs[1], (send, operands))
            cores[k - 1] = near(keep, send)

    def onward(value, d):
        pairs = [
            (p * sub + s, ((p + d) % blocks) * sub + s) for p in range(blocks) for s in range(sub)
        ]
        return lax.ppermute(value, "tile", pairs)

    own, *sends = gather(own, incoming[0], blocks)
    matrix, vector = finish(sub, own, *(onward(v, d + 1) for d, v in enumerate(sends)), blocks)
    if sub > 1:
        part = tile % sub
        rows = width // sub
        matrix = lax.dynamic_slice(matrix, (part * rows, 0), (rows, blocks * width))
        vector = lax.dynamic_slice(vector, (0, part * rows), (1, rows))
    return matrix[None], vector


def solution(mesh):
    return jax.shard_map(
        functools.partial(local, mesh.shape["tile"]),
        mesh=mesh,
        in_specs=(
            P(("region", "tile"), None, None),
            P(("region", "tile"), None, None),
            P(("region", "tile"), None),
            P(("region", "tile"), None),
            P(("region", "tile"), None),
            P(("region", "tile")),
            P(("region", "tile"), None),
            P(),
        ),
        out_specs=(P("region", "tile", None), P("region", "tile")),
        check_vma=False,
    )
```

```python
import functools
import jax
import jax.numpy as jnp
from jax import lax
from jax.experimental import pallas as pl
from jax.experimental.pallas import tpu as pltpu
from jax.sharding import PartitionSpec as P

F32 = jnp.float32
BF16 = jnp.bfloat16
GROUP = 8
PAIR = 2 * GROUP
DEPTH = 256

NT = (((1,), (1,)), ((), ()))


def iota(shape, axis):
    return lax.broadcasted_iota(jnp.int32, shape, axis)


def fit(ld, weight, resid, counts):
    hits = weight.shape[0]
    live = iota(weight.shape, 0) < counts.astype(jnp.int32)
    masked_w = jnp.where(live, weight, 0.0)
    weighted_l = [v * masked_w for v in ld]
    gamma = [[None] * 5 for _ in range(5)]
    for a in range(5):
        for b in range(a + 1):
            gamma[a][b] = jnp.sum(weighted_l[a] * ld[b], axis=0, keepdims=True)
            if a == b:
                gamma[a][b] = gamma[a][b] + 1.0
    beta = [jnp.sum(weighted_l[a] * resid, axis=0, keepdims=True) for a in range(5)]
    factor = [[None] * 5 for _ in range(5)]
    inverse = [None] * 5
    for j in range(5):
        center = gamma[j][j]
        for k in range(j):
            center = center - factor[j][k] * factor[j][k]
        factor[j][j] = jnp.sqrt(center)
        inverse[j] = 1.0 / factor[j][j]
        for i in range(j + 1, 5):
            offdiag = gamma[i][j]
            for k in range(j):
                offdiag = offdiag - factor[i][k] * factor[j][k]
            factor[i][j] = offdiag * inverse[j]
    solved, rhs = [], []
    for j in range(5):
        current, target = weighted_l[j], beta[j]
        for k in range(j):
            current = current - factor[j][k] * solved[k]
            target = target - factor[j][k] * rhs[k]
        solved.append(current * inverse[j])
        rhs.append(target * inverse[j])
    projection = solved[0] * rhs[0]
    for k in range(1, 5):
        projection = projection + solved[k] * rhs[k]
    return solved, masked_w * resid - projection, masked_w


def prepare(
    place_ref, region_ref, count_ref, ld_ref, weight_ref, resid_ref, ids_ref, shared_ref, table_ref,
    table_copy,
):
    tracks = region_ref.shape[1]
    slots = table_ref.shape[1]
    groups = slots // GROUP
    hits = weight_ref.shape[0]
    depth = hits * GROUP
    lanes_at, column_at = groups * 5 * GROUP, groups * (5 * GROUP + 4)
    blocks = place_ref.shape[0]
    rr = table_ref.shape[0] - 8
    member = (iota((rr, tracks), 0) == region_ref[...]).astype(F32)
    before = (iota((tracks, tracks), 0) < iota((tracks, tracks), 1)).astype(F32).astype(BF16)
    rank = jnp.dot(member.astype(BF16), before, preferred_element_type=F32)
    count = jnp.sum(member, axis=1, keepdims=True)
    room = (count.astype(jnp.int32) + (PAIR - 1)) & -PAIR
    room = jnp.broadcast_to(room.astype(F32), (rr, slots))
    lower = (iota((rr, rr), 1) < iota((rr, rr), 0)).astype(F32)
    start = jnp.zeros((rr, slots), F32)
    for g in range(rr):
        start = start + lower[:, g : g + 1] * room[g : g + 1, :]
    slot = jnp.sum(member * (rank + start[:, 0:1]), axis=0, keepdims=True)
    perm = (iota((slots, tracks), 0) == slot.astype(jnp.int32)).astype(F32).astype(BF16)
    numbers = jnp.where(
        iota((8, tracks), 0) == 0, iota((8, tracks), 1), jnp.broadcast_to(count_ref[...], (8, tracks))
    )

    def sort(value):
        return lax.dot_general(value, perm, NT, preferred_element_type=F32)

    numbers = sort(numbers.astype(F32).astype(BF16))
    table_ref[0:8, :] = numbers.astype(jnp.int32)
    table_ref[8:, :] = jnp.where(
        iota((rr, slots), 1) == 0, start.astype(jnp.int32), (start + room).astype(jnp.int32)
    )
    table_copy.start()
    flat = sort(ld_ref[...])
    ld = [flat[c * hits : (c + 1) * hits] for c in range(5)]
    solved, hit_factor, masked_w = fit(
        ld, sort(weight_ref[...]), sort(resid_ref[...]), numbers[1:2]
    )
    ids = sort(ids_ref[...].astype(F32).astype(BF16))
    position = jnp.zeros_like(ids)
    for b in range(blocks):
        position = jnp.where(ids == float(b), place_ref[b].astype(F32), position)
    own = (iota((depth, slots), 0) // hits) == (iota((depth, slots), 1) % GROUP)

    def spread_out(value):
        return jnp.where(own, jnp.concatenate([value] * GROUP, axis=0), 0.0)

    grouping = (iota((groups, slots), 1) // GROUP == iota((groups, slots), 0)).astype(F32)
    for n, value in enumerate((masked_w, hit_factor)):
        value = lax.dot_general(
            grouping.astype(BF16), spread_out(value).astype(BF16), NT, preferred_element_type=F32
        )
        for half in range(2):
            at = lanes_at + (2 * n + half) * groups
            shared_ref[at : at + groups, :] = value[:, half * depth // 2 : (half + 1) * depth // 2]
    columns = 128
    grouping = (iota((columns, slots), 1) // GROUP == iota((columns, slots), 0)).astype(F32)
    shared_ref[column_at : column_at + depth, :columns] = lax.dot_general(
        spread_out(position).astype(BF16), grouping.astype(BF16), NT, preferred_element_type=F32
    )
    own = (iota((depth // 2, slots), 0) // hits) == (iota((depth // 2, slots), 1) % (GROUP // 2))
    for c in range(5):
        value = jnp.where(own, jnp.concatenate([solved[c]] * (GROUP // 2), axis=0), 0.0).T
        for g in range(groups):
            at = (g * 5 + c) * GROUP
            shared_ref[at : at + GROUP, :] = value[g * GROUP : (g + 1) * GROUP, :]


def one_step(step, at, table_ref, shared_ref, g_ref, g_s, direct_s, spread_s):
    hits, width = g_ref.shape[1:]
    depth = GROUP * hits
    blocks = spread_s.shape[1] // width
    rows = 5 * GROUP
    head = width + 8
    groups = table_ref.shape[1] // GROUP
    lanes_at, column_at = groups * rows, groups * (rows + 4)
    column = shared_ref[column_at : column_at + depth, :]
    early = iota((rows, depth // 2), 0) % GROUP < GROUP // 2

    def lanes(which, group):
        return jnp.concatenate(
            [
                shared_ref[pl.ds(lanes_at + (2 * which + half) * groups + group, 1), :]
                for half in range(2)
            ],
            axis=1,
        )

    lefts, values, positions = [], [], []
    for u in range(2):
        group = step * 2 + u
        for i in range(GROUP):
            g_s[u, i * hits : (i + 1) * hits, :] = g_ref[table_ref[0, group * GROUP + i]]
        g = g_s[u]
        chosen = jnp.full(column.shape, group, jnp.int32)
        position = jnp.take_along_axis(column, chosen, axis=1, mode="promise_in_bounds")
        turned = g.T.astype(F32)
        weighted = turned * lanes(0, group)
        factor = jnp.where(iota((8, depth), 0) == 0, lanes(1, group), 0.0)
        scaled = shared_ref[pl.ds(pl.multiple_of(group * rows, GROUP), rows), :]
        scaled = jnp.concatenate(
            [jnp.where(early, scaled, 0.0), jnp.where(early, 0.0, scaled)], axis=1
        )
        high = scaled.astype(BF16).astype(F32)
        left = jnp.concatenate(
            [weighted, factor, high, scaled - high, jnp.zeros((8, depth), F32)], axis=0
        )
        lefts.append(left.astype(BF16))
        values.append(g)
        positions.append(position.astype(BF16))
    for p in range(0, blocks, 2):
        columns = slice(p * width, (p + 2) * width)
        direct = direct_s[:, columns]
        for u in range(2):
            right = jnp.concatenate(
                [
                    jnp.where(positions[u] == jnp.bfloat16(q), values[u], jnp.bfloat16(0))
                    for q in (p, p + 1)
                ],
                axis=1,
            )
            total = jnp.dot(lefts[u], right, preferred_element_type=F32)
            direct = direct + total[:head]
            spread_s[pl.ds(pl.multiple_of(at + u * rows, GROUP), rows), columns] = (
                total[head : head + rows] + total[head + rows : head + 2 * rows]
            )
        direct_s[:, columns] = direct


EVEN = (0, 4, 2, 6)
ODD = (0, 2, 4, 6)


def lead_kernel(ks, sub, *refs):
    small, g_hbm, (keep_ref, send_ref, shared_ref, table_ref) = refs[:7], refs[7], refs[8:12]
    local_small, g_ref, table_s, sems, scratch = refs[12:19], refs[19], refs[20], refs[21], refs[22:]
    copies = [
        pltpu.make_async_copy(source, target, sems.at[n])
        for n, (source, target) in enumerate([*zip(small, local_small), (g_hbm, g_ref)])
    ]
    for copy in copies:
        copy.start()
    for copy in copies[:-1]:
        copy.wait()
    table_copy = pltpu.make_async_copy(table_ref, table_s, sems.at[0])
    prepare(*local_small, shared_ref, table_ref, table_copy)
    table_copy.wait()
    copies[-1].wait()

    def region(n, carry):
        assemble_region(
            n, ks, sub, table_s, shared_ref, g_ref, keep_ref, send_ref, *scratch
        )
        return carry

    lax.fori_loop(0, len(ks), region, 0)


def follow_kernel(ks, sub, shared_ref, table_ref, g_ref, *refs):
    def region(n, carry):
        assemble_region(n, ks, sub, table_ref, shared_ref, g_ref, *refs)
        return carry

    if len(ks) == 1:
        region(0, 0)
    else:
        lax.fori_loop(0, len(ks), region, 0)


def assemble_region(
    number, ks, sub, table_ref, shared_ref, g_ref,
    keep_ref, send_ref, g_s, direct_s, spread_s, wide_s, turned_s, acc_s,
):
    k = jnp.where(number == 0, ks[0], ks[-1])
    width = g_ref.shape[2]
    blocks = spread_s.shape[1] // width
    many = blocks // 2
    region = lax.axis_index("region") ^ k
    block = lax.axis_index("tile") // sub
    first = table_ref[8 + region, 0] // PAIR
    steps = table_ref[8 + region, 1] // PAIR - first
    direct_s[...] = jnp.zeros_like(direct_s)

    def group_step(n, carry):
        one_step(
            first + n, n * (10 * GROUP), table_ref, shared_ref, g_ref, g_s, direct_s, spread_s
        )
        return carry

    lax.fori_loop(0, steps, group_step, 0)
    used = steps * 10
    depth_tiles = DEPTH // 8
    chunks = jnp.maximum((used + depth_tiles - 1) // depth_tiles, 1)

    def clear(tile, carry):
        spread_s[pl.ds(pl.multiple_of(tile * 8, 8), 8), :] = jnp.zeros((8, blocks * width), F32)
        return carry

    lax.fori_loop(used, chunks * depth_tiles, clear, 0)

    def chunk_step(chunk, carry):
        at = pl.multiple_of(chunk * DEPTH, DEPTH)
        wide_s[...] = spread_s[pl.ds(at, DEPTH), :].astype(BF16)
        for p in range(blocks):
            turned = -wide_s[:, p * width : (p + 1) * width].T
            turned_s[p * width : (p + 1) * width] = turned
            if p < many:
                turned_s[(blocks + p) * width : (blocks + p + 1) * width] = turned

        def products(add):
            for q in range(0, blocks, 2):
                reach = many if q >= many else many - 1
                upper = (q + blocks - reach) % blocks
                value = jnp.dot(
                    turned_s[upper * width : (upper + reach + 2) * width],
                    wide_s[:, q * width : (q + 2) * width],
                    preferred_element_type=F32,
                )
                for r in range(reach + 2):
                    p = (upper + r) % blocks
                    for c in range(2):
                        d = reach - r + c
                        if 0 <= d <= many and (d < many or p < many):
                            part = value[r * width : (r + 1) * width, c * width : (c + 1) * width]
                            columns = slice(d * width, (d + 1) * width)
                            acc_s[p, :, columns] = acc_s[p, :, columns] + part if add else part

        @pl.when(chunk == 0)
        def _():
            products(False)

        @pl.when(chunk > 0)
        def _():
            products(True)

        return carry

    lax.fori_loop(0, chunks, chunk_step, 0)
    half = width // 2
    for n in range(blocks // 2):
        for odd, out_ref in ((0, keep_ref), (1, send_ref)):
            p = block ^ (jnp.where(block % 2 == 1 - odd, ODD[n], EVEN[n]) + odd)
            columns = pl.ds(pl.multiple_of(p * width, width), width)
            parts = [direct_s[0:width, columns] + acc_s[p, :, 0:width]]
            parts += [acc_s[p, :, d * width : (d + 1) * width] for d in range(1, many)]
            upper = pl.multiple_of((p // many) * half, half)
            parts.append(acc_s[p % many, pl.ds(upper, half), many * width :])
            row = direct_s[width : width + 1, columns]
            high = row.astype(BF16).astype(F32)
            sub = iota((16, width), 0)
            parts.append(jnp.where(sub == 0, high, jnp.where(sub == 1, row - high, 0.0)))
            out_ref[n, number] = jnp.concatenate(parts, axis=0).astype(BF16)


def assemble(ks, sub, inputs, g, blocks, regions):
    tracks, hits, width = g.shape
    lead = len(inputs) == 7
    rows = width * (blocks // 2) + width // 2 + 16
    longest = -(-(-(-tracks // PAIR) * 5 * PAIR) // DEPTH) * DEPTH
    rr = -(-regions // 8) * 8
    slots = -(-(tracks + regions * (PAIR - 1)) // 128) * 128
    shared = [
        jax.ShapeDtypeStruct(
            (slots // GROUP * (5 * GROUP + 4) + GROUP * hits, GROUP * hits // 2), F32
        ),
        jax.ShapeDtypeStruct((8 + rr, slots), jnp.int32),
    ]
    out = jax.ShapeDtypeStruct((blocks // 2, len(ks), rows, width), BF16)
    vmem = pl.BlockSpec(memory_space=pltpu.VMEM)
    smem = pl.BlockSpec(memory_space=pltpu.SMEM)
    copies = [pltpu.SMEM(inputs[0].shape, jnp.int32)]
    copies += [pltpu.VMEM(value.shape, value.dtype) for value in inputs[1:]]
    copies += [
        pltpu.VMEM(g.shape, g.dtype),
        pltpu.SMEM(shared[1].shape, jnp.int32),
        pltpu.SemaphoreType.DMA((8,)),
    ]
    return pl.pallas_call(
        functools.partial(lead_kernel if lead else follow_kernel, ks, sub),
        in_specs=[pl.BlockSpec(memory_space=pltpu.HBM)] * 8 if lead else [vmem, smem, vmem],
        out_specs=[vmem] * (4 if lead else 2),
        out_shape=[out, out] + shared * lead,
        scratch_shapes=copies * lead
        + [
            pltpu.VMEM((2, GROUP * hits, width), BF16),
            pltpu.VMEM((width + 8, blocks * width), F32),
            pltpu.VMEM((longest, blocks * width), F32),
            pltpu.VMEM((DEPTH, blocks * width), BF16),
            pltpu.VMEM(((blocks + blocks // 2) * width, DEPTH), BF16),
            pltpu.VMEM((blocks, width, (blocks // 2 + 1) * width), F32),
        ],
        compiler_params=pltpu.CompilerParams(vmem_limit_bytes=(60 if lead else 28) * 1024 * 1024),
        cost_estimate=pl.CostEstimate(
            flops=10**9 * len(ks), bytes_accessed=4 * 10**6, transcendentals=0
        ),
        name="assemble",
    )(*inputs, g)


def finish_kernel(sub, own_ref, r1_ref, r2_ref, r3_ref, e_ref, out_ref, vec_ref):
    width = own_ref.shape[1]
    p = lax.axis_index("tile") // sub
    blocks = out_ref.shape[1] // width
    many = blocks // 2

    def put(column, value):
        column = pl.multiple_of(((column + blocks) % blocks) * width, width)
        out_ref[:, pl.ds(column, width)] = value

    for d in range(many):
        put(p + d, own_ref[d * width : (d + 1) * width, :])
    for d, ref in ((1, r1_ref), (2, r2_ref), (3, r3_ref)):
        put(p - d, ref[...].astype(F32).T)
    tail = many * width + width // 2
    mine = own_ref[many * width : tail, :]
    other = e_ref[...].astype(F32)

    @pl.when(p < many)
    def _():
        put(p + many, jnp.concatenate([mine, other], axis=0))

    @pl.when(p >= many)
    def _():
        put(p + many, jnp.concatenate([other, mine], axis=0).T)

    vec_ref[...] = own_ref[tail : tail + 1, :] + own_ref[tail + 1 : tail + 2, :]


def gather_kernel(number, own_ref, *refs):
    crossed, total_ref, sends = refs[:number], refs[number], refs[number + 1 :]
    width = own_ref.shape[1]
    total = own_ref[...]
    for ref in crossed:
        total = total + ref[...].astype(F32)
    total_ref[...] = total
    for n, ref in enumerate(sends):
        at = (n + 1) * width
        ref[...] = total[at : at + ref.shape[0]].astype(BF16)


def gather(own, crossed, blocks):
    width = own.shape[1]
    vmem = pl.BlockSpec(memory_space=pltpu.VMEM)
    rows = [width] * (blocks // 2 - 1) + [width // 2]
    return pl.pallas_call(
        functools.partial(gather_kernel, len(crossed)),
        in_specs=[vmem] * (1 + len(crossed)),
        out_specs=[vmem] * (1 + len(rows)),
        out_shape=[jax.ShapeDtypeStruct(own.shape, F32)]
        + [jax.ShapeDtypeStruct((n, width), BF16) for n in rows],
        compiler_params=pltpu.CompilerParams(vmem_limit_bytes=8 * 1024 * 1024),
        name="gather",
    )(own, *crossed)


def finish(sub, own, r1, r2, r3, ext, blocks):
    width = own.shape[1]
    vmem = pl.BlockSpec(memory_space=pltpu.VMEM)
    return pl.pallas_call(
        functools.partial(finish_kernel, sub),
        in_specs=[vmem] * 5,
        out_specs=[vmem, vmem],
        out_shape=[
            jax.ShapeDtypeStruct((width, blocks * width), F32),
            jax.ShapeDtypeStruct((1, width), F32),
        ],
        compiler_params=pltpu.CompilerParams(vmem_limit_bytes=8 * 1024 * 1024),
        name="finish",
    )(own, r1, r2, r3, ext)


def local(
    tiles, global_deriv, local_deriv, hit_weight, hit_resid, block_ids, hit_count, track_region,
    block_place,
):
    regions = lax.axis_size("region")
    tracks, hits, width = global_deriv.shape
    blocks = block_place.shape[0]
    sub = tiles // blocks
    tile = lax.axis_index("tile")
    inputs = (
        block_place,
        track_region.reshape(1, tracks),
        hit_count.reshape(1, tracks),
        local_deriv.transpose(1, 2, 0).reshape(-1, tracks),
        hit_weight.T,
        hit_resid.T,
        block_ids.T,
    )

    def swap(value, even, odd):
        pairs = [(t, t ^ (sub * (odd if t // sub % 2 else even))) for t in range(tiles)]
        return lax.ppermute(value, "tile", pairs)

    def across(value, k):
        return lax.ppermute(value.astype(BF16), "region", [(r, r ^ k) for r in range(regions)])

    def near(keep, send):
        bit = 1
        while bit < sub:
            pairs = [(t, t ^ bit) for t in range(tiles)]
            keep, send = (v + lax.ppermute(v, "tile", pairs) for v in (keep, send))
            bit *= 2
        return keep, swap(send, 1, 1)

    def both(pair, part):
        return pair[0][part].astype(F32) + pair[1][part].astype(F32)

    low, top = slice(0, blocks // 4), slice(blocks // 4, blocks // 2)
    def after(value, other):
        return value if other is None else lax.optimization_barrier((value, other))[0]

    cores, firsts, seconds = ([None] * regions for _ in range(3))
    incoming = [[] for _ in range(regions)]
    own = None
    for slot in range(regions + 3):
        done, operands = None, []
        if slot < regions:
            k = regions - 1 - slot
            keep, send, *made = assemble((k,), sub, inputs, global_deriv, blocks, regions)
            inputs = tuple(made) if made else inputs
            done = send
        elif slot == regions:
            done = both(cores[0], top)[:, 0].astype(BF16)
        k = regions - 1 - (slot - 3)

        def lowered(k, done):
            total = both(cores[k], low)[:, 0] + after(firsts[k], done).astype(F32)
            seconds[k] = total[0], swap(total[1].astype(BF16), 4, 2)
            return total[1].astype(BF16)

        if slot > regions and k > 0:
            done = lowered(k - 1, done)
        if 0 <= k < regions:
            total = seconds[k][0] + after(seconds[k][1], done).astype(F32)
            if k:
                for value in incoming[k]:
                    total = total + value.astype(F32)
                operands.append(total.astype(BF16))
                step = 1 << (k.bit_length() - 1)
                incoming[k - step].append(across(operands[-1], step))
            else:
                own = total
        k -= 1
        if 0 <= k < regions and slot <= regions:
            operands.append(lowered(k, (done, operands) if slot == regions else done))
        k -= 1
        if 0 <= k < regions:
            if slot < regions:
                cores[k] = after(cores[k], (done, operands) if slot == regions - 1 else done)
            operands.append(both(cores[k], top)[:, 0].astype(BF16))
            firsts[k] = swap(operands[-1], 2, 4)
        if slot < regions:
            inputs = inputs[0], after(inputs[1], (send, operands))
            cores[k - 1] = near(keep, send)

    def onward(value, d):
        pairs = [
            (p * sub + s, ((p + d) % blocks) * sub + s) for p in range(blocks) for s in range(sub)
        ]
        return lax.ppermute(value, "tile", pairs)

    own, *sends = gather(own, incoming[0], blocks)
    matrix, vector = finish(sub, own, *(onward(v, d + 1) for d, v in enumerate(sends)), blocks)
    if sub > 1:
        part = tile % sub
        rows = width // sub
        matrix = lax.dynamic_slice(matrix, (part * rows, 0), (rows, blocks * width))
        vector = lax.dynamic_slice(vector, (0, part * rows), (1, rows))
    return matrix[None], vector


def solution(mesh):
    return jax.shard_map(
        functools.partial(local, mesh.shape["tile"]),
        mesh=mesh,
        in_specs=(
            P(("region", "tile"), None, None),
            P(("region", "tile"), None, None),
            P(("region", "tile"), None),
            P(("region", "tile"), None),
            P(("region", "tile"), None),
            P(("region", "tile")),
            P(("region", "tile"), None),
            P(),
        ),
        out_specs=(P("region", "tile", None), P("region", "tile")),
        check_vma=False,
    )
```

```python
import functools
import jax
import jax.numpy as jnp
from jax import lax
from jax.experimental import pallas as pl
from jax.experimental.pallas import tpu as pltpu
from jax.sharding import PartitionSpec as P

F32 = jnp.float32
BF16 = jnp.bfloat16
GROUP = 8
PAIR = 2 * GROUP
DEPTH = 256

NT = (((1,), (1,)), ((), ()))


def iota(shape, axis):
    return lax.broadcasted_iota(jnp.int32, shape, axis)


def fit(ld, weight, resid, counts):
    hits = weight.shape[0]
    live = iota(weight.shape, 0) < counts.astype(jnp.int32)
    masked_w = jnp.where(live, weight, 0.0)
    weighted_l = [v * masked_w for v in ld]
    gamma = [[None] * 5 for _ in range(5)]
    for a in range(5):
        for b in range(a + 1):
            gamma[a][b] = jnp.sum(weighted_l[a] * ld[b], axis=0, keepdims=True)
            if a == b:
                gamma[a][b] = gamma[a][b] + 1.0
    beta = [jnp.sum(weighted_l[a] * resid, axis=0, keepdims=True) for a in range(5)]
    factor = [[None] * 5 for _ in range(5)]
    inverse = [None] * 5
    for j in range(5):
        center = gamma[j][j]
        for k in range(j):
            center = center - factor[j][k] * factor[j][k]
        factor[j][j] = jnp.sqrt(center)
        inverse[j] = 1.0 / factor[j][j]
        for i in range(j + 1, 5):
            offdiag = gamma[i][j]
            for k in range(j):
                offdiag = offdiag - factor[i][k] * factor[j][k]
            factor[i][j] = offdiag * inverse[j]
    solved, rhs = [], []
    for j in range(5):
        current, target = weighted_l[j], beta[j]
        for k in range(j):
            current = current - factor[j][k] * solved[k]
            target = target - factor[j][k] * rhs[k]
        solved.append(current * inverse[j])
        rhs.append(target * inverse[j])
    projection = solved[0] * rhs[0]
    for k in range(1, 5):
        projection = projection + solved[k] * rhs[k]
    return solved, masked_w * resid - projection, masked_w


def prepare(
    place_ref, region_ref, count_ref, ld_ref, weight_ref, resid_ref, ids_ref, shared_ref, table_ref,
    table_copy,
):
    tracks = region_ref.shape[1]
    slots = table_ref.shape[1]
    groups = slots // GROUP
    hits = weight_ref.shape[0]
    depth = hits * GROUP
    lanes_at, column_at = groups * 5 * GROUP, groups * (5 * GROUP + 4)
    blocks = place_ref.shape[0]
    rr = table_ref.shape[0] - 8
    member = (iota((rr, tracks), 0) == region_ref[...]).astype(F32)
    before = (iota((tracks, tracks), 0) < iota((tracks, tracks), 1)).astype(F32).astype(BF16)
    rank = jnp.dot(member.astype(BF16), before, preferred_element_type=F32)
    count = jnp.sum(member, axis=1, keepdims=True)
    room = (count.astype(jnp.int32) + (PAIR - 1)) & -PAIR
    room = jnp.broadcast_to(room.astype(F32), (rr, slots))
    lower = (iota((rr, rr), 1) < iota((rr, rr), 0)).astype(F32)
    start = jnp.zeros((rr, slots), F32)
    for g in range(rr):
        start = start + lower[:, g : g + 1] * room[g : g + 1, :]
    slot = jnp.sum(member * (rank + start[:, 0:1]), axis=0, keepdims=True)
    perm = (iota((slots, tracks), 0) == slot.astype(jnp.int32)).astype(F32).astype(BF16)
    numbers = jnp.where(
        iota((8, tracks), 0) == 0, iota((8, tracks), 1), jnp.broadcast_to(count_ref[...], (8, tracks))
    )

    def sort(value):
        return lax.dot_general(value, perm, NT, preferred_element_type=F32)

    numbers = sort(numbers.astype(F32).astype(BF16))
    table_ref[0:8, :] = numbers.astype(jnp.int32)
    table_ref[8:, :] = jnp.where(
        iota((rr, slots), 1) == 0, start.astype(jnp.int32), (start + room).astype(jnp.int32)
    )
    table_copy.start()
    flat = sort(ld_ref[...])
    ld = [flat[c * hits : (c + 1) * hits] for c in range(5)]
    solved, hit_factor, masked_w = fit(
        ld, sort(weight_ref[...]), sort(resid_ref[...]), numbers[1:2]
    )
    ids = sort(ids_ref[...].astype(F32).astype(BF16))
    position = jnp.zeros_like(ids)
    for b in range(blocks):
        position = jnp.where(ids == float(b), place_ref[b].astype(F32), position)
    own = (iota((depth, slots), 0) // hits) == (iota((depth, slots), 1) % GROUP)

    def spread_out(value):
        return jnp.where(own, jnp.concatenate([value] * GROUP, axis=0), 0.0)

    grouping = (iota((groups, slots), 1) // GROUP == iota((groups, slots), 0)).astype(F32)
    for n, value in enumerate((masked_w, hit_factor)):
        value = lax.dot_general(
            grouping.astype(BF16), spread_out(value).astype(BF16), NT, preferred_element_type=F32
        )
        for half in range(2):
            at = lanes_at + (2 * n + half) * groups
            shared_ref[at : at + groups, :] = value[:, half * depth // 2 : (half + 1) * depth // 2]
    columns = 128
    grouping = (iota((columns, slots), 1) // GROUP == iota((columns, slots), 0)).astype(F32)
    shared_ref[column_at : column_at + depth, :columns] = lax.dot_general(
        spread_out(position).astype(BF16), grouping.astype(BF16), NT, preferred_element_type=F32
    )
    own = (iota((depth // 2, slots), 0) // hits) == (iota((depth // 2, slots), 1) % (GROUP // 2))
    for c in range(5):
        value = jnp.where(own, jnp.concatenate([solved[c]] * (GROUP // 2), axis=0), 0.0).T
        for g in range(groups):
            at = (g * 5 + c) * GROUP
            shared_ref[at : at + GROUP, :] = value[g * GROUP : (g + 1) * GROUP, :]


def one_step(step, at, table_ref, shared_ref, g_ref, g_s, direct_s, spread_s):
    hits, width = g_ref.shape[1:]
    depth = GROUP * hits
    blocks = spread_s.shape[1] // width
    rows = 5 * GROUP
    head = width + 8
    groups = table_ref.shape[1] // GROUP
    lanes_at, column_at = groups * rows, groups * (rows + 4)
    column = shared_ref[column_at : column_at + depth, :]
    early = iota((rows, depth // 2), 0) % GROUP < GROUP // 2

    def lanes(which, group):
        return jnp.concatenate(
            [
                shared_ref[pl.ds(lanes_at + (2 * which + half) * groups + group, 1), :]
                for half in range(2)
            ],
            axis=1,
        )

    lefts, values, positions = [], [], []
    for u in range(2):
        group = step * 2 + u
        for i in range(GROUP):
            g_s[u, i * hits : (i + 1) * hits, :] = g_ref[table_ref[0, group * GROUP + i]]
        g = g_s[u]
        chosen = jnp.full(column.shape, group, jnp.int32)
        position = jnp.take_along_axis(column, chosen, axis=1, mode="promise_in_bounds")
        turned = g.T.astype(F32)
        weighted = turned * lanes(0, group)
        factor = jnp.where(iota((8, depth), 0) == 0, lanes(1, group), 0.0)
        scaled = shared_ref[pl.ds(pl.multiple_of(group * rows, GROUP), rows), :]
        scaled = jnp.concatenate(
            [jnp.where(early, scaled, 0.0), jnp.where(early, 0.0, scaled)], axis=1
        )
        high = scaled.astype(BF16).astype(F32)
        left = jnp.concatenate(
            [weighted, factor, high, scaled - high, jnp.zeros((8, depth), F32)], axis=0
        )
        lefts.append(left.astype(BF16))
        values.append(g)
        positions.append(position.astype(BF16))
    for p in range(0, blocks, 2):
        columns = slice(p * width, (p + 2) * width)
        direct = direct_s[:, columns]
        for u in range(2):
            right = jnp.concatenate(
                [
                    jnp.where(positions[u] == jnp.bfloat16(q), values[u], jnp.bfloat16(0))
                    for q in (p, p + 1)
                ],
                axis=1,
            )
            total = jnp.dot(lefts[u], right, preferred_element_type=F32)
            direct = direct + total[:head]
            spread_s[pl.ds(pl.multiple_of(at + u * rows, GROUP), rows), columns] = (
                total[head : head + rows] + total[head + rows : head + 2 * rows]
            )
        direct_s[:, columns] = direct


EVEN = (0, 4, 2, 6)
ODD = (0, 2, 4, 6)


def lead_kernel(ks, sub, *refs):
    small, g_hbm, (keep_ref, send_ref, shared_ref, table_ref) = refs[:7], refs[7], refs[8:12]
    local_small, g_ref, table_s, sems, scratch = refs[12:19], refs[19], refs[20], refs[21], refs[22:]
    copies = [
        pltpu.make_async_copy(source, target, sems.at[n])
        for n, (source, target) in enumerate([*zip(small, local_small), (g_hbm, g_ref)])
    ]
    for copy in copies:
        copy.start()
    for copy in copies[:-1]:
        copy.wait()
    table_copy = pltpu.make_async_copy(table_ref, table_s, sems.at[0])
    prepare(*local_small, shared_ref, table_ref, table_copy)
    table_copy.wait()
    copies[-1].wait()

    def region(n, carry):
        assemble_region(
            n, ks, sub, table_s, shared_ref, g_ref, keep_ref, send_ref, *scratch
        )
        return carry

    lax.fori_loop(0, len(ks), region, 0)


def follow_kernel(ks, sub, shared_ref, table_ref, g_ref, *refs):
    def region(n, carry):
        assemble_region(n, ks, sub, table_ref, shared_ref, g_ref, *refs)
        return carry

    if len(ks) == 1:
        region(0, 0)
    else:
        lax.fori_loop(0, len(ks), region, 0)


def assemble_region(
    number, ks, sub, table_ref, shared_ref, g_ref,
    keep_ref, send_ref, g_s, direct_s, spread_s, wide_s, turned_s, acc_s,
):
    k = jnp.where(number == 0, ks[0], ks[-1])
    width = g_ref.shape[2]
    blocks = spread_s.shape[1] // width
    many = blocks // 2
    region = lax.axis_index("region") ^ k
    block = lax.axis_index("tile") // sub
    first = table_ref[8 + region, 0] // PAIR
    steps = table_ref[8 + region, 1] // PAIR - first
    direct_s[...] = jnp.zeros_like(direct_s)

    def group_step(n, carry):
        one_step(
            first + n, n * (10 * GROUP), table_ref, shared_ref, g_ref, g_s, direct_s, spread_s
        )
        return carry

    lax.fori_loop(0, steps, group_step, 0)
    used = steps * 10
    depth_tiles = DEPTH // 8
    chunks = jnp.maximum((used + depth_tiles - 1) // depth_tiles, 1)

    def clear(tile, carry):
        spread_s[pl.ds(pl.multiple_of(tile * 8, 8), 8), :] = jnp.zeros((8, blocks * width), F32)
        return carry

    lax.fori_loop(used, chunks * depth_tiles, clear, 0)

    def chunk_step(chunk, carry):
        at = pl.multiple_of(chunk * DEPTH, DEPTH)
        wide_s[...] = spread_s[pl.ds(at, DEPTH), :].astype(BF16)
        for p in range(blocks):
            turned = -wide_s[:, p * width : (p + 1) * width].T
            turned_s[p * width : (p + 1) * width] = turned
            if p < many:
                turned_s[(blocks + p) * width : (blocks + p + 1) * width] = turned

        def products(add):
            for q in range(0, blocks, 2):
                reach = many if q >= many else many - 1
                upper = (q + blocks - reach) % blocks
                value = jnp.dot(
                    turned_s[upper * width : (upper + reach + 2) * width],
                    wide_s[:, q * width : (q + 2) * width],
                    preferred_element_type=F32,
                )
                for r in range(reach + 2):
                    p = (upper + r) % blocks
                    for c in range(2):
                        d = reach - r + c
                        if 0 <= d <= many and (d < many or p < many):
                            part = value[r * width : (r + 1) * width, c * width : (c + 1) * width]
                            columns = slice(d * width, (d + 1) * width)
                            acc_s[p, :, columns] = acc_s[p, :, columns] + part if add else part

        @pl.when(chunk == 0)
        def _():
            products(False)

        @pl.when(chunk > 0)
        def _():
            products(True)

        return carry

    lax.fori_loop(0, chunks, chunk_step, 0)
    half = width // 2
    for n in range(blocks // 2):
        for odd, out_ref in ((0, keep_ref), (1, send_ref)):
            p = block ^ (jnp.where(block % 2 == 1 - odd, ODD[n], EVEN[n]) + odd)
            columns = pl.ds(pl.multiple_of(p * width, width), width)
            parts = [direct_s[0:width, columns] + acc_s[p, :, 0:width]]
            parts += [acc_s[p, :, d * width : (d + 1) * width] for d in range(1, many)]
            upper = pl.multiple_of((p // many) * half, half)
            parts.append(acc_s[p % many, pl.ds(upper, half), many * width :])
            row = direct_s[width : width + 1, columns]
            high = row.astype(BF16).astype(F32)
            sub = iota((16, width), 0)
            parts.append(jnp.where(sub == 0, high, jnp.where(sub == 1, row - high, 0.0)))
            out_ref[n, number] = jnp.concatenate(parts, axis=0).astype(BF16)


def assemble(ks, sub, inputs, g, blocks, regions):
    tracks, hits, width = g.shape
    lead = len(inputs) == 7
    rows = width * (blocks // 2) + width // 2 + 16
    longest = -(-(-(-tracks // PAIR) * 5 * PAIR) // DEPTH) * DEPTH
    rr = -(-regions // 8) * 8
    slots = -(-(tracks + regions * (PAIR - 1)) // 128) * 128
    shared = [
        jax.ShapeDtypeStruct(
            (slots // GROUP * (5 * GROUP + 4) + GROUP * hits, GROUP * hits // 2), F32
        ),
        jax.ShapeDtypeStruct((8 + rr, slots), jnp.int32),
    ]
    out = jax.ShapeDtypeStruct((blocks // 2, len(ks), rows, width), BF16)
    vmem = pl.BlockSpec(memory_space=pltpu.VMEM)
    smem = pl.BlockSpec(memory_space=pltpu.SMEM)
    copies = [pltpu.SMEM(inputs[0].shape, jnp.int32)]
    copies += [pltpu.VMEM(value.shape, value.dtype) for value in inputs[1:]]
    copies += [
        pltpu.VMEM(g.shape, g.dtype),
        pltpu.SMEM(shared[1].shape, jnp.int32),
        pltpu.SemaphoreType.DMA((8,)),
    ]
    return pl.pallas_call(
        functools.partial(lead_kernel if lead else follow_kernel, ks, sub),
        in_specs=[pl.BlockSpec(memory_space=pltpu.HBM)] * 8 if lead else [vmem, smem, vmem],
        out_specs=[vmem] * (4 if lead else 2),
        out_shape=[out, out] + shared * lead,
        scratch_shapes=copies * lead
        + [
            pltpu.VMEM((2, GROUP * hits, width), BF16),
            pltpu.VMEM((width + 8, blocks * width), F32),
            pltpu.VMEM((longest, blocks * width), F32),
            pltpu.VMEM((DEPTH, blocks * width), BF16),
            pltpu.VMEM(((blocks + blocks // 2) * width, DEPTH), BF16),
            pltpu.VMEM((blocks, width, (blocks // 2 + 1) * width), F32),
        ],
        compiler_params=pltpu.CompilerParams(vmem_limit_bytes=(60 if lead else 28) * 1024 * 1024),
        cost_estimate=pl.CostEstimate(
            flops=10**9 * len(ks), bytes_accessed=4 * 10**6, transcendentals=0
        ),
        name="assemble",
    )(*inputs, g)


def finish_kernel(sub, own_ref, r1_ref, r2_ref, r3_ref, e_ref, out_ref, vec_ref):
    width = own_ref.shape[1]
    p = lax.axis_index("tile") // sub
    blocks = out_ref.shape[1] // width
    many = blocks // 2

    def put(column, value):
        column = pl.multiple_of(((column + blocks) % blocks) * width, width)
        out_ref[:, pl.ds(column, width)] = value

    for d in range(many):
        put(p + d, own_ref[d * width : (d + 1) * width, :])
    for d, ref in ((1, r1_ref), (2, r2_ref), (3, r3_ref)):
        put(p - d, ref[...].astype(F32).T)
    tail = many * width + width // 2
    mine = own_ref[many * width : tail, :]
    other = e_ref[...].astype(F32)

    @pl.when(p < many)
    def _():
        put(p + many, jnp.concatenate([mine, other], axis=0))

    @pl.when(p >= many)
    def _():
        put(p + many, jnp.concatenate([other, mine], axis=0).T)

    vec_ref[...] = own_ref[tail : tail + 1, :] + own_ref[tail + 1 : tail + 2, :]


def gather_kernel(number, own_ref, *refs):
    crossed, total_ref, sends = refs[:number], refs[number], refs[number + 1 :]
    width = own_ref.shape[1]
    total = own_ref[...]
    for ref in crossed:
        total = total + ref[...].astype(F32)
    total_ref[...] = total
    for n, ref in enumerate(sends):
        at = (n + 1) * width
        ref[...] = total[at : at + ref.shape[0]].astype(BF16)


def gather(own, crossed, blocks):
    width = own.shape[1]
    vmem = pl.BlockSpec(memory_space=pltpu.VMEM)
    rows = [width] * (blocks // 2 - 1) + [width // 2]
    return pl.pallas_call(
        functools.partial(gather_kernel, len(crossed)),
        in_specs=[vmem] * (1 + len(crossed)),
        out_specs=[vmem] * (1 + len(rows)),
        out_shape=[jax.ShapeDtypeStruct(own.shape, F32)]
        + [jax.ShapeDtypeStruct((n, width), BF16) for n in rows],
        compiler_params=pltpu.CompilerParams(vmem_limit_bytes=8 * 1024 * 1024),
        name="gather",
    )(own, *crossed)


def finish(sub, own, r1, r2, r3, ext, blocks):
    width = own.shape[1]
    vmem = pl.BlockSpec(memory_space=pltpu.VMEM)
    return pl.pallas_call(
        functools.partial(finish_kernel, sub),
        in_specs=[vmem] * 5,
        out_specs=[vmem, vmem],
        out_shape=[
            jax.ShapeDtypeStruct((width, blocks * width), F32),
            jax.ShapeDtypeStruct((1, width), F32),
        ],
        compiler_params=pltpu.CompilerParams(vmem_limit_bytes=8 * 1024 * 1024),
        name="finish",
    )(own, r1, r2, r3, ext)


def local(
    tiles, global_deriv, local_deriv, hit_weight, hit_resid, block_ids, hit_count, track_region,
    block_place,
):
    regions = lax.axis_size("region")
    tracks, hits, width = global_deriv.shape
    blocks = block_place.shape[0]
    sub = tiles // blocks
    tile = lax.axis_index("tile")
    inputs = (
        block_place,
        track_region.reshape(1, tracks),
        hit_count.reshape(1, tracks),
        local_deriv.transpose(1, 2, 0).reshape(-1, tracks),
        hit_weight.T,
        hit_resid.T,
        block_ids.T,
    )

    def swap(value, even, odd):
        pairs = [(t, t ^ (sub * (odd if t // sub % 2 else even))) for t in range(tiles)]
        return lax.ppermute(value, "tile", pairs)

    def across(value, k):
        return lax.ppermute(value.astype(BF16), "region", [(r, r ^ k) for r in range(regions)])

    def near(keep, send):
        bit = 1
        while bit < sub:
            pairs = [(t, t ^ bit) for t in range(tiles)]
            keep, send = (v + lax.ppermute(v, "tile", pairs) for v in (keep, send))
            bit *= 2
        return keep, swap(send, 1, 1)

    def both(pair, part):
        return pair[0][part].astype(F32) + pair[1][part].astype(F32)

    low, top = slice(0, blocks // 4), slice(blocks // 4, blocks // 2)
    def after(value, other):
        return value if other is None else lax.optimization_barrier((value, other))[0]

    cores, firsts, seconds = ([None] * regions for _ in range(3))
    incoming = [[] for _ in range(regions)]
    own = None
    order = [*range(regions - 1, 2, -1), 1, 2, 0]

    def at(n):
        return order[n] if 0 <= n < regions else None

    for slot in range(regions + 3):
        done, operands = None, []
        if slot < regions:
            k = at(slot)
            keep, send, *made = assemble((k,), sub, inputs, global_deriv, blocks, regions)
            inputs = tuple(made) if made else inputs
            done = send
        elif slot == regions:
            done = both(cores[0], top)[:, 0].astype(BF16)
        k = at(slot - 3)

        def lowered(k, done):
            total = both(cores[k], low)[:, 0] + after(firsts[k], done).astype(F32)
            seconds[k] = total[0], swap(total[1].astype(BF16), 4, 2)
            return total[1].astype(BF16)

        if slot == regions + 1:
            done = lowered(at(slot - 2), done)
        if k is not None:
            total = seconds[k][0] + after(seconds[k][1], done).astype(F32)
            if k:
                for value in incoming[k]:
                    total = total + value.astype(F32)
                operands.append(total.astype(BF16))
                incoming[k - (k & -k)].append(across(operands[-1], k & -k))
            else:
                own = total
        k = at(slot - 2)
        if k is not None and slot <= regions:
            operands.append(lowered(k, (done, operands) if slot == regions else done))
        k = at(slot - 1)
        if k is not None:
            if slot < regions:
                cores[k] = after(cores[k], (done, operands) if slot == regions - 1 else done)
            operands.append(both(cores[k], top)[:, 0].astype(BF16))
            firsts[k] = swap(operands[-1], 2, 4)
        if slot < regions:
            inputs = inputs[0], after(inputs[1], (send, operands))
            cores[at(slot)] = near(keep, send)

    def onward(value, d):
        pairs = [
            (p * sub + s, ((p + d) % blocks) * sub + s) for p in range(blocks) for s in range(sub)
        ]
        return lax.ppermute(value, "tile", pairs)

    own, *sends = gather(own, incoming[0], blocks)
    matrix, vector = finish(sub, own, *(onward(v, d + 1) for d, v in enumerate(sends)), blocks)
    if sub > 1:
        part = tile % sub
        rows = width // sub
        matrix = lax.dynamic_slice(matrix, (part * rows, 0), (rows, blocks * width))
        vector = lax.dynamic_slice(vector, (0, part * rows), (1, rows))
    return matrix[None], vector


def solution(mesh):
    return jax.shard_map(
        functools.partial(local, mesh.shape["tile"]),
        mesh=mesh,
        in_specs=(
            P(("region", "tile"), None, None),
            P(("region", "tile"), None, None),
            P(("region", "tile"), None),
            P(("region", "tile"), None),
            P(("region", "tile"), None),
            P(("region", "tile")),
            P(("region", "tile"), None),
            P(),
        ),
        out_specs=(P("region", "tile", None), P("region", "tile")),
        check_vma=False,
    )
```

```python
import functools
import jax
import jax.numpy as jnp
from jax import lax
from jax.experimental import pallas as pl
from jax.experimental.pallas import tpu as pltpu
from jax.sharding import PartitionSpec as P

F32 = jnp.float32
BF16 = jnp.bfloat16
GROUP = 8
PAIR = 2 * GROUP
DEPTH = 256

NT = (((1,), (1,)), ((), ()))


def iota(shape, axis):
    return lax.broadcasted_iota(jnp.int32, shape, axis)


def fit(ld, weight, resid, counts):
    hits = weight.shape[0]
    live = iota(weight.shape, 0) < counts.astype(jnp.int32)
    masked_w = jnp.where(live, weight, 0.0)
    weighted_l = [v * masked_w for v in ld]
    gamma = [[None] * 5 for _ in range(5)]
    for a in range(5):
        for b in range(a + 1):
            gamma[a][b] = jnp.sum(weighted_l[a] * ld[b], axis=0, keepdims=True)
            if a == b:
                gamma[a][b] = gamma[a][b] + 1.0
    beta = [jnp.sum(weighted_l[a] * resid, axis=0, keepdims=True) for a in range(5)]
    factor = [[None] * 5 for _ in range(5)]
    inverse = [None] * 5
    for j in range(5):
        center = gamma[j][j]
        for k in range(j):
            center = center - factor[j][k] * factor[j][k]
        factor[j][j] = jnp.sqrt(center)
        inverse[j] = 1.0 / factor[j][j]
        for i in range(j + 1, 5):
            offdiag = gamma[i][j]
            for k in range(j):
                offdiag = offdiag - factor[i][k] * factor[j][k]
            factor[i][j] = offdiag * inverse[j]
    solved, rhs = [], []
    for j in range(5):
        current, target = weighted_l[j], beta[j]
        for k in range(j):
            current = current - factor[j][k] * solved[k]
            target = target - factor[j][k] * rhs[k]
        solved.append(current * inverse[j])
        rhs.append(target * inverse[j])
    projection = solved[0] * rhs[0]
    for k in range(1, 5):
        projection = projection + solved[k] * rhs[k]
    return solved, masked_w * resid - projection, masked_w


def prepare(
    place_ref, region_ref, count_ref, ld_ref, weight_ref, resid_ref, ids_ref, shared_ref, table_ref,
    table_copy,
):
    tracks = region_ref.shape[1]
    slots = table_ref.shape[1]
    groups = slots // GROUP
    hits = weight_ref.shape[0]
    depth = hits * GROUP
    lanes_at, column_at = groups * 5 * GROUP, groups * (5 * GROUP + 4)
    blocks = place_ref.shape[0]
    rr = table_ref.shape[0] - 8
    member = (iota((rr, tracks), 0) == region_ref[...]).astype(F32)
    before = (iota((tracks, tracks), 0) < iota((tracks, tracks), 1)).astype(F32).astype(BF16)
    rank = jnp.dot(member.astype(BF16), before, preferred_element_type=F32)
    count = jnp.sum(member, axis=1, keepdims=True)
    room = (count.astype(jnp.int32) + (PAIR - 1)) & -PAIR
    room = jnp.broadcast_to(room.astype(F32), (rr, slots))
    lower = (iota((rr, rr), 1) < iota((rr, rr), 0)).astype(F32)
    start = jnp.zeros((rr, slots), F32)
    for g in range(rr):
        start = start + lower[:, g : g + 1] * room[g : g + 1, :]
    slot = jnp.sum(member * (rank + start[:, 0:1]), axis=0, keepdims=True)
    perm = (iota((slots, tracks), 0) == slot.astype(jnp.int32)).astype(F32).astype(BF16)
    numbers = jnp.where(
        iota((8, tracks), 0) == 0, iota((8, tracks), 1), jnp.broadcast_to(count_ref[...], (8, tracks))
    )

    def sort(value):
        return lax.dot_general(value, perm, NT, preferred_element_type=F32)

    numbers = sort(numbers.astype(F32).astype(BF16))
    table_ref[0:8, :] = numbers.astype(jnp.int32)
    table_ref[8:, :] = jnp.where(
        iota((rr, slots), 1) == 0, start.astype(jnp.int32), (start + room).astype(jnp.int32)
    )
    table_copy.start()
    flat = sort(ld_ref[...])
    ld = [flat[c * hits : (c + 1) * hits] for c in range(5)]
    solved, hit_factor, masked_w = fit(
        ld, sort(weight_ref[...]), sort(resid_ref[...]), numbers[1:2]
    )
    ids = sort(ids_ref[...].astype(F32).astype(BF16))
    position = jnp.zeros_like(ids)
    for b in range(blocks):
        position = jnp.where(ids == float(b), place_ref[b].astype(F32), position)
    own = (iota((depth, slots), 0) // hits) == (iota((depth, slots), 1) % GROUP)

    def spread_out(value):
        return jnp.where(own, jnp.concatenate([value] * GROUP, axis=0), 0.0)

    grouping = (iota((groups, slots), 1) // GROUP == iota((groups, slots), 0)).astype(F32)
    for n, value in enumerate((masked_w, hit_factor)):
        value = lax.dot_general(
            grouping.astype(BF16), spread_out(value).astype(BF16), NT, preferred_element_type=F32
        )
        for half in range(2):
            at = lanes_at + (2 * n + half) * groups
            shared_ref[at : at + groups, :] = value[:, half * depth // 2 : (half + 1) * depth // 2]
    columns = 128
    grouping = (iota((columns, slots), 1) // GROUP == iota((columns, slots), 0)).astype(F32)
    shared_ref[column_at : column_at + depth, :columns] = lax.dot_general(
        spread_out(position).astype(BF16), grouping.astype(BF16), NT, preferred_element_type=F32
    )
    own = (iota((depth // 2, slots), 0) // hits) == (iota((depth // 2, slots), 1) % (GROUP // 2))
    for c in range(5):
        value = jnp.where(own, jnp.concatenate([solved[c]] * (GROUP // 2), axis=0), 0.0).T
        for g in range(groups):
            at = (g * 5 + c) * GROUP
            shared_ref[at : at + GROUP, :] = value[g * GROUP : (g + 1) * GROUP, :]


def one_step(step, at, table_ref, shared_ref, g_ref, g_s, direct_s, spread_s):
    hits, width = g_ref.shape[1:]
    depth = GROUP * hits
    blocks = spread_s.shape[1] // width
    rows = 5 * GROUP
    head = width + 8
    groups = table_ref.shape[1] // GROUP
    lanes_at, column_at = groups * rows, groups * (rows + 4)
    column = shared_ref[column_at : column_at + depth, :]
    early = iota((rows, depth // 2), 0) % GROUP < GROUP // 2

    def lanes(which, group):
        return jnp.concatenate(
            [
                shared_ref[pl.ds(lanes_at + (2 * which + half) * groups + group, 1), :]
                for half in range(2)
            ],
            axis=1,
        )

    lefts, values, positions = [], [], []
    for u in range(2):
        group = step * 2 + u
        for i in range(GROUP):
            g_s[u, i * hits : (i + 1) * hits, :] = g_ref[table_ref[0, group * GROUP + i]]
        g = g_s[u]
        chosen = jnp.full(column.shape, group, jnp.int32)
        position = jnp.take_along_axis(column, chosen, axis=1, mode="promise_in_bounds")
        turned = g.T.astype(F32)
        weighted = turned * lanes(0, group)
        factor = jnp.where(iota((8, depth), 0) == 0, lanes(1, group), 0.0)
        scaled = shared_ref[pl.ds(pl.multiple_of(group * rows, GROUP), rows), :]
        scaled = jnp.concatenate(
            [jnp.where(early, scaled, 0.0), jnp.where(early, 0.0, scaled)], axis=1
        )
        high = scaled.astype(BF16).astype(F32)
        left = jnp.concatenate([weighted, factor, high, scaled - high], axis=0)
        lefts.append(left.astype(BF16))
        values.append(g)
        positions.append(position.astype(BF16))
    for p in range(0, blocks, 2):
        columns = slice(p * width, (p + 2) * width)
        direct = direct_s[:, columns]
        for u in range(2):
            right = jnp.concatenate(
                [
                    jnp.where(positions[u] == jnp.bfloat16(q), values[u], jnp.bfloat16(0))
                    for q in (p, p + 1)
                ],
                axis=1,
            )
            total = jnp.dot(lefts[u], right, preferred_element_type=F32)
            direct = direct + total[:head]
            spread_s[pl.ds(pl.multiple_of(at + u * rows, GROUP), rows), columns] = (
                total[head : head + rows] + total[head + rows : head + 2 * rows]
            )
        direct_s[:, columns] = direct


EVEN = (0, 4, 2, 6)
ODD = (0, 2, 4, 6)


def lead_kernel(ks, sub, *refs):
    small, g_hbm, (keep_ref, send_ref, shared_ref, table_ref) = refs[:7], refs[7], refs[8:12]
    local_small, g_ref, table_s, sems, scratch = refs[12:19], refs[19], refs[20], refs[21], refs[22:]
    copies = [
        pltpu.make_async_copy(source, target, sems.at[n])
        for n, (source, target) in enumerate([*zip(small, local_small), (g_hbm, g_ref)])
    ]
    for copy in copies:
        copy.start()
    for copy in copies[:-1]:
        copy.wait()
    table_copy = pltpu.make_async_copy(table_ref, table_s, sems.at[0])
    prepare(*local_small, shared_ref, table_ref, table_copy)
    table_copy.wait()
    copies[-1].wait()

    def region(n, carry):
        assemble_region(
            n, ks, sub, table_s, shared_ref, g_ref, keep_ref, send_ref, *scratch
        )
        return carry

    lax.fori_loop(0, len(ks), region, 0)


def follow_kernel(ks, sub, shared_ref, table_ref, g_ref, *refs):
    def region(n, carry):
        assemble_region(n, ks, sub, table_ref, shared_ref, g_ref, *refs)
        return carry

    if len(ks) == 1:
        region(0, 0)
    else:
        lax.fori_loop(0, len(ks), region, 0)


def assemble_region(
    number, ks, sub, table_ref, shared_ref, g_ref,
    keep_ref, send_ref, g_s, direct_s, spread_s, wide_s, turned_s, acc_s,
):
    k = jnp.where(number == 0, ks[0], ks[-1])
    width = g_ref.shape[2]
    blocks = spread_s.shape[1] // width
    many = blocks // 2
    region = lax.axis_index("region") ^ k
    block = lax.axis_index("tile") // sub
    first = table_ref[8 + region, 0] // PAIR
    steps = table_ref[8 + region, 1] // PAIR - first
    direct_s[...] = jnp.zeros_like(direct_s)

    def group_step(n, carry):
        one_step(
            first + n, n * (10 * GROUP), table_ref, shared_ref, g_ref, g_s, direct_s, spread_s
        )
        return carry

    lax.fori_loop(0, steps, group_step, 0)
    used = steps * 10
    depth_tiles = DEPTH // 8
    chunks = jnp.maximum((used + depth_tiles - 1) // depth_tiles, 1)

    def clear(tile, carry):
        spread_s[pl.ds(pl.multiple_of(tile * 8, 8), 8), :] = jnp.zeros((8, blocks * width), F32)
        return carry

    lax.fori_loop(used, chunks * depth_tiles, clear, 0)

    def chunk_step(chunk, carry):
        at = pl.multiple_of(chunk * DEPTH, DEPTH)
        wide_s[...] = spread_s[pl.ds(at, DEPTH), :].astype(BF16)
        for p in range(blocks):
            turned = -wide_s[:, p * width : (p + 1) * width].T
            turned_s[p * width : (p + 1) * width] = turned
            if p < many:
                turned_s[(blocks + p) * width : (blocks + p + 1) * width] = turned

        def products(add):
            for q in range(0, blocks, 2):
                reach = many if q >= many else many - 1
                upper = (q + blocks - reach) % blocks
                value = jnp.dot(
                    turned_s[upper * width : (upper + reach + 2) * width],
                    wide_s[:, q * width : (q + 2) * width],
                    preferred_element_type=F32,
                )
                for r in range(reach + 2):
                    p = (upper + r) % blocks
                    for c in range(2):
                        d = reach - r + c
                        if 0 <= d <= many and (d < many or p < many):
                            part = value[r * width : (r + 1) * width, c * width : (c + 1) * width]
                            columns = slice(d * width, (d + 1) * width)
                            acc_s[p, :, columns] = acc_s[p, :, columns] + part if add else part

        @pl.when(chunk == 0)
        def _():
            products(False)

        @pl.when(chunk > 0)
        def _():
            products(True)

        return carry

    lax.fori_loop(0, chunks, chunk_step, 0)
    half = width // 2
    for n in range(blocks // 2):
        for odd, out_ref in ((0, keep_ref), (1, send_ref)):
            p = block ^ (jnp.where(block % 2 == 1 - odd, ODD[n], EVEN[n]) + odd)
            columns = pl.ds(pl.multiple_of(p * width, width), width)
            parts = [direct_s[0:width, columns] + acc_s[p, :, 0:width]]
            parts += [acc_s[p, :, d * width : (d + 1) * width] for d in range(1, many)]
            upper = pl.multiple_of((p // many) * half, half)
            parts.append(acc_s[p % many, pl.ds(upper, half), many * width :])
            row = direct_s[width : width + 1, columns]
            high = row.astype(BF16).astype(F32)
            sub = iota((16, width), 0)
            parts.append(jnp.where(sub == 0, high, jnp.where(sub == 1, row - high, 0.0)))
            out_ref[n, number] = jnp.concatenate(parts, axis=0).astype(BF16)


def assemble(ks, sub, inputs, g, blocks, regions):
    tracks, hits, width = g.shape
    lead = len(inputs) == 7
    rows = width * (blocks // 2) + width // 2 + 16
    longest = -(-(-(-tracks // PAIR) * 5 * PAIR) // DEPTH) * DEPTH
    rr = -(-regions // 8) * 8
    slots = -(-(tracks + regions * (PAIR - 1)) // 128) * 128
    shared = [
        jax.ShapeDtypeStruct(
            (slots // GROUP * (5 * GROUP + 4) + GROUP * hits, GROUP * hits // 2), F32
        ),
        jax.ShapeDtypeStruct((8 + rr, slots), jnp.int32),
    ]
    out = jax.ShapeDtypeStruct((blocks // 2, len(ks), rows, width), BF16)
    vmem = pl.BlockSpec(memory_space=pltpu.VMEM)
    smem = pl.BlockSpec(memory_space=pltpu.SMEM)
    copies = [pltpu.SMEM(inputs[0].shape, jnp.int32)]
    copies += [pltpu.VMEM(value.shape, value.dtype) for value in inputs[1:]]
    copies += [
        pltpu.VMEM(g.shape, g.dtype),
        pltpu.SMEM(shared[1].shape, jnp.int32),
        pltpu.SemaphoreType.DMA((8,)),
    ]
    return pl.pallas_call(
        functools.partial(lead_kernel if lead else follow_kernel, ks, sub),
        in_specs=[pl.BlockSpec(memory_space=pltpu.HBM)] * 8 if lead else [vmem, smem, vmem],
        out_specs=[vmem] * (4 if lead else 2),
        out_shape=[out, out] + shared * lead,
        scratch_shapes=copies * lead
        + [
            pltpu.VMEM((2, GROUP * hits, width), BF16),
            pltpu.VMEM((width + 8, blocks * width), F32),
            pltpu.VMEM((longest, blocks * width), F32),
            pltpu.VMEM((DEPTH, blocks * width), BF16),
            pltpu.VMEM(((blocks + blocks // 2) * width, DEPTH), BF16),
            pltpu.VMEM((blocks, width, (blocks // 2 + 1) * width), F32),
        ],
        compiler_params=pltpu.CompilerParams(vmem_limit_bytes=(60 if lead else 28) * 1024 * 1024),
        cost_estimate=pl.CostEstimate(
            flops=10**9 * len(ks), bytes_accessed=4 * 10**6, transcendentals=0
        ),
        name="assemble",
    )(*inputs, g)


def finish_kernel(sub, own_ref, r1_ref, r2_ref, r3_ref, e_ref, out_ref, vec_ref):
    width = own_ref.shape[1]
    p = lax.axis_index("tile") // sub
    blocks = out_ref.shape[1] // width
    many = blocks // 2

    def put(column, value):
        column = pl.multiple_of(((column + blocks) % blocks) * width, width)
        out_ref[:, pl.ds(column, width)] = value

    for d in range(many):
        put(p + d, own_ref[d * width : (d + 1) * width, :])
    for d, ref in ((1, r1_ref), (2, r2_ref), (3, r3_ref)):
        put(p - d, ref[...].astype(F32).T)
    tail = many * width + width // 2
    mine = own_ref[many * width : tail, :]
    other = e_ref[...].astype(F32)

    @pl.when(p < many)
    def _():
        put(p + many, jnp.concatenate([mine, other], axis=0))

    @pl.when(p >= many)
    def _():
        put(p + many, jnp.concatenate([other, mine], axis=0).T)

    vec_ref[...] = own_ref[tail : tail + 1, :] + own_ref[tail + 1 : tail + 2, :]


def gather_kernel(number, own_ref, *refs):
    crossed, total_ref, sends = refs[:number], refs[number], refs[number + 1 :]
    width = own_ref.shape[1]
    total = own_ref[...]
    for ref in crossed:
        total = total + ref[...].astype(F32)
    total_ref[...] = total
    for n, ref in enumerate(sends):
        at = (n + 1) * width
        ref[...] = total[at : at + ref.shape[0]].astype(BF16)


def gather(own, crossed, blocks):
    width = own.shape[1]
    vmem = pl.BlockSpec(memory_space=pltpu.VMEM)
    rows = [width] * (blocks // 2 - 1) + [width // 2]
    return pl.pallas_call(
        functools.partial(gather_kernel, len(crossed)),
        in_specs=[vmem] * (1 + len(crossed)),
        out_specs=[vmem] * (1 + len(rows)),
        out_shape=[jax.ShapeDtypeStruct(own.shape, F32)]
        + [jax.ShapeDtypeStruct((n, width), BF16) for n in rows],
        compiler_params=pltpu.CompilerParams(vmem_limit_bytes=8 * 1024 * 1024),
        name="gather",
    )(own, *crossed)


def finish(sub, own, r1, r2, r3, ext, blocks):
    width = own.shape[1]
    vmem = pl.BlockSpec(memory_space=pltpu.VMEM)
    return pl.pallas_call(
        functools.partial(finish_kernel, sub),
        in_specs=[vmem] * 5,
        out_specs=[vmem, vmem],
        out_shape=[
            jax.ShapeDtypeStruct((width, blocks * width), F32),
            jax.ShapeDtypeStruct((1, width), F32),
        ],
        compiler_params=pltpu.CompilerParams(vmem_limit_bytes=8 * 1024 * 1024),
        name="finish",
    )(own, r1, r2, r3, ext)


def local(
    tiles, global_deriv, local_deriv, hit_weight, hit_resid, block_ids, hit_count, track_region,
    block_place,
):
    regions = lax.axis_size("region")
    tracks, hits, width = global_deriv.shape
    blocks = block_place.shape[0]
    sub = tiles // blocks
    tile = lax.axis_index("tile")
    inputs = (
        block_place,
        track_region.reshape(1, tracks),
        hit_count.reshape(1, tracks),
        local_deriv.transpose(1, 2, 0).reshape(-1, tracks),
        hit_weight.T,
        hit_resid.T,
        block_ids.T,
    )

    def swap(value, even, odd):
        pairs = [(t, t ^ (sub * (odd if t // sub % 2 else even))) for t in range(tiles)]
        return lax.ppermute(value, "tile", pairs)

    def across(value, k):
        return lax.ppermute(value.astype(BF16), "region", [(r, r ^ k) for r in range(regions)])

    def near(keep, send):
        bit = 1
        while bit < sub:
            pairs = [(t, t ^ bit) for t in range(tiles)]
            keep, send = (v + lax.ppermute(v, "tile", pairs) for v in (keep, send))
            bit *= 2
        return keep, swap(send, 1, 1)

    def both(pair, part):
        return pair[0][part].astype(F32) + pair[1][part].astype(F32)

    low, top = slice(0, blocks // 4), slice(blocks // 4, blocks // 2)
    def after(value, other):
        return value if other is None else lax.optimization_barrier((value, other))[0]

    cores, firsts, seconds = ([None] * regions for _ in range(3))
    incoming = [[] for _ in range(regions)]
    own = None
    for slot in range(regions + 3):
        done, operands = None, []
        if slot < regions:
            k = regions - 1 - slot
            keep, send, *made = assemble((k,), sub, inputs, global_deriv, blocks, regions)
            inputs = tuple(made) if made else inputs
            done = send
        elif slot == regions:
            done = both(cores[0], top)[:, 0].astype(BF16)
        k = regions - 1 - (slot - 3)

        def lowered(k, done):
            total = both(cores[k], low)[:, 0] + after(firsts[k], done).astype(F32)
            seconds[k] = total[0], swap(total[1].astype(BF16), 4, 2)
            return total[1].astype(BF16)

        if slot > regions and k > 0:
            done = lowered(k - 1, done)
        if 0 <= k < regions:
            total = seconds[k][0] + after(seconds[k][1], done).astype(F32)
            if k:
                for value in incoming[k]:
                    total = total + value.astype(F32)
                operands.append(total.astype(BF16))
                incoming[k - (k & -k)].append(across(operands[-1], k & -k))
            else:
                own = total
        k -= 1
        if 0 <= k < regions and slot <= regions:
            operands.append(lowered(k, (done, operands) if slot == regions else done))
        k -= 1
        if 0 <= k < regions:
            if slot < regions:
                cores[k] = after(cores[k], (done, operands) if slot == regions - 1 else done)
            operands.append(both(cores[k], top)[:, 0].astype(BF16))
            firsts[k] = swap(operands[-1], 2, 4)
        if slot < regions:
            inputs = inputs[0], after(inputs[1], (send, operands))
            cores[k - 1] = near(keep, send)

    def onward(value, d):
        pairs = [
            (p * sub + s, ((p + d) % blocks) * sub + s) for p in range(blocks) for s in range(sub)
        ]
        return lax.ppermute(value, "tile", pairs)

    own, *sends = gather(own, incoming[0], blocks)
    matrix, vector = finish(sub, own, *(onward(v, d + 1) for d, v in enumerate(sends)), blocks)
    if sub > 1:
        part = tile % sub
        rows = width // sub
        matrix = lax.dynamic_slice(matrix, (part * rows, 0), (rows, blocks * width))
        vector = lax.dynamic_slice(vector, (0, part * rows), (1, rows))
    return matrix[None], vector


def solution(mesh):
    return jax.shard_map(
        functools.partial(local, mesh.shape["tile"]),
        mesh=mesh,
        in_specs=(
            P(("region", "tile"), None, None),
            P(("region", "tile"), None, None),
            P(("region", "tile"), None),
            P(("region", "tile"), None),
            P(("region", "tile"), None),
            P(("region", "tile")),
            P(("region", "tile"), None),
            P(),
        ),
        out_specs=(P("region", "tile", None), P("region", "tile")),
        check_vma=False,
    )
```
